32 devices in a mesh: case: 2 (over y), px: 4 (over z), py: 4 (over x, core).
Axes of the slice: x: 2, y: 2, z: 4, core: 2. Of those that a mesh axis runs over, the one named last changes fastest.
Arguments:
- prior_basis: float32 [256, 8, 16, 128], P('case', 'px', 'py'), parts along dimension 0, may hold values from -6 to 6
- previous: float32 [64, 8, 16, 128], P('case', 'px', 'py'), parts along dimension 0, may hold values from -6 to 6
- neighbours: int32 [5, 8, 16], P(None, 'px', 'py'), may hold values from 0 to 8
- tile_kinds: int32 [5, 8, 16], P(None, 'px', 'py'), may hold values from 0 to 7
- stiff_tiles: float32 [8, 128, 128], replicated, may hold values from -0.3 to 0.3
- mass_tiles: float32 [8, 128, 128], replicated, may hold values from -0.18 to 0.18
Outputs:
- new_block: float32 [64, 8, 16, 128], P('case', 'px', 'py'), parts along dimension 0
- coupling: float32 [256, 32], P('case'), parts along dimension 0
- r_factor: float32 [64, 32], P('case'), parts along dimension 0
- reduced: float32 [4, 160, 32], P('case'), parts along dimension 0
The draws below stay inside these ranges and needn't reach their ends.
There are 2 independent parts, one for each index of `case`. The reference program is written for one: setup_inputs(seed, part) draws one part's arguments, and reference() takes and returns one part's arrays. A program takes and returns all parts, laid end to end along the dimension named above; an argument that names none is the same for every part. Nothing has to cross between parts.
Inputs may be any that keep to these rules, and one draw needn't show every extreme that they name: `neighbours`: entry v couples a tile to the tile offset by (v // 3 - 1, v % 3 - 1) along the two tile indices.
All inputs are finite; a program needn't handle non-finite values.
Results may differ from the reference program's by a relative error of at most 0.0003.
Values sent between devices are 32-bit elements; how exact they have to be, the bound alone decides.
No kernel may reach another device: no remote copies, remote signals or barrier semaphores. Data moves between devices by JAX's collectives and lax.ppermute only.
A program may use at most 64 MiB of HBM per device.

```python
import jax
import jax.numpy as jnp
from jax import lax

B = 32
NB = 128
TILE = 128
NNZ = 5
LIB = 8
GX = 8
GY = 16
ROWS = 16384


def with_ends(result, stream_key, smallest, high):
    place = [jax.random.randint(jax.random.fold_in(stream_key, axis), (), 0, length) for axis, length in enumerate(result.shape)]
    widest = result.shape.index(max(result.shape))
    beside = place[:widest] + [(place[widest] + 1) % result.shape[widest]] + place[widest + 1:]
    return result.at[tuple(place)].set(smallest).at[tuple(beside)].set(high)


def level_of(own_key, shape, cuts, least, top_value):
    loudness, own = 1.0, jax.random.fold_in(own_key, 6)
    for dim, blocks in cuts:
        heights = jnp.exp(jax.random.uniform(jax.random.fold_in(own, dim), (blocks,), jnp.float32, least / len(cuts), top_value / len(cuts)))
        loudness = loudness * jnp.repeat(heights, shape[dim] // blocks).reshape([-1 if axis == dim else 1 for axis in range(len(shape))])
    return loudness


def noise(rng, extent, deviation, limit, shards=(), held_as=jnp.bfloat16):
    values = jax.random.normal(rng, extent, jnp.float32) * deviation
    if len(shards) > 0:
        values = level_of(rng, extent, shards, -0.22, 0.18) * values
    return jnp.clip(values, min=-limit, max=limit).astype(held_as)


def setup_inputs(seed: int = 0, part: int = 0) -> dict:
    arg_keys = jax.random.split(jax.random.key(seed), 7)
    own_keys = jax.random.split(jax.random.fold_in(arg_keys[6], part), 7)
    prior_basis = noise(own_keys[0], (NB, GX, GY, TILE), 1.0, 6.0, ((1, 4), (2, 4)), jnp.float32)
    previous = noise(own_keys[1], (B, GX, GY, TILE), 1.0, 6.0, ((1, 4), (2, 4)), jnp.float32)
    neighbours = with_ends(jax.random.randint(arg_keys[2], (NNZ, GX, GY), 0, 9), jax.random.fold_in(arg_keys[2], 1), 0, 8).astype(jnp.int32)
    tile_kinds = with_ends(jax.random.randint(arg_keys[3], (NNZ, GX, GY), 0, LIB), jax.random.fold_in(arg_keys[3], 1), 0, LIB - 1).astype(jnp.int32)
    stiff_tiles = noise(arg_keys[4], (LIB, TILE, TILE), 0.05, 0.3, (), jnp.float32)
    mass_tiles = noise(arg_keys[5], (LIB, TILE, TILE), 0.03, 0.18, (), jnp.float32)
    return {"prior_basis": prior_basis, "previous": previous, "neighbours": neighbours, "tile_kinds": tile_kinds, "stiff_tiles": stiff_tiles, "mass_tiles": mass_tiles}


def row_product(pieces):
    chosen_row, kind_row, tile_table = pieces
    return jnp.einsum('byc,ycd->byd', chosen_row, tile_table[kind_row], precision=lax.Precision.HIGHEST)

def apply_pattern(field, neighbours, tile_kinds, tile_table, diagonal):
    count_x, count_y = (field.shape[1], field.shape[2])
    padded = jnp.pad(field, ((0, 0), (1, 1), (1, 1), (0, 0)))
    result_sum = diagonal * field
    for entry_index in range(NNZ):
        chosen = jnp.zeros_like(field)
        for neighbour in range(9):
            shifted = padded[:, neighbour // 3:neighbour // 3 + count_x, neighbour % 3:neighbour % 3 + count_y, :]
            chosen = chosen + jnp.where((neighbours[entry_index] == neighbour)[None, :, :, None], shifted, jnp.zeros_like(shifted))

        def one_row(pieces):
            return row_product((pieces[0], pieces[1], tile_table))
        moved = lax.map(one_row, (jnp.moveaxis(chosen, 1, 0), tile_kinds[entry_index]))
        result_sum = result_sum + jnp.moveaxis(moved, 0, 1)
    return result_sum

def pair_products(left, right):
    return jnp.einsum('nxyt,bxyt->nb', left, right, precision=lax.Precision.HIGHEST) / ROWS

def reference(prior_basis, previous, neighbours, tile_kinds, stiff_tiles, mass_tiles):
    current = prior_basis[NB - B:]
    residual = apply_pattern(current, neighbours, tile_kinds, stiff_tiles, 4.0) + apply_pattern(previous, neighbours, tile_kinds, mass_tiles, 1.0)
    coupling = pair_products(prior_basis, residual)
    weighted = residual - jnp.einsum('nb,nxyt->bxyt', coupling, prior_basis, precision=lax.Precision.HIGHEST)
    gram = pair_products(weighted, weighted)
    lower_factor = jnp.linalg.cholesky(gram)
    new_block = jax.scipy.linalg.solve_triangular(lower_factor, weighted.reshape(B, -1), lower=True).reshape(weighted.shape)
    stiff_new = apply_pattern(new_block, neighbours, tile_kinds, stiff_tiles, 4.0)
    mass_new = apply_pattern(new_block, neighbours, tile_kinds, mass_tiles, 1.0)
    reduced = jnp.stack([jnp.concatenate([pair_products(prior_basis, stiff_new), pair_products(new_block, stiff_new)], axis=0), jnp.concatenate([pair_products(prior_basis, mass_new), pair_products(new_block, mass_new)], axis=0)])
    return (new_block, coupling, lower_factor.T, reduced)
```

```python
import jax
import jax.numpy as jnp
from jax import lax
from jax.sharding import PartitionSpec as P

NNZ = 5
HIGHEST = lax.Precision.HIGHEST


def extended(block, sides, width):
    for axis, dim in sides:
        count = lax.axis_size(axis)
        forward = [(i, i + 1) for i in range(count - 1)]
        backward = [(target, source) for source, target in forward]
        low = lax.ppermute(
            lax.slice_in_dim(block, block.shape[dim] - width, None, axis=dim), axis, forward
        )
        high = lax.ppermute(lax.slice_in_dim(block, 0, width, axis=dim), axis, backward)
        block = jnp.concatenate([low, block, high], axis=dim)
    return block


def chosen_tiles(padded, center, neighbours, entry_index):
    count_x, count_y = (center.shape[1], center.shape[2])
    chosen = jnp.zeros_like(center)
    for neighbour in range(9):
        shifted = padded[
            :,
            neighbour // 3 : neighbour // 3 + count_x,
            neighbour % 3 : neighbour % 3 + count_y,
            :,
        ]
        chosen = chosen + jnp.where(
            (neighbours[entry_index] == neighbour)[None, :, :, None],
            shifted,
            jnp.zeros_like(shifted),
        )
    return chosen


def tile_products(chosen, tile_blocks):
    return jnp.einsum("bxyc,xycd->bxyd", chosen, tile_blocks, precision=HIGHEST)


def pair_products(left, right):
    return jnp.einsum("nxyt,bxyt->nb", left, right, precision=HIGHEST)


def butterfly_sum(value):
    for axis in ("py", "px"):
        count = lax.axis_size(axis)
        step = 1
        while step < count:
            swap = [(i, i ^ step) for i in range(count)]
            value = value + lax.ppermute(value, axis, swap)
            step *= 2
    return value


def exchange_sum(value):
    axes = ("px", "py")
    count = lax.axis_size(axes)
    copies = jnp.broadcast_to(value[None], (count,) + value.shape)
    return jnp.sum(lax.all_to_all(copies, axes, 0, 0), axis=0)


def shards(prior_basis, previous, neighbours, tile_kinds, stiff_tiles, mass_tiles):
    block = previous.shape[0]
    prior = prior_basis.shape[0]
    total_rows = (
        prior_basis.shape[1]
        * prior_basis.shape[2]
        * prior_basis.shape[3]
        * lax.axis_size("px")
        * lax.axis_size("py")
    )
    inverse_rows = 1.0 / total_rows
    both = jnp.concatenate([prior_basis[prior - block :], previous], axis=0)
    padded = extended(both, (("px", 1), ("py", 2)), 1)
    residual = 4.0 * both[:block] + both[block:]
    stiff_blocks = [stiff_tiles[tile_kinds[k]] for k in range(NNZ)]
    mass_blocks = [mass_tiles[tile_kinds[k]] for k in range(NNZ)]
    for k in range(NNZ):
        chosen = chosen_tiles(padded, both, neighbours, k)
        residual = residual + tile_products(chosen[:block], stiff_blocks[k])
        residual = residual + tile_products(chosen[block:], mass_blocks[k])
    coupling = exchange_sum(pair_products(prior_basis, residual)) * inverse_rows
    weighted = residual - jnp.einsum("nb,nxyt->bxyt", coupling, prior_basis, precision=HIGHEST)
    padded = extended(weighted, (("px", 1), ("py", 2)), 1)
    stiff_weighted = 4.0 * weighted
    mass_weighted = weighted
    for k in range(NNZ):
        chosen = chosen_tiles(padded, weighted, neighbours, k)
        stiff_weighted = stiff_weighted + tile_products(chosen, stiff_blocks[k])
        mass_weighted = mass_weighted + tile_products(chosen, mass_blocks[k])
    left = jnp.concatenate([prior_basis, weighted], axis=0)
    right = jnp.concatenate([stiff_weighted, mass_weighted, weighted], axis=0)
    sums = butterfly_sum(pair_products(left, right)) * inverse_rows
    gram = sums[prior:, 2 * block :]
    lower = jnp.linalg.cholesky(gram)
    inverse = jax.scipy.linalg.solve_triangular(
        lower, jnp.eye(block, dtype=jnp.float32), lower=True
    )
    new_block = jnp.einsum("ab,bxyt->axyt", inverse, weighted, precision=HIGHEST)
    rows = jnp.concatenate(
        [sums[:prior], jnp.dot(inverse, sums[prior:], precision=HIGHEST)], axis=0
    )
    rows = rows[:, : 2 * block].reshape(-1, 2, block)
    reduced = jnp.einsum("nmb,ab->mna", rows, inverse, precision=HIGHEST)
    return (new_block, coupling, lower.T, reduced)


def solution(mesh):
    placed = (
        P("case", "px", "py", None),
        P("case", "px", "py", None),
        P(None, "px", "py"),
        P(None, "px", "py"),
        P(),
        P(),
    )
    return jax.shard_map(
        shards,
        mesh=mesh,
        in_specs=placed,
        out_specs=(
            P("case", "px", "py", None),
            P("case", None),
            P("case", None),
            P("case", None, None),
        ),
        check_vma=False,
    )
```

```python
import functools

import jax
import jax.numpy as jnp
from jax import lax
from jax.experimental import pallas as pl
from jax.experimental.pallas import tpu as pltpu
from jax.sharding import PartitionSpec as P

F32 = jnp.float32
BF16 = jnp.bfloat16
VMEM = pl.BlockSpec(memory_space=pltpu.VMEM)
SMEM = pl.BlockSpec(memory_space=pltpu.SMEM)
PARAMS = pltpu.CompilerParams(vmem_limit_bytes=24 * 1024 * 1024)


def split(value):
    high = value.astype(BF16)
    return high, (value - high.astype(F32)).astype(BF16)


def mul(left, right):
    return jnp.dot(left, right, preferred_element_type=F32)


def mul_t(left, right):
    return lax.dot_general(left, right, (((1,), (1,)), ((), ())), preferred_element_type=F32)


def mul3(left, right):
    left_high, left_low = split(left)
    right_high, right_low = split(right)
    return mul(left_high, right_high) + (mul(left_high, right_low) + mul(left_low, right_high))


def mul3_t(left, right):
    left_high, left_low = split(left)
    right_high, right_low = split(right)
    return mul_t(left_high, right_high) + (
        mul_t(left_high, right_low) + mul_t(left_low, right_high)
    )


def tables_kernel(stiff_ref, mass_ref, high_ref, low_ref):
    side = stiff_ref.shape[1]
    for kind in range(stiff_ref.shape[0]):
        for place, ref in enumerate((stiff_ref, mass_ref)):
            high, low = split(ref[kind])
            high_ref[kind, place * side : (place + 1) * side, :] = high
            low_ref[kind, place * side : (place + 1) * side, :] = low


def pack_kernel(count_x, count_y, basis_ref, previous_ref, low_ref, high_ref):
    tiles = count_x * count_y
    block = previous_ref.shape[0] // tiles
    first = basis_ref.shape[0] - block * tiles
    for row, ref in ((0, low_ref), (count_x - 1, high_ref)):
        for j in range(count_y):
            tile = row * count_y + j
            ref[j, :block, :] = basis_ref[pl.ds(first + tile, block, stride=tiles), :]
            ref[j, block:, :] = previous_ref[pl.ds(tile, block, stride=tiles), :]


def fill_extended(ext_ref, store, rows, sides):
    width = len(rows) and rows[0].shape[0]
    for i, row in enumerate(rows):
        for j in range(width):
            store(ext_ref, i * (width + 2) + j + 1, row[j])
    for i in range(len(rows)):
        store(ext_ref, i * (width + 2), sides[0][i])
        store(ext_ref, i * (width + 2) + width + 1, sides[1][i])


def source_of(neighbours_ref, k, tile, count_y):
    neighbour = neighbours_ref[k, tile]
    down = neighbour // 3
    return (tile // count_y + down) * (count_y + 2) + tile % count_y + neighbour - 3 * down


def residual_kernel(
    neighbours_ref,
    kinds_ref,
    low_ref,
    high_ref,
    from_low_ref,
    from_high_ref,
    side_low_ref,
    side_high_ref,
    basis_ref,
    table_high_ref,
    table_low_ref,
    residual_low_ref,
    residual_high_ref,
    partial_ref,
    ext_ref,
):
    count_y = low_ref.shape[0]
    block = low_ref.shape[1] // 2
    tiles = 2 * count_y
    prior = basis_ref.shape[0] // tiles

    def store(ext, place, value):
        for part in range(2):
            high, low = split(value[part * block : (part + 1) * block])
            ext[place, :block, part * 128 : (part + 1) * 128] = high
            ext[place, block:, part * 128 : (part + 1) * 128] = low

    fill_extended(
        ext_ref,
        store,
        (from_low_ref, low_ref, high_ref, from_high_ref),
        (side_low_ref, side_high_ref),
    )
    partial = jnp.zeros((block, prior), F32)
    for tile in range(tiles):
        own = (low_ref, high_ref)[tile // count_y][tile % count_y]
        total = 4.0 * own[:block] + own[block:]
        for k in range(neighbours_ref.shape[0]):
            source = source_of(neighbours_ref, k, tile, count_y)
            kind = kinds_ref[k, tile]
            chosen = ext_ref[source]
            both = mul(chosen, table_high_ref[kind])
            total = total + (
                both[:block] + (both[block:] + mul(chosen[:block], table_low_ref[kind]))
            )
        (residual_low_ref, residual_high_ref)[tile // count_y][tile % count_y] = total
        partial = partial + mul3_t(total, basis_ref[pl.ds(tile, prior, stride=tiles), :])
    partial_ref[...] = partial


def weighted_kernel(
    inverse_rows,
    partial_ref,
    other_ref,
    residual_low_ref,
    residual_high_ref,
    basis_ref,
    weighted_low_ref,
    weighted_high_ref,
    coupling_ref,
):
    count_y = residual_low_ref.shape[0]
    tiles = 2 * count_y
    prior = basis_ref.shape[0] // tiles
    coupling = (partial_ref[...] + other_ref[...]) * inverse_rows
    for tile in range(tiles):
        place = (tile // count_y, tile % count_y)
        moved = mul3(coupling, basis_ref[pl.ds(tile, prior, stride=tiles), :])
        (weighted_low_ref, weighted_high_ref)[place[0]][place[1]] = (
            (residual_low_ref, residual_high_ref)[place[0]][place[1]] - moved
        )
    coupling_ref[...] = coupling.T


def operators_kernel(
    neighbours_ref,
    kinds_ref,
    low_ref,
    high_ref,
    from_low_ref,
    from_high_ref,
    side_low_ref,
    side_high_ref,
    basis_ref,
    table_high_ref,
    table_low_ref,
    sums_ref,
    ext_ref,
):
    count_y, block, side = low_ref.shape
    tiles = 2 * count_y
    prior = basis_ref.shape[0] // tiles

    def store(ext, place, value):
        high, low = split(value)
        ext[place, :block, :] = high
        ext[place, block:, :] = low

    fill_extended(
        ext_ref,
        store,
        (from_low_ref, low_ref, high_ref, from_high_ref),
        (side_low_ref, side_high_ref),
    )
    with_basis = jnp.zeros((2 * block, prior), F32)
    with_own = jnp.zeros((block, 4 * block), F32)
    for tile in range(tiles):
        own = (low_ref, high_ref)[tile // count_y][tile % count_y]
        totals = [4.0 * own, own]
        for k in range(neighbours_ref.shape[0]):
            source = source_of(neighbours_ref, k, tile, count_y)
            kind = kinds_ref[k, tile]
            chosen = ext_ref[source]
            for part in range(2):
                span = slice(part * side, (part + 1) * side)
                both = mul(chosen, table_high_ref[kind, span, :])
                totals[part] = totals[part] + (
                    both[:block] + (both[block:] + mul(chosen[:block], table_low_ref[kind, span, :]))
                )
        applied = jnp.concatenate(totals, axis=0)
        with_basis = with_basis + mul3_t(applied, basis_ref[pl.ds(tile, prior, stride=tiles), :])
        right = jnp.concatenate([applied, own, jnp.zeros_like(own)], axis=0)
        with_own = with_own + mul3_t(own, right)
    sums_ref[: 2 * block, :] = with_basis
    sums_ref[2 * block :, :] = with_own


def factor_kernel(
    inverse_rows,
    sums_ref,
    weighted_low_ref,
    weighted_high_ref,
    new_ref,
    factor_ref,
    reduced_ref,
):
    count_y, block, _ = weighted_low_ref.shape
    prior = sums_ref.shape[1]
    tiles = 2 * count_y
    with_own = sums_ref[2 * block :, :] * inverse_rows
    gram = with_own[:, 2 * block : 3 * block]
    row_ids = lax.broadcasted_iota(jnp.int32, (block, block), 0)
    column_ids = lax.broadcasted_iota(jnp.int32, (block, block), 1)
    unit = jnp.where(row_ids == column_ids, 1.0, 0.0).astype(F32)
    work = jnp.concatenate([gram, unit], axis=1)
    rows = lax.broadcasted_iota(jnp.int32, (block, 1), 0)
    scale = jnp.zeros((block, 1), F32)
    for j in range(block):
        row = work[j : j + 1, :]
        pivot = row[:, j : j + 1]
        ratio = work[:, j : j + 1] / pivot
        scale = jnp.where(rows == j, lax.rsqrt(pivot), scale)
        work = work - jnp.where(rows > j, ratio, 0.0) * row
    work = work * scale
    factor_ref[...] = jnp.where(column_ids >= row_ids, work[:, :block], 0.0)
    inverse = work[:, block:]
    for tile in range(tiles):
        own = (weighted_low_ref, weighted_high_ref)[tile // count_y][tile % count_y]
        new_ref[pl.ds(tile, block, stride=tiles), :] = mul3(inverse, own)
    for part in range(2):
        span = slice(part * block, (part + 1) * block)
        from_basis = mul3(inverse, sums_ref[span, :] * inverse_rows)
        reduced_ref[part, :prior, :] = from_basis.T
        reduced_ref[part, prior:, :] = mul3_t(mul3(inverse, with_own[:, span]), inverse)


def swap(value, axis, step):
    count = lax.axis_size(axis)
    return lax.ppermute(value, axis, [(i, i ^ step) for i in range(count)])


def butterfly_steps():
    steps = []
    for axis in ("py", "px"):
        step = 1
        while step < lax.axis_size(axis):
            steps.append((axis, step))
            step *= 2
    return steps


def halved_sum(value):
    half = value.shape[0] // 2
    upper = lax.axis_index("py") % 2 == 1
    first, second = value[:half], value[half:]
    kept = jnp.where(upper, second, first)
    kept = kept + swap(jnp.where(upper, first, second), "py", 1)
    for axis, step in butterfly_steps()[1:]:
        kept = kept + swap(kept, axis, step)
    other = swap(kept, "py", 1)
    return jnp.concatenate(
        [jnp.where(upper, other, kept), jnp.where(upper, kept, other)], axis=0
    )


def line(value, axis, forward):
    count = lax.axis_size(axis)
    pairs = [(i, i + 1) for i in range(count - 1)]
    if not forward:
        pairs = [(target, source) for source, target in pairs]
    return lax.ppermute(value, axis, pairs)


def halo(low, high):
    from_low = line(high, "px", True)
    from_high = line(low, "px", False)
    rows = (from_low, low, high, from_high)
    side_low = line(jnp.concatenate([row[-1:] for row in rows], axis=0), "py", True)
    side_high = line(jnp.concatenate([row[:1] for row in rows], axis=0), "py", False)
    return from_low, from_high, side_low, side_high


def shape(*dims, dtype=F32):
    return jax.ShapeDtypeStruct(dims, dtype)


def shards(prior_basis, previous, neighbours, tile_kinds, stiff_tiles, mass_tiles):
    block = previous.shape[0]
    prior, count_x, count_y, side = prior_basis.shape
    tiles = count_x * count_y
    inverse_rows = 1.0 / (tiles * side * lax.axis_size("px") * lax.axis_size("py"))
    basis = prior_basis.reshape(-1, side)
    neighbours = neighbours.reshape(-1, tiles)
    tile_kinds = tile_kinds.reshape(-1, tiles)
    places = 4 * (count_y + 2)

    def call(kernel, inputs, outputs, scratch=(), smem=0):
        return pl.pallas_call(
            kernel,
            out_shape=outputs,
            in_specs=[SMEM] * smem + [VMEM] * (len(inputs) - smem),
            out_specs=[VMEM] * len(outputs),
            scratch_shapes=scratch,
            compiler_params=PARAMS,
        )(*inputs)

    low, high = call(
        functools.partial(pack_kernel, count_x, count_y),
        (basis, previous.reshape(-1, side)),
        [shape(count_y, 2 * block, side)] * 2,
    )
    table_high, table_low = call(
        tables_kernel,
        (stiff_tiles, mass_tiles),
        [shape(stiff_tiles.shape[0], 2 * side, side, dtype=BF16)] * 2,
    )
    residual_low, residual_high, partial = call(
        residual_kernel,
        (neighbours, tile_kinds, low, high, *halo(low, high), basis, table_high, table_low),
        [shape(count_y, block, side)] * 2 + [shape(block, prior)],
        [pltpu.VMEM((places, 2 * block, 2 * side), BF16)],
        smem=2,
    )
    steps = butterfly_steps()
    for axis, step in steps[:-1]:
        partial = partial + swap(partial, axis, step)
    weighted_low, weighted_high, coupling = call(
        functools.partial(weighted_kernel, inverse_rows),
        (partial, swap(partial, *steps[-1]), residual_low, residual_high, basis),
        [shape(count_y, block, side)] * 2 + [shape(prior, block)],
    )
    (sums,) = call(
        operators_kernel,
        (
            neighbours,
            tile_kinds,
            weighted_low,
            weighted_high,
            *halo(weighted_low, weighted_high),
            basis,
            table_high,
            table_low,
        ),
        [shape(3 * block, prior)],
        [pltpu.VMEM((places, 2 * block, side), BF16)],
        smem=2,
    )
    new_block, factor, reduced = call(
        functools.partial(factor_kernel, inverse_rows),
        (halved_sum(sums), weighted_low, weighted_high),
        [
            shape(block * tiles, side),
            shape(block, block),
            shape(2, prior + block, block),
        ],
    )
    return (new_block.reshape(previous.shape), coupling, factor, reduced)


def solution(mesh):
    placed = (
        P("case", "px", "py", None),
        P("case", "px", "py", None),
        P(None, "px", "py"),
        P(None, "px", "py"),
        P(),
        P(),
    )
    return jax.shard_map(
        shards,
        mesh=mesh,
        in_specs=placed,
        out_specs=(
            P("case", "px", "py", None),
            P("case", None),
            P("case", None),
            P("case", None, None),
        ),
        check_vma=False,
    )
```

```python
import functools

import jax
import jax.numpy as jnp
from jax import lax
from jax.experimental import pallas as pl
from jax.experimental.pallas import tpu as pltpu
from jax.sharding import PartitionSpec as P

F32 = jnp.float32
BF16 = jnp.bfloat16
VMEM = pl.BlockSpec(memory_space=pltpu.VMEM)
SMEM = pl.BlockSpec(memory_space=pltpu.SMEM)
PARAMS = pltpu.CompilerParams(vmem_limit_bytes=24 * 1024 * 1024)


def split(value):
    high = value.astype(BF16)
    return high, (value - high.astype(F32)).astype(BF16)


def mul(left, right):
    return jnp.dot(left, right, preferred_element_type=F32)


def mul_t(left, right):
    return lax.dot_general(left, right, (((1,), (1,)), ((), ())), preferred_element_type=F32)


def mul3(left, right):
    left_high, left_low = split(left)
    right_high, right_low = split(right)
    return mul(left_high, right_high) + (mul(left_high, right_low) + mul(left_low, right_high))


def mul3_t(left, right):
    left_high, left_low = split(left)
    right_high, right_low = split(right)
    return mul_t(left_high, right_high) + (
        mul_t(left_high, right_low) + mul_t(left_low, right_high)
    )


def tables_kernel(stiff_ref, mass_ref, high_ref, low_ref):
    side = stiff_ref.shape[1]
    for kind in range(stiff_ref.shape[0]):
        for place, ref in enumerate((stiff_ref, mass_ref)):
            high, low = split(ref[kind])
            high_ref[kind, place * side : (place + 1) * side, :] = high
            low_ref[kind, place * side : (place + 1) * side, :] = low


def pack_kernel(count_x, count_y, basis_ref, previous_ref, low_ref, high_ref):
    tiles = count_x * count_y
    block = previous_ref.shape[0] // tiles
    first = basis_ref.shape[0] - block * tiles
    for row, ref in ((0, low_ref), (count_x - 1, high_ref)):
        for j in range(count_y):
            tile = row * count_y + j
            ref[j, :block, :] = basis_ref[pl.ds(first + tile, block, stride=tiles), :]
            ref[j, block:, :] = previous_ref[pl.ds(tile, block, stride=tiles), :]


def fill_extended(ext_ref, store, rows, sides):
    width = len(rows) and rows[0].shape[0]
    for i, row in enumerate(rows):
        for j in range(width):
            store(ext_ref, i * (width + 2) + j + 1, row[j])
    for i in range(len(rows)):
        store(ext_ref, i * (width + 2), sides[0][i])
        store(ext_ref, i * (width + 2) + width + 1, sides[1][i])


def source_of(neighbours_ref, k, tile, count_y):
    neighbour = neighbours_ref[k, tile]
    down = neighbour // 3
    return (tile // count_y + down) * (count_y + 2) + tile % count_y + neighbour - 3 * down


def residual_kernel(
    neighbours_ref,
    kinds_ref,
    low_ref,
    high_ref,
    from_low_ref,
    from_high_ref,
    side_low_ref,
    side_high_ref,
    basis_ref,
    table_high_ref,
    table_low_ref,
    residual_low_ref,
    residual_high_ref,
    partial_ref,
    ext_ref,
):
    count_y = low_ref.shape[0]
    block = low_ref.shape[1] // 2
    tiles = 2 * count_y
    prior = basis_ref.shape[0] // tiles

    def store(ext, place, value):
        for part in range(2):
            high, low = split(value[part * block : (part + 1) * block])
            ext[place, :block, part * 128 : (part + 1) * 128] = high
            ext[place, block:, part * 128 : (part + 1) * 128] = low

    fill_extended(
        ext_ref,
        store,
        (from_low_ref, low_ref, high_ref, from_high_ref),
        (side_low_ref, side_high_ref),
    )
    partial = jnp.zeros((block, prior), F32)
    for tile in range(tiles):
        own = (low_ref, high_ref)[tile // count_y][tile % count_y]
        total = 4.0 * own[:block] + own[block:]
        for k in range(neighbours_ref.shape[0]):
            source = source_of(neighbours_ref, k, tile, count_y)
            kind = kinds_ref[k, tile]
            chosen = ext_ref[source]
            both = mul(chosen, table_high_ref[kind])
            total = total + (
                both[:block] + (both[block:] + mul(chosen[:block], table_low_ref[kind]))
            )
        (residual_low_ref, residual_high_ref)[tile // count_y][tile % count_y] = total
        partial = partial + mul3_t(total, basis_ref[pl.ds(tile, prior, stride=tiles), :])
    partial_ref[...] = partial


def weighted_kernel(
    inverse_rows,
    partial_ref,
    residual_low_ref,
    residual_high_ref,
    basis_ref,
    weighted_low_ref,
    weighted_high_ref,
    coupling_ref,
):
    count_y = residual_low_ref.shape[0]
    tiles = 2 * count_y
    prior = basis_ref.shape[0] // tiles
    coupling = partial_ref[...] * inverse_rows
    for tile in range(tiles):
        place = (tile // count_y, tile % count_y)
        moved = mul3(coupling, basis_ref[pl.ds(tile, prior, stride=tiles), :])
        (weighted_low_ref, weighted_high_ref)[place[0]][place[1]] = (
            (residual_low_ref, residual_high_ref)[place[0]][place[1]] - moved
        )
    coupling_ref[...] = coupling


def operators_kernel(
    neighbours_ref,
    kinds_ref,
    low_ref,
    high_ref,
    from_low_ref,
    from_high_ref,
    side_low_ref,
    side_high_ref,
    basis_ref,
    table_high_ref,
    table_low_ref,
    sums_ref,
    ext_ref,
):
    count_y, block, side = low_ref.shape
    tiles = 2 * count_y
    prior = basis_ref.shape[0] // tiles

    def store(ext, place, value):
        high, low = split(value)
        ext[place, :block, :] = high
        ext[place, block:, :] = low

    fill_extended(
        ext_ref,
        store,
        (from_low_ref, low_ref, high_ref, from_high_ref),
        (side_low_ref, side_high_ref),
    )
    with_basis = jnp.zeros((2 * block, prior), F32)
    with_own = jnp.zeros((block, 4 * block), F32)
    for tile in range(tiles):
        own = (low_ref, high_ref)[tile // count_y][tile % count_y]
        totals = [4.0 * own, own]
        for k in range(neighbours_ref.shape[0]):
            source = source_of(neighbours_ref, k, tile, count_y)
            kind = kinds_ref[k, tile]
            chosen = ext_ref[source]
            for part in range(2):
                span = slice(part * side, (part + 1) * side)
                both = mul(chosen, table_high_ref[kind, span, :])
                totals[part] = totals[part] + (
                    both[:block] + (both[block:] + mul(chosen[:block], table_low_ref[kind, span, :]))
                )
        applied = jnp.concatenate(totals, axis=0)
        with_basis = with_basis + mul3_t(applied, basis_ref[pl.ds(tile, prior, stride=tiles), :])
        right = jnp.concatenate([applied, own, jnp.zeros_like(own)], axis=0)
        with_own = with_own + mul3_t(own, right)
    sums_ref[: 2 * block, :] = with_basis
    sums_ref[2 * block :, :] = with_own


def factor_kernel(
    inverse_rows,
    sums_ref,
    weighted_low_ref,
    weighted_high_ref,
    new_ref,
    factor_ref,
    reduced_ref,
):
    count_y, block, _ = weighted_low_ref.shape
    prior = sums_ref.shape[1]
    tiles = 2 * count_y
    with_own = sums_ref[2 * block :, :] * inverse_rows
    gram = with_own[:, 2 * block : 3 * block]
    row_ids = lax.broadcasted_iota(jnp.int32, (block, block), 0)
    column_ids = lax.broadcasted_iota(jnp.int32, (block, block), 1)
    unit = jnp.where(row_ids == column_ids, 1.0, 0.0).astype(F32)
    work = jnp.concatenate([gram, unit], axis=1)
    rows = lax.broadcasted_iota(jnp.int32, (block, 1), 0)
    scale = jnp.zeros((block, 1), F32)
    for j in range(block):
        row = work[j : j + 1, :]
        pivot = row[:, j : j + 1]
        ratio = work[:, j : j + 1] / pivot
        scale = jnp.where(rows == j, lax.rsqrt(pivot), scale)
        work = work - jnp.where(rows > j, ratio, 0.0) * row
    work = work * scale
    factor_ref[...] = jnp.where(column_ids >= row_ids, work[:, :block], 0.0)
    inverse = work[:, block:]
    for tile in range(tiles):
        own = (weighted_low_ref, weighted_high_ref)[tile // count_y][tile % count_y]
        new_ref[pl.ds(tile, block, stride=tiles), :] = mul3(inverse, own)
    for part in range(2):
        span = slice(part * block, (part + 1) * block)
        reduced_ref[part, :, :prior] = mul3(inverse, sums_ref[span, :] * inverse_rows)
        reduced_ref[part, :, prior:] = mul3_t(mul3_t(inverse, with_own[:, span]), inverse)


def total_over_mesh(value):
    axes = ("px", "py")
    count = lax.axis_size(axes)
    chunk = value.size // count
    width = 128 if chunk % 128 == 0 else chunk
    parts = lax.all_to_all(value.reshape(count, chunk // width, width), axes, 0, 0)
    own = jnp.sum(parts, axis=0)
    parts = lax.all_to_all(jnp.broadcast_to(own[None], parts.shape), axes, 0, 0)
    return parts.reshape(value.shape)


def line(value, axis, forward):
    count = lax.axis_size(axis)
    pairs = [(i, i + 1) for i in range(count - 1)]
    if not forward:
        pairs = [(target, source) for source, target in pairs]
    return lax.ppermute(value, axis, pairs)


def halo(low, high):
    from_low = line(high, "px", True)
    from_high = line(low, "px", False)
    rows = (from_low, low, high, from_high)
    side_low = line(jnp.concatenate([row[-1:] for row in rows], axis=0), "py", True)
    side_high = line(jnp.concatenate([row[:1] for row in rows], axis=0), "py", False)
    return from_low, from_high, side_low, side_high


def shape(*dims, dtype=F32):
    return jax.ShapeDtypeStruct(dims, dtype)


def shards(prior_basis, previous, neighbours, tile_kinds, stiff_tiles, mass_tiles):
    block = previous.shape[0]
    prior, count_x, count_y, side = prior_basis.shape
    tiles = count_x * count_y
    inverse_rows = 1.0 / (tiles * side * lax.axis_size("px") * lax.axis_size("py"))
    basis = prior_basis.reshape(-1, side)
    neighbours = neighbours.reshape(-1, tiles)
    tile_kinds = tile_kinds.reshape(-1, tiles)
    places = 4 * (count_y + 2)

    def call(kernel, inputs, outputs, scratch=(), smem=0):
        return pl.pallas_call(
            kernel,
            out_shape=outputs,
            in_specs=[SMEM] * smem + [VMEM] * (len(inputs) - smem),
            out_specs=[VMEM] * len(outputs),
            scratch_shapes=scratch,
            compiler_params=PARAMS,
        )(*inputs)

    low, high = call(
        functools.partial(pack_kernel, count_x, count_y),
        (basis, previous.reshape(-1, side)),
        [shape(count_y, 2 * block, side)] * 2,
    )
    table_high, table_low = call(
        tables_kernel,
        (stiff_tiles, mass_tiles),
        [shape(stiff_tiles.shape[0], 2 * side, side, dtype=BF16)] * 2,
    )
    residual_low, residual_high, partial = call(
        residual_kernel,
        (neighbours, tile_kinds, low, high, *halo(low, high), basis, table_high, table_low),
        [shape(count_y, block, side)] * 2 + [shape(block, prior)],
        [pltpu.VMEM((places, 2 * block, 2 * side), BF16)],
        smem=2,
    )
    weighted_low, weighted_high, coupling = call(
        functools.partial(weighted_kernel, inverse_rows),
        (total_over_mesh(partial), residual_low, residual_high, basis),
        [shape(count_y, block, side)] * 2 + [shape(block, prior)],
    )
    (sums,) = call(
        operators_kernel,
        (
            neighbours,
            tile_kinds,
            weighted_low,
            weighted_high,
            *halo(weighted_low, weighted_high),
            basis,
            table_high,
            table_low,
        ),
        [shape(3 * block, prior)],
        [pltpu.VMEM((places, 2 * block, side), BF16)],
        smem=2,
    )
    new_block, factor, reduced = call(
        functools.partial(factor_kernel, inverse_rows),
        (total_over_mesh(sums), weighted_low, weighted_high),
        [
            shape(block * tiles, side),
            shape(block, block),
            shape(2, block, prior + block),
        ],
    )
    return (
        new_block.reshape(previous.shape),
        coupling.T,
        factor,
        reduced.swapaxes(1, 2),
    )


def solution(mesh):
    placed = (
        P("case", "px", "py", None),
        P("case", "px", "py", None),
        P(None, "px", "py"),
        P(None, "px", "py"),
        P(),
        P(),
    )
    return jax.shard_map(
        shards,
        mesh=mesh,
        in_specs=placed,
        out_specs=(
            P("case", "px", "py", None),
            P("case", None),
            P("case", None),
            P("case", None, None),
        ),
        check_vma=False,
    )
```

```python
import functools

import jax
import jax.numpy as jnp
from jax import lax
from jax.experimental import pallas as pl
from jax.experimental.pallas import tpu as pltpu
from jax.sharding import PartitionSpec as P

F32 = jnp.float32
BF16 = jnp.bfloat16
VMEM = pl.BlockSpec(memory_space=pltpu.VMEM)
SMEM = pl.BlockSpec(memory_space=pltpu.SMEM)
PARAMS = pltpu.CompilerParams(vmem_limit_bytes=24 * 1024 * 1024)


def split(value):
    high = value.astype(BF16)
    return high, (value - high.astype(F32)).astype(BF16)


def mul(left, right):
    return jnp.dot(left, right, preferred_element_type=F32)


def mul_t(left, right):
    return lax.dot_general(left, right, (((1,), (1,)), ((), ())), preferred_element_type=F32)


def mul3(left, right):
    left_high, left_low = split(left)
    right_high, right_low = split(right)
    return mul(left_high, right_high) + (mul(left_high, right_low) + mul(left_low, right_high))


def mul3_t(left, right):
    left_high, left_low = split(left)
    right_high, right_low = split(right)
    return mul_t(left_high, right_high) + (
        mul_t(left_high, right_low) + mul_t(left_low, right_high)
    )


def tables_kernel(stiff_ref, mass_ref, deep_high_ref, deep_low_ref, wide_high_ref, wide_low_ref):
    side = stiff_ref.shape[1]
    for kind in range(stiff_ref.shape[0]):
        for place, ref in enumerate((stiff_ref, mass_ref)):
            high, low = split(ref[kind])
            span = slice(place * side, (place + 1) * side)
            deep_high_ref[kind, span, :] = high
            deep_low_ref[kind, span, :] = low
            wide_high_ref[kind, :, span] = high
            wide_low_ref[kind, :, span] = low


def pack_kernel(
    count_x, count_y, basis_ref, previous_ref, low_ref, high_ref, low_rest_ref, high_rest_ref
):
    tiles = count_x * count_y
    block = previous_ref.shape[0] // tiles
    rest = low_rest_ref.shape[1]
    for row, ref, rest_ref in ((0, low_ref, low_rest_ref), (count_x - 1, high_ref, high_rest_ref)):
        for j in range(count_y):
            tile = row * count_y + j
            ref[j, :block, :] = basis_ref[pl.ds(rest * tiles + tile, block, stride=tiles), :]
            ref[j, block:, :] = previous_ref[pl.ds(tile, block, stride=tiles), :]
            rest_ref[j] = basis_ref[pl.ds(tile, rest, stride=tiles), :]


def fill_extended(ext_ref, store, rows, sides):
    width = len(rows) and rows[0].shape[0]
    for i, row in enumerate(rows):
        for j in range(width):
            store(ext_ref, i * (width + 2) + j + 1, row[j])
    for i in range(len(rows)):
        store(ext_ref, i * (width + 2), sides[0][i])
        store(ext_ref, i * (width + 2) + width + 1, sides[1][i])


def source_of(neighbours_ref, k, tile, count_y):
    neighbour = neighbours_ref[k, tile]
    down = neighbour // 3
    return (tile // count_y + down) * (count_y + 2) + tile % count_y + neighbour - 3 * down


def residual_kernel(
    neighbours_ref,
    kinds_ref,
    low_ref,
    high_ref,
    from_low_ref,
    from_high_ref,
    side_low_ref,
    side_high_ref,
    basis_ref,
    table_high_ref,
    table_low_ref,
    message_low_ref,
    message_high_ref,
    partial_ref,
    ext_ref,
):
    count_y = low_ref.shape[0]
    block = low_ref.shape[1] // 2
    tiles = 2 * count_y
    prior = basis_ref.shape[0] // tiles

    def store(ext, place, value):
        for part in range(2):
            high, low = split(value[part * block : (part + 1) * block])
            ext[place, :block, part * 128 : (part + 1) * 128] = high
            ext[place, block:, part * 128 : (part + 1) * 128] = low

    fill_extended(
        ext_ref,
        store,
        (from_low_ref, low_ref, high_ref, from_high_ref),
        (side_low_ref, side_high_ref),
    )
    partial = jnp.zeros((block, prior), F32)
    for tile in range(tiles):
        own = (low_ref, high_ref)[tile // count_y][tile % count_y]
        total = 4.0 * own[:block] + own[block:]
        for k in range(neighbours_ref.shape[0]):
            source = source_of(neighbours_ref, k, tile, count_y)
            kind = kinds_ref[k, tile]
            chosen = ext_ref[source]
            both = mul(chosen, table_high_ref[kind])
            total = total + (
                both[:block] + (both[block:] + mul(chosen[:block], table_low_ref[kind]))
            )
        (message_low_ref, message_high_ref)[tile // count_y][tile % count_y] = total
        partial = partial + mul3_t(total, basis_ref[pl.ds(tile, prior, stride=tiles), :])
    partial_ref[...] = partial
    message_low_ref[count_y] = partial
    message_high_ref[count_y] = partial


def sides_kernel(
    ends_ref, low_ref, high_ref, from_low_ref, from_high_ref, partial_ref, side_low_ref, side_high_ref
):
    last = low_ref.shape[0] - 2
    keep_low = ends_ref[0].astype(F32)
    keep_high = ends_ref[1].astype(F32)
    for ref, j in ((side_low_ref, 0), (side_high_ref, last)):
        ref[0] = from_low_ref[j] * keep_low
        ref[1] = low_ref[j]
        ref[2] = high_ref[j]
        ref[3] = from_high_ref[j] * keep_high
        ref[4] = partial_ref[...]


def operators_kernel(
    inverse_rows,
    ends_ref,
    neighbours_ref,
    kinds_ref,
    partial_ref,
    low_ref,
    high_ref,
    from_low_ref,
    from_high_ref,
    side_low_ref,
    side_high_ref,
    block_from_low_ref,
    block_from_high_ref,
    block_side_low_ref,
    block_side_high_ref,
    rest_from_low_ref,
    rest_from_high_ref,
    rest_side_low_ref,
    rest_side_high_ref,
    basis_ref,
    table_high_ref,
    table_low_ref,
    weighted_low_ref,
    weighted_high_ref,
    coupling_ref,
    sums_ref,
    ext_ref,
):
    count_y, block, side = weighted_low_ref.shape
    tiles = 2 * count_y
    prior = basis_ref.shape[0] // tiles
    wide = count_y + 2
    coupling = partial_ref[...] * inverse_rows
    coupling_ref[...] = coupling
    coupling_high, coupling_low = split(coupling)

    def moved(basis_tile):
        high, low = split(basis_tile)
        return mul(coupling_high, high) + (mul(coupling_high, low) + mul(coupling_low, high))

    def store(place, value):
        high, low = split(value)
        ext_ref[place, :block, :] = high
        ext_ref[place, block:, :] = low

    for tile in range(tiles):
        i, j = tile // count_y, tile % count_y
        value = (low_ref, high_ref)[i][j] - moved(basis_ref[pl.ds(tile, prior, stride=tiles), :])
        (weighted_low_ref, weighted_high_ref)[i][j] = value
        store((i + 1) * wide + j + 1, value)
    outside = [
        (j + 1, from_low_ref, block_from_low_ref, rest_from_low_ref, j, 0)
        for j in range(count_y)
    ]
    outside += [
        (3 * wide + j + 1, from_high_ref, block_from_high_ref, rest_from_high_ref, j, 1)
        for j in range(count_y)
    ]
    outside += [
        (i * wide, side_low_ref, block_side_low_ref, rest_side_low_ref, i, 2) for i in range(4)
    ]
    outside += [
        (i * wide + wide - 1, side_high_ref, block_side_high_ref, rest_side_high_ref, i, 3)
        for i in range(4)
    ]
    for place, ref, block_ref, rest_ref, at, end in outside:
        basis_tile = jnp.concatenate([rest_ref[at], block_ref[at, :block]], axis=0)
        store(place, ref[at] * ends_ref[end].astype(F32) - moved(basis_tile))
    with_basis = jnp.zeros((2 * block, prior), F32)
    with_own = jnp.zeros((block, 4 * block), F32)
    for tile in range(tiles):
        own = (weighted_low_ref, weighted_high_ref)[tile // count_y][tile % count_y]
        totals = jnp.concatenate([4.0 * own, own], axis=1)
        for k in range(neighbours_ref.shape[0]):
            source = source_of(neighbours_ref, k, tile, count_y)
            kind = kinds_ref[k, tile]
            chosen = ext_ref[source]
            both = mul(chosen, table_high_ref[kind])
            totals = totals + (
                both[:block] + (both[block:] + mul(chosen[:block], table_low_ref[kind]))
            )
        applied = jnp.concatenate([totals[:, :side], totals[:, side:]], axis=0)
        with_basis = with_basis + mul3_t(applied, basis_ref[pl.ds(tile, prior, stride=tiles), :])
        right = jnp.concatenate([applied, own, jnp.zeros_like(own)], axis=0)
        with_own = with_own + mul3_t(own, right)
    sums_ref[: 2 * block, :] = with_basis
    sums_ref[2 * block :, :] = with_own


def factor_kernel(
    inverse_rows,
    sums_ref,
    weighted_low_ref,
    weighted_high_ref,
    new_ref,
    factor_ref,
    reduced_ref,
):
    count_y, block, _ = weighted_low_ref.shape
    prior = sums_ref.shape[1]
    tiles = 2 * count_y
    with_own = sums_ref[2 * block :, :] * inverse_rows
    gram = with_own[:, 2 * block : 3 * block]
    row_ids = lax.broadcasted_iota(jnp.int32, (block, block), 0)
    column_ids = lax.broadcasted_iota(jnp.int32, (block, block), 1)
    unit = jnp.where(row_ids == column_ids, 1.0, 0.0).astype(F32)
    work = jnp.concatenate([gram, unit], axis=1)
    rows = lax.broadcasted_iota(jnp.int32, (block, 1), 0)
    for j in range(0, block, 2):
        first, second = work[j : j + 1, :], work[j + 1 : j + 2, :]
        inverse_first = 1.0 / first[:, j : j + 1]
        across = first[:, j + 1 : j + 2]
        ratio = second[:, j : j + 1] * inverse_first
        second = second - ratio * first
        inverse_second = 1.0 / second[:, j + 1 : j + 2]
        first_ratio = work[:, j : j + 1] * inverse_first
        second_ratio = (work[:, j + 1 : j + 2] - first_ratio * across) * inverse_second
        work = work - (
            jnp.where(rows > j, first_ratio, 0.0) * first
            + jnp.where(rows > j + 1, second_ratio, 0.0) * second
        )
    work = work * lax.rsqrt(jnp.sum(work[:, :block] * unit, axis=1, keepdims=True))
    factor_ref[...] = jnp.where(column_ids >= row_ids, work[:, :block], 0.0)
    inverse = work[:, block:]
    for tile in range(tiles):
        own = (weighted_low_ref, weighted_high_ref)[tile // count_y][tile % count_y]
        new_ref[pl.ds(tile, block, stride=tiles), :] = mul3(inverse, own)
    for part in range(2):
        span = slice(part * block, (part + 1) * block)
        reduced_ref[part, :, :prior] = mul3(inverse, sums_ref[span, :] * inverse_rows)
        reduced_ref[part, :, prior:] = mul3_t(mul3_t(inverse, with_own[:, span]), inverse)


def swap(value, axis, step):
    count = lax.axis_size(axis)
    return lax.ppermute(value, axis, [(i, i ^ step) for i in range(count)])


def shift(value, axis, step):
    count = lax.axis_size(axis)
    return lax.ppermute(value, axis, [(i, (i + step) % count) for i in range(count)])


def total_along(value, axis, first=1):
    if lax.axis_size(axis) == 4 and first == 1:
        opposite = shift(value, axis, 2)
        return (value + opposite) + (shift(value, axis, 1) + shift(value, axis, -1))
    step = first
    while step < lax.axis_size(axis):
        value = value + swap(value, axis, step)
        step *= 2
    return value


def halved_total(value):
    half = value.shape[0] // 2
    upper = lax.axis_index("py") % 2 == 1
    first, second = value[:half], value[half:]
    kept = jnp.where(upper, second, first)
    kept = kept + swap(jnp.where(upper, first, second), "py", 1)
    kept = total_along(kept, "py", 2)
    kept = total_along(kept, "px")
    other = swap(kept, "py", 1)
    return jnp.concatenate(
        [jnp.where(upper, other, kept), jnp.where(upper, kept, other)], axis=0
    )


def halo_and_total(low, high, partial, axis):
    if lax.axis_size(axis) == 4:
        from_low, from_high = shift(high, axis, 1), shift(low, axis, -1)
        opposite = shift(partial, axis, 2)
        return from_low, from_high, (partial + opposite) + (from_low[-1] + from_high[-1])
    return line(high, axis, True), line(low, axis, False), total_along(partial, axis)


def line(value, axis, forward):
    count = lax.axis_size(axis)
    pairs = [(i, i + 1) for i in range(count - 1)]
    if not forward:
        pairs = [(target, source) for source, target in pairs]
    return lax.ppermute(value, axis, pairs)


def sides(low, high, from_low, from_high):
    rows = (from_low, low, high, from_high)
    return (
        jnp.concatenate([row[:1] for row in rows], axis=0),
        jnp.concatenate([row[-1:] for row in rows], axis=0),
    )


def halo(low, high, axis):
    return line(high, axis, True), line(low, axis, False)


def shape(*dims, dtype=F32):
    return jax.ShapeDtypeStruct(dims, dtype)


def shards(prior_basis, previous, neighbours, tile_kinds, stiff_tiles, mass_tiles):
    block = previous.shape[0]
    prior, count_x, count_y, side = prior_basis.shape
    tiles = count_x * count_y
    inverse_rows = 1.0 / (tiles * side * lax.axis_size("px") * lax.axis_size("py"))
    basis = prior_basis.reshape(-1, side)
    neighbours = neighbours.reshape(-1, tiles)
    tile_kinds = tile_kinds.reshape(-1, tiles)
    places = 4 * (count_y + 2)

    def call(kernel, inputs, outputs, scratch=(), smem=0):
        return pl.pallas_call(
            kernel,
            out_shape=outputs,
            in_specs=[SMEM] * smem + [VMEM] * (len(inputs) - smem),
            out_specs=[VMEM] * len(outputs),
            scratch_shapes=scratch,
            compiler_params=PARAMS,
        )(*inputs)

    low, high, low_rest, high_rest = call(
        functools.partial(pack_kernel, count_x, count_y),
        (basis, previous.reshape(-1, side)),
        [shape(count_y, 2 * block, side)] * 2 + [shape(count_y, prior - block, side)] * 2,
    )
    kinds = stiff_tiles.shape[0]
    deep_high, deep_low, wide_high, wide_low = call(
        tables_kernel,
        (stiff_tiles, mass_tiles),
        [shape(kinds, 2 * side, side, dtype=BF16)] * 2
        + [shape(kinds, side, 2 * side, dtype=BF16)] * 2,
    )
    ends = []
    for axis in ("px", "py"):
        ends += [lax.axis_index(axis) > 0, lax.axis_index(axis) < lax.axis_size(axis) - 1]
    ends = jnp.stack(ends).astype(jnp.int32)

    block_rows = halo(low, high, "px")
    side_low, side_high = sides(low, high, *block_rows)
    block_sides = halo(side_low, side_high, "py")
    low_rest, high_rest, _ = lax.optimization_barrier((low_rest, high_rest, side_low))
    rest_rows = halo(low_rest, high_rest, "px")
    rest_sides = halo(*sides(low_rest, high_rest, *rest_rows), "py")

    message_low, message_high, partial = call(
        residual_kernel,
        (
            neighbours,
            tile_kinds,
            low,
            high,
            *block_rows,
            *block_sides,
            basis,
            deep_high,
            deep_low,
        ),
        [shape(count_y + 1, block, side)] * 2 + [shape(block, prior)],
        [pltpu.VMEM((places, 2 * block, 2 * side), BF16)],
        smem=2,
    )
    from_low, from_high, partial = halo_and_total(message_low, message_high, partial, "px")
    side_low, side_high = call(
        sides_kernel,
        (ends, message_low, message_high, from_low, from_high, partial),
        [shape(5, block, side)] * 2,
        smem=1,
    )
    from_side_low, from_side_high, partial = halo_and_total(side_low, side_high, partial, "py")
    weighted_low, weighted_high, coupling, sums = call(
        functools.partial(operators_kernel, inverse_rows),
        (
            ends,
            neighbours,
            tile_kinds,
            partial,
            message_low,
            message_high,
            from_low,
            from_high,
            from_side_low,
            from_side_high,
            *block_rows,
            *block_sides,
            *rest_rows,
            *rest_sides,
            basis,
            wide_high,
            wide_low,
        ),
        [shape(count_y, block, side)] * 2 + [shape(block, prior), shape(3 * block, prior)],
        [pltpu.VMEM((places, 2 * block, side), BF16)],
        smem=3,
    )
    new_block, factor, reduced = call(
        functools.partial(factor_kernel, inverse_rows),
        (halved_total(sums), weighted_low, weighted_high),
        [
            shape(block * tiles, side),
            shape(block, block),
            shape(2, block, prior + block),
        ],
    )
    return (
        new_block.reshape(previous.shape),
        coupling.T,
        factor,
        reduced.swapaxes(1, 2),
    )


def solution(mesh):
    placed = (
        P("case", "px", "py", None),
        P("case", "px", "py", None),
        P(None, "px", "py"),
        P(None, "px", "py"),
        P(),
        P(),
    )
    return jax.shard_map(
        shards,
        mesh=mesh,
        in_specs=placed,
        out_specs=(
            P("case", "px", "py", None),
            P("case", None),
            P("case", None),
            P("case", None, None),
        ),
        check_vma=False,
    )
```

```python
import functools

import jax
import jax.numpy as jnp
from jax import lax
from jax.experimental import pallas as pl
from jax.experimental.pallas import tpu as pltpu
from jax.sharding import PartitionSpec as P

F32 = jnp.float32
BF16 = jnp.bfloat16
VMEM = pl.BlockSpec(memory_space=pltpu.VMEM)
SMEM = pl.BlockSpec(memory_space=pltpu.SMEM)
PARAMS = pltpu.CompilerParams(vmem_limit_bytes=24 * 1024 * 1024)


def split(value):
    high = value.astype(BF16)
    return high, (value - high.astype(F32)).astype(BF16)


def mul(left, right):
    return jnp.dot(left, right, preferred_element_type=F32)


def mul_t(left, right):
    return lax.dot_general(left, right, (((1,), (1,)), ((), ())), preferred_element_type=F32)


def mul3(left, right):
    left_high, left_low = split(left)
    right_high, right_low = split(right)
    return mul(left_high, right_high) + (mul(left_high, right_low) + mul(left_low, right_high))


def mul3_t(left, right):
    left_high, left_low = split(left)
    right_high, right_low = split(right)
    return mul_t(left_high, right_high) + (
        mul_t(left_high, right_low) + mul_t(left_low, right_high)
    )


def tables_kernel(stiff_ref, mass_ref, deep_high_ref, deep_low_ref, wide_high_ref, wide_low_ref):
    side = stiff_ref.shape[1]
    for kind in range(stiff_ref.shape[0]):
        for place, ref in enumerate((stiff_ref, mass_ref)):
            high, low = split(ref[kind])
            span = slice(place * side, (place + 1) * side)
            deep_high_ref[kind, span, :] = high
            deep_low_ref[kind, span, :] = low
            wide_high_ref[kind, :, span] = high
            wide_low_ref[kind, :, span] = low


def pack_kernel(count_x, count_y, basis_ref, previous_ref, low_ref, high_ref):
    tiles = count_x * count_y
    prior, block = basis_ref.shape[0] // tiles, previous_ref.shape[0] // tiles
    for column, ref in ((0, low_ref), (count_y - 1, high_ref)):
        for i in range(count_x):
            tile = i * count_y + column
            ref[i, :prior, :] = basis_ref[pl.ds(tile, prior, stride=tiles), :]
            ref[i, prior:, :] = previous_ref[pl.ds(tile, block, stride=tiles), :]


def rows_kernel(
    basis_ref,
    previous_ref,
    side_low_ref,
    side_high_ref,
    low_ref,
    high_ref,
    low_rest_ref,
    high_rest_ref,
):
    wide, rest, _ = low_rest_ref.shape
    block = low_ref.shape[1] // 2
    tiles = 2 * (wide - 2)
    for i, ref, rest_ref in ((0, low_ref, low_rest_ref), (1, high_ref, high_rest_ref)):
        for j, side_ref in ((0, side_low_ref), (wide - 1, side_high_ref)):
            rest_ref[j] = side_ref[i, :rest, :]
            ref[j] = side_ref[i, rest:, :]
        for j in range(wide - 2):
            tile = i * (wide - 2) + j
            rest_ref[j + 1] = basis_ref[pl.ds(tile, rest, stride=tiles), :]
            ref[j + 1, :block, :] = basis_ref[pl.ds(rest * tiles + tile, block, stride=tiles), :]
            ref[j + 1, block:, :] = previous_ref[pl.ds(tile, block, stride=tiles), :]


def source_of(neighbours_ref, k, tile, count_y):
    neighbour = neighbours_ref[k, tile]
    down = neighbour // 3
    return (tile // count_y + down) * (count_y + 2) + tile % count_y + neighbour - 3 * down


def residual_kernel(
    neighbours_ref,
    kinds_ref,
    from_low_ref,
    low_ref,
    high_ref,
    from_high_ref,
    low_rest_ref,
    high_rest_ref,
    table_high_ref,
    table_low_ref,
    residual_low_ref,
    residual_high_ref,
    message_low_ref,
    message_high_ref,
    partial_ref,
    ext_ref,
):
    wide = low_ref.shape[0]
    count_y = wide - 2
    block = low_ref.shape[1] // 2
    side = low_ref.shape[2]
    prior = low_rest_ref.shape[1] + block
    for i, ref in enumerate((from_low_ref, low_ref, high_ref, from_high_ref)):
        for j in range(wide):
            for part in range(2):
                high, low = split(ref[j, part * block : (part + 1) * block, :])
                ext_ref[i * wide + j, :block, part * side : (part + 1) * side] = high
                ext_ref[i * wide + j, block:, part * side : (part + 1) * side] = low
    partial = jnp.zeros((block, prior), F32)
    for tile in range(2 * count_y):
        i, j = tile // count_y, tile % count_y
        own = (low_ref, high_ref)[i][j + 1]
        total = 4.0 * own[:block] + own[block:]
        for k in range(neighbours_ref.shape[0]):
            source = source_of(neighbours_ref, k, tile, count_y)
            kind = kinds_ref[k, tile]
            chosen = ext_ref[source]
            both = mul(chosen, table_high_ref[kind])
            total = total + (
                both[:block] + (both[block:] + mul(chosen[:block], table_low_ref[kind]))
            )
        (residual_low_ref, residual_high_ref)[i][j] = total
        if j == 0:
            message_low_ref[i] = total
        if j == count_y - 1:
            message_high_ref[i] = total
        basis_tile = jnp.concatenate(
            [(low_rest_ref, high_rest_ref)[i][j + 1], own[:block]], axis=0
        )
        partial = partial + mul3_t(total, basis_tile)
    partial_ref[...] = partial
    message_low_ref[2] = partial
    message_high_ref[2] = partial


def residual_rows_kernel(
    low_ref, high_ref, side_low_ref, side_high_ref, partial_ref, row_low_ref, row_high_ref
):
    count_y = low_ref.shape[0]
    for i, ref, row_ref in ((0, low_ref, row_low_ref), (1, high_ref, row_high_ref)):
        row_ref[0] = side_low_ref[i]
        row_ref[1 : count_y + 1] = ref[...]
        row_ref[count_y + 1] = side_high_ref[i]
        row_ref[count_y + 2] = partial_ref[...]


def operators_kernel(
    inverse_rows,
    ends_ref,
    neighbours_ref,
    kinds_ref,
    partial_ref,
    *refs,
):
    row_refs, block_refs, rest_refs = refs[:4], refs[4:8], refs[8:12]
    table_high_ref, table_low_ref = refs[12:14]
    weighted_low_ref, weighted_high_ref, coupling_ref, sums_ref, ext_ref = refs[14:]
    count_y, block, side = weighted_low_ref.shape
    wide = count_y + 2
    prior = rest_refs[0].shape[1] + block
    coupling = partial_ref[...] * inverse_rows
    coupling_ref[...] = coupling
    coupling_high, coupling_low = split(coupling)

    def basis_tile(i, j):
        return jnp.concatenate([rest_refs[i][j], block_refs[i][j, :block, :]], axis=0)

    for i in range(4):
        for j in range(wide):
            high, low = split(basis_tile(i, j))
            moved = mul(coupling_high, high) + (
                mul(coupling_high, low) + mul(coupling_low, high)
            )
            value = row_refs[i][j]
            if j == 0:
                value = value * ends_ref[0].astype(F32)
            if j == wide - 1:
                value = value * ends_ref[1].astype(F32)
            value = value - moved
            if 0 < i < 3 and 0 < j < wide - 1:
                (weighted_low_ref, weighted_high_ref)[i - 1][j - 1] = value
            high, low = split(value)
            ext_ref[i * wide + j, :block, :] = high
            ext_ref[i * wide + j, block:, :] = low
    with_basis = jnp.zeros((2 * block, prior), F32)
    with_own = jnp.zeros((block, 4 * block), F32)
    for tile in range(2 * count_y):
        i, j = tile // count_y, tile % count_y
        own = (weighted_low_ref, weighted_high_ref)[i][j]
        totals = jnp.concatenate([4.0 * own, own], axis=1)
        for k in range(neighbours_ref.shape[0]):
            source = source_of(neighbours_ref, k, tile, count_y)
            kind = kinds_ref[k, tile]
            chosen = ext_ref[source]
            both = mul(chosen, table_high_ref[kind])
            totals = totals + (
                both[:block] + (both[block:] + mul(chosen[:block], table_low_ref[kind]))
            )
        applied = jnp.concatenate([totals[:, :side], totals[:, side:]], axis=0)
        with_basis = with_basis + mul3_t(applied, basis_tile(i + 1, j + 1))
        right = jnp.concatenate([applied, own, jnp.zeros_like(own)], axis=0)
        with_own = with_own + mul3_t(own, right)
    sums_ref[: 2 * block, :] = with_basis
    sums_ref[2 * block :, :] = with_own


def factor_kernel(
    inverse_rows,
    sums_ref,
    weighted_low_ref,
    weighted_high_ref,
    new_ref,
    factor_ref,
    reduced_ref,
):
    count_y, block, _ = weighted_low_ref.shape
    prior = sums_ref.shape[1]
    tiles = 2 * count_y
    with_own = sums_ref[2 * block :, :] * inverse_rows
    gram = with_own[:, 2 * block : 3 * block]
    row_ids = lax.broadcasted_iota(jnp.int32, (block, block), 0)
    column_ids = lax.broadcasted_iota(jnp.int32, (block, block), 1)
    unit = jnp.where(row_ids == column_ids, 1.0, 0.0).astype(F32)
    work = jnp.concatenate([gram, unit], axis=1)
    rows = lax.broadcasted_iota(jnp.int32, work.shape, 0)
    group = 4
    for j in range(0, block, group):
        columns = [
            jnp.broadcast_to(work[:, j + a : j + a + 1], work.shape) for a in range(group)
        ]
        pivots = [work[j + a : j + a + 1, :] for a in range(group)]
        for a in range(group):
            at = j + a
            ratio = columns[a] * (1.0 / columns[a][at : at + 1, :])
            for b in range(a + 1, group):
                columns[b] = columns[b] - ratio * columns[b][at : at + 1, :]
                pivots[b] = pivots[b] - ratio[j + b : j + b + 1, :] * pivots[a]
            work = work - jnp.where(rows > at, ratio, 0.0) * pivots[a]
    work = work * lax.rsqrt(jnp.sum(work[:, :block] * unit, axis=1, keepdims=True))
    factor_ref[...] = jnp.where(column_ids >= row_ids, work[:, :block], 0.0)
    inverse = work[:, block:]
    for tile in range(tiles):
        own = (weighted_low_ref, weighted_high_ref)[tile // count_y][tile % count_y]
        new_ref[pl.ds(tile, block, stride=tiles), :] = mul3(inverse, own)
    for part in range(2):
        span = slice(part * block, (part + 1) * block)
        reduced_ref[part, :, :prior] = mul3(inverse, sums_ref[span, :] * inverse_rows)
        reduced_ref[part, :, prior:] = mul3_t(mul3_t(inverse, with_own[:, span]), inverse)


def permute(value, axis, target):
    count = lax.axis_size(axis)
    pairs = [(i, target(i)) for i in range(count)]
    return lax.ppermute(value, axis, [pair for pair in pairs if 0 <= pair[1] < count])


def swap(value, axis, step):
    return permute(value, axis, lambda i: i ^ step)


def shift(value, axis, step):
    count = lax.axis_size(axis)
    return permute(value, axis, lambda i: (i + step) % count)


def line(value, axis, step):
    return permute(value, axis, lambda i: i + step)


def total_along(value, axis, first=1):
    if lax.axis_size(axis) == 4 and first == 1:
        opposite = shift(value, axis, 2)
        return (value + opposite) + (shift(value, axis, 1) + shift(value, axis, -1))
    step = first
    while step < lax.axis_size(axis):
        value = value + swap(value, axis, step)
        step *= 2
    return value


def halved_total(value):
    half = value.shape[0] // 2
    upper = lax.axis_index("py") % 2 == 1
    first, second = value[:half], value[half:]
    kept = jnp.where(upper, second, first)
    kept = kept + swap(jnp.where(upper, first, second), "py", 1)
    kept = total_along(kept, "py", 2)
    kept = total_along(kept, "px")
    other = swap(kept, "py", 1)
    return jnp.concatenate(
        [jnp.where(upper, other, kept), jnp.where(upper, kept, other)], axis=0
    )


def ring_with_total(low, high, partial, axis):
    if lax.axis_size(axis) == 4:
        from_low, from_high = shift(high, axis, 1), shift(low, axis, -1)
        opposite = shift(partial, axis, 2)
        return from_low, from_high, (partial + opposite) + (from_low[-1] + from_high[-1])
    return line(high, axis, 1), line(low, axis, -1), total_along(partial, axis)


def line_with_total(low, high, partial, axis):
    from_low, from_high = line(high, axis, 1), line(low, axis, -1)
    if lax.axis_size(axis) == 4:
        opposite = swap(partial, axis, 2)
        far = permute(partial, axis, lambda i: {0: 3, 3: 0}.get(i, -1))
        near = from_low[-1] + from_high[-1]
        return from_low, from_high, (partial + opposite) + (near + far)
    return from_low, from_high, total_along(partial, axis)


def shape(*dims, dtype=F32):
    return jax.ShapeDtypeStruct(dims, dtype)


def shards(prior_basis, previous, neighbours, tile_kinds, stiff_tiles, mass_tiles):
    block = previous.shape[0]
    prior, count_x, count_y, side = prior_basis.shape
    tiles = count_x * count_y
    wide = count_y + 2
    rest = prior - block
    kinds = stiff_tiles.shape[0]
    inverse_rows = 1.0 / (tiles * side * lax.axis_size("px") * lax.axis_size("py"))
    basis = prior_basis.reshape(-1, side)
    previous_rows = previous.reshape(-1, side)
    neighbours = neighbours.reshape(-1, tiles)
    tile_kinds = tile_kinds.reshape(-1, tiles)
    position = lax.axis_index("py")
    ends = jnp.stack([position > 0, position < lax.axis_size("py") - 1]).astype(jnp.int32)

    def call(kernel, inputs, outputs, scratch=(), smem=0):
        return pl.pallas_call(
            kernel,
            out_shape=outputs,
            in_specs=[SMEM] * smem + [VMEM] * (len(inputs) - smem),
            out_specs=[VMEM] * len(outputs),
            scratch_shapes=scratch,
            compiler_params=PARAMS,
        )(*inputs)

    side_low, side_high = call(
        functools.partial(pack_kernel, count_x, count_y),
        (basis, previous_rows),
        [shape(count_x, prior + block, side)] * 2,
    )
    deep_high, deep_low, wide_high, wide_low = call(
        tables_kernel,
        (stiff_tiles, mass_tiles),
        [shape(kinds, 2 * side, side, dtype=BF16)] * 2
        + [shape(kinds, side, 2 * side, dtype=BF16)] * 2,
    )
    from_side_low, from_side_high = line(side_high, "py", 1), line(side_low, "py", -1)
    low, high, low_rest, high_rest = call(
        rows_kernel,
        (basis, previous_rows, from_side_low, from_side_high),
        [shape(wide, 2 * block, side)] * 2 + [shape(wide, rest, side)] * 2,
    )
    block_rows = (line(high, "px", 1), low, high, line(low, "px", -1))
    rest_rows = (line(high_rest, "px", 1), low_rest, high_rest, line(low_rest, "px", -1))
    residual_low, residual_high, message_low, message_high, partial = call(
        residual_kernel,
        (neighbours, tile_kinds, *block_rows, low_rest, high_rest, deep_high, deep_low),
        [shape(count_y, block, side)] * 2 + [shape(3, block, side)] * 2 + [shape(block, prior)],
        [pltpu.VMEM((4 * wide, 2 * block, 2 * side), BF16)],
        smem=2,
    )
    from_side_low, from_side_high, partial = ring_with_total(
        message_low, message_high, partial, "py"
    )
    from_side_low, *rest_rows = lax.optimization_barrier((from_side_low, *rest_rows))
    row_low, row_high = call(
        residual_rows_kernel,
        (residual_low, residual_high, from_side_low, from_side_high, partial),
        [shape(wide + 1, block, side)] * 2,
    )
    from_low, from_high, partial = line_with_total(row_low, row_high, partial, "px")
    weighted_low, weighted_high, coupling, sums = call(
        functools.partial(operators_kernel, inverse_rows),
        (
            ends,
            neighbours,
            tile_kinds,
            partial,
            *(from_low, row_low, row_high, from_high),
            *block_rows,
            *rest_rows,
            wide_high,
            wide_low,
        ),
        [shape(count_y, block, side)] * 2 + [shape(block, prior), shape(3 * block, prior)],
        [pltpu.VMEM((4 * wide, 2 * block, side), BF16)],
        smem=3,
    )
    new_block, factor, reduced = call(
        functools.partial(factor_kernel, inverse_rows),
        (halved_total(sums), weighted_low, weighted_high),
        [
            shape(block * tiles, side),
            shape(block, block),
            shape(2, block, prior + block),
        ],
    )
    return (
        new_block.reshape(previous.shape),
        coupling.T,
        factor,
        reduced.swapaxes(1, 2),
    )


def solution(mesh):
    placed = (
        P("case", "px", "py", None),
        P("case", "px", "py", None),
        P(None, "px", "py"),
        P(None, "px", "py"),
        P(),
        P(),
    )
    return jax.shard_map(
        shards,
        mesh=mesh,
        in_specs=placed,
        out_specs=(
            P("case", "px", "py", None),
            P("case", None),
            P("case", None),
            P("case", None, None),
        ),
        check_vma=False,
    )
```

```python
import functools

import jax
import jax.numpy as jnp
from jax import lax
from jax.experimental import pallas as pl
from jax.experimental.pallas import tpu as pltpu
from jax.sharding import PartitionSpec as P

F32 = jnp.float32
BF16 = jnp.bfloat16
VMEM = pl.BlockSpec(memory_space=pltpu.VMEM)
SMEM = pl.BlockSpec(memory_space=pltpu.SMEM)
PARAMS = pltpu.CompilerParams(vmem_limit_bytes=24 * 1024 * 1024)


def split(value):
    high = value.astype(BF16)
    return high, (value - high.astype(F32)).astype(BF16)


def mul(left, right):
    return jnp.dot(left, right, preferred_element_type=F32)


def mul_t(left, right):
    return lax.dot_general(left, right, (((1,), (1,)), ((), ())), preferred_element_type=F32)


def mul3(left, right):
    left_high, left_low = split(left)
    right_high, right_low = split(right)
    return mul(left_high, right_high) + (mul(left_high, right_low) + mul(left_low, right_high))


def mul3_t(left, right):
    left_high, left_low = split(left)
    right_high, right_low = split(right)
    return mul_t(left_high, right_high) + (
        mul_t(left_high, right_low) + mul_t(left_low, right_high)
    )


def tables_kernel(stiff_ref, mass_ref, deep_high_ref, deep_low_ref, wide_high_ref, wide_low_ref):
    side = stiff_ref.shape[1]
    for kind in range(stiff_ref.shape[0]):
        for place, ref in enumerate((stiff_ref, mass_ref)):
            high, low = split(ref[kind])
            span = slice(place * side, (place + 1) * side)
            deep_high_ref[kind, span, :] = high
            deep_low_ref[kind, span, :] = low
            wide_high_ref[kind, :, span] = high
            wide_low_ref[kind, :, span] = low


def pick(flag, first, second):
    flag = flag > 0.0
    return jnp.where(flag, first, second), jnp.where(flag, second, first)


def flag_at(flags_ref, place):
    return flags_ref[place : place + 1, :]


def pack_kernel(flags_ref, basis_ref, previous_ref, side_a_ref, side_b_ref, row_a_ref, row_b_ref):
    count_x, sides, side = side_a_ref.shape
    count_y, both, _ = row_a_ref.shape
    tiles = count_x * count_y
    block = both // 2
    rest = sides - both

    def tile_of(i, j):
        tile = i * count_y + j
        return (
            basis_ref[pl.ds(tile, rest, stride=tiles), :],
            basis_ref[pl.ds(rest * tiles + tile, block, stride=tiles), :],
            previous_ref[pl.ds(tile, block, stride=tiles), :],
        )

    spans = (slice(0, rest), slice(rest, rest + block), slice(rest + block, sides))
    for i in range(count_x):
        for span, low, high in zip(spans, tile_of(i, 0), tile_of(i, count_y - 1)):
            side_a_ref[i, span, :], side_b_ref[i, span, :] = pick(
                flag_at(flags_ref, 0), low, high
            )
    for j in range(count_y):
        for part in range(2):
            span = slice(part * block, (part + 1) * block)
            row_a_ref[j, span, :], row_b_ref[j, span, :] = pick(
                flag_at(flags_ref, 1), tile_of(0, j)[part + 1], tile_of(1, j)[part + 1]
            )


def corners_kernel(
    flags_ref,
    basis_ref,
    side_a_ref,
    side_b_ref,
    corner_a_ref,
    corner_b_ref,
    rest_a_ref,
    rest_b_ref,
):
    wide, rest, _ = rest_a_ref.shape
    tiles = 2 * (wide - 2)
    odd_y, odd_x = flag_at(flags_ref, 0), flag_at(flags_ref, 1)
    ends = [pick(odd_y, side_a_ref[i], side_b_ref[i]) for i in range(2)]
    for place, j in ((0, 0), (1, wide - 1)):
        corner_a_ref[place], corner_b_ref[place] = pick(
            odd_x, ends[0][place][rest:], ends[1][place][rest:]
        )
        rest_a_ref[j], rest_b_ref[j] = pick(
            odd_x, ends[0][place][:rest], ends[1][place][:rest]
        )
    for j in range(wide - 2):
        rest_a_ref[j + 1], rest_b_ref[j + 1] = pick(
            odd_x,
            basis_ref[pl.ds(j, rest, stride=tiles), :],
            basis_ref[pl.ds(wide - 2 + j, rest, stride=tiles), :],
        )


def source_of(neighbours_ref, k, tile, count_y):
    neighbour = neighbours_ref[k, tile]
    down = neighbour // 3
    return (tile // count_y + down) * (count_y + 2) + tile % count_y + neighbour - 3 * down


def residual_kernel(
    neighbours_ref,
    kinds_ref,
    flags_ref,
    row_a_ref,
    row_b_ref,
    from_row_a_ref,
    from_row_b_ref,
    from_side_a_ref,
    from_side_b_ref,
    from_corner_a_ref,
    from_corner_b_ref,
    rest_a_ref,
    rest_b_ref,
    table_high_ref,
    table_low_ref,
    residual_low_ref,
    residual_high_ref,
    message_a_ref,
    message_b_ref,
    partial_ref,
    current_ref,
    ext_ref,
):
    count_y, both, side = row_a_ref.shape
    wide = count_y + 2
    block = both // 2
    rest = rest_a_ref.shape[1]
    odd_y, odd_x, in_low_y, in_high_y, in_low_x, in_high_x = (
        flag_at(flags_ref, place) for place in range(6)
    )

    def store(i, j, value):
        current_ref[i * wide + j] = value[:block]
        for part in range(2):
            high, low = split(value[part * block : (part + 1) * block])
            ext_ref[i * wide + j, :block, part * side : (part + 1) * side] = high
            ext_ref[i * wide + j, block:, part * side : (part + 1) * side] = low

    own = {}
    for j in range(count_y):
        own[0, j], own[1, j] = pick(odd_x, row_a_ref[j], row_b_ref[j])
        store(1, j + 1, own[0, j])
        store(2, j + 1, own[1, j])
        low, high = pick(odd_x, from_row_a_ref[j], from_row_b_ref[j])
        store(0, j + 1, low * in_low_x)
        store(3, j + 1, high * in_high_x)
    for i in range(2):
        low, high = pick(odd_y, from_side_a_ref[i, rest:, :], from_side_b_ref[i, rest:, :])
        store(i + 1, 0, low * in_low_y)
        store(i + 1, wide - 1, high * in_high_y)
    for place, j, inside in ((0, 0, in_low_y), (1, wide - 1, in_high_y)):
        low, high = pick(odd_x, from_corner_a_ref[place], from_corner_b_ref[place])
        store(0, j, low * (in_low_x * inside))
        store(3, j, high * (in_high_x * inside))
    partial = jnp.zeros((block, rest + block), F32)
    ends = {}
    for tile in range(2 * count_y):
        i, j = tile // count_y, tile % count_y
        total = 4.0 * own[i, j][:block] + own[i, j][block:]
        for k in range(neighbours_ref.shape[0]):
            source = source_of(neighbours_ref, k, tile, count_y)
            kind = kinds_ref[k, tile]
            chosen = ext_ref[source]
            pair = mul(chosen, table_high_ref[kind])
            total = total + (
                pair[:block] + (pair[block:] + mul(chosen[:block], table_low_ref[kind]))
            )
        (residual_low_ref, residual_high_ref)[i][j] = total
        ends[i, j] = total
        rest_tile = pick(odd_x, rest_a_ref[j + 1], rest_b_ref[j + 1])[i]
        basis_tile = jnp.concatenate([rest_tile, own[i, j][:block]], axis=0)
        partial = partial + mul3_t(total, basis_tile)
    for i in range(2):
        message_a_ref[i], message_b_ref[i] = pick(odd_y, ends[i, 0], ends[i, count_y - 1])
    message_a_ref[2] = partial
    partial_ref[...] = partial


def residual_rows_kernel(
    flags_ref, low_ref, high_ref, side_a_ref, side_b_ref, partial_ref, row_a_ref, row_b_ref
):
    count_y = low_ref.shape[0]
    odd_y, odd_x = flag_at(flags_ref, 0), flag_at(flags_ref, 1)
    sides = [pick(odd_y, side_a_ref[i], side_b_ref[i]) for i in range(2)]
    for place, j in ((0, 0), (1, count_y + 1)):
        row_a_ref[j], row_b_ref[j] = pick(odd_x, sides[0][place], sides[1][place])
    for j in range(count_y):
        row_a_ref[j + 1], row_b_ref[j + 1] = pick(odd_x, low_ref[j], high_ref[j])
    row_a_ref[count_y + 2] = partial_ref[...]


def operators_kernel(
    inverse_rows,
    neighbours_ref,
    kinds_ref,
    flags_ref,
    partial_ref,
    row_a_ref,
    row_b_ref,
    from_row_a_ref,
    from_row_b_ref,
    rest_a_ref,
    rest_b_ref,
    from_rest_a_ref,
    from_rest_b_ref,
    current_ref,
    table_high_ref,
    table_low_ref,
    weighted_low_ref,
    weighted_high_ref,
    coupling_ref,
    sums_ref,
    ext_ref,
    basis_ref,
):
    count_y, block, side = weighted_low_ref.shape
    wide, rest, _ = rest_a_ref.shape
    prior = rest + block
    odd_y, odd_x, in_low_y, in_high_y, in_low_x, in_high_x = (
        flag_at(flags_ref, place) for place in range(6)
    )
    coupling = partial_ref[...] * inverse_rows
    coupling_ref[...] = coupling
    coupling_high, coupling_low = split(coupling)

    for j in range(wide):
        rows = list(pick(odd_x, from_row_a_ref[j], from_row_b_ref[j]))
        rows[1:1] = pick(odd_x, row_a_ref[j], row_b_ref[j])
        rests = list(pick(odd_x, from_rest_a_ref[j], from_rest_b_ref[j]))
        rests[1:1] = pick(odd_x, rest_a_ref[j], rest_b_ref[j])
        for i in range(4):
            tile = jnp.concatenate([rests[i], current_ref[i * wide + j]], axis=0)
            high, low = split(tile)
            value = rows[i] - (
                mul(coupling_high, high) + (mul(coupling_high, low) + mul(coupling_low, high))
            )
            if i == 0:
                value = value * in_low_x
            if i == 3:
                value = value * in_high_x
            if j == 0:
                value = value * in_low_y
            if j == wide - 1:
                value = value * in_high_y
            if 0 < i < 3 and 0 < j < wide - 1:
                (weighted_low_ref, weighted_high_ref)[i - 1][j - 1] = value
                place = (i - 1) * count_y + j - 1
                basis_ref[place, :prior, :] = high
                basis_ref[place, prior:, :] = low
            high, low = split(value)
            ext_ref[i * wide + j, :block, :] = high
            ext_ref[i * wide + j, block:, :] = low
    with_basis = jnp.zeros((2 * block, prior), F32)
    with_own = jnp.zeros((block, 4 * block), F32)
    for tile in range(2 * count_y):
        i, j = tile // count_y, tile % count_y
        own = (weighted_low_ref, weighted_high_ref)[i][j]
        totals = jnp.concatenate([4.0 * own, own], axis=1)
        for k in range(neighbours_ref.shape[0]):
            source = source_of(neighbours_ref, k, tile, count_y)
            kind = kinds_ref[k, tile]
            chosen = ext_ref[source]
            pair = mul(chosen, table_high_ref[kind])
            totals = totals + (
                pair[:block] + (pair[block:] + mul(chosen[:block], table_low_ref[kind]))
            )
        applied = jnp.concatenate([totals[:, :side], totals[:, side:]], axis=0)
        high, low = split(applied)
        basis_high, basis_low = basis_ref[tile, :prior, :], basis_ref[tile, prior:, :]
        with_basis = with_basis + (
            mul_t(high, basis_high) + (mul_t(high, basis_low) + mul_t(low, basis_high))
        )
        right = jnp.concatenate([applied, own, jnp.zeros_like(own)], axis=0)
        with_own = with_own + mul3_t(own, right)
    sums_ref[: 2 * block, :] = with_basis
    sums_ref[2 * block :, :] = with_own


def factor_kernel(
    inverse_rows,
    sums_ref,
    weighted_low_ref,
    weighted_high_ref,
    new_ref,
    factor_ref,
    reduced_ref,
):
    count_y, block, _ = weighted_low_ref.shape
    prior = sums_ref.shape[1]
    tiles = 2 * count_y
    with_own = sums_ref[2 * block :, :] * inverse_rows
    gram = with_own[:, 2 * block : 3 * block]
    row_ids = lax.broadcasted_iota(jnp.int32, (block, block), 0)
    column_ids = lax.broadcasted_iota(jnp.int32, (block, block), 1)
    unit = jnp.where(row_ids == column_ids, 1.0, 0.0).astype(F32)
    work = jnp.concatenate([gram, unit], axis=1)
    rows = lax.broadcasted_iota(jnp.int32, work.shape, 0)
    group = 4
    for j in range(0, block, group):
        columns = [
            jnp.broadcast_to(work[:, j + a : j + a + 1], work.shape) for a in range(group)
        ]
        pivots = [work[j + a : j + a + 1, :] for a in range(group)]
        for a in range(group):
            at = j + a
            ratio = columns[a] * (1.0 / columns[a][at : at + 1, :])
            for b in range(a + 1, group):
                columns[b] = columns[b] - ratio * columns[b][at : at + 1, :]
                pivots[b] = pivots[b] - ratio[j + b : j + b + 1, :] * pivots[a]
            work = work - jnp.where(rows > at, ratio, 0.0) * pivots[a]
    work = work * lax.rsqrt(jnp.sum(work[:, :block] * unit, axis=1, keepdims=True))
    factor_ref[...] = jnp.where(column_ids >= row_ids, work[:, :block], 0.0)
    inverse = work[:, block:]
    for tile in range(tiles):
        own = (weighted_low_ref, weighted_high_ref)[tile // count_y][tile % count_y]
        new_ref[pl.ds(tile, block, stride=tiles), :] = mul3(inverse, own)
    for part in range(2):
        span = slice(part * block, (part + 1) * block)
        reduced_ref[part, :, :prior] = mul3(inverse, sums_ref[span, :] * inverse_rows)
        reduced_ref[part, :, prior:] = mul3_t(mul3_t(inverse, with_own[:, span]), inverse)


def swap(value, axis, step):
    return lax.ppermute(value, axis, [(i, i ^ step) for i in range(lax.axis_size(axis))])


def other_swap(value, axis):
    count = lax.axis_size(axis)
    pairs = [(i, ((i + 1) ^ 1) - 1) for i in range(count)]
    return lax.ppermute(value, axis, [(i, j if 0 <= j < count else i) for i, j in pairs])


def exchange(message_a, message_b, axis):
    return swap(message_a, axis, 1), other_swap(message_b, axis)


def total_along(value, axis, first=1, near=None):
    if lax.axis_size(axis) == 4 and first == 1:
        near = swap(value, axis, 1) if near is None else near
        return (value + swap(value, axis, 2)) + (near + swap(value, axis, 3))
    step = first
    while step < lax.axis_size(axis):
        value = value + swap(value, axis, step)
        step *= 2
    return value


def halved_total(value):
    half = value.shape[0] // 2
    upper = lax.axis_index("py") % 2 == 1
    first, second = value[:half], value[half:]
    kept = jnp.where(upper, second, first)
    kept = kept + swap(jnp.where(upper, first, second), "py", 1)
    kept = total_along(kept, "py", 2)
    kept = total_along(kept, "px")
    other = swap(kept, "py", 1)
    return jnp.concatenate(
        [jnp.where(upper, other, kept), jnp.where(upper, kept, other)], axis=0
    )


def shape(*dims, dtype=F32):
    return jax.ShapeDtypeStruct(dims, dtype)


def shards(prior_basis, previous, neighbours, tile_kinds, stiff_tiles, mass_tiles):
    block = previous.shape[0]
    prior, count_x, count_y, side = prior_basis.shape
    tiles = count_x * count_y
    wide = count_y + 2
    rest = prior - block
    kinds = stiff_tiles.shape[0]
    inverse_rows = 1.0 / (tiles * side * lax.axis_size("px") * lax.axis_size("py"))
    basis = prior_basis.reshape(-1, side)
    previous_rows = previous.reshape(-1, side)
    neighbours = neighbours.reshape(-1, tiles)
    tile_kinds = tile_kinds.reshape(-1, tiles)
    at_y, at_x = lax.axis_index("py"), lax.axis_index("px")
    flags = [at_y % 2 == 1, at_x % 2 == 1]
    flags += [at_y > 0, at_y < lax.axis_size("py") - 1]
    flags += [at_x > 0, at_x < lax.axis_size("px") - 1]
    flags = jnp.stack(flags + flags[:2]).astype(F32)
    flags = jnp.broadcast_to(flags[:, None], (8, side))

    def call(kernel, inputs, outputs, scratch=(), smem=0):
        return pl.pallas_call(
            kernel,
            out_shape=outputs,
            in_specs=[SMEM] * smem + [VMEM] * (len(inputs) - smem),
            out_specs=[VMEM] * len(outputs),
            scratch_shapes=scratch,
            compiler_params=PARAMS,
        )(*inputs)

    side_a, side_b, row_a, row_b = call(
        pack_kernel,
        (flags, basis, previous_rows),
        [shape(count_x, prior + block, side)] * 2 + [shape(count_y, 2 * block, side)] * 2,
    )
    tables = call(
        tables_kernel,
        (stiff_tiles, mass_tiles),
        [shape(kinds, 2 * side, side, dtype=BF16)] * 2
        + [shape(kinds, side, 2 * side, dtype=BF16)] * 2,
    )
    from_side_a, from_side_b = exchange(side_a, side_b, "py")
    from_row_a, from_row_b = exchange(row_a, row_b, "px")
    from_side_a, neighbours, tile_kinds, *tables = lax.optimization_barrier(
        (from_side_a, neighbours, tile_kinds, *tables)
    )
    corner_a, corner_b, rest_a, rest_b = call(
        corners_kernel,
        (flags, basis, from_side_a, from_side_b),
        [shape(2, 2 * block, side)] * 2 + [shape(wide, rest, side)] * 2,
    )
    from_corner_a, from_corner_b = exchange(corner_a, corner_b, "px")
    from_rest_a, from_rest_b = exchange(rest_a, rest_b, "px")
    residual_low, residual_high, message_a, message_b, partial, current = call(
        residual_kernel,
        (
            neighbours,
            tile_kinds,
            flags,
            row_a,
            row_b,
            from_row_a,
            from_row_b,
            from_side_a,
            from_side_b,
            from_corner_a,
            from_corner_b,
            rest_a,
            rest_b,
            *tables[:2],
        ),
        [shape(count_y, block, side)] * 2
        + [shape(3, block, side), shape(2, block, side)]
        + [shape(block, prior), shape(4 * wide, block, side)],
        [pltpu.VMEM((4 * wide, 2 * block, 2 * side), BF16)],
        smem=2,
    )
    from_side_a, from_side_b = exchange(message_a, message_b, "py")
    partial = total_along(partial + from_side_a[-1], "py", 2)
    from_side_a, from_rest_a, from_rest_b = lax.optimization_barrier(
        (from_side_a, from_rest_a, from_rest_b)
    )
    row_a, row_b = call(
        residual_rows_kernel,
        (flags, residual_low, residual_high, from_side_a, from_side_b, partial),
        [shape(wide + 1, block, side), shape(wide, block, side)],
    )
    from_row_a, from_row_b = exchange(row_a, row_b, "px")
    partial = total_along(partial, "px", near=from_row_a[-1])
    weighted_low, weighted_high, coupling, sums = call(
        functools.partial(operators_kernel, inverse_rows),
        (
            neighbours,
            tile_kinds,
            flags,
            partial,
            row_a,
            row_b,
            from_row_a,
            from_row_b,
            rest_a,
            rest_b,
            from_rest_a,
            from_rest_b,
            current,
            *tables[2:],
        ),
        [shape(count_y, block, side)] * 2 + [shape(block, prior), shape(3 * block, prior)],
        [
            pltpu.VMEM((4 * wide, 2 * block, side), BF16),
            pltpu.VMEM((tiles, 2 * prior, side), BF16),
        ],
        smem=2,
    )
    new_block, factor, reduced = call(
        functools.partial(factor_kernel, inverse_rows),
        (halved_total(sums), weighted_low, weighted_high),
        [
            shape(block * tiles, side),
            shape(block, block),
            shape(2, block, prior + block),
        ],
    )
    return (
        new_block.reshape(previous.shape),
        coupling.T,
        factor,
        reduced.swapaxes(1, 2),
    )


def solution(mesh):
    placed = (
        P("case", "px", "py", None),
        P("case", "px", "py", None),
        P(None, "px", "py"),
        P(None, "px", "py"),
        P(),
        P(),
    )
    return jax.shard_map(
        shards,
        mesh=mesh,
        in_specs=placed,
        out_specs=(
            P("case", "px", "py", None),
            P("case", None),
            P("case", None),
            P("case", None, None),
        ),
        check_vma=False,
    )
```

```python
import functools

import jax
import jax.numpy as jnp
from jax import lax
from jax.experimental import pallas as pl
from jax.experimental.pallas import tpu as pltpu
from jax.sharding import PartitionSpec as P

F32 = jnp.float32
BF16 = jnp.bfloat16
VMEM = pl.BlockSpec(memory_space=pltpu.VMEM)
SMEM = pl.BlockSpec(memory_space=pltpu.SMEM)
MIB = 1024 * 1024


def split(value):
    high = value.astype(BF16)
    return high, (value - high.astype(F32)).astype(BF16)


def mul(left, right):
    return jnp.dot(left, right, preferred_element_type=F32)


def mul_t(left, right):
    return lax.dot_general(left, right, (((1,), (1,)), ((), ())), preferred_element_type=F32)


def mul3(left, right):
    left_high, left_low = split(left)
    right_high, right_low = split(right)
    return mul(left_high, right_high) + (mul(left_high, right_low) + mul(left_low, right_high))


def mul3_t(left, right):
    left_high, left_low = split(left)
    right_high, right_low = split(right)
    return mul_t(left_high, right_high) + (
        mul_t(left_high, right_low) + mul_t(left_low, right_high)
    )


def split_tables(stiff_ref, mass_ref, high_ref, low_ref, axis):
    side = stiff_ref.shape[1]
    for kind in range(stiff_ref.shape[0]):
        for place, ref in enumerate((stiff_ref, mass_ref)):
            span = [kind, slice(None), slice(None)]
            span[axis] = slice(place * side, (place + 1) * side)
            high_ref[tuple(span)], low_ref[tuple(span)] = split(ref[kind])


def pick(flag, first, second):
    flag = flag > 0.0
    return jnp.where(flag, first, second), jnp.where(flag, second, first)


def flag_at(flags_ref, place):
    return flags_ref[place : place + 1, :]


def pack_kernel(flags_ref, vectors_ref, side_a_ref, side_b_ref, row_a_ref, row_b_ref):
    count_x, sides, _ = side_a_ref.shape
    count_y, both, _ = row_a_ref.shape
    tiles = count_x * count_y
    odd_y, odd_x = flag_at(flags_ref, 0), flag_at(flags_ref, 1)

    def tile_of(i, j, count):
        first = (sides - count) * tiles + i * count_y + j
        return vectors_ref[pl.ds(first, count, stride=tiles), :]

    for i in range(count_x):
        side_a_ref[i], side_b_ref[i] = pick(
            odd_y, tile_of(i, 0, sides), tile_of(i, count_y - 1, sides)
        )
    for j in range(count_y):
        row_a_ref[j], row_b_ref[j] = pick(odd_x, tile_of(0, j, both), tile_of(1, j, both))


def corners_kernel(
    flags_ref,
    vectors_ref,
    side_a_ref,
    side_b_ref,
    corner_a_ref,
    corner_b_ref,
    rest_a_ref,
    rest_b_ref,
):
    wide, rest, _ = rest_a_ref.shape
    tiles = 2 * (wide - 2)
    odd_y, odd_x = flag_at(flags_ref, 0), flag_at(flags_ref, 1)
    ends = [pick(odd_y, side_a_ref[i], side_b_ref[i]) for i in range(2)]
    for place, j in ((0, 0), (1, wide - 1)):
        corner_a_ref[place], corner_b_ref[place] = pick(
            odd_x, ends[0][place][rest:], ends[1][place][rest:]
        )
        rest_a_ref[j], rest_b_ref[j] = pick(
            odd_x, ends[0][place][:rest], ends[1][place][:rest]
        )
    for j in range(wide - 2):
        rest_a_ref[j + 1], rest_b_ref[j + 1] = pick(
            odd_x,
            vectors_ref[pl.ds(j, rest, stride=tiles), :],
            vectors_ref[pl.ds(wide - 2 + j, rest, stride=tiles), :],
        )


def residual_kernel(
    codes_ref,
    flags_ref,
    row_a_ref,
    row_b_ref,
    from_row_a_ref,
    from_row_b_ref,
    from_side_a_ref,
    from_side_b_ref,
    from_corner_a_ref,
    from_corner_b_ref,
    rest_a_ref,
    rest_b_ref,
    stiff_ref,
    mass_ref,
    residual_low_ref,
    residual_high_ref,
    message_a_ref,
    message_b_ref,
    partial_ref,
    current_ref,
    ext_ref,
    table_high_ref,
    table_low_ref,
):
    split_tables(stiff_ref, mass_ref, table_high_ref, table_low_ref, 1)
    count_y, both, side = row_a_ref.shape
    wide = count_y + 2
    block = both // 2
    rest = rest_a_ref.shape[1]
    odd_y, odd_x, in_low_y, in_high_y, in_low_x, in_high_x = (
        flag_at(flags_ref, place) for place in range(6)
    )

    def store(i, j, value):
        current_ref[i * wide + j] = value[:block]
        for part in range(2):
            high, low = split(value[part * block : (part + 1) * block])
            ext_ref[i * wide + j, :block, part * side : (part + 1) * side] = high
            ext_ref[i * wide + j, block:, part * side : (part + 1) * side] = low

    own = {}
    for j in range(count_y):
        own[0, j], own[1, j] = pick(odd_x, row_a_ref[j], row_b_ref[j])
        store(1, j + 1, own[0, j])
        store(2, j + 1, own[1, j])
        low, high = pick(odd_x, from_row_a_ref[j], from_row_b_ref[j])
        store(0, j + 1, low * in_low_x)
        store(3, j + 1, high * in_high_x)
    for i in range(2):
        low, high = pick(odd_y, from_side_a_ref[i, rest:, :], from_side_b_ref[i, rest:, :])
        store(i + 1, 0, low * in_low_y)
        store(i + 1, wide - 1, high * in_high_y)
    for place, j, inside in ((0, 0, in_low_y), (1, wide - 1, in_high_y)):
        low, high = pick(odd_x, from_corner_a_ref[place], from_corner_b_ref[place])
        store(0, j, low * (in_low_x * inside))
        store(3, j, high * (in_high_x * inside))
    partial = jnp.zeros((block, rest + block), F32)
    ends = {}
    for tile in range(2 * count_y):
        i, j = tile // count_y, tile % count_y
        total = 4.0 * own[i, j][:block] + own[i, j][block:]
        for k in range(codes_ref.shape[1]):
            kind = codes_ref[1, k, tile]
            chosen = ext_ref[codes_ref[0, k, tile]]
            pair = mul(chosen, table_high_ref[kind])
            total = total + (
                pair[:block] + (pair[block:] + mul(chosen[:block], table_low_ref[kind]))
            )
        (residual_low_ref, residual_high_ref)[i][j] = total
        ends[i, j] = total
        rest_tile = pick(odd_x, rest_a_ref[j + 1], rest_b_ref[j + 1])[i]
        basis_tile = jnp.concatenate([rest_tile, own[i, j][:block]], axis=0)
        partial = partial + mul3_t(total, basis_tile)
    for i in range(2):
        message_a_ref[i], message_b_ref[i] = pick(odd_y, ends[i, 0], ends[i, count_y - 1])
    message_a_ref[2] = partial
    partial_ref[...] = partial


def residual_rows_kernel(
    flags_ref, low_ref, high_ref, side_a_ref, side_b_ref, row_a_ref, row_b_ref
):
    count_y = low_ref.shape[0]
    odd_y, odd_x = flag_at(flags_ref, 0), flag_at(flags_ref, 1)
    sides = [pick(odd_y, side_a_ref[i], side_b_ref[i]) for i in range(2)]
    for place, j in ((0, 0), (1, count_y + 1)):
        row_a_ref[j], row_b_ref[j] = pick(odd_x, sides[0][place], sides[1][place])
    for j in range(count_y):
        row_a_ref[j + 1], row_b_ref[j + 1] = pick(odd_x, low_ref[j], high_ref[j])


def operators_kernel(
    inverse_rows,
    codes_ref,
    flags_ref,
    partial_ref,
    row_a_ref,
    row_b_ref,
    from_row_a_ref,
    from_row_b_ref,
    rest_a_ref,
    rest_b_ref,
    from_rest_a_ref,
    from_rest_b_ref,
    current_ref,
    stiff_ref,
    mass_ref,
    weighted_low_ref,
    weighted_high_ref,
    coupling_ref,
    sums_ref,
    ext_ref,
    basis_ref,
    table_high_ref,
    table_low_ref,
):
    split_tables(stiff_ref, mass_ref, table_high_ref, table_low_ref, 2)
    count_y, block, side = weighted_low_ref.shape
    wide, rest, _ = rest_a_ref.shape
    prior = rest + block
    odd_y, odd_x, in_low_y, in_high_y, in_low_x, in_high_x = (
        flag_at(flags_ref, place) for place in range(6)
    )
    coupling = partial_ref[...] * inverse_rows
    coupling_ref[...] = coupling
    coupling_high, coupling_low = split(coupling)

    for j in range(wide):
        rows = list(pick(odd_x, from_row_a_ref[j], from_row_b_ref[j]))
        rows[1:1] = pick(odd_x, row_a_ref[j], row_b_ref[j])
        rests = list(pick(odd_x, from_rest_a_ref[j], from_rest_b_ref[j]))
        rests[1:1] = pick(odd_x, rest_a_ref[j], rest_b_ref[j])
        for i in range(4):
            tile = jnp.concatenate([rests[i], current_ref[i * wide + j]], axis=0)
            high, low = split(tile)
            value = rows[i] - (
                mul(coupling_high, high) + (mul(coupling_high, low) + mul(coupling_low, high))
            )
            if i == 0:
                value = value * in_low_x
            if i == 3:
                value = value * in_high_x
            if j == 0:
                value = value * in_low_y
            if j == wide - 1:
                value = value * in_high_y
            if 0 < i < 3 and 0 < j < wide - 1:
                (weighted_low_ref, weighted_high_ref)[i - 1][j - 1] = value
                place = (i - 1) * count_y + j - 1
                basis_ref[place, :prior, :] = high
                basis_ref[place, prior:, :] = low
            high, low = split(value)
            ext_ref[i * wide + j, :block, :] = high
            ext_ref[i * wide + j, block:, :] = low
    with_basis = jnp.zeros((2 * block, prior), F32)
    with_own = jnp.zeros((block, 4 * block), F32)
    for tile in range(2 * count_y):
        i, j = tile // count_y, tile % count_y
        own = (weighted_low_ref, weighted_high_ref)[i][j]
        totals = jnp.concatenate([4.0 * own, own], axis=1)
        for k in range(codes_ref.shape[1]):
            kind = codes_ref[1, k, tile]
            chosen = ext_ref[codes_ref[0, k, tile]]
            pair = mul(chosen, table_high_ref[kind])
            totals = totals + (
                pair[:block] + (pair[block:] + mul(chosen[:block], table_low_ref[kind]))
            )
        applied = jnp.concatenate([totals[:, :side], totals[:, side:]], axis=0)
        high, low = split(applied)
        basis_high, basis_low = basis_ref[tile, :prior, :], basis_ref[tile, prior:, :]
        with_basis = with_basis + (
            mul_t(high, basis_high) + (mul_t(high, basis_low) + mul_t(low, basis_high))
        )
        right = jnp.concatenate([applied, own, jnp.zeros_like(own)], axis=0)
        with_own = with_own + mul3_t(own, right)
    sums_ref[: 2 * block, :] = with_basis
    sums_ref[2 * block :, :] = with_own


def factor_kernel(
    inverse_rows,
    sums_ref,
    weighted_low_ref,
    weighted_high_ref,
    new_ref,
    factor_ref,
    reduced_ref,
):
    count_y, block, _ = weighted_low_ref.shape
    prior = sums_ref.shape[1]
    tiles = 2 * count_y
    with_own = sums_ref[2 * block :, :] * inverse_rows
    gram = with_own[:, 2 * block : 3 * block]
    row_ids = lax.broadcasted_iota(jnp.int32, (block, block), 0)
    column_ids = lax.broadcasted_iota(jnp.int32, (block, block), 1)
    unit = jnp.where(row_ids == column_ids, 1.0, 0.0).astype(F32)
    work = jnp.concatenate([gram, unit], axis=1)
    rows = lax.broadcasted_iota(jnp.int32, work.shape, 0)
    group = 4
    for j in range(0, block, group):
        columns = [
            jnp.broadcast_to(work[:, j + a : j + a + 1], work.shape) for a in range(group)
        ]
        pivots = [work[j + a : j + a + 1, :] for a in range(group)]
        for a in range(group):
            at = j + a
            ratio = columns[a] * (1.0 / columns[a][at : at + 1, :])
            for b in range(a + 1, group):
                columns[b] = columns[b] - ratio * columns[b][at : at + 1, :]
                pivots[b] = pivots[b] - ratio[j + b : j + b + 1, :] * pivots[a]
            work = work - jnp.where(rows > at, ratio, 0.0) * pivots[a]
    work = work * lax.rsqrt(jnp.sum(work[:, :block] * unit, axis=1, keepdims=True))
    factor_ref[...] = jnp.where(column_ids >= row_ids, work[:, :block], 0.0)
    inverse = work[:, block:]
    for tile in range(tiles):
        own = (weighted_low_ref, weighted_high_ref)[tile // count_y][tile % count_y]
        new_ref[pl.ds(tile, block, stride=tiles), :] = mul3(inverse, own)
    for part in range(2):
        span = slice(part * block, (part + 1) * block)
        reduced_ref[part, :, :prior] = mul3(inverse, sums_ref[span, :] * inverse_rows)
        reduced_ref[part, :, prior:] = mul3_t(mul3_t(inverse, with_own[:, span]), inverse)


def swap(value, axis, step):
    return lax.ppermute(value, axis, [(i, i ^ step) for i in range(lax.axis_size(axis))])


def other_swap(value, axis):
    count = lax.axis_size(axis)
    pairs = [(i, ((i + 1) ^ 1) - 1) for i in range(count)]
    return lax.ppermute(value, axis, [(i, j if 0 <= j < count else i) for i, j in pairs])


def exchange(message_a, message_b, axis):
    return swap(message_a, axis, 1), other_swap(message_b, axis)


def total_at_once(value, axis):
    if lax.axis_size(axis) != 4:
        return total_along(value, axis)
    return (value + swap(value, axis, 2)) + (swap(value, axis, 1) + swap(value, axis, 3))


def total_along(value, axis, first=1):
    step = first
    while step < lax.axis_size(axis):
        value = value + swap(value, axis, step)
        step *= 2
    return value


def halved_total(value):
    half = value.shape[0] // 2
    upper = lax.axis_index("py") % 2 == 1
    first, second = value[:half], value[half:]
    kept = jnp.where(upper, second, first)
    kept = kept + swap(jnp.where(upper, first, second), "py", 1)
    kept = total_along(kept, "py", 2)
    kept = total_at_once(kept, "px")
    other = swap(kept, "py", 1)
    return jnp.concatenate(
        [jnp.where(upper, other, kept), jnp.where(upper, kept, other)], axis=0
    )


def shape(*dims, dtype=F32):
    return jax.ShapeDtypeStruct(dims, dtype)


def shards(prior_basis, previous, neighbours, tile_kinds, stiff_tiles, mass_tiles):
    block = previous.shape[0]
    prior, count_x, count_y, side = prior_basis.shape
    tiles = count_x * count_y
    wide = count_y + 2
    rest = prior - block
    kinds = stiff_tiles.shape[0]
    inverse_rows = 1.0 / (tiles * side * lax.axis_size("px") * lax.axis_size("py"))
    vectors = jnp.concatenate(
        [prior_basis.reshape(-1, side), previous.reshape(-1, side)], axis=0
    )
    place = jnp.arange(count_x)[:, None] * wide + jnp.arange(count_y)[None, :]
    sources = place[None] + (neighbours // 3) * wide + neighbours % 3
    codes = jnp.stack([sources, tile_kinds]).astype(jnp.int32).reshape(2, -1, tiles)
    at_y, at_x = lax.axis_index("py"), lax.axis_index("px")
    flags = [at_y % 2 == 1, at_x % 2 == 1]
    flags += [at_y > 0, at_y < lax.axis_size("py") - 1]
    flags += [at_x > 0, at_x < lax.axis_size("px") - 1]
    flags = jnp.stack(flags + flags[:2]).astype(F32)
    flags = jnp.broadcast_to(flags[:, None], (8, side))

    def call(kernel, inputs, outputs, scratch=(), smem=0, limit=8):
        specs = [SMEM] * smem + [VMEM] * (len(inputs) - smem)
        return pl.pallas_call(
            kernel,
            out_shape=outputs,
            in_specs=specs,
            out_specs=[VMEM] * len(outputs),
            scratch_shapes=scratch,
            compiler_params=pltpu.CompilerParams(vmem_limit_bytes=limit * MIB),
        )(*inputs)

    side_a, side_b, row_a, row_b = call(
        pack_kernel,
        (flags, vectors),
        [shape(count_x, prior + block, side)] * 2 + [shape(count_y, 2 * block, side)] * 2,
    )
    from_side_a, from_side_b = exchange(side_a, side_b, "py")
    from_row_a, from_row_b = exchange(row_a, row_b, "px")
    from_side_a, codes = lax.optimization_barrier((from_side_a, codes))
    corner_a, corner_b, rest_a, rest_b = call(
        corners_kernel,
        (flags, vectors, from_side_a, from_side_b),
        [shape(2, 2 * block, side)] * 2 + [shape(wide, rest, side)] * 2,
    )
    from_corner_a, from_corner_b = exchange(corner_a, corner_b, "px")
    from_rest_a, from_rest_b = exchange(rest_a, rest_b, "px")
    residual_low, residual_high, message_a, message_b, partial, current = call(
        residual_kernel,
        (
            codes,
            flags,
            row_a,
            row_b,
            from_row_a,
            from_row_b,
            from_side_a,
            from_side_b,
            from_corner_a,
            from_corner_b,
            rest_a,
            rest_b,
            stiff_tiles,
            mass_tiles,
        ),
        [shape(count_y, block, side)] * 2
        + [shape(3, block, side), shape(2, block, side)]
        + [shape(block, prior), shape(4 * wide, block, side)],
        [pltpu.VMEM((4 * wide, 2 * block, 2 * side), BF16)]
        + [pltpu.VMEM((kinds, 2 * side, side), BF16)] * 2,
        smem=1,
    )
    from_side_a, from_side_b = exchange(message_a, message_b, "py")
    partial = total_along(partial + from_side_a[-1], "py", 2)
    partial, from_rest_a, from_rest_b = lax.optimization_barrier(
        (partial, from_rest_a, from_rest_b)
    )
    row_a, row_b = call(
        residual_rows_kernel,
        (flags, residual_low, residual_high, from_side_a, from_side_b),
        [shape(wide, block, side)] * 2,
    )
    from_row_a, from_row_b = exchange(row_a, row_b, "px")
    partial = total_along(partial, "px")
    weighted_low, weighted_high, coupling, sums = call(
        functools.partial(operators_kernel, inverse_rows),
        (
            codes,
            flags,
            partial,
            row_a,
            row_b,
            from_row_a,
            from_row_b,
            rest_a,
            rest_b,
            from_rest_a,
            from_rest_b,
            current,
            stiff_tiles,
            mass_tiles,
        ),
        [shape(count_y, block, side)] * 2 + [shape(block, prior), shape(3 * block, prior)],
        [
            pltpu.VMEM((4 * wide, 2 * block, side), BF16),
            pltpu.VMEM((tiles, 2 * prior, side), BF16),
        ]
        + [pltpu.VMEM((kinds, side, 2 * side), BF16)] * 2,
        smem=1,
    )
    new_block, factor, reduced = call(
        functools.partial(factor_kernel, inverse_rows),
        (halved_total(sums), weighted_low, weighted_high),
        [
            shape(block * tiles, side),
            shape(block, block),
            shape(2, block, prior + block),
        ],
    )
    return (
        new_block.reshape(previous.shape),
        coupling.T,
        factor,
        reduced.swapaxes(1, 2),
    )


def solution(mesh):
    placed = (
        P("case", "px", "py", None),
        P("case", "px", "py", None),
        P(None, "px", "py"),
        P(None, "px", "py"),
        P(),
        P(),
    )
    return jax.shard_map(
        shards,
        mesh=mesh,
        in_specs=placed,
        out_specs=(
            P("case", "px", "py", None),
            P("case", None),
            P("case", None),
            P("case", None, None),
        ),
        check_vma=False,
    )
```

```python
import functools

import jax
import jax.numpy as jnp
from jax import lax
from jax.experimental import pallas as pl
from jax.experimental.pallas import tpu as pltpu
from jax.sharding import PartitionSpec as P

F32 = jnp.float32
BF16 = jnp.bfloat16
VMEM = pl.BlockSpec(memory_space=pltpu.VMEM)
SMEM = pl.BlockSpec(memory_space=pltpu.SMEM)
MIB = 1024 * 1024


def split(value):
    high = value.astype(BF16)
    return high, (value - high.astype(F32)).astype(BF16)


def mul(left, right):
    return jnp.dot(left, right, preferred_element_type=F32)


def mul_t(left, right):
    return lax.dot_general(left, right, (((1,), (1,)), ((), ())), preferred_element_type=F32)


def mul3(left, right):
    left_high, left_low = split(left)
    right_high, right_low = split(right)
    return mul(left_high, right_high) + (mul(left_high, right_low) + mul(left_low, right_high))


def mul3_t(left, right):
    left_high, left_low = split(left)
    right_high, right_low = split(right)
    return mul_t(left_high, right_high) + (
        mul_t(left_high, right_low) + mul_t(left_low, right_high)
    )


def split_tables(stiff_ref, mass_ref, high_ref, low_ref, axis):
    side = stiff_ref.shape[1]
    for kind in range(stiff_ref.shape[0]):
        for place, ref in enumerate((stiff_ref, mass_ref)):
            span = [kind, slice(None), slice(None)]
            span[axis] = slice(place * side, (place + 1) * side)
            high_ref[tuple(span)], low_ref[tuple(span)] = split(ref[kind])


def pick(flag, first, second):
    flag = flag > 0.0
    return jnp.where(flag, first, second), jnp.where(flag, second, first)


def flag_at(flags_ref, place):
    return flags_ref[place : place + 1, :]


def pack_kernel(
    flags_ref,
    vectors_ref,
    side_a_ref,
    side_b_ref,
    row_a_ref,
    row_b_ref,
    rest_a_ref,
    rest_b_ref,
):
    count_y, both, _ = row_a_ref.shape
    rest = rest_a_ref.shape[1]
    tiles = 2 * count_y
    odd_y, odd_x = flag_at(flags_ref, 0), flag_at(flags_ref, 1)

    def block_tile(i, j):
        return vectors_ref[pl.ds(rest * tiles + i * count_y + j, both, stride=tiles), :]

    def rest_tile(i, j):
        return vectors_ref[pl.ds(i * count_y + j, rest, stride=tiles), :]

    for i in range(2):
        side_a_ref[i], side_b_ref[i] = pick(odd_y, block_tile(i, 0), block_tile(i, count_y - 1))
    for j in range(count_y):
        row_a_ref[j], row_b_ref[j] = pick(odd_x, block_tile(0, j), block_tile(1, j))
        rest_a_ref[j], rest_b_ref[j] = pick(odd_x, rest_tile(0, j), rest_tile(1, j))


def corners_kernel(flags_ref, side_a_ref, side_b_ref, corner_a_ref, corner_b_ref):
    odd_y, odd_x = flag_at(flags_ref, 0), flag_at(flags_ref, 1)
    ends = [pick(odd_y, side_a_ref[i], side_b_ref[i]) for i in range(2)]
    for place in range(2):
        corner_a_ref[place], corner_b_ref[place] = pick(odd_x, ends[0][place], ends[1][place])


def columns_kernel(
    flags_ref, row_a_ref, row_b_ref, from_row_a_ref, from_row_b_ref, *refs
):
    odd_y, odd_x = flag_at(flags_ref, 0), flag_at(flags_ref, 1)
    side_a_ref, side_b_ref = refs[-2:]
    columns = []
    for j in (0, row_b_ref.shape[0] - 1):
        column = list(pick(odd_x, from_row_a_ref[j], from_row_b_ref[j]))
        column[1:1] = pick(odd_x, row_a_ref[j], row_b_ref[j])
        columns.append(column)
    for i in range(4):
        side_a_ref[i], side_b_ref[i] = pick(odd_y, columns[0][i], columns[1][i])
    if len(refs) == 3:
        side_a_ref[4] = refs[0][...]


def residual_kernel(
    codes_ref,
    flags_ref,
    row_a_ref,
    row_b_ref,
    from_row_a_ref,
    from_row_b_ref,
    from_side_a_ref,
    from_side_b_ref,
    from_corner_a_ref,
    from_corner_b_ref,
    rest_a_ref,
    rest_b_ref,
    stiff_ref,
    mass_ref,
    residual_a_ref,
    residual_b_ref,
    partial_ref,
    current_ref,
    ext_ref,
    table_high_ref,
    table_low_ref,
):
    split_tables(stiff_ref, mass_ref, table_high_ref, table_low_ref, 1)
    count_y, both, side = row_a_ref.shape
    wide = count_y + 2
    block = both // 2
    rest = rest_a_ref.shape[1]
    odd_y, odd_x, in_low_y, in_high_y, in_low_x, in_high_x = (
        flag_at(flags_ref, place) for place in range(6)
    )

    def store(i, j, value):
        current_ref[i * wide + j] = value[:block]
        for part in range(2):
            high, low = split(value[part * block : (part + 1) * block])
            ext_ref[i * wide + j, :block, part * side : (part + 1) * side] = high
            ext_ref[i * wide + j, block:, part * side : (part + 1) * side] = low

    own = {}
    for j in range(count_y):
        own[0, j], own[1, j] = pick(odd_x, row_a_ref[j], row_b_ref[j])
        store(1, j + 1, own[0, j])
        store(2, j + 1, own[1, j])
        low, high = pick(odd_x, from_row_a_ref[j], from_row_b_ref[j])
        store(0, j + 1, low * in_low_x)
        store(3, j + 1, high * in_high_x)
    for i in range(2):
        low, high = pick(odd_y, from_side_a_ref[i], from_side_b_ref[i])
        store(i + 1, 0, low * in_low_y)
        store(i + 1, wide - 1, high * in_high_y)
    for place, j, inside in ((0, 0, in_low_y), (1, wide - 1, in_high_y)):
        low, high = pick(odd_x, from_corner_a_ref[place], from_corner_b_ref[place])
        store(0, j, low * (in_low_x * inside))
        store(3, j, high * (in_high_x * inside))
    partial = jnp.zeros((block, rest + block), F32)
    totals = {}
    for tile in range(2 * count_y):
        i, j = tile // count_y, tile % count_y
        total = 4.0 * own[i, j][:block] + own[i, j][block:]
        for k in range(codes_ref.shape[1]):
            kind = codes_ref[1, k, tile]
            chosen = ext_ref[codes_ref[0, k, tile]]
            pair = mul(chosen, table_high_ref[kind])
            total = total + (
                pair[:block] + (pair[block:] + mul(chosen[:block], table_low_ref[kind]))
            )
        totals[i, j] = total
        rest_tile = pick(odd_x, rest_a_ref[j], rest_b_ref[j])[i]
        basis_tile = jnp.concatenate([rest_tile, own[i, j][:block]], axis=0)
        partial = partial + mul3_t(total, basis_tile)
    for j in range(count_y):
        residual_a_ref[j], residual_b_ref[j] = pick(odd_x, totals[0, j], totals[1, j])
    residual_a_ref[count_y] = partial
    partial_ref[...] = partial


def operators_kernel(
    inverse_rows,
    codes_ref,
    flags_ref,
    partial_ref,
    row_a_ref,
    row_b_ref,
    from_row_a_ref,
    from_row_b_ref,
    from_side_a_ref,
    from_side_b_ref,
    rest_a_ref,
    rest_b_ref,
    from_rest_a_ref,
    from_rest_b_ref,
    rest_side_a_ref,
    rest_side_b_ref,
    current_ref,
    stiff_ref,
    mass_ref,
    weighted_low_ref,
    weighted_high_ref,
    coupling_ref,
    sums_ref,
    ext_ref,
    basis_ref,
    table_high_ref,
    table_low_ref,
):
    split_tables(stiff_ref, mass_ref, table_high_ref, table_low_ref, 2)
    count_y, block, side = weighted_low_ref.shape
    wide = count_y + 2
    rest = rest_a_ref.shape[1]
    prior = rest + block
    odd_y, odd_x, in_low_y, in_high_y, in_low_x, in_high_x = (
        flag_at(flags_ref, place) for place in range(6)
    )
    coupling = partial_ref[...] * inverse_rows
    coupling_ref[...] = coupling
    coupling_high, coupling_low = split(coupling)

    for j in range(wide):
        if 0 < j < wide - 1:
            rows = list(pick(odd_x, from_row_a_ref[j - 1], from_row_b_ref[j - 1]))
            rows[1:1] = pick(odd_x, row_a_ref[j - 1], row_b_ref[j - 1])
            rests = list(pick(odd_x, from_rest_a_ref[j - 1], from_rest_b_ref[j - 1]))
            rests[1:1] = pick(odd_x, rest_a_ref[j - 1], rest_b_ref[j - 1])
        else:
            high = j // (wide - 1)
            rows = [pick(odd_y, from_side_a_ref[i], from_side_b_ref[i])[high] for i in range(4)]
            rests = [pick(odd_y, rest_side_a_ref[i], rest_side_b_ref[i])[high] for i in range(4)]
        for i in range(4):
            tile = jnp.concatenate([rests[i], current_ref[i * wide + j]], axis=0)
            high, low = split(tile)
            value = rows[i] - (
                mul(coupling_high, high) + (mul(coupling_high, low) + mul(coupling_low, high))
            )
            if i == 0:
                value = value * in_low_x
            if i == 3:
                value = value * in_high_x
            if j == 0:
                value = value * in_low_y
            if j == wide - 1:
                value = value * in_high_y
            if 0 < i < 3 and 0 < j < wide - 1:
                (weighted_low_ref, weighted_high_ref)[i - 1][j - 1] = value
                place = (i - 1) * count_y + j - 1
                basis_ref[place, :prior, :] = high
                basis_ref[place, prior:, :] = low
            high, low = split(value)
            ext_ref[i * wide + j, :block, :] = high
            ext_ref[i * wide + j, block:, :] = low
    with_basis = jnp.zeros((2 * block, prior), F32)
    with_own = jnp.zeros((block, 4 * block), F32)
    for tile in range(2 * count_y):
        i, j = tile // count_y, tile % count_y
        own = (weighted_low_ref, weighted_high_ref)[i][j]
        totals = jnp.concatenate([4.0 * own, own], axis=1)
        for k in range(codes_ref.shape[1]):
            kind = codes_ref[1, k, tile]
            chosen = ext_ref[codes_ref[0, k, tile]]
            pair = mul(chosen, table_high_ref[kind])
            totals = totals + (
                pair[:block] + (pair[block:] + mul(chosen[:block], table_low_ref[kind]))
            )
        applied = jnp.concatenate([totals[:, :side], totals[:, side:]], axis=0)
        high, low = split(applied)
        basis_high, basis_low = basis_ref[tile, :prior, :], basis_ref[tile, prior:, :]
        with_basis = with_basis + (
            mul_t(high, basis_high) + (mul_t(high, basis_low) + mul_t(low, basis_high))
        )
        right = jnp.concatenate([applied, own, jnp.zeros_like(own)], axis=0)
        with_own = with_own + mul3_t(own, right)
    sums_ref[: 2 * block, :] = with_basis
    sums_ref[2 * block :, :] = with_own


def factor_kernel(
    inverse_rows,
    sums_ref,
    weighted_low_ref,
    weighted_high_ref,
    new_ref,
    factor_ref,
    reduced_ref,
):
    count_y, block, _ = weighted_low_ref.shape
    prior = sums_ref.shape[1]
    tiles = 2 * count_y
    with_own = sums_ref[2 * block :, :] * inverse_rows
    gram = with_own[:, 2 * block : 3 * block]
    row_ids = lax.broadcasted_iota(jnp.int32, (block, block), 0)
    column_ids = lax.broadcasted_iota(jnp.int32, (block, block), 1)
    unit = jnp.where(row_ids == column_ids, 1.0, 0.0).astype(F32)
    work = jnp.concatenate([gram, unit], axis=1)
    rows = lax.broadcasted_iota(jnp.int32, work.shape, 0)
    group = 4
    for j in range(0, block, group):
        columns = [
            jnp.broadcast_to(work[:, j + a : j + a + 1], work.shape) for a in range(group)
        ]
        pivots = [work[j + a : j + a + 1, :] for a in range(group)]
        for a in range(group):
            at = j + a
            ratio = columns[a] * (1.0 / columns[a][at : at + 1, :])
            for b in range(a + 1, group):
                columns[b] = columns[b] - ratio * columns[b][at : at + 1, :]
                pivots[b] = pivots[b] - ratio[j + b : j + b + 1, :] * pivots[a]
            work = work - jnp.where(rows > at, ratio, 0.0) * pivots[a]
    work = work * lax.rsqrt(jnp.sum(work[:, :block] * unit, axis=1, keepdims=True))
    factor_ref[...] = jnp.where(column_ids >= row_ids, work[:, :block], 0.0)
    inverse = work[:, block:]
    for tile in range(tiles):
        own = (weighted_low_ref, weighted_high_ref)[tile // count_y][tile % count_y]
        new_ref[pl.ds(tile, block, stride=tiles), :] = mul3(inverse, own)
    for part in range(2):
        span = slice(part * block, (part + 1) * block)
        reduced_ref[part, :, :prior] = mul3(inverse, sums_ref[span, :] * inverse_rows)
        reduced_ref[part, :, prior:] = mul3_t(mul3_t(inverse, with_own[:, span]), inverse)


def swap(value, mask):
    axes = ("px", "py")
    pairs = [(i, i ^ mask) for i in range(lax.axis_size(axes))]
    return lax.ppermute(value, axes, pairs)


def exchange(message_a, message_b, axis):
    count = lax.axis_size(axis)
    pairs = [(i, ((i + 1) ^ 1) - 1) for i in range(count)]
    pairs = [(i, j if 0 <= j < count else i) for i, j in pairs]
    near = [(i, i ^ 1) for i in range(count)]
    return lax.ppermute(message_a, axis, near), lax.ppermute(message_b, axis, pairs)


def total_over(value, first, last):
    while first < last:
        value = value + swap(value, first)
        first *= 2
    return value


def halved_total(value):
    half = value.shape[0] // 2
    upper = lax.axis_index("py") % 2 == 1
    first, second = value[:half], value[half:]
    kept = jnp.where(upper, second, first)
    kept = kept + swap(jnp.where(upper, first, second), 1)
    kept = (kept + swap(kept, 6)) + (swap(kept, 2) + swap(kept, 4))
    kept = total_over(kept, 8, lax.axis_size(("px", "py")))
    other = swap(kept, 1)
    return jnp.concatenate(
        [jnp.where(upper, other, kept), jnp.where(upper, kept, other)], axis=0
    )


def shape(*dims, dtype=F32):
    return jax.ShapeDtypeStruct(dims, dtype)


def shards(prior_basis, previous, neighbours, tile_kinds, stiff_tiles, mass_tiles):
    block = previous.shape[0]
    prior, count_x, count_y, side = prior_basis.shape
    tiles = count_x * count_y
    wide = count_y + 2
    rest = prior - block
    kinds = stiff_tiles.shape[0]
    inverse_rows = 1.0 / (tiles * side * lax.axis_size("px") * lax.axis_size("py"))
    vectors = jnp.concatenate(
        [prior_basis.reshape(-1, side), previous.reshape(-1, side)], axis=0
    )
    place = jnp.arange(count_x)[:, None] * wide + jnp.arange(count_y)[None, :]
    sources = place[None] + (neighbours // 3) * wide + neighbours % 3
    codes = jnp.stack([sources, tile_kinds]).astype(jnp.int32).reshape(2, -1, tiles)
    at_y, at_x = lax.axis_index("py"), lax.axis_index("px")
    flags = [at_y % 2 == 1, at_x % 2 == 1]
    flags += [at_y > 0, at_y < lax.axis_size("py") - 1]
    flags += [at_x > 0, at_x < lax.axis_size("px") - 1]
    flags = jnp.stack(flags + flags[:2]).astype(F32)
    flags = jnp.broadcast_to(flags[:, None], (8, side))

    def call(kernel, inputs, outputs, scratch=(), smem=0, limit=8, cost=None):
        specs = [SMEM] * smem + [VMEM] * (len(inputs) - smem)
        return pl.pallas_call(
            kernel,
            out_shape=outputs,
            in_specs=specs,
            out_specs=[VMEM] * len(outputs),
            scratch_shapes=scratch,
            compiler_params=pltpu.CompilerParams(vmem_limit_bytes=limit * MIB),
            cost_estimate=cost,
        )(*inputs)

    side_a, side_b, row_a, row_b, rest_a, rest_b = call(
        pack_kernel,
        (flags, vectors),
        [shape(count_x, 2 * block, side)] * 2
        + [shape(count_y, 2 * block, side)] * 2
        + [shape(count_y, rest, side)] * 2,
    )
    from_side_a, from_side_b = exchange(side_a, side_b, "py")
    from_row_a, from_row_b = exchange(row_a, row_b, "px")
    from_rest_a, from_rest_b = exchange(rest_a, rest_b, "px")
    from_side_a, codes = lax.optimization_barrier((from_side_a, codes))
    corner_a, corner_b = call(
        corners_kernel,
        (flags, from_side_a, from_side_b),
        [shape(2, 2 * block, side)] * 2,
    )
    from_corner_a, from_corner_b = exchange(corner_a, corner_b, "px")
    rest_side_a, rest_side_b = call(
        columns_kernel,
        (flags, rest_a, rest_b, from_rest_a, from_rest_b),
        [shape(4, rest, side)] * 2,
    )
    rest_side_a, rest_side_b = exchange(rest_side_a, rest_side_b, "py")
    residual_a, residual_b, partial, current = call(
        residual_kernel,
        (
            codes,
            flags,
            row_a,
            row_b,
            from_row_a,
            from_row_b,
            from_side_a,
            from_side_b,
            from_corner_a,
            from_corner_b,
            rest_a,
            rest_b,
            stiff_tiles,
            mass_tiles,
        ),
        [shape(count_y + 1, block, side), shape(count_y, block, side)]
        + [shape(block, prior), shape(4 * wide, block, side)],
        [pltpu.VMEM((4 * wide, 2 * block, 2 * side), BF16)]
        + [pltpu.VMEM((kinds, 2 * side, side), BF16)] * 2,
        smem=1,
        cost=pl.CostEstimate(flops=10**9, bytes_accessed=0, transcendentals=0),
    )
    count_py = lax.axis_size("py")
    from_row_a, from_row_b = exchange(residual_a, residual_b, "px")
    partial = total_over(
        partial + from_row_a[-1], 2 * count_py, count_py * lax.axis_size("px")
    )
    partial, rest_side_a, rest_side_b = lax.optimization_barrier(
        (partial, rest_side_a, rest_side_b)
    )
    side_a, side_b = call(
        columns_kernel,
        (flags, residual_a, residual_b, from_row_a, from_row_b, partial),
        [shape(5, block, side), shape(4, block, side)],
    )
    from_side_a, from_side_b = exchange(side_a, side_b, "py")
    partial = total_over(partial + from_side_a[-1], 2, count_py)
    weighted_low, weighted_high, coupling, sums = call(
        functools.partial(operators_kernel, inverse_rows),
        (
            codes,
            flags,
            partial,
            residual_a,
            residual_b,
            from_row_a,
            from_row_b,
            from_side_a,
            from_side_b,
            rest_a,
            rest_b,
            from_rest_a,
            from_rest_b,
            rest_side_a,
            rest_side_b,
            current,
            stiff_tiles,
            mass_tiles,
        ),
        [shape(count_y, block, side)] * 2 + [shape(block, prior), shape(3 * block, prior)],
        [
            pltpu.VMEM((4 * wide, 2 * block, side), BF16),
            pltpu.VMEM((tiles, 2 * prior, side), BF16),
        ]
        + [pltpu.VMEM((kinds, side, 2 * side), BF16)] * 2,
        smem=1,
    )
    new_block, factor, reduced = call(
        functools.partial(factor_kernel, inverse_rows),
        (halved_total(sums), weighted_low, weighted_high),
        [
            shape(block * tiles, side),
            shape(block, block),
            shape(2, block, prior + block),
        ],
    )
    return (
        new_block.reshape(previous.shape),
        coupling.T,
        factor,
        reduced.swapaxes(1, 2),
    )


def solution(mesh):
    placed = (
        P("case", "px", "py", None),
        P("case", "px", "py", None),
        P(None, "px", "py"),
        P(None, "px", "py"),
        P(),
        P(),
    )
    return jax.shard_map(
        shards,
        mesh=mesh,
        in_specs=placed,
        out_specs=(
            P("case", "px", "py", None),
            P("case", None),
            P("case", None),
            P("case", None, None),
        ),
        check_vma=False,
    )
```

```python
import functools

import jax
import jax.numpy as jnp
from jax import lax
from jax.experimental import pallas as pl
from jax.experimental.pallas import tpu as pltpu
from jax.sharding import PartitionSpec as P

F32 = jnp.float32
BF16 = jnp.bfloat16
VMEM = pl.BlockSpec(memory_space=pltpu.VMEM)
ANY = pl.BlockSpec(memory_space=pl.ANY)
MIB = 1024 * 1024


def split(value):
    high = value.astype(BF16)
    return high, (value - high.astype(F32)).astype(BF16)


def mul(left, right):
    return jnp.dot(left, right, preferred_element_type=F32)


def mul_t(left, right):
    return lax.dot_general(left, right, (((1,), (1,)), ((), ())), preferred_element_type=F32)


def mul3(left, right):
    left_high, left_low = split(left)
    right_high, right_low = split(right)
    return mul(left_high, right_high) + (mul(left_high, right_low) + mul(left_low, right_high))


def mul3_t(left, right):
    left_high, left_low = split(left)
    right_high, right_low = split(right)
    return mul_t(left_high, right_high) + (
        mul_t(left_high, right_low) + mul_t(left_low, right_high)
    )


def split_tables(stiff_ref, mass_ref, high_ref, low_ref, axis):
    side = stiff_ref.shape[1]
    for kind in range(stiff_ref.shape[0]):
        for place, ref in enumerate((stiff_ref, mass_ref)):
            span = [kind, slice(None), slice(None)]
            span[axis] = slice(place * side, (place + 1) * side)
            high_ref[tuple(span)], low_ref[tuple(span)] = split(ref[kind])


def pick(flag, first, second):
    flag = flag > 0.0
    return jnp.where(flag, first, second), jnp.where(flag, second, first)


def flag_at(flags_ref, place):
    return flags_ref[place : place + 1, :]


def code_copies(code_refs, local_refs, semaphores):
    return [
        pltpu.make_async_copy(ref, local, semaphores.at[n])
        for n, (ref, local) in enumerate(zip(code_refs, local_refs))
    ]


def source_and_kind(neighbours_ref, kinds_ref, tile, k, count_y):
    neighbour = neighbours_ref[tile, k]
    down = (neighbour * 11) >> 5
    first = (tile // count_y) * (count_y + 2) + tile % count_y
    return first + neighbour + down * (count_y - 1), kinds_ref[tile, k]


def pack_kernel(flags_ref, block_ref, side_a_ref, side_b_ref, row_a_ref, row_b_ref):
    count_y, both, _ = row_a_ref.shape
    tiles = 2 * count_y
    odd_y, odd_x = flag_at(flags_ref, 0), flag_at(flags_ref, 1)

    def tile_of(i, j):
        return block_ref[pl.ds(i * count_y + j, both, stride=tiles), :]

    for i in range(2):
        side_a_ref[i], side_b_ref[i] = pick(odd_y, tile_of(i, 0), tile_of(i, count_y - 1))
    for j in range(count_y):
        row_a_ref[j], row_b_ref[j] = pick(odd_x, tile_of(0, j), tile_of(1, j))


def rest_kernel(flags_ref, basis_ref, rest_a_ref, rest_b_ref):
    count_y, rest, _ = rest_a_ref.shape
    odd_x = flag_at(flags_ref, 1)
    for j in range(count_y):
        rest_a_ref[j], rest_b_ref[j] = pick(
            odd_x,
            basis_ref[pl.ds(j, rest, stride=2 * count_y), :],
            basis_ref[pl.ds(count_y + j, rest, stride=2 * count_y), :],
        )


def corners_kernel(flags_ref, side_a_ref, side_b_ref, corner_a_ref, corner_b_ref):
    odd_y, odd_x = flag_at(flags_ref, 0), flag_at(flags_ref, 1)
    ends = [pick(odd_y, side_a_ref[i], side_b_ref[i]) for i in range(2)]
    for place in range(2):
        corner_a_ref[place], corner_b_ref[place] = pick(odd_x, ends[0][place], ends[1][place])


def columns_kernel(
    flags_ref, row_a_ref, row_b_ref, from_row_a_ref, from_row_b_ref, *refs
):
    odd_y, odd_x = flag_at(flags_ref, 0), flag_at(flags_ref, 1)
    side_a_ref, side_b_ref = refs[-2:]
    columns = []
    for j in (0, row_b_ref.shape[0] - 1):
        column = list(pick(odd_x, from_row_a_ref[j], from_row_b_ref[j]))
        column[1:1] = pick(odd_x, row_a_ref[j], row_b_ref[j])
        columns.append(column)
    for i in range(4):
        side_a_ref[i], side_b_ref[i] = pick(odd_y, columns[0][i], columns[1][i])
    if len(refs) == 3:
        side_a_ref[4] = refs[0][...]


def residual_kernel(
    neighbours_hbm_ref,
    kinds_hbm_ref,
    flags_ref,
    row_a_ref,
    row_b_ref,
    from_row_a_ref,
    from_row_b_ref,
    from_side_a_ref,
    from_side_b_ref,
    from_corner_a_ref,
    from_corner_b_ref,
    rest_a_ref,
    rest_b_ref,
    stiff_ref,
    mass_ref,
    residual_a_ref,
    residual_b_ref,
    partial_ref,
    current_ref,
    ext_ref,
    table_high_ref,
    table_low_ref,
    neighbours_ref,
    kinds_ref,
    semaphores,
):
    copies = code_copies(
        (neighbours_hbm_ref, kinds_hbm_ref), (neighbours_ref, kinds_ref), semaphores
    )
    for copy in copies:
        copy.start()
    split_tables(stiff_ref, mass_ref, table_high_ref, table_low_ref, 1)
    count_y, both, side = row_a_ref.shape
    wide = count_y + 2
    block = both // 2
    rest = rest_a_ref.shape[1]
    odd_y, odd_x, in_low_y, in_high_y, in_low_x, in_high_x = (
        flag_at(flags_ref, place) for place in range(6)
    )

    def store(i, j, value):
        current_ref[i * wide + j] = value[:block]
        for part in range(2):
            high, low = split(value[part * block : (part + 1) * block])
            ext_ref[i * wide + j, :block, part * side : (part + 1) * side] = high
            ext_ref[i * wide + j, block:, part * side : (part + 1) * side] = low

    own = {}
    for j in range(count_y):
        own[0, j], own[1, j] = pick(odd_x, row_a_ref[j], row_b_ref[j])
        store(1, j + 1, own[0, j])
        store(2, j + 1, own[1, j])
        low, high = pick(odd_x, from_row_a_ref[j], from_row_b_ref[j])
        store(0, j + 1, low * in_low_x)
        store(3, j + 1, high * in_high_x)
    for i in range(2):
        low, high = pick(odd_y, from_side_a_ref[i], from_side_b_ref[i])
        store(i + 1, 0, low * in_low_y)
        store(i + 1, wide - 1, high * in_high_y)
    for place, j, inside in ((0, 0, in_low_y), (1, wide - 1, in_high_y)):
        low, high = pick(odd_x, from_corner_a_ref[place], from_corner_b_ref[place])
        store(0, j, low * (in_low_x * inside))
        store(3, j, high * (in_high_x * inside))
    for copy in copies:
        copy.wait()
    partial = jnp.zeros((block, rest + block), F32)
    totals = {}
    for tile in range(2 * count_y):
        i, j = tile // count_y, tile % count_y
        total = 4.0 * own[i, j][:block] + own[i, j][block:]
        for k in range(neighbours_ref.shape[1]):
            source, kind = source_and_kind(neighbours_ref, kinds_ref, tile, k, count_y)
            chosen = ext_ref[source]
            pair = mul(chosen, table_high_ref[kind])
            total = total + (
                pair[:block] + (pair[block:] + mul(chosen[:block], table_low_ref[kind]))
            )
        totals[i, j] = total
        rest_tile = pick(odd_x, rest_a_ref[j], rest_b_ref[j])[i]
        basis_tile = jnp.concatenate([rest_tile, own[i, j][:block]], axis=0)
        partial = partial + mul3_t(total, basis_tile)
    for j in range(count_y):
        residual_a_ref[j], residual_b_ref[j] = pick(odd_x, totals[0, j], totals[1, j])
    residual_a_ref[count_y] = partial
    partial_ref[...] = partial


def prepare_kernel(
    flags_ref,
    rest_a_ref,
    rest_b_ref,
    from_rest_a_ref,
    from_rest_b_ref,
    current_ref,
    stiff_ref,
    mass_ref,
    basis_ref,
    table_high_ref,
    table_low_ref,
):
    count_y, rest, _ = rest_a_ref.shape
    prior = rest + current_ref.shape[1]
    odd_x = flag_at(flags_ref, 1)
    split_tables(stiff_ref, mass_ref, table_high_ref, table_low_ref, 2)
    for j in range(count_y):
        rests = list(pick(odd_x, from_rest_a_ref[j], from_rest_b_ref[j]))
        rests[1:1] = pick(odd_x, rest_a_ref[j], rest_b_ref[j])
        for i in range(4):
            tile = jnp.concatenate([rests[i], current_ref[i * (count_y + 2) + j + 1]], axis=0)
            high, low = split(tile)
            basis_ref[i * count_y + j, :prior, :] = high
            basis_ref[i * count_y + j, prior:, :] = low


def operators_kernel(
    inverse_rows,
    neighbours_hbm_ref,
    kinds_hbm_ref,
    flags_ref,
    partial_ref,
    row_a_ref,
    row_b_ref,
    from_row_a_ref,
    from_row_b_ref,
    from_side_a_ref,
    from_side_b_ref,
    rest_side_a_ref,
    rest_side_b_ref,
    current_ref,
    basis_ref,
    table_high_ref,
    table_low_ref,
    weighted_low_ref,
    weighted_high_ref,
    coupling_ref,
    sent_ref,
    kept_ref,
    ext_ref,
    neighbours_ref,
    kinds_ref,
    semaphores,
):
    copies = code_copies(
        (neighbours_hbm_ref, kinds_hbm_ref), (neighbours_ref, kinds_ref), semaphores
    )
    for copy in copies:
        copy.start()
    count_y, block, side = weighted_low_ref.shape
    wide = count_y + 2
    rest = rest_side_a_ref.shape[1]
    prior = rest + block
    odd_y, odd_x, in_low_y, in_high_y, in_low_x, in_high_x = (
        flag_at(flags_ref, place) for place in range(6)
    )
    coupling = partial_ref[...] * inverse_rows
    coupling_ref[...] = coupling
    coupling_high, coupling_low = split(coupling)

    def basis_parts(i, j):
        if 0 < j < wide - 1:
            place = i * count_y + j - 1
            return basis_ref[place, :prior, :], basis_ref[place, prior:, :]
        rest_tile = pick(odd_y, rest_side_a_ref[i], rest_side_b_ref[i])[j // (wide - 1)]
        return split(jnp.concatenate([rest_tile, current_ref[i * wide + j]], axis=0))

    for j in range(wide):
        if 0 < j < wide - 1:
            rows = list(pick(odd_x, from_row_a_ref[j - 1], from_row_b_ref[j - 1]))
            rows[1:1] = pick(odd_x, row_a_ref[j - 1], row_b_ref[j - 1])
        else:
            rows = [
                pick(odd_y, from_side_a_ref[i], from_side_b_ref[i])[j // (wide - 1)]
                for i in range(4)
            ]
        for i in range(4):
            high, low = basis_parts(i, j)
            value = rows[i] - (
                mul(coupling_high, high) + (mul(coupling_high, low) + mul(coupling_low, high))
            )
            if i == 0:
                value = value * in_low_x
            if i == 3:
                value = value * in_high_x
            if j == 0:
                value = value * in_low_y
            if j == wide - 1:
                value = value * in_high_y
            if 0 < i < 3 and 0 < j < wide - 1:
                (weighted_low_ref, weighted_high_ref)[i - 1][j - 1] = value
            high, low = split(value)
            ext_ref[i * wide + j, :block, :] = high
            ext_ref[i * wide + j, block:, :] = low
    for copy in copies:
        copy.wait()
    with_basis = jnp.zeros((2 * block, prior), F32)
    with_own = jnp.zeros((block, 4 * block), F32)
    for tile in range(2 * count_y):
        i, j = tile // count_y, tile % count_y
        own = (weighted_low_ref, weighted_high_ref)[i][j]
        totals = jnp.concatenate([4.0 * own, own], axis=1)
        for k in range(neighbours_ref.shape[1]):
            source, kind = source_and_kind(neighbours_ref, kinds_ref, tile, k, count_y)
            chosen = ext_ref[source]
            pair = mul(chosen, table_high_ref[kind])
            totals = totals + (
                pair[:block] + (pair[block:] + mul(chosen[:block], table_low_ref[kind]))
            )
        applied = jnp.concatenate([totals[:, :side], totals[:, side:]], axis=0)
        high, low = split(applied)
        basis_high, basis_low = basis_parts(i + 1, j + 1)
        with_basis = with_basis + (
            mul_t(high, basis_high) + (mul_t(high, basis_low) + mul_t(low, basis_high))
        )
        right = jnp.concatenate([applied, own, jnp.zeros_like(own)], axis=0)
        with_own = with_own + mul3_t(own, right)
    halves = [
        jnp.concatenate(
            [
                with_basis[part * block : (part + 1) * block],
                folded(with_own[:, part * block : (part + 1) * block]),
                folded(with_own[:, 2 * block : 3 * block]),
            ],
            axis=0,
        )
        for part in range(2)
    ]
    sent_ref[...], kept_ref[...] = pick(odd_y, halves[0], halves[1])


def folded(square):
    return jnp.concatenate([square[n * 8 : (n + 1) * 8] for n in range(4)], axis=1)


def unfolded(rows):
    return jnp.concatenate([rows[:, n * 32 : (n + 1) * 32] for n in range(4)], axis=0)


def factor_kernel(
    inverse_rows,
    sums_ref,
    weighted_low_ref,
    weighted_high_ref,
    new_ref,
    factor_ref,
    inverse_ref,
    reduced_ref,
):
    count_y, block, _ = weighted_low_ref.shape
    prior = sums_ref.shape[1]
    tiles = 2 * count_y
    gram = unfolded(sums_ref[block + 8 :, :]) * inverse_rows
    row_ids = lax.broadcasted_iota(jnp.int32, (block, block), 0)
    column_ids = lax.broadcasted_iota(jnp.int32, (block, block), 1)
    unit = jnp.where(row_ids == column_ids, 1.0, 0.0).astype(F32)
    work = jnp.concatenate([gram, unit], axis=1)
    rows = lax.broadcasted_iota(jnp.int32, work.shape, 0)
    group = 4
    for j in range(0, block, group):
        columns = [
            jnp.broadcast_to(work[:, j + a : j + a + 1], work.shape) for a in range(group)
        ]
        pivots = [work[j + a : j + a + 1, :] for a in range(group)]
        for a in range(group):
            at = j + a
            ratio = columns[a] * (1.0 / columns[a][at : at + 1, :])
            for b in range(a + 1, group):
                columns[b] = columns[b] - ratio * columns[b][at : at + 1, :]
                pivots[b] = pivots[b] - ratio[j + b : j + b + 1, :] * pivots[a]
            work = work - jnp.where(rows > at, ratio, 0.0) * pivots[a]
    work = work * lax.rsqrt(jnp.sum(work[:, :block] * unit, axis=1, keepdims=True))
    factor_ref[...] = jnp.where(column_ids >= row_ids, work[:, :block], 0.0)
    inverse = work[:, block:]
    for tile in range(tiles):
        own = (weighted_low_ref, weighted_high_ref)[tile // count_y][tile % count_y]
        new_ref[pl.ds(tile, block, stride=tiles), :] = mul3(inverse, own)
    inverse_ref[...] = inverse
    reduce_half(inverse, sums_ref, inverse_rows, reduced_ref)


def reduce_half(inverse, sums_ref, inverse_rows, out_ref):
    block, prior = inverse.shape[0], sums_ref.shape[1]
    out_ref[:, :prior] = mul3(inverse, sums_ref[:block, :] * inverse_rows)
    own = unfolded(sums_ref[block : block + 8, :]) * inverse_rows
    out_ref[:, prior:] = mul3_t(mul3_t(inverse, own), inverse)


def reduced_kernel(inverse_rows, flags_ref, inverse_ref, other_ref, half_ref, out_ref, work_ref):
    reduce_half(inverse_ref[...], other_ref, inverse_rows, work_ref)
    odd_y = flag_at(flags_ref, 0)
    for span in (slice(0, 128), slice(128, out_ref.shape[2])):
        flag = odd_y[:, : work_ref[:, span].shape[1]]
        out_ref[0, :, span], out_ref[1, :, span] = pick(
            flag, work_ref[:, span], half_ref[:, span]
        )


def swap(value, mask):
    axes = ("px", "py")
    pairs = [(i, i ^ mask) for i in range(lax.axis_size(axes))]
    return lax.ppermute(value, axes, pairs)


def exchange(message_a, message_b, axis):
    count = lax.axis_size(axis)
    pairs = [(i, ((i + 1) ^ 1) - 1) for i in range(count)]
    pairs = [(i, j if 0 <= j < count else i) for i, j in pairs]
    near = [(i, i ^ 1) for i in range(count)]
    return lax.ppermute(message_a, axis, near), lax.ppermute(message_b, axis, pairs)


def total_over(value, first, last):
    while first < last:
        value = value + swap(value, first)
        first *= 2
    return value


def half_total(sent, kept):
    kept = kept + swap(sent, 1)
    kept = (kept + swap(kept, 6)) + (swap(kept, 2) + swap(kept, 4))
    return total_over(kept, 8, lax.axis_size(("px", "py")))


def shape(*dims, dtype=F32):
    return jax.ShapeDtypeStruct(dims, dtype)


def shards(prior_basis, previous, neighbours, tile_kinds, stiff_tiles, mass_tiles):
    block = previous.shape[0]
    prior, count_x, count_y, side = prior_basis.shape
    tiles = count_x * count_y
    wide = count_y + 2
    rest = prior - block
    kinds = stiff_tiles.shape[0]
    inverse_rows = 1.0 / (tiles * side * lax.axis_size("px") * lax.axis_size("py"))
    basis = prior_basis.reshape(-1, side)
    block_vectors = jnp.concatenate([basis[rest * tiles :], previous.reshape(-1, side)], axis=0)
    codes = [array.transpose(1, 2, 0).reshape(tiles, -1) for array in (neighbours, tile_kinds)]
    code_scratch = [pltpu.SMEM(array.shape, jnp.int32) for array in codes]
    code_scratch += [pltpu.SemaphoreType.DMA((2,))]
    at_y, at_x = lax.axis_index("py"), lax.axis_index("px")
    bits = (at_y & 1) + 2 * (at_x & 1)
    bits += 4 * (at_y > 0) + 8 * (at_y < lax.axis_size("py") - 1)
    bits += 16 * (at_x > 0) + 32 * (at_x < lax.axis_size("px") - 1)
    flags = ((bits >> lax.broadcasted_iota(jnp.int32, (8, side), 0)) & 1).astype(F32)

    def call(kernel, inputs, outputs, scratch=(), plain=0, limit=8, cost=None):
        specs = [ANY] * plain + [VMEM] * (len(inputs) - plain)
        return pl.pallas_call(
            kernel,
            out_shape=outputs,
            in_specs=specs,
            out_specs=[VMEM] * len(outputs),
            scratch_shapes=scratch,
            compiler_params=pltpu.CompilerParams(vmem_limit_bytes=limit * MIB),
            cost_estimate=cost,
        )(*inputs)

    side_a, side_b, row_a, row_b = call(
        pack_kernel,
        (flags, block_vectors),
        [shape(count_x, 2 * block, side)] * 2 + [shape(count_y, 2 * block, side)] * 2,
    )
    rest_a, rest_b = call(rest_kernel, (flags, basis), [shape(count_y, rest, side)] * 2)
    from_side_a, from_side_b = exchange(side_a, side_b, "py")
    from_row_a, from_row_b = exchange(row_a, row_b, "px")
    from_side_a, rest_a, rest_b = lax.optimization_barrier((from_side_a, rest_a, rest_b))
    from_rest_a, from_rest_b = exchange(rest_a, rest_b, "px")
    corner_a, corner_b = call(
        corners_kernel,
        (flags, from_side_a, from_side_b),
        [shape(2, 2 * block, side)] * 2,
    )
    from_corner_a, from_corner_b = exchange(corner_a, corner_b, "px")
    rest_side_a, rest_side_b = call(
        columns_kernel,
        (flags, rest_a, rest_b, from_rest_a, from_rest_b),
        [shape(4, rest, side)] * 2,
    )
    rest_side_a, rest_side_b = exchange(rest_side_a, rest_side_b, "py")
    residual_a, residual_b, partial, current = call(
        residual_kernel,
        (
            *codes,
            flags,
            row_a,
            row_b,
            from_row_a,
            from_row_b,
            from_side_a,
            from_side_b,
            from_corner_a,
            from_corner_b,
            rest_a,
            rest_b,
            stiff_tiles,
            mass_tiles,
        ),
        [shape(count_y + 1, block, side), shape(count_y, block, side)]
        + [shape(block, prior), shape(4 * wide, block, side)],
        [pltpu.VMEM((4 * wide, 2 * block, 2 * side), BF16)]
        + [pltpu.VMEM((kinds, 2 * side, side), BF16)] * 2
        + code_scratch,
        plain=2,
        cost=pl.CostEstimate(flops=10**9, bytes_accessed=0, transcendentals=0),
    )
    count_py = lax.axis_size("py")
    from_row_a, from_row_b = exchange(residual_a, residual_b, "px")
    partial = total_over(
        partial + from_row_a[-1], 2 * count_py, count_py * lax.axis_size("px")
    )
    partial, rest_side_a, rest_side_b = lax.optimization_barrier(
        (partial, rest_side_a, rest_side_b)
    )
    side_a, side_b = call(
        columns_kernel,
        (flags, residual_a, residual_b, from_row_a, from_row_b, partial),
        [shape(5, block, side), shape(4, block, side)],
    )
    from_side_a, from_side_b = exchange(side_a, side_b, "py")
    partial = total_over(partial + from_side_a[-1], 2, count_py)
    basis_parts, wide_high, wide_low = call(
        prepare_kernel,
        (flags, rest_a, rest_b, from_rest_a, from_rest_b, current, stiff_tiles, mass_tiles),
        [shape(4 * count_y, 2 * prior, side, dtype=BF16)]
        + [shape(kinds, side, 2 * side, dtype=BF16)] * 2,
        cost=pl.CostEstimate(flops=10**9, bytes_accessed=0, transcendentals=0),
    )
    weighted_low, weighted_high, coupling, sent, kept = call(
        functools.partial(operators_kernel, inverse_rows),
        (
            *codes,
            flags,
            partial,
            residual_a,
            residual_b,
            from_row_a,
            from_row_b,
            from_side_a,
            from_side_b,
            rest_side_a,
            rest_side_b,
            current,
            basis_parts,
            wide_high,
            wide_low,
        ),
        [shape(count_y, block, side)] * 2
        + [shape(block, prior)]
        + [shape(block + 16, prior)] * 2,
        [pltpu.VMEM((4 * wide, 2 * block, side), BF16)] + code_scratch,
        plain=2,
    )
    kept = half_total(sent, kept)
    other = swap(kept[: block + 8], 1)
    new_block, factor, inverse, half = call(
        functools.partial(factor_kernel, inverse_rows),
        (kept, weighted_low, weighted_high),
        [
            shape(block * tiles, side),
            shape(block, block),
            shape(block, block),
            shape(block, prior + block),
        ],
        cost=pl.CostEstimate(flops=10**9, bytes_accessed=0, transcendentals=0),
    )
    (reduced,) = call(
        functools.partial(reduced_kernel, inverse_rows),
        (flags, inverse, other, half),
        [shape(2, block, prior + block)],
        [pltpu.VMEM((block, prior + block), F32)],
    )
    return (
        new_block.reshape(previous.shape),
        coupling.T,
        factor,
        reduced.swapaxes(1, 2),
    )


def solution(mesh):
    placed = (
        P("case", "px", "py", None),
        P("case", "px", "py", None),
        P(None, "px", "py"),
        P(None, "px", "py"),
        P(),
        P(),
    )
    return jax.shard_map(
        shards,
        mesh=mesh,
        in_specs=placed,
        out_specs=(
            P("case", "px", "py", None),
            P("case", None),
            P("case", None),
            P("case", None, None),
        ),
        check_vma=False,
    )
```

```python
import functools

import jax
import jax.numpy as jnp
from jax import lax
from jax.experimental import pallas as pl
from jax.experimental.pallas import tpu as pltpu
from jax.sharding import PartitionSpec as P

F32 = jnp.float32
BF16 = jnp.bfloat16
VMEM = pl.BlockSpec(memory_space=pltpu.VMEM)
ANY = pl.BlockSpec(memory_space=pl.ANY)
MIB = 1024 * 1024


def split(value):
    high = value.astype(BF16)
    return high, (value - high.astype(F32)).astype(BF16)


def mul(left, right):
    return jnp.dot(left, right, preferred_element_type=F32)


def mul_t(left, right):
    return lax.dot_general(left, right, (((1,), (1,)), ((), ())), preferred_element_type=F32)


def mul3(left, right):
    left_high, left_low = split(left)
    right_high, right_low = split(right)
    return mul(left_high, right_high) + (mul(left_high, right_low) + mul(left_low, right_high))


def mul3_t(left, right):
    left_high, left_low = split(left)
    right_high, right_low = split(right)
    return mul_t(left_high, right_high) + (
        mul_t(left_high, right_low) + mul_t(left_low, right_high)
    )


def split_tables(stiff_ref, mass_ref, table_ref, parts_axis):
    side = stiff_ref.shape[1]
    spans = (slice(0, side), slice(side, 2 * side))
    for kind in range(stiff_ref.shape[0]):
        for matrix, ref in zip(spans, (stiff_ref, mass_ref)):
            for part, value in zip(spans, split(ref[kind])):
                if parts_axis == 1:
                    table_ref[kind, matrix, part] = value
                else:
                    table_ref[kind, part, matrix] = value


def stacked(value):
    return jnp.concatenate(split(value), axis=0)


def deep(value):
    high, low = split(value)
    upper = jnp.concatenate([high, high], axis=1)
    return jnp.concatenate([upper, jnp.concatenate([low, jnp.zeros_like(low)], axis=1)], axis=0)


def halves_sum(value):
    half = value.shape[0] // 2
    return value[:half] + value[half:]


def pair_sum(left, right_high, right_low):
    rows = left.shape[0] // 2
    return halves_sum(mul_t(left, right_high)) + mul_t(left[:rows], right_low)


def pick(flag, first, second):
    flag = flag > 0.0
    return jnp.where(flag, first, second), jnp.where(flag, second, first)


def flag_at(flags_ref, place):
    return flags_ref[place : place + 1, :]


def code_copies(code_refs, local_refs, semaphores):
    return [
        pltpu.make_async_copy(ref, local, semaphores.at[n])
        for n, (ref, local) in enumerate(zip(code_refs, local_refs))
    ]


def source_and_kind(neighbours_ref, kinds_ref, tile, k, count_y):
    neighbour = neighbours_ref[tile, k]
    down = (neighbour * 11) >> 5
    first = (tile // count_y) * (count_y + 2) + tile % count_y
    return first + neighbour + down * (count_y - 1), kinds_ref[tile, k]


def pack_kernel(flags_ref, vectors_ref, side_a_ref, side_b_ref, row_a_ref, row_b_ref):
    count_y, both, _ = row_a_ref.shape
    tiles = 2 * count_y
    odd_y, odd_x = flag_at(flags_ref, 0), flag_at(flags_ref, 1)

    first = vectors_ref.shape[0] - both * tiles

    def tile_of(i, j):
        return vectors_ref[pl.ds(first + i * count_y + j, both, stride=tiles), :]

    for i in range(2):
        side_a_ref[i], side_b_ref[i] = pick(odd_y, tile_of(i, 0), tile_of(i, count_y - 1))
    for j in range(count_y):
        row_a_ref[j], row_b_ref[j] = pick(odd_x, tile_of(0, j), tile_of(1, j))


def rest_kernel(flags_ref, vectors_ref, rest_a_ref, rest_b_ref):
    count_y, rest, _ = rest_a_ref.shape
    odd_x = flag_at(flags_ref, 1)
    for j in range(count_y):
        rest_a_ref[j], rest_b_ref[j] = pick(
            odd_x,
            vectors_ref[pl.ds(j, rest, stride=2 * count_y), :],
            vectors_ref[pl.ds(count_y + j, rest, stride=2 * count_y), :],
        )


def corners_kernel(flags_ref, side_a_ref, side_b_ref, corner_a_ref, corner_b_ref):
    odd_y, odd_x = flag_at(flags_ref, 0), flag_at(flags_ref, 1)
    ends = [pick(odd_y, side_a_ref[i], side_b_ref[i]) for i in range(2)]
    for place in range(2):
        corner_a_ref[place], corner_b_ref[place] = pick(odd_x, ends[0][place], ends[1][place])


def columns_kernel(
    flags_ref, row_a_ref, row_b_ref, from_row_a_ref, from_row_b_ref, *refs
):
    odd_y, odd_x = flag_at(flags_ref, 0), flag_at(flags_ref, 1)
    side_a_ref, side_b_ref = refs[-2:]
    columns = []
    for j in (0, row_b_ref.shape[0] - 1):
        column = list(pick(odd_x, from_row_a_ref[j], from_row_b_ref[j]))
        column[1:1] = pick(odd_x, row_a_ref[j], row_b_ref[j])
        columns.append(column)
    for i in range(4):
        side_a_ref[i], side_b_ref[i] = pick(odd_y, columns[0][i], columns[1][i])
    if len(refs) == 3:
        side_a_ref[4] = refs[0][...]


def residual_kernel(
    neighbours_hbm_ref,
    kinds_hbm_ref,
    flags_ref,
    row_a_ref,
    row_b_ref,
    from_row_a_ref,
    from_row_b_ref,
    from_side_a_ref,
    from_side_b_ref,
    from_corner_a_ref,
    from_corner_b_ref,
    rest_a_ref,
    rest_b_ref,
    stiff_ref,
    mass_ref,
    residual_a_ref,
    residual_b_ref,
    partial_ref,
    current_ref,
    ext_ref,
    table_ref,
    neighbours_ref,
    kinds_ref,
    semaphores,
):
    copies = code_copies(
        (neighbours_hbm_ref, kinds_hbm_ref), (neighbours_ref, kinds_ref), semaphores
    )
    for copy in copies:
        copy.start()
    split_tables(stiff_ref, mass_ref, table_ref, 1)
    count_y, both, side = row_a_ref.shape
    wide = count_y + 2
    block = both // 2
    rest = rest_a_ref.shape[1]
    odd_y, odd_x, in_low_y, in_high_y, in_low_x, in_high_x = (
        flag_at(flags_ref, place) for place in range(6)
    )

    def store(i, j, value):
        current_ref[i * wide + j] = value[:block]
        for part in range(2):
            high, low = split(value[part * block : (part + 1) * block])
            ext_ref[i * wide + j, :block, part * side : (part + 1) * side] = high
            ext_ref[i * wide + j, block:, part * side : (part + 1) * side] = low

    own = {}
    for j in range(count_y):
        own[0, j], own[1, j] = pick(odd_x, row_a_ref[j], row_b_ref[j])
        store(1, j + 1, own[0, j])
        store(2, j + 1, own[1, j])
        low, high = pick(odd_x, from_row_a_ref[j], from_row_b_ref[j])
        store(0, j + 1, low * in_low_x)
        store(3, j + 1, high * in_high_x)
    for i in range(2):
        low, high = pick(odd_y, from_side_a_ref[i], from_side_b_ref[i])
        store(i + 1, 0, low * in_low_y)
        store(i + 1, wide - 1, high * in_high_y)
    for place, j, inside in ((0, 0, in_low_y), (1, wide - 1, in_high_y)):
        low, high = pick(odd_x, from_corner_a_ref[place], from_corner_b_ref[place])
        store(0, j, low * (in_low_x * inside))
        store(3, j, high * (in_high_x * inside))
    for copy in copies:
        copy.wait()
    partial = jnp.zeros((block, rest + block), F32)
    totals = {}
    for tile in range(2 * count_y):
        i, j = tile // count_y, tile % count_y
        total = 4.0 * own[i, j][:block] + own[i, j][block:]
        for k in range(neighbours_ref.shape[1]):
            source, kind = source_and_kind(neighbours_ref, kinds_ref, tile, k, count_y)
            pair = mul(ext_ref[source], table_ref[kind])
            total = total + (pair[:block, :side] + (pair[block:, :side] + pair[:block, side:]))
        totals[i, j] = total
        rest_tile = pick(odd_x, rest_a_ref[j], rest_b_ref[j])[i]
        basis_tile = jnp.concatenate([rest_tile, own[i, j][:block]], axis=0)
        partial = partial + pair_sum(stacked(total), *split(basis_tile))
    for j in range(count_y):
        residual_a_ref[j], residual_b_ref[j] = pick(odd_x, totals[0, j], totals[1, j])
    residual_a_ref[count_y] = partial
    partial_ref[...] = partial


def prepare_kernel(
    flags_ref,
    rest_a_ref,
    rest_b_ref,
    from_rest_a_ref,
    from_rest_b_ref,
    current_ref,
    stiff_ref,
    mass_ref,
    basis_ref,
    table_ref,
):
    count_y, rest, _ = rest_a_ref.shape
    prior = rest + current_ref.shape[1]
    odd_x = flag_at(flags_ref, 1)
    split_tables(stiff_ref, mass_ref, table_ref, 0)
    for j in range(count_y):
        rests = list(pick(odd_x, from_rest_a_ref[j], from_rest_b_ref[j]))
        rests[1:1] = pick(odd_x, rest_a_ref[j], rest_b_ref[j])
        for i in range(4):
            tile = jnp.concatenate([rests[i], current_ref[i * (count_y + 2) + j + 1]], axis=0)
            basis_ref[i * count_y + j, :prior, :], basis_ref[i * count_y + j, prior:, :] = split(
                tile
            )


def operators_kernel(
    inverse_rows,
    neighbours_hbm_ref,
    kinds_hbm_ref,
    flags_ref,
    partial_ref,
    row_a_ref,
    row_b_ref,
    from_row_a_ref,
    from_row_b_ref,
    from_side_a_ref,
    from_side_b_ref,
    rest_side_a_ref,
    rest_side_b_ref,
    current_ref,
    basis_ref,
    table_ref,
    weighted_low_ref,
    weighted_high_ref,
    coupling_ref,
    sent_ref,
    kept_ref,
    ext_ref,
    neighbours_ref,
    kinds_ref,
    semaphores,
):
    copies = code_copies(
        (neighbours_hbm_ref, kinds_hbm_ref), (neighbours_ref, kinds_ref), semaphores
    )
    for copy in copies:
        copy.start()
    count_y, block, side = weighted_low_ref.shape
    wide = count_y + 2
    rest = rest_side_a_ref.shape[1]
    prior = rest + block
    odd_y, odd_x, in_low_y, in_high_y, in_low_x, in_high_x = (
        flag_at(flags_ref, place) for place in range(6)
    )
    coupling = partial_ref[...] * inverse_rows
    coupling_ref[...] = coupling
    coupling_deep = deep(coupling)

    def basis_parts(i, j):
        if 0 < j < wide - 1:
            return basis_ref[i * count_y + j - 1]
        rest_tile = pick(odd_y, rest_side_a_ref[i], rest_side_b_ref[i])[j // (wide - 1)]
        return stacked(jnp.concatenate([rest_tile, current_ref[i * wide + j]], axis=0))

    for j in range(wide):
        if 0 < j < wide - 1:
            rows = list(pick(odd_x, from_row_a_ref[j - 1], from_row_b_ref[j - 1]))
            rows[1:1] = pick(odd_x, row_a_ref[j - 1], row_b_ref[j - 1])
        else:
            rows = [
                pick(odd_y, from_side_a_ref[i], from_side_b_ref[i])[j // (wide - 1)]
                for i in range(4)
            ]
        for i in range(4):
            value = rows[i] - halves_sum(mul(coupling_deep, basis_parts(i, j)))
            if i == 0:
                value = value * in_low_x
            if i == 3:
                value = value * in_high_x
            if j == 0:
                value = value * in_low_y
            if j == wide - 1:
                value = value * in_high_y
            if 0 < i < 3 and 0 < j < wide - 1:
                (weighted_low_ref, weighted_high_ref)[i - 1][j - 1] = value
            ext_ref[i * wide + j] = deep(value)
    for copy in copies:
        copy.wait()
    with_basis = jnp.zeros((2 * block, prior), F32)
    with_own = jnp.zeros((block, 4 * block), F32)
    for tile in range(2 * count_y):
        i, j = tile // count_y, tile % count_y
        own = (weighted_low_ref, weighted_high_ref)[i][j]
        totals = jnp.concatenate([4.0 * own, own], axis=1)
        for k in range(neighbours_ref.shape[1]):
            source, kind = source_and_kind(neighbours_ref, kinds_ref, tile, k, count_y)
            totals = totals + halves_sum(mul(ext_ref[source], table_ref[kind]))
        applied = jnp.concatenate([totals[:, :side], totals[:, side:]], axis=0)
        basis_tile = basis_parts(i + 1, j + 1)
        with_basis = with_basis + pair_sum(
            stacked(applied), basis_tile[:prior], basis_tile[prior:]
        )
        right = jnp.concatenate([applied, own, jnp.zeros_like(own)], axis=0)
        with_own = with_own + pair_sum(stacked(own), *split(right))
    halves = [
        jnp.concatenate(
            [
                with_basis[part * block : (part + 1) * block],
                folded(with_own[:, part * block : (part + 1) * block]),
                folded(with_own[:, 2 * block : 3 * block]),
            ],
            axis=0,
        )
        for part in range(2)
    ]
    sent_ref[...], kept_ref[...] = pick(odd_y, halves[0], halves[1])


def folded(square):
    return jnp.concatenate([square[n * 8 : (n + 1) * 8] for n in range(4)], axis=1)


def unfolded(rows):
    return jnp.concatenate([rows[:, n * 32 : (n + 1) * 32] for n in range(4)], axis=0)


def factor_kernel(
    inverse_rows,
    sums_ref,
    weighted_low_ref,
    weighted_high_ref,
    new_hbm_ref,
    factor_ref,
    inverse_ref,
    reduced_ref,
    new_ref,
    semaphore,
):
    count_y, block, _ = weighted_low_ref.shape
    prior = sums_ref.shape[1]
    tiles = 2 * count_y
    gram = unfolded(sums_ref[block + 8 :, :]) * inverse_rows
    row_ids = lax.broadcasted_iota(jnp.int32, (block, block), 0)
    column_ids = lax.broadcasted_iota(jnp.int32, (block, block), 1)
    unit = jnp.where(row_ids == column_ids, 1.0, 0.0).astype(F32)
    work = jnp.concatenate([gram, unit], axis=1)
    rows = lax.broadcasted_iota(jnp.int32, work.shape, 0)
    group = 4
    for j in range(0, block, group):
        columns = [
            jnp.broadcast_to(work[:, j + a : j + a + 1], work.shape) for a in range(group)
        ]
        pivots = [work[j + a : j + a + 1, :] for a in range(group)]
        for a in range(group):
            at = j + a
            ratio = columns[a] * (1.0 / columns[a][at : at + 1, :])
            for b in range(a + 1, group):
                columns[b] = columns[b] - ratio * columns[b][at : at + 1, :]
                pivots[b] = pivots[b] - ratio[j + b : j + b + 1, :] * pivots[a]
            work = work - jnp.where(rows > at, ratio, 0.0) * pivots[a]
    work = work * lax.rsqrt(jnp.sum(work[:, :block] * unit, axis=1, keepdims=True))
    inverse = work[:, block:]
    for tile in range(tiles):
        own = (weighted_low_ref, weighted_high_ref)[tile // count_y][tile % count_y]
        new_ref[pl.ds(tile, block, stride=tiles), :] = mul3(inverse, own)
    copy = pltpu.make_async_copy(new_ref, new_hbm_ref, semaphore)
    copy.start()
    factor_ref[...] = jnp.where(column_ids >= row_ids, work[:, :block], 0.0)
    inverse_ref[...] = inverse
    reduce_half(inverse, sums_ref, inverse_rows, reduced_ref)
    copy.wait()


def reduce_half(inverse, sums_ref, inverse_rows, out_ref):
    block, prior = inverse.shape[0], sums_ref.shape[1]
    out_ref[:, :prior] = mul3(inverse, sums_ref[:block, :] * inverse_rows)
    own = unfolded(sums_ref[block : block + 8, :]) * inverse_rows
    out_ref[:, prior:] = mul3_t(mul3_t(inverse, own), inverse)


def reduced_kernel(inverse_rows, flags_ref, inverse_ref, other_ref, half_ref, out_ref, work_ref):
    reduce_half(inverse_ref[...], other_ref, inverse_rows, work_ref)
    odd_y = flag_at(flags_ref, 0)
    for span in (slice(0, 128), slice(128, out_ref.shape[2])):
        flag = odd_y[:, : work_ref[:, span].shape[1]]
        out_ref[0, :, span], out_ref[1, :, span] = pick(
            flag, work_ref[:, span], half_ref[:, span]
        )


def swap(value, mask):
    axes = ("px", "py")
    pairs = [(i, i ^ mask) for i in range(lax.axis_size(axes))]
    return lax.ppermute(value, axes, pairs)


def exchange(message_a, message_b, axis):
    count = lax.axis_size(axis)
    pairs = [(i, ((i + 1) ^ 1) - 1) for i in range(count)]
    pairs = [(i, j if 0 <= j < count else i) for i, j in pairs]
    near = [(i, i ^ 1) for i in range(count)]
    return lax.ppermute(message_a, axis, near), lax.ppermute(message_b, axis, pairs)


def total_over(value, first, last):
    while first < last:
        value = value + swap(value, first)
        first *= 2
    return value


def half_total(sent, kept):
    kept = kept + swap(sent, 1)
    kept = (kept + swap(kept, 6)) + (swap(kept, 2) + swap(kept, 4))
    return total_over(kept, 8, lax.axis_size(("px", "py")))


def shape(*dims, dtype=F32):
    return jax.ShapeDtypeStruct(dims, dtype)


def shards(prior_basis, previous, neighbours, tile_kinds, stiff_tiles, mass_tiles):
    block = previous.shape[0]
    prior, count_x, count_y, side = prior_basis.shape
    tiles = count_x * count_y
    wide = count_y + 2
    rest = prior - block
    kinds = stiff_tiles.shape[0]
    inverse_rows = 1.0 / (tiles * side * lax.axis_size("px") * lax.axis_size("py"))
    basis = prior_basis.reshape(-1, side)
    vectors = jnp.concatenate([basis, previous.reshape(-1, side)], axis=0)
    codes = [array.transpose(1, 2, 0).reshape(tiles, -1) for array in (neighbours, tile_kinds)]
    code_scratch = [pltpu.SMEM(array.shape, jnp.int32) for array in codes]
    code_scratch += [pltpu.SemaphoreType.DMA((2,))]
    at_y, at_x = lax.axis_index("py"), lax.axis_index("px")
    bits = (at_y & 1) + 2 * (at_x & 1)
    bits += 4 * (at_y > 0) + 8 * (at_y < lax.axis_size("py") - 1)
    bits += 16 * (at_x > 0) + 32 * (at_x < lax.axis_size("px") - 1)
    flags = ((bits >> lax.broadcasted_iota(jnp.int32, (8, side), 0)) & 1).astype(F32)

    def call(kernel, inputs, outputs, scratch=(), plain=0, plain_out=0, limit=8, cost=None):
        specs = [ANY] * plain + [VMEM] * (len(inputs) - plain)
        return pl.pallas_call(
            kernel,
            out_shape=outputs,
            in_specs=specs,
            out_specs=[ANY] * plain_out + [VMEM] * (len(outputs) - plain_out),
            scratch_shapes=scratch,
            compiler_params=pltpu.CompilerParams(vmem_limit_bytes=limit * MIB),
            cost_estimate=cost,
        )(*inputs)

    side_a, side_b, row_a, row_b = call(
        pack_kernel,
        (flags, vectors),
        [shape(count_x, 2 * block, side)] * 2 + [shape(count_y, 2 * block, side)] * 2,
    )
    rest_a, rest_b = call(rest_kernel, (flags, vectors), [shape(count_y, rest, side)] * 2)
    from_side_a, from_side_b = exchange(side_a, side_b, "py")
    from_row_a, from_row_b = exchange(row_a, row_b, "px")
    from_side_a, rest_a, rest_b = lax.optimization_barrier((from_side_a, rest_a, rest_b))
    from_rest_a, from_rest_b = exchange(rest_a, rest_b, "px")
    corner_a, corner_b = call(
        corners_kernel,
        (flags, from_side_a, from_side_b),
        [shape(2, 2 * block, side)] * 2,
    )
    from_corner_a, from_corner_b = exchange(corner_a, corner_b, "px")
    rest_side_a, rest_side_b = call(
        columns_kernel,
        (flags, rest_a, rest_b, from_rest_a, from_rest_b),
        [shape(4, rest, side)] * 2,
    )
    rest_side_a, rest_side_b = exchange(rest_side_a, rest_side_b, "py")
    residual_a, residual_b, partial, current = call(
        residual_kernel,
        (
            *codes,
            flags,
            row_a,
            row_b,
            from_row_a,
            from_row_b,
            from_side_a,
            from_side_b,
            from_corner_a,
            from_corner_b,
            rest_a,
            rest_b,
            stiff_tiles,
            mass_tiles,
        ),
        [shape(count_y + 1, block, side), shape(count_y, block, side)]
        + [shape(block, prior), shape(4 * wide, block, side)],
        [pltpu.VMEM((4 * wide, 2 * block, 2 * side), BF16)]
        + [pltpu.VMEM((kinds, 2 * side, 2 * side), BF16)]
        + code_scratch,
        plain=2,
        cost=pl.CostEstimate(flops=10**9, bytes_accessed=0, transcendentals=0),
    )
    count_py = lax.axis_size("py")
    from_row_a, from_row_b = exchange(residual_a, residual_b, "px")
    partial = total_over(
        partial + from_row_a[-1], 2 * count_py, count_py * lax.axis_size("px")
    )
    partial, rest_side_a, rest_side_b = lax.optimization_barrier(
        (partial, rest_side_a, rest_side_b)
    )
    side_a, side_b = call(
        columns_kernel,
        (flags, residual_a, residual_b, from_row_a, from_row_b, partial),
        [shape(5, block, side), shape(4, block, side)],
    )
    from_side_a, from_side_b = exchange(side_a, side_b, "py")
    partial = total_over(partial + from_side_a[-1], 2, count_py)
    basis_parts, table = call(
        prepare_kernel,
        (flags, rest_a, rest_b, from_rest_a, from_rest_b, current, stiff_tiles, mass_tiles),
        [shape(4 * count_y, 2 * prior, side, dtype=BF16)]
        + [shape(kinds, 2 * side, 2 * side, dtype=BF16)],
        cost=pl.CostEstimate(flops=10**9, bytes_accessed=0, transcendentals=0),
    )
    weighted_low, weighted_high, coupling, sent, kept = call(
        functools.partial(operators_kernel, inverse_rows),
        (
            *codes,
            flags,
            partial,
            residual_a,
            residual_b,
            from_row_a,
            from_row_b,
            from_side_a,
            from_side_b,
            rest_side_a,
            rest_side_b,
            current,
            basis_parts,
            table,
        ),
        [shape(count_y, block, side)] * 2
        + [shape(block, prior)]
        + [shape(block + 16, prior)] * 2,
        [pltpu.VMEM((4 * wide, 2 * block, 2 * side), BF16)] + code_scratch,
        plain=2,
    )
    kept = half_total(sent, kept)
    other = swap(kept[: block + 8], 1)
    new_block, factor, inverse, half = call(
        functools.partial(factor_kernel, inverse_rows),
        (kept, weighted_low, weighted_high),
        [
            shape(block * tiles, side),
            shape(block, block),
            shape(block, block),
            shape(block, prior + block),
        ],
        [pltpu.VMEM((block * tiles, side), F32), pltpu.SemaphoreType.DMA],
        plain_out=1,
        cost=pl.CostEstimate(flops=10**9, bytes_accessed=0, transcendentals=0),
    )
    (reduced,) = call(
        functools.partial(reduced_kernel, inverse_rows),
        (flags, inverse, other, half),
        [shape(2, block, prior + block)],
        [pltpu.VMEM((block, prior + block), F32)],
    )
    return (
        new_block.reshape(previous.shape),
        coupling.T,
        factor,
        reduced.swapaxes(1, 2),
    )


def solution(mesh):
    placed = (
        P("case", "px", "py", None),
        P("case", "px", "py", None),
        P(None, "px", "py"),
        P(None, "px", "py"),
        P(),
        P(),
    )
    return jax.shard_map(
        shards,
        mesh=mesh,
        in_specs=placed,
        out_specs=(
            P("case", "px", "py", None),
            P("case", None),
            P("case", None),
            P("case", None, None),
        ),
        check_vma=False,
    )
```

```python
import functools

import jax
import jax.numpy as jnp
from jax import lax
from jax.experimental import pallas as pl
from jax.experimental.pallas import tpu as pltpu
from jax.sharding import PartitionSpec as P

F32 = jnp.float32
BF16 = jnp.bfloat16
VMEM = pl.BlockSpec(memory_space=pltpu.VMEM)
ANY = pl.BlockSpec(memory_space=pl.ANY)
MIB = 1024 * 1024


def split(value):
    high = value.astype(BF16)
    return high, (value - high.astype(F32)).astype(BF16)


def mul(left, right):
    return jnp.dot(left, right, preferred_element_type=F32)


def mul_t(left, right):
    return lax.dot_general(left, right, (((1,), (1,)), ((), ())), preferred_element_type=F32)


def mul3(left, right):
    left_high, left_low = split(left)
    right_high, right_low = split(right)
    return mul(left_high, right_high) + (mul(left_high, right_low) + mul(left_low, right_high))


def mul3_t(left, right):
    left_high, left_low = split(left)
    right_high, right_low = split(right)
    return mul_t(left_high, right_high) + (
        mul_t(left_high, right_low) + mul_t(left_low, right_high)
    )


def split_tables(stiff_ref, mass_ref, table_ref, parts_axis):
    side = stiff_ref.shape[1]
    spans = (slice(0, side), slice(side, 2 * side))
    for kind in range(stiff_ref.shape[0]):
        for matrix, ref in zip(spans, (stiff_ref, mass_ref)):
            for part, value in zip(spans, split(ref[kind])):
                if parts_axis == 1:
                    table_ref[kind, matrix, part] = value
                else:
                    table_ref[kind, part, matrix] = value


def stacked(value):
    return jnp.concatenate(split(value), axis=0)


def deep(value):
    high, low = split(value)
    upper = jnp.concatenate([high, high], axis=1)
    return jnp.concatenate([upper, jnp.concatenate([low, jnp.zeros_like(low)], axis=1)], axis=0)


def halves_sum(value):
    half = value.shape[0] // 2
    return value[:half] + value[half:]


def pair_sum(left, right_high, right_low):
    rows = left.shape[0] // 2
    return halves_sum(mul_t(left, right_high)) + mul_t(left[:rows], right_low)


def pick(flag, first, second):
    flag = flag > 0.0
    return jnp.where(flag, first, second), jnp.where(flag, second, first)


def flag_at(flags_ref, place):
    return flags_ref[place : place + 1, :]


def code_copies(code_refs, local_refs, semaphores):
    return [
        pltpu.make_async_copy(ref, local, semaphores.at[n])
        for n, (ref, local) in enumerate(zip(code_refs, local_refs))
    ]


def source_and_kind(neighbours_ref, kinds_ref, tile, k, count_y):
    neighbour = neighbours_ref[tile, k]
    down = (neighbour * 11) >> 5
    first = (tile // count_y) * (count_y + 2) + tile % count_y
    return first + neighbour + down * (count_y - 1), kinds_ref[tile, k]


def pack_kernel(flags_ref, vectors_ref, side_a_ref, side_b_ref, row_a_ref, row_b_ref):
    count_y, both, _ = row_a_ref.shape
    tiles = 2 * count_y
    odd_y, odd_x = flag_at(flags_ref, 0), flag_at(flags_ref, 1)

    first = vectors_ref.shape[0] - both * tiles

    def tile_of(i, j):
        return vectors_ref[pl.ds(first + i * count_y + j, both, stride=tiles), :]

    for i in range(2):
        side_a_ref[i], side_b_ref[i] = pick(odd_y, tile_of(i, 0), tile_of(i, count_y - 1))
    for j in range(count_y):
        row_a_ref[j], row_b_ref[j] = pick(odd_x, tile_of(0, j), tile_of(1, j))


def rest_kernel(flags_ref, vectors_ref, rest_a_ref, rest_b_ref):
    count_y, rest, _ = rest_a_ref.shape
    odd_x = flag_at(flags_ref, 1)
    for j in range(count_y):
        rest_a_ref[j], rest_b_ref[j] = pick(
            odd_x,
            vectors_ref[pl.ds(j, rest, stride=2 * count_y), :],
            vectors_ref[pl.ds(count_y + j, rest, stride=2 * count_y), :],
        )


def corners_kernel(flags_ref, side_a_ref, side_b_ref, corner_a_ref, corner_b_ref):
    odd_y, odd_x = flag_at(flags_ref, 0), flag_at(flags_ref, 1)
    ends = [pick(odd_y, side_a_ref[i], side_b_ref[i]) for i in range(2)]
    for place in range(2):
        corner_a_ref[place], corner_b_ref[place] = pick(odd_x, ends[0][place], ends[1][place])


def columns_kernel(
    flags_ref, row_a_ref, row_b_ref, from_row_a_ref, from_row_b_ref, *refs
):
    odd_y, odd_x = flag_at(flags_ref, 0), flag_at(flags_ref, 1)
    side_a_ref, side_b_ref = refs[-2:]
    columns = []
    for j in (0, row_b_ref.shape[0] - 1):
        column = list(pick(odd_x, from_row_a_ref[j], from_row_b_ref[j]))
        column[1:1] = pick(odd_x, row_a_ref[j], row_b_ref[j])
        columns.append(column)
    for i in range(4):
        side_a_ref[i], side_b_ref[i] = pick(odd_y, columns[0][i], columns[1][i])
    if len(refs) == 3:
        side_a_ref[4] = refs[0][...]


def residual_kernel(
    neighbours_hbm_ref,
    kinds_hbm_ref,
    flags_ref,
    row_a_ref,
    row_b_ref,
    from_row_a_ref,
    from_row_b_ref,
    from_side_a_ref,
    from_side_b_ref,
    from_corner_a_ref,
    from_corner_b_ref,
    rest_a_ref,
    rest_b_ref,
    stiff_ref,
    mass_ref,
    residual_a_ref,
    residual_b_ref,
    partial_ref,
    current_ref,
    ext_ref,
    table_ref,
    neighbours_ref,
    kinds_ref,
    semaphores,
):
    copies = code_copies(
        (neighbours_hbm_ref, kinds_hbm_ref), (neighbours_ref, kinds_ref), semaphores
    )
    for copy in copies:
        copy.start()
    split_tables(stiff_ref, mass_ref, table_ref, 1)
    count_y, both, side = row_a_ref.shape
    wide = count_y + 2
    block = both // 2
    rest = rest_a_ref.shape[1]
    odd_y, odd_x, in_low_y, in_high_y, in_low_x, in_high_x = (
        flag_at(flags_ref, place) for place in range(6)
    )

    def store(i, j, value):
        current_ref[i * wide + j] = value[:block]
        for part in range(2):
            high, low = split(value[part * block : (part + 1) * block])
            ext_ref[i * wide + j, :block, part * side : (part + 1) * side] = high
            ext_ref[i * wide + j, block:, part * side : (part + 1) * side] = low

    own = {}
    for j in range(count_y):
        own[0, j], own[1, j] = pick(odd_x, row_a_ref[j], row_b_ref[j])
        store(1, j + 1, own[0, j])
        store(2, j + 1, own[1, j])
        low, high = pick(odd_x, from_row_a_ref[j], from_row_b_ref[j])
        store(0, j + 1, low * in_low_x)
        store(3, j + 1, high * in_high_x)
    for i in range(2):
        low, high = pick(odd_y, from_side_a_ref[i], from_side_b_ref[i])
        store(i + 1, 0, low * in_low_y)
        store(i + 1, wide - 1, high * in_high_y)
    for place, j, inside in ((0, 0, in_low_y), (1, wide - 1, in_high_y)):
        low, high = pick(odd_x, from_corner_a_ref[place], from_corner_b_ref[place])
        store(0, j, low * (in_low_x * inside))
        store(3, j, high * (in_high_x * inside))
    for copy in copies:
        copy.wait()
    partial = jnp.zeros((block, rest + block), F32)
    totals = {}
    for tile in range(2 * count_y):
        i, j = tile // count_y, tile % count_y
        total = 4.0 * own[i, j][:block] + own[i, j][block:]
        for k in range(neighbours_ref.shape[1]):
            source, kind = source_and_kind(neighbours_ref, kinds_ref, tile, k, count_y)
            pair = mul(ext_ref[source], table_ref[kind])
            total = total + (pair[:block, :side] + (pair[block:, :side] + pair[:block, side:]))
        totals[i, j] = total
        rest_tile = pick(odd_x, rest_a_ref[j], rest_b_ref[j])[i]
        basis_tile = jnp.concatenate([rest_tile, own[i, j][:block]], axis=0)
        partial = partial + pair_sum(stacked(total), *split(basis_tile))
    for j in range(count_y):
        residual_a_ref[j], residual_b_ref[j] = pick(odd_x, totals[0, j], totals[1, j])
    partial_ref[...] = partial


def tables_kernel(stiff_ref, mass_ref, table_ref):
    split_tables(stiff_ref, mass_ref, table_ref, 0)


def prepare_kernel(
    flags_ref,
    rest_a_ref,
    rest_b_ref,
    from_rest_a_ref,
    from_rest_b_ref,
    current_ref,
    basis_ref,
):
    count_y, rest, _ = rest_a_ref.shape
    prior = rest + current_ref.shape[1]
    odd_x = flag_at(flags_ref, 1)
    for j in range(count_y):
        rests = list(pick(odd_x, from_rest_a_ref[j], from_rest_b_ref[j]))
        rests[1:1] = pick(odd_x, rest_a_ref[j], rest_b_ref[j])
        for i in range(4):
            tile = jnp.concatenate([rests[i], current_ref[i * (count_y + 2) + j + 1]], axis=0)
            basis_ref[i * count_y + j, :prior, :], basis_ref[i * count_y + j, prior:, :] = split(
                tile
            )


def operators_kernel(
    inverse_rows,
    neighbours_hbm_ref,
    kinds_hbm_ref,
    flags_ref,
    partial_ref,
    row_a_ref,
    row_b_ref,
    from_row_a_ref,
    from_row_b_ref,
    from_side_a_ref,
    from_side_b_ref,
    rest_side_a_ref,
    rest_side_b_ref,
    current_ref,
    basis_ref,
    table_ref,
    weighted_low_ref,
    weighted_high_ref,
    coupling_ref,
    sent_ref,
    kept_ref,
    ext_ref,
    neighbours_ref,
    kinds_ref,
    semaphores,
):
    copies = code_copies(
        (neighbours_hbm_ref, kinds_hbm_ref), (neighbours_ref, kinds_ref), semaphores
    )
    for copy in copies:
        copy.start()
    count_y, block, side = weighted_low_ref.shape
    wide = count_y + 2
    rest = rest_side_a_ref.shape[1]
    prior = rest + block
    odd_y, odd_x, in_low_y, in_high_y, in_low_x, in_high_x = (
        flag_at(flags_ref, place) for place in range(6)
    )
    coupling = partial_ref[...] * inverse_rows
    coupling_ref[...] = coupling
    coupling_deep = deep(coupling)

    def basis_parts(i, j):
        if 0 < j < wide - 1:
            return basis_ref[i * count_y + j - 1]
        rest_tile = pick(odd_y, rest_side_a_ref[i], rest_side_b_ref[i])[j // (wide - 1)]
        return stacked(jnp.concatenate([rest_tile, current_ref[i * wide + j]], axis=0))

    for j in range(wide):
        if 0 < j < wide - 1:
            rows = list(pick(odd_x, from_row_a_ref[j - 1], from_row_b_ref[j - 1]))
            rows[1:1] = pick(odd_x, row_a_ref[j - 1], row_b_ref[j - 1])
        else:
            rows = [
                pick(odd_y, from_side_a_ref[i], from_side_b_ref[i])[j // (wide - 1)]
                for i in range(4)
            ]
        for i in range(4):
            value = rows[i] - halves_sum(mul(coupling_deep, basis_parts(i, j)))
            if i == 0:
                value = value * in_low_x
            if i == 3:
                value = value * in_high_x
            if j == 0:
                value = value * in_low_y
            if j == wide - 1:
                value = value * in_high_y
            if 0 < i < 3 and 0 < j < wide - 1:
                (weighted_low_ref, weighted_high_ref)[i - 1][j - 1] = value
            ext_ref[i * wide + j] = deep(value)
    for copy in copies:
        copy.wait()
    with_basis = jnp.zeros((2 * block, prior), F32)
    with_own = jnp.zeros((block, 4 * block), F32)
    for tile in range(2 * count_y):
        i, j = tile // count_y, tile % count_y
        own = (weighted_low_ref, weighted_high_ref)[i][j]
        totals = jnp.concatenate([4.0 * own, own], axis=1)
        for k in range(neighbours_ref.shape[1]):
            source, kind = source_and_kind(neighbours_ref, kinds_ref, tile, k, count_y)
            totals = totals + halves_sum(mul(ext_ref[source], table_ref[kind]))
        applied = jnp.concatenate([totals[:, :side], totals[:, side:]], axis=0)
        basis_tile = basis_parts(i + 1, j + 1)
        with_basis = with_basis + pair_sum(
            stacked(applied), basis_tile[:prior], basis_tile[prior:]
        )
        right = jnp.concatenate([applied, own, jnp.zeros_like(own)], axis=0)
        with_own = with_own + pair_sum(stacked(own), *split(right))
    halves = [
        jnp.concatenate(
            [
                with_basis[part * block : (part + 1) * block],
                folded(with_own[:, part * block : (part + 1) * block]),
                folded(with_own[:, 2 * block : 3 * block]),
            ],
            axis=0,
        )
        for part in range(2)
    ]
    sent_ref[...], kept_ref[...] = pick(odd_y, halves[0], halves[1])


def folded(square):
    return jnp.concatenate([square[n * 8 : (n + 1) * 8] for n in range(4)], axis=1)


def unfolded(rows):
    return jnp.concatenate([rows[:, n * 32 : (n + 1) * 32] for n in range(4)], axis=0)


def factor_kernel(inverse_rows, sums_ref, work_ref):
    block = work_ref.shape[0]
    gram = unfolded(sums_ref[block + 8 :, :]) * inverse_rows
    row_ids = lax.broadcasted_iota(jnp.int32, (block, block), 0)
    column_ids = lax.broadcasted_iota(jnp.int32, (block, block), 1)
    unit = jnp.where(row_ids == column_ids, 1.0, 0.0).astype(F32)
    work = jnp.concatenate([gram, unit], axis=1)
    rows = lax.broadcasted_iota(jnp.int32, work.shape, 0)
    group = 4
    for j in range(0, block, group):
        columns = [
            jnp.broadcast_to(work[:, j + a : j + a + 1], work.shape) for a in range(group)
        ]
        pivots = [work[j + a : j + a + 1, :] for a in range(group)]
        for a in range(group):
            at = j + a
            ratio = columns[a] * (1.0 / columns[a][at : at + 1, :])
            for b in range(a + 1, group):
                columns[b] = columns[b] - ratio * columns[b][at : at + 1, :]
                pivots[b] = pivots[b] - ratio[j + b : j + b + 1, :] * pivots[a]
            work = work - jnp.where(rows > at, ratio, 0.0) * pivots[a]
    work = work * lax.rsqrt(jnp.sum(work[:, :block] * unit, axis=1, keepdims=True))
    work_ref[...] = work


def finish_kernel(
    inverse_rows,
    flags_ref,
    work_ref,
    sums_ref,
    other_ref,
    weighted_low_ref,
    weighted_high_ref,
    new_ref,
    factor_ref,
    reduced_ref,
):
    count_y, block, _ = weighted_low_ref.shape
    prior = sums_ref.shape[1]
    tiles = 2 * count_y
    row_ids = lax.broadcasted_iota(jnp.int32, (block, block), 0)
    column_ids = lax.broadcasted_iota(jnp.int32, (block, block), 1)
    factor_ref[...] = jnp.where(column_ids >= row_ids, work_ref[:, :block], 0.0)
    inverse = work_ref[:, block:]
    for tile in range(tiles):
        own = (weighted_low_ref, weighted_high_ref)[tile // count_y][tile % count_y]
        new_ref[pl.ds(tile, block, stride=tiles), :] = mul3(inverse, own)
    odd_y = flag_at(flags_ref, 0)
    halves = pick(odd_y, other_ref[...], sums_ref[: block + 8, :])
    for part, half in enumerate(halves):
        reduced_ref[part, :, :prior] = mul3(inverse, half[:block] * inverse_rows)
        own = unfolded(half[block:]) * inverse_rows
        reduced_ref[part, :, prior:] = mul3_t(mul3_t(inverse, own), inverse)


def swap(value, mask):
    axes = ("px", "py")
    pairs = [(i, i ^ mask) for i in range(lax.axis_size(axes))]
    return lax.ppermute(value, axes, pairs)


def exchange(message_a, message_b, axis):
    count = lax.axis_size(axis)
    pairs = [(i, ((i + 1) ^ 1) - 1) for i in range(count)]
    pairs = [(i, j if 0 <= j < count else i) for i, j in pairs]
    near = [(i, i ^ 1) for i in range(count)]
    return lax.ppermute(message_a, axis, near), lax.ppermute(message_b, axis, pairs)


def total_over(value, first, last):
    while first < last:
        value = value + swap(value, first)
        first *= 2
    return value


def half_total(sent, kept):
    kept = kept + swap(sent, 1)
    kept = (kept + swap(kept, 6)) + (swap(kept, 2) + swap(kept, 4))
    return total_over(kept, 8, lax.axis_size(("px", "py")))


def shape(*dims, dtype=F32):
    return jax.ShapeDtypeStruct(dims, dtype)


def shards(prior_basis, previous, neighbours, tile_kinds, stiff_tiles, mass_tiles):
    block = previous.shape[0]
    prior, count_x, count_y, side = prior_basis.shape
    tiles = count_x * count_y
    wide = count_y + 2
    rest = prior - block
    kinds = stiff_tiles.shape[0]
    inverse_rows = 1.0 / (tiles * side * lax.axis_size("px") * lax.axis_size("py"))
    basis = prior_basis.reshape(-1, side)
    vectors = jnp.concatenate([basis, previous.reshape(-1, side)], axis=0)
    codes = [array.transpose(1, 2, 0).reshape(tiles, -1) for array in (neighbours, tile_kinds)]
    code_scratch = [pltpu.SMEM(array.shape, jnp.int32) for array in codes]
    code_scratch += [pltpu.SemaphoreType.DMA((2,))]
    at_y, at_x = lax.axis_index("py"), lax.axis_index("px")
    bits = (at_y & 1) + 2 * (at_x & 1)
    bits += 4 * (at_y > 0) + 8 * (at_y < lax.axis_size("py") - 1)
    bits += 16 * (at_x > 0) + 32 * (at_x < lax.axis_size("px") - 1)
    flags = ((bits >> lax.broadcasted_iota(jnp.int32, (8, side), 0)) & 1).astype(F32)

    def call(kernel, inputs, outputs, scratch=(), plain=0, limit=8, cost=None):
        specs = [ANY] * plain + [VMEM] * (len(inputs) - plain)
        return pl.pallas_call(
            kernel,
            out_shape=outputs,
            in_specs=specs,
            out_specs=[VMEM] * len(outputs),
            scratch_shapes=scratch,
            compiler_params=pltpu.CompilerParams(vmem_limit_bytes=limit * MIB),
            cost_estimate=cost,
        )(*inputs)

    side_a, side_b, row_a, row_b = call(
        pack_kernel,
        (flags, vectors),
        [shape(count_x, 2 * block, side)] * 2 + [shape(count_y, 2 * block, side)] * 2,
    )
    rest_a, rest_b = call(rest_kernel, (flags, vectors), [shape(count_y, rest, side)] * 2)
    from_side_a, from_side_b = exchange(side_a, side_b, "py")
    from_row_a, from_row_b = exchange(row_a, row_b, "px")
    from_side_a, rest_a, rest_b = lax.optimization_barrier((from_side_a, rest_a, rest_b))
    from_rest_a, from_rest_b = exchange(rest_a, rest_b, "px")
    corner_a, corner_b = call(
        corners_kernel,
        (flags, from_side_a, from_side_b),
        [shape(2, 2 * block, side)] * 2,
    )
    from_corner_a, from_corner_b = exchange(corner_a, corner_b, "px")
    rest_side_a, rest_side_b = call(
        columns_kernel,
        (flags, rest_a, rest_b, from_rest_a, from_rest_b),
        [shape(4, rest, side)] * 2,
    )
    rest_side_a, rest_side_b = exchange(rest_side_a, rest_side_b, "py")
    residual_a, residual_b, partial, current = call(
        residual_kernel,
        (
            *codes,
            flags,
            row_a,
            row_b,
            from_row_a,
            from_row_b,
            from_side_a,
            from_side_b,
            from_corner_a,
            from_corner_b,
            rest_a,
            rest_b,
            stiff_tiles,
            mass_tiles,
        ),
        [shape(count_y, block, side)] * 2
        + [shape(block, prior), shape(4 * wide, block, side)],
        [pltpu.VMEM((4 * wide, 2 * block, 2 * side), BF16)]
        + [pltpu.VMEM((kinds, 2 * side, 2 * side), BF16)]
        + code_scratch,
        plain=2,
        cost=pl.CostEstimate(flops=10**9, bytes_accessed=0, transcendentals=0),
    )
    count_py = lax.axis_size("py")
    stiff_tiles, residual_a = lax.optimization_barrier((stiff_tiles, residual_a))
    (table,) = call(
        tables_kernel,
        (stiff_tiles, mass_tiles),
        [shape(kinds, 2 * side, 2 * side, dtype=BF16)],
        cost=pl.CostEstimate(flops=10**9, bytes_accessed=0, transcendentals=0),
    )
    partial = total_over(partial, 2 * count_py, count_py * lax.axis_size("px"))
    partial, table = lax.optimization_barrier((partial, table))
    from_row_a, from_row_b = exchange(
        jnp.concatenate([residual_a, partial[None]], axis=0), residual_b, "px"
    )
    partial = partial + from_row_a[-1]
    partial, rest_side_a, rest_side_b = lax.optimization_barrier(
        (partial, rest_side_a, rest_side_b)
    )
    side_a, side_b = call(
        columns_kernel,
        (flags, residual_a, residual_b, from_row_a, from_row_b, partial),
        [shape(5, block, side), shape(4, block, side)],
    )
    from_side_a, from_side_b = exchange(side_a, side_b, "py")
    partial = total_over(partial + from_side_a[-1], 2, count_py)
    (basis_parts,) = call(
        prepare_kernel,
        (flags, rest_a, rest_b, from_rest_a, from_rest_b, current),
        [shape(4 * count_y, 2 * prior, side, dtype=BF16)],
        cost=pl.CostEstimate(flops=10**9, bytes_accessed=0, transcendentals=0),
    )
    weighted_low, weighted_high, coupling, sent, kept = call(
        functools.partial(operators_kernel, inverse_rows),
        (
            *codes,
            flags,
            partial,
            residual_a,
            residual_b,
            from_row_a,
            from_row_b,
            from_side_a,
            from_side_b,
            rest_side_a,
            rest_side_b,
            current,
            basis_parts,
            table,
        ),
        [shape(count_y, block, side)] * 2
        + [shape(block, prior)]
        + [shape(block + 16, prior)] * 2,
        [pltpu.VMEM((4 * wide, 2 * block, 2 * side), BF16)] + code_scratch,
        plain=2,
    )
    kept = half_total(sent, kept)
    other = swap(kept[: block + 8], 1)
    (work,) = call(
        functools.partial(factor_kernel, inverse_rows),
        (kept,),
        [shape(block, 2 * block)],
        cost=pl.CostEstimate(flops=10**9, bytes_accessed=0, transcendentals=0),
    )
    new_block, factor, reduced = call(
        functools.partial(finish_kernel, inverse_rows),
        (flags, work, kept, other, weighted_low, weighted_high),
        [
            shape(block * tiles, side),
            shape(block, block),
            shape(2, block, prior + block),
        ],
    )
    return (
        new_block.reshape(previous.shape),
        coupling.T,
        factor,
        reduced.swapaxes(1, 2),
    )


def solution(mesh):
    placed = (
        P("case", "px", "py", None),
        P("case", "px", "py", None),
        P(None, "px", "py"),
        P(None, "px", "py"),
        P(),
        P(),
    )
    return jax.shard_map(
        shards,
        mesh=mesh,
        in_specs=placed,
        out_specs=(
            P("case", "px", "py", None),
            P("case", None),
            P("case", None),
            P("case", None, None),
        ),
        check_vma=False,
    )
```

```python
import functools

import jax
import jax.numpy as jnp
from jax import lax
from jax.experimental import pallas as pl
from jax.experimental.pallas import tpu as pltpu
from jax.sharding import PartitionSpec as P

F32 = jnp.float32
BF16 = jnp.bfloat16
VMEM = pl.BlockSpec(memory_space=pltpu.VMEM)
ANY = pl.BlockSpec(memory_space=pl.ANY)
MIB = 1024 * 1024


def split(value):
    high = value.astype(BF16)
    return high, (value - high.astype(F32)).astype(BF16)


def mul(left, right):
    return jnp.dot(left, right, preferred_element_type=F32)


def mul_t(left, right):
    return lax.dot_general(left, right, (((1,), (1,)), ((), ())), preferred_element_type=F32)


def mul3(left, right):
    left_high, left_low = split(left)
    right_high, right_low = split(right)
    return mul(left_high, right_high) + (mul(left_high, right_low) + mul(left_low, right_high))


def mul3_t(left, right):
    left_high, left_low = split(left)
    right_high, right_low = split(right)
    return mul_t(left_high, right_high) + (
        mul_t(left_high, right_low) + mul_t(left_low, right_high)
    )


def split_tables(stiff_ref, mass_ref, table_ref, parts_axis):
    side = stiff_ref.shape[1]
    spans = (slice(0, side), slice(side, 2 * side))
    for kind in range(stiff_ref.shape[0]):
        for matrix, ref in zip(spans, (stiff_ref, mass_ref)):
            for part, value in zip(spans, split(ref[kind])):
                if parts_axis == 1:
                    table_ref[kind, matrix, part] = value
                else:
                    table_ref[kind, part, matrix] = value


def stacked(value):
    return jnp.concatenate(split(value), axis=0)


def deep(value):
    high, low = split(value)
    upper = jnp.concatenate([high, high], axis=1)
    return jnp.concatenate([upper, jnp.concatenate([low, jnp.zeros_like(low)], axis=1)], axis=0)


def halves_sum(value):
    half = value.shape[0] // 2
    return value[:half] + value[half:]


def pair_sum(left, right_high, right_low):
    rows = left.shape[0] // 2
    return halves_sum(mul_t(left, right_high)) + mul_t(left[:rows], right_low)


def pick(flag, first, second):
    flag = flag > 0.0
    return jnp.where(flag, first, second), jnp.where(flag, second, first)


def flag_at(flags_ref, place):
    return flags_ref[place : place + 1, :]


def code_copies(code_refs, local_refs, semaphores):
    return [
        pltpu.make_async_copy(ref, local, semaphores.at[n])
        for n, (ref, local) in enumerate(zip(code_refs, local_refs))
    ]


def source_and_kind(neighbours_ref, kinds_ref, tile, k, count_y):
    neighbour = neighbours_ref[tile, k]
    down = (neighbour * 11) >> 5
    first = (tile // count_y) * (count_y + 2) + tile % count_y
    return first + neighbour + down * (count_y - 1), kinds_ref[tile, k]


def pack_kernel(flags_ref, vectors_ref, side_a_ref, side_b_ref, row_a_ref, row_b_ref):
    count_y, both, _ = row_a_ref.shape
    tiles = 2 * count_y
    odd_y, odd_x = flag_at(flags_ref, 0), flag_at(flags_ref, 1)

    first = vectors_ref.shape[0] - both * tiles

    def tile_of(i, j):
        return vectors_ref[pl.ds(first + i * count_y + j, both, stride=tiles), :]

    for i in range(2):
        side_a_ref[i], side_b_ref[i] = pick(odd_y, tile_of(i, 0), tile_of(i, count_y - 1))
    for j in range(count_y):
        row_a_ref[j], row_b_ref[j] = pick(odd_x, tile_of(0, j), tile_of(1, j))


def rest_kernel(flags_ref, vectors_ref, rest_a_ref, rest_b_ref):
    count_y, rest, _ = rest_a_ref.shape
    odd_x = flag_at(flags_ref, 1)
    for j in range(count_y):
        rest_a_ref[j], rest_b_ref[j] = pick(
            odd_x,
            vectors_ref[pl.ds(j, rest, stride=2 * count_y), :],
            vectors_ref[pl.ds(count_y + j, rest, stride=2 * count_y), :],
        )


def corners_kernel(flags_ref, side_a_ref, side_b_ref, corner_a_ref, corner_b_ref):
    odd_y, odd_x = flag_at(flags_ref, 0), flag_at(flags_ref, 1)
    ends = [pick(odd_y, side_a_ref[i], side_b_ref[i]) for i in range(2)]
    for place in range(2):
        corner_a_ref[place], corner_b_ref[place] = pick(odd_x, ends[0][place], ends[1][place])


def columns_kernel(
    flags_ref, row_a_ref, row_b_ref, from_row_a_ref, from_row_b_ref, *refs
):
    odd_y, odd_x = flag_at(flags_ref, 0), flag_at(flags_ref, 1)
    side_a_ref, side_b_ref = refs[-2:]
    columns = []
    for j in (0, row_b_ref.shape[0] - 1):
        column = list(pick(odd_x, from_row_a_ref[j], from_row_b_ref[j]))
        column[1:1] = pick(odd_x, row_a_ref[j], row_b_ref[j])
        columns.append(column)
    for i in range(4):
        side_a_ref[i], side_b_ref[i] = pick(odd_y, columns[0][i], columns[1][i])
    if len(refs) == 3:
        side_a_ref[4] = refs[0][...]


def residual_kernel(
    neighbours_hbm_ref,
    kinds_hbm_ref,
    flags_ref,
    row_a_ref,
    row_b_ref,
    from_row_a_ref,
    from_row_b_ref,
    from_side_a_ref,
    from_side_b_ref,
    from_corner_a_ref,
    from_corner_b_ref,
    rest_a_ref,
    rest_b_ref,
    stiff_ref,
    mass_ref,
    residual_a_ref,
    residual_b_ref,
    partial_ref,
    current_ref,
    ext_ref,
    table_ref,
    neighbours_ref,
    kinds_ref,
    semaphores,
):
    copies = code_copies(
        (neighbours_hbm_ref, kinds_hbm_ref), (neighbours_ref, kinds_ref), semaphores
    )
    for copy in copies:
        copy.start()
    split_tables(stiff_ref, mass_ref, table_ref, 1)
    count_y, both, side = row_a_ref.shape
    wide = count_y + 2
    block = both // 2
    rest = rest_a_ref.shape[1]
    odd_y, odd_x, in_low_y, in_high_y, in_low_x, in_high_x = (
        flag_at(flags_ref, place) for place in range(6)
    )

    def store(i, j, value):
        current_ref[i * wide + j] = value[:block]
        for part in range(2):
            high, low = split(value[part * block : (part + 1) * block])
            ext_ref[i * wide + j, :block, part * side : (part + 1) * side] = high
            ext_ref[i * wide + j, block:, part * side : (part + 1) * side] = low

    own = {}
    for j in range(count_y):
        own[0, j], own[1, j] = pick(odd_x, row_a_ref[j], row_b_ref[j])
        store(1, j + 1, own[0, j])
        store(2, j + 1, own[1, j])
        low, high = pick(odd_x, from_row_a_ref[j], from_row_b_ref[j])
        store(0, j + 1, low * in_low_x)
        store(3, j + 1, high * in_high_x)
    for i in range(2):
        low, high = pick(odd_y, from_side_a_ref[i], from_side_b_ref[i])
        store(i + 1, 0, low * in_low_y)
        store(i + 1, wide - 1, high * in_high_y)
    for place, j, inside in ((0, 0, in_low_y), (1, wide - 1, in_high_y)):
        low, high = pick(odd_x, from_corner_a_ref[place], from_corner_b_ref[place])
        store(0, j, low * (in_low_x * inside))
        store(3, j, high * (in_high_x * inside))
    for copy in copies:
        copy.wait()
    partial = jnp.zeros((block, rest + block), F32)
    totals = {}
    for tile in range(2 * count_y):
        i, j = tile // count_y, tile % count_y
        total = 4.0 * own[i, j][:block] + own[i, j][block:]
        for k in range(neighbours_ref.shape[1]):
            source, kind = source_and_kind(neighbours_ref, kinds_ref, tile, k, count_y)
            pair = mul(ext_ref[source], table_ref[kind])
            total = total + (pair[:block, :side] + (pair[block:, :side] + pair[:block, side:]))
        totals[i, j] = total
        rest_tile = pick(odd_x, rest_a_ref[j], rest_b_ref[j])[i]
        basis_tile = jnp.concatenate([rest_tile, own[i, j][:block]], axis=0)
        partial = partial + pair_sum(stacked(total), *split(basis_tile))
    for j in range(count_y):
        residual_a_ref[j], residual_b_ref[j] = pick(odd_x, totals[0, j], totals[1, j])
    residual_a_ref[count_y] = partial
    partial_ref[...] = partial


def prepare_kernel(
    flags_ref,
    rest_a_ref,
    rest_b_ref,
    from_rest_a_ref,
    from_rest_b_ref,
    current_ref,
    stiff_ref,
    mass_ref,
    basis_ref,
    table_ref,
):
    count_y, rest, _ = rest_a_ref.shape
    prior = rest + current_ref.shape[1]
    odd_x = flag_at(flags_ref, 1)
    split_tables(stiff_ref, mass_ref, table_ref, 0)
    for j in range(count_y):
        rests = list(pick(odd_x, from_rest_a_ref[j], from_rest_b_ref[j]))
        rests[1:1] = pick(odd_x, rest_a_ref[j], rest_b_ref[j])
        for i in range(4):
            tile = jnp.concatenate([rests[i], current_ref[i * (count_y + 2) + j + 1]], axis=0)
            basis_ref[i * count_y + j, :prior, :], basis_ref[i * count_y + j, prior:, :] = split(
                tile
            )


def operators_kernel(
    inverse_rows,
    neighbours_hbm_ref,
    kinds_hbm_ref,
    flags_ref,
    partial_ref,
    row_a_ref,
    row_b_ref,
    from_row_a_ref,
    from_row_b_ref,
    from_side_a_ref,
    from_side_b_ref,
    rest_side_a_ref,
    rest_side_b_ref,
    current_ref,
    basis_ref,
    table_ref,
    weighted_low_ref,
    weighted_high_ref,
    coupling_ref,
    sent_ref,
    kept_ref,
    ext_ref,
    neighbours_ref,
    kinds_ref,
    semaphores,
):
    copies = code_copies(
        (neighbours_hbm_ref, kinds_hbm_ref), (neighbours_ref, kinds_ref), semaphores
    )
    for copy in copies:
        copy.start()
    count_y, block, side = weighted_low_ref.shape
    wide = count_y + 2
    rest = rest_side_a_ref.shape[1]
    prior = rest + block
    odd_y, odd_x, in_low_y, in_high_y, in_low_x, in_high_x = (
        flag_at(flags_ref, place) for place in range(6)
    )
    coupling = partial_ref[...] * inverse_rows
    coupling_ref[...] = coupling
    coupling_deep = deep(coupling)

    def basis_parts(i, j):
        if 0 < j < wide - 1:
            return basis_ref[i * count_y + j - 1]
        rest_tile = pick(odd_y, rest_side_a_ref[i], rest_side_b_ref[i])[j // (wide - 1)]
        return stacked(jnp.concatenate([rest_tile, current_ref[i * wide + j]], axis=0))

    for j in range(wide):
        if 0 < j < wide - 1:
            rows = list(pick(odd_x, from_row_a_ref[j - 1], from_row_b_ref[j - 1]))
            rows[1:1] = pick(odd_x, row_a_ref[j - 1], row_b_ref[j - 1])
        else:
            rows = [
                pick(odd_y, from_side_a_ref[i], from_side_b_ref[i])[j // (wide - 1)]
                for i in range(4)
            ]
        for i in range(4):
            value = rows[i] - halves_sum(mul(coupling_deep, basis_parts(i, j)))
            if i == 0:
                value = value * in_low_x
            if i == 3:
                value = value * in_high_x
            if j == 0:
                value = value * in_low_y
            if j == wide - 1:
                value = value * in_high_y
            if 0 < i < 3 and 0 < j < wide - 1:
                (weighted_low_ref, weighted_high_ref)[i - 1][j - 1] = value
            ext_ref[i * wide + j] = deep(value)
    for copy in copies:
        copy.wait()
    with_basis = jnp.zeros((2 * block, prior), F32)
    with_own = jnp.zeros((block, 4 * block), F32)
    for tile in range(2 * count_y):
        i, j = tile // count_y, tile % count_y
        own = (weighted_low_ref, weighted_high_ref)[i][j]
        totals = jnp.concatenate([4.0 * own, own], axis=1)
        for k in range(neighbours_ref.shape[1]):
            source, kind = source_and_kind(neighbours_ref, kinds_ref, tile, k, count_y)
            totals = totals + halves_sum(mul(ext_ref[source], table_ref[kind]))
        applied = jnp.concatenate([totals[:, :side], totals[:, side:]], axis=0)
        basis_tile = basis_parts(i + 1, j + 1)
        with_basis = with_basis + pair_sum(
            stacked(applied), basis_tile[:prior], basis_tile[prior:]
        )
        right = jnp.concatenate([applied, own, jnp.zeros_like(own)], axis=0)
        with_own = with_own + pair_sum(stacked(own), *split(right))
    halves = [
        jnp.concatenate(
            [
                with_basis[part * block : (part + 1) * block],
                folded(with_own[:, part * block : (part + 1) * block]),
                folded(with_own[:, 2 * block : 3 * block]),
            ],
            axis=0,
        )
        for part in range(2)
    ]
    sent_ref[...], kept_ref[...] = pick(odd_y, halves[0], halves[1])


def folded(square):
    return jnp.concatenate([square[n * 8 : (n + 1) * 8] for n in range(4)], axis=1)


def unfolded(rows):
    return jnp.concatenate([rows[:, n * 32 : (n + 1) * 32] for n in range(4)], axis=0)


def factor_kernel(inverse_rows, sums_ref, work_ref):
    block = work_ref.shape[0]
    gram = unfolded(sums_ref[block + 8 :, :]) * inverse_rows
    row_ids = lax.broadcasted_iota(jnp.int32, (block, block), 0)
    column_ids = lax.broadcasted_iota(jnp.int32, (block, block), 1)
    unit = jnp.where(row_ids == column_ids, 1.0, 0.0).astype(F32)
    work = jnp.concatenate([gram, unit], axis=1)
    rows = lax.broadcasted_iota(jnp.int32, work.shape, 0)
    group = 4
    for j in range(0, block, group):
        columns = [
            jnp.broadcast_to(work[:, j + a : j + a + 1], work.shape) for a in range(group)
        ]
        pivots = [work[j + a : j + a + 1, :] for a in range(group)]
        for a in range(group):
            at = j + a
            ratio = columns[a] * (1.0 / columns[a][at : at + 1, :])
            for b in range(a + 1, group):
                columns[b] = columns[b] - ratio * columns[b][at : at + 1, :]
                pivots[b] = pivots[b] - ratio[j + b : j + b + 1, :] * pivots[a]
            work = work - jnp.where(rows > at, ratio, 0.0) * pivots[a]
    work = work * lax.rsqrt(jnp.sum(work[:, :block] * unit, axis=1, keepdims=True))
    work_ref[...] = work


def finish_kernel(
    inverse_rows,
    flags_ref,
    work_ref,
    sums_ref,
    other_ref,
    weighted_low_ref,
    weighted_high_ref,
    new_ref,
    factor_ref,
    reduced_ref,
):
    count_y, block, _ = weighted_low_ref.shape
    prior = sums_ref.shape[1]
    tiles = 2 * count_y
    row_ids = lax.broadcasted_iota(jnp.int32, (block, block), 0)
    column_ids = lax.broadcasted_iota(jnp.int32, (block, block), 1)
    factor_ref[...] = jnp.where(column_ids >= row_ids, work_ref[:, :block], 0.0)
    inverse = work_ref[:, block:]
    for tile in range(tiles):
        own = (weighted_low_ref, weighted_high_ref)[tile // count_y][tile % count_y]
        new_ref[pl.ds(tile, block, stride=tiles), :] = mul3(inverse, own)
    odd_y = flag_at(flags_ref, 0)
    halves = pick(odd_y, other_ref[...], sums_ref[: block + 8, :])
    for part, half in enumerate(halves):
        reduced_ref[part, :, :prior] = mul3(inverse, half[:block] * inverse_rows)
        own = unfolded(half[block:]) * inverse_rows
        reduced_ref[part, :, prior:] = mul3_t(mul3_t(inverse, own), inverse)


def swap(value, mask):
    axes = ("px", "py")
    pairs = [(i, i ^ mask) for i in range(lax.axis_size(axes))]
    return lax.ppermute(value, axes, pairs)


def exchange(message_a, message_b, axis):
    count = lax.axis_size(axis)
    pairs = [(i, ((i + 1) ^ 1) - 1) for i in range(count)]
    pairs = [(i, j if 0 <= j < count else i) for i, j in pairs]
    near = [(i, i ^ 1) for i in range(count)]
    return lax.ppermute(message_a, axis, near), lax.ppermute(message_b, axis, pairs)


def total_over(value, first, last):
    while first < last:
        value = value + swap(value, first)
        first *= 2
    return value


def half_total(sent, kept):
    kept = kept + swap(sent, 1)
    kept = (kept + swap(kept, 6)) + (swap(kept, 2) + swap(kept, 4))
    return total_over(kept, 8, lax.axis_size(("px", "py")))


def shape(*dims, dtype=F32):
    return jax.ShapeDtypeStruct(dims, dtype)


def shards(prior_basis, previous, neighbours, tile_kinds, stiff_tiles, mass_tiles):
    block = previous.shape[0]
    prior, count_x, count_y, side = prior_basis.shape
    tiles = count_x * count_y
    wide = count_y + 2
    rest = prior - block
    kinds = stiff_tiles.shape[0]
    inverse_rows = 1.0 / (tiles * side * lax.axis_size("px") * lax.axis_size("py"))
    basis = prior_basis.reshape(-1, side)
    vectors = jnp.concatenate([basis, previous.reshape(-1, side)], axis=0)
    codes = [array.transpose(1, 2, 0).reshape(tiles, -1) for array in (neighbours, tile_kinds)]
    code_scratch = [pltpu.SMEM(array.shape, jnp.int32) for array in codes]
    code_scratch += [pltpu.SemaphoreType.DMA((2,))]
    at_y, at_x = lax.axis_index("py"), lax.axis_index("px")
    bits = (at_y & 1) + 2 * (at_x & 1)
    bits += 4 * (at_y > 0) + 8 * (at_y < lax.axis_size("py") - 1)
    bits += 16 * (at_x > 0) + 32 * (at_x < lax.axis_size("px") - 1)
    flags = ((bits >> lax.broadcasted_iota(jnp.int32, (8, side), 0)) & 1).astype(F32)

    def call(kernel, inputs, outputs, scratch=(), plain=0, limit=8, cost=None):
        specs = [ANY] * plain + [VMEM] * (len(inputs) - plain)
        return pl.pallas_call(
            kernel,
            out_shape=outputs,
            in_specs=specs,
            out_specs=[VMEM] * len(outputs),
            scratch_shapes=scratch,
            compiler_params=pltpu.CompilerParams(vmem_limit_bytes=limit * MIB),
            cost_estimate=cost,
        )(*inputs)

    side_a, side_b, row_a, row_b = call(
        pack_kernel,
        (flags, vectors),
        [shape(count_x, 2 * block, side)] * 2 + [shape(count_y, 2 * block, side)] * 2,
    )
    rest_a, rest_b = call(rest_kernel, (flags, vectors), [shape(count_y, rest, side)] * 2)
    from_side_a, from_side_b = exchange(side_a, side_b, "py")
    from_row_a, from_row_b = exchange(row_a, row_b, "px")
    from_side_a, rest_a, rest_b = lax.optimization_barrier((from_side_a, rest_a, rest_b))
    from_rest_a, from_rest_b = exchange(rest_a, rest_b, "px")
    corner_a, corner_b = call(
        corners_kernel,
        (flags, from_side_a, from_side_b),
        [shape(2, 2 * block, side)] * 2,
    )
    from_corner_a, from_corner_b = exchange(corner_a, corner_b, "px")
    rest_side_a, rest_side_b = call(
        columns_kernel,
        (flags, rest_a, rest_b, from_rest_a, from_rest_b),
        [shape(4, rest, side)] * 2,
    )
    rest_side_a, rest_side_b = exchange(rest_side_a, rest_side_b, "py")
    residual_a, residual_b, partial, current = call(
        residual_kernel,
        (
            *codes,
            flags,
            row_a,
            row_b,
            from_row_a,
            from_row_b,
            from_side_a,
            from_side_b,
            from_corner_a,
            from_corner_b,
            rest_a,
            rest_b,
            stiff_tiles,
            mass_tiles,
        ),
        [shape(count_y + 1, block, side), shape(count_y, block, side)]
        + [shape(block, prior), shape(4 * wide, block, side)],
        [pltpu.VMEM((4 * wide, 2 * block, 2 * side), BF16)]
        + [pltpu.VMEM((kinds, 2 * side, 2 * side), BF16)]
        + code_scratch,
        plain=2,
        cost=pl.CostEstimate(flops=10**9, bytes_accessed=0, transcendentals=0),
    )
    count_py = lax.axis_size("py")
    from_row_a, from_row_b = exchange(residual_a, residual_b, "px")
    partial = total_over(
        partial + from_row_a[-1], 2 * count_py, count_py * lax.axis_size("px")
    )
    partial, rest_side_a, rest_side_b = lax.optimization_barrier(
        (partial, rest_side_a, rest_side_b)
    )
    side_a, side_b = call(
        columns_kernel,
        (flags, residual_a, residual_b, from_row_a, from_row_b, partial),
        [shape(5, block, side), shape(4, block, side)],
    )
    from_side_a, from_side_b = exchange(side_a, side_b, "py")
    partial = total_over(partial + from_side_a[-1], 2, count_py)
    basis_parts, table = call(
        prepare_kernel,
        (flags, rest_a, rest_b, from_rest_a, from_rest_b, current, stiff_tiles, mass_tiles),
        [shape(4 * count_y, 2 * prior, side, dtype=BF16)]
        + [shape(kinds, 2 * side, 2 * side, dtype=BF16)],
        cost=pl.CostEstimate(flops=10**9, bytes_accessed=0, transcendentals=0),
    )
    weighted_low, weighted_high, coupling, sent, kept = call(
        functools.partial(operators_kernel, inverse_rows),
        (
            *codes,
            flags,
            partial,
            residual_a,
            residual_b,
            from_row_a,
            from_row_b,
            from_side_a,
            from_side_b,
            rest_side_a,
            rest_side_b,
            current,
            basis_parts,
            table,
        ),
        [shape(count_y, block, side)] * 2
        + [shape(block, prior)]
        + [shape(block + 16, prior)] * 2,
        [pltpu.VMEM((4 * wide, 2 * block, 2 * side), BF16)] + code_scratch,
        plain=2,
    )
    kept = half_total(sent, kept)
    other = swap(kept[: block + 8], 1)
    (work,) = call(
        functools.partial(factor_kernel, inverse_rows),
        (kept,),
        [shape(block, 2 * block)],
        cost=pl.CostEstimate(flops=10**9, bytes_accessed=0, transcendentals=0),
    )
    new_block, factor, reduced = call(
        functools.partial(finish_kernel, inverse_rows),
        (flags, work, kept, other, weighted_low, weighted_high),
        [
            shape(block * tiles, side),
            shape(block, block),
            shape(2, block, prior + block),
        ],
    )
    return (
        new_block.reshape(previous.shape),
        coupling.T,
        factor,
        reduced.swapaxes(1, 2),
    )


def solution(mesh):
    placed = (
        P("case", "px", "py", None),
        P("case", "px", "py", None),
        P(None, "px", "py"),
        P(None, "px", "py"),
        P(),
        P(),
    )
    return jax.shard_map(
        shards,
        mesh=mesh,
        in_specs=placed,
        out_specs=(
            P("case", "px", "py", None),
            P("case", None),
            P("case", None),
            P("case", None, None),
        ),
        check_vma=False,
    )
```

```python
import functools

import jax
import jax.numpy as jnp
from jax import lax
from jax.experimental import pallas as pl
from jax.experimental.pallas import tpu as pltpu
from jax.sharding import PartitionSpec as P

F32 = jnp.float32
BF16 = jnp.bfloat16
VMEM = pl.BlockSpec(memory_space=pltpu.VMEM)
ANY = pl.BlockSpec(memory_space=pl.ANY)
MIB = 1024 * 1024


def split(value):
    high = value.astype(BF16)
    return high, (value - high.astype(F32)).astype(BF16)


def mul(left, right):
    return jnp.dot(left, right, preferred_element_type=F32)


def mul_t(left, right):
    return lax.dot_general(left, right, (((1,), (1,)), ((), ())), preferred_element_type=F32)


def mul3(left, right):
    left_high, left_low = split(left)
    right_high, right_low = split(right)
    return mul(left_high, right_high) + (mul(left_high, right_low) + mul(left_low, right_high))


def mul3_t(left, right):
    left_high, left_low = split(left)
    right_high, right_low = split(right)
    return mul_t(left_high, right_high) + (
        mul_t(left_high, right_low) + mul_t(left_low, right_high)
    )


def split_tables(stiff_ref, mass_ref, table_ref, parts_axis):
    side = stiff_ref.shape[1]
    spans = (slice(0, side), slice(side, 2 * side))
    for kind in range(stiff_ref.shape[0]):
        for matrix, ref in zip(spans, (stiff_ref, mass_ref)):
            for part, value in zip(spans, split(ref[kind])):
                if parts_axis == 1:
                    table_ref[kind, matrix, part] = value
                else:
                    table_ref[kind, part, matrix] = value


def stacked(value):
    return jnp.concatenate(split(value), axis=0)


def deep(value):
    high, low = split(value)
    upper = jnp.concatenate([high, high], axis=1)
    return jnp.concatenate([upper, jnp.concatenate([low, jnp.zeros_like(low)], axis=1)], axis=0)


def halves_sum(value):
    half = value.shape[0] // 2
    return value[:half] + value[half:]


def pair_sum(left, right_high, right_low):
    rows = left.shape[0] // 2
    return halves_sum(mul_t(left, right_high)) + mul_t(left[:rows], right_low)


def pick(flag, first, second):
    flag = flag > 0.0
    return jnp.where(flag, first, second), jnp.where(flag, second, first)


def flag_at(flags_ref, place):
    return flags_ref[place : place + 1, :]


def code_copies(code_refs, local_refs, semaphores):
    return [
        pltpu.make_async_copy(ref, local, semaphores.at[n])
        for n, (ref, local) in enumerate(zip(code_refs, local_refs))
    ]


def source_and_kind(neighbours_ref, kinds_ref, tile, k, count_y):
    neighbour = neighbours_ref[tile, k]
    down = (neighbour * 11) >> 5
    first = (tile // count_y) * (count_y + 2) + tile % count_y
    return first + neighbour + down * (count_y - 1), kinds_ref[tile, k]


def pack_kernel(flags_ref, vectors_ref, side_a_ref, side_b_ref, row_a_ref, row_b_ref):
    count_y, both, _ = row_a_ref.shape
    tiles = 2 * count_y
    odd_y, odd_x = flag_at(flags_ref, 0), flag_at(flags_ref, 1)

    first = vectors_ref.shape[0] - both * tiles

    def tile_of(i, j):
        return vectors_ref[pl.ds(first + i * count_y + j, both, stride=tiles), :]

    for i in range(2):
        side_a_ref[i], side_b_ref[i] = pick(odd_y, tile_of(i, 0), tile_of(i, count_y - 1))
    for j in range(count_y):
        row_a_ref[j], row_b_ref[j] = pick(odd_x, tile_of(0, j), tile_of(1, j))


def rest_kernel(flags_ref, vectors_ref, rest_a_ref, rest_b_ref):
    count_y, rest, _ = rest_a_ref.shape
    odd_x = flag_at(flags_ref, 1)
    for j in range(count_y):
        rest_a_ref[j], rest_b_ref[j] = pick(
            odd_x,
            vectors_ref[pl.ds(j, rest, stride=2 * count_y), :],
            vectors_ref[pl.ds(count_y + j, rest, stride=2 * count_y), :],
        )


def corners_kernel(flags_ref, side_a_ref, side_b_ref, corner_a_ref, corner_b_ref):
    odd_y, odd_x = flag_at(flags_ref, 0), flag_at(flags_ref, 1)
    ends = [pick(odd_y, side_a_ref[i], side_b_ref[i]) for i in range(2)]
    for place in range(2):
        corner_a_ref[place], corner_b_ref[place] = pick(odd_x, ends[0][place], ends[1][place])


def columns_kernel(
    flags_ref, row_a_ref, row_b_ref, from_row_a_ref, from_row_b_ref, *refs
):
    odd_y, odd_x = flag_at(flags_ref, 0), flag_at(flags_ref, 1)
    side_a_ref, side_b_ref = refs[-2:]
    columns = []
    for j in (0, row_b_ref.shape[0] - 1):
        column = list(pick(odd_x, from_row_a_ref[j], from_row_b_ref[j]))
        column[1:1] = pick(odd_x, row_a_ref[j], row_b_ref[j])
        columns.append(column)
    for i in range(4):
        side_a_ref[i], side_b_ref[i] = pick(odd_y, columns[0][i], columns[1][i])
    if len(refs) == 3:
        side_a_ref[4] = refs[0][...]


def residual_kernel(
    neighbours_hbm_ref,
    kinds_hbm_ref,
    flags_ref,
    row_a_ref,
    row_b_ref,
    from_row_a_ref,
    from_row_b_ref,
    from_side_a_ref,
    from_side_b_ref,
    from_corner_a_ref,
    from_corner_b_ref,
    rest_a_ref,
    rest_b_ref,
    stiff_ref,
    mass_ref,
    residual_a_ref,
    residual_b_ref,
    partial_ref,
    current_ref,
    ext_ref,
    table_ref,
    neighbours_ref,
    kinds_ref,
    semaphores,
):
    copies = code_copies(
        (neighbours_hbm_ref, kinds_hbm_ref), (neighbours_ref, kinds_ref), semaphores
    )
    for copy in copies:
        copy.start()
    split_tables(stiff_ref, mass_ref, table_ref, 1)
    count_y, both, side = row_a_ref.shape
    wide = count_y + 2
    block = both // 2
    rest = rest_a_ref.shape[1]
    odd_y, odd_x, in_low_y, in_high_y, in_low_x, in_high_x = (
        flag_at(flags_ref, place) for place in range(6)
    )

    def store(i, j, value):
        current_ref[i * wide + j] = value[:block]
        for part in range(2):
            high, low = split(value[part * block : (part + 1) * block])
            ext_ref[i * wide + j, :block, part * side : (part + 1) * side] = high
            ext_ref[i * wide + j, block:, part * side : (part + 1) * side] = low

    own = {}
    for j in range(count_y):
        own[0, j], own[1, j] = pick(odd_x, row_a_ref[j], row_b_ref[j])
        store(1, j + 1, own[0, j])
        store(2, j + 1, own[1, j])
        low, high = pick(odd_x, from_row_a_ref[j], from_row_b_ref[j])
        store(0, j + 1, low * in_low_x)
        store(3, j + 1, high * in_high_x)
    for i in range(2):
        low, high = pick(odd_y, from_side_a_ref[i], from_side_b_ref[i])
        store(i + 1, 0, low * in_low_y)
        store(i + 1, wide - 1, high * in_high_y)
    for place, j, inside in ((0, 0, in_low_y), (1, wide - 1, in_high_y)):
        low, high = pick(odd_x, from_corner_a_ref[place], from_corner_b_ref[place])
        store(0, j, low * (in_low_x * inside))
        store(3, j, high * (in_high_x * inside))
    for copy in copies:
        copy.wait()
    partial = jnp.zeros((block, rest + block), F32)
    totals = {}
    for tile in range(2 * count_y):
        i, j = tile // count_y, tile % count_y
        total = 4.0 * own[i, j][:block] + own[i, j][block:]
        for k in range(neighbours_ref.shape[1]):
            source, kind = source_and_kind(neighbours_ref, kinds_ref, tile, k, count_y)
            pair = mul(ext_ref[source], table_ref[kind])
            total = total + (pair[:block, :side] + (pair[block:, :side] + pair[:block, side:]))
        totals[i, j] = total
        rest_tile = pick(odd_x, rest_a_ref[j], rest_b_ref[j])[i]
        basis_tile = jnp.concatenate([rest_tile, own[i, j][:block]], axis=0)
        partial = partial + pair_sum(stacked(total), *split(basis_tile))
    for j in range(count_y):
        residual_a_ref[j], residual_b_ref[j] = pick(odd_x, totals[0, j], totals[1, j])
    residual_a_ref[count_y] = partial
    partial_ref[...] = partial


def prepare_kernel(
    flags_ref,
    rest_a_ref,
    rest_b_ref,
    from_rest_a_ref,
    from_rest_b_ref,
    current_ref,
    stiff_ref,
    mass_ref,
    basis_ref,
    table_ref,
):
    count_y, rest, _ = rest_a_ref.shape
    prior = rest + current_ref.shape[1]
    odd_x = flag_at(flags_ref, 1)
    split_tables(stiff_ref, mass_ref, table_ref, 0)
    for j in range(count_y):
        rests = list(pick(odd_x, from_rest_a_ref[j], from_rest_b_ref[j]))
        rests[1:1] = pick(odd_x, rest_a_ref[j], rest_b_ref[j])
        for i in range(4):
            tile = jnp.concatenate([rests[i], current_ref[i * (count_y + 2) + j + 1]], axis=0)
            basis_ref[i * count_y + j, :prior, :], basis_ref[i * count_y + j, prior:, :] = split(
                tile
            )


def operators_kernel(
    inverse_rows,
    neighbours_hbm_ref,
    kinds_hbm_ref,
    flags_ref,
    partial_ref,
    row_a_ref,
    row_b_ref,
    from_row_a_ref,
    from_row_b_ref,
    from_side_a_ref,
    from_side_b_ref,
    rest_side_a_ref,
    rest_side_b_ref,
    current_ref,
    basis_ref,
    table_ref,
    weighted_low_ref,
    weighted_high_ref,
    coupling_ref,
    sent_ref,
    kept_ref,
    ext_ref,
    neighbours_ref,
    kinds_ref,
    semaphores,
):
    copies = code_copies(
        (neighbours_hbm_ref, kinds_hbm_ref), (neighbours_ref, kinds_ref), semaphores
    )
    for copy in copies:
        copy.start()
    count_y, block, side = weighted_low_ref.shape
    wide = count_y + 2
    rest = rest_side_a_ref.shape[1]
    prior = rest + block
    odd_y, odd_x, in_low_y, in_high_y, in_low_x, in_high_x = (
        flag_at(flags_ref, place) for place in range(6)
    )
    coupling = partial_ref[...] * inverse_rows
    coupling_ref[...] = coupling
    coupling_deep = deep(coupling)

    def basis_parts(i, j):
        if 0 < j < wide - 1:
            return basis_ref[i * count_y + j - 1]
        rest_tile = pick(odd_y, rest_side_a_ref[i], rest_side_b_ref[i])[j // (wide - 1)]
        return stacked(jnp.concatenate([rest_tile, current_ref[i * wide + j]], axis=0))

    for j in range(wide):
        if 0 < j < wide - 1:
            rows = list(pick(odd_x, from_row_a_ref[j - 1], from_row_b_ref[j - 1]))
            rows[1:1] = pick(odd_x, row_a_ref[j - 1], row_b_ref[j - 1])
        else:
            rows = [
                pick(odd_y, from_side_a_ref[i], from_side_b_ref[i])[j // (wide - 1)]
                for i in range(4)
            ]
        for i in range(4):
            value = rows[i] - halves_sum(mul(coupling_deep, basis_parts(i, j)))
            if i == 0:
                value = value * in_low_x
            if i == 3:
                value = value * in_high_x
            if j == 0:
                value = value * in_low_y
            if j == wide - 1:
                value = value * in_high_y
            if 0 < i < 3 and 0 < j < wide - 1:
                (weighted_low_ref, weighted_high_ref)[i - 1][j - 1] = value
            ext_ref[i * wide + j] = deep(value)
    for copy in copies:
        copy.wait()
    with_basis = jnp.zeros((2 * block, prior), F32)
    with_own = jnp.zeros((block, 4 * block), F32)
    for tile in range(2 * count_y):
        i, j = tile // count_y, tile % count_y
        own = (weighted_low_ref, weighted_high_ref)[i][j]
        totals = jnp.concatenate([4.0 * own, own], axis=1)
        for k in range(neighbours_ref.shape[1]):
            source, kind = source_and_kind(neighbours_ref, kinds_ref, tile, k, count_y)
            totals = totals + halves_sum(mul(ext_ref[source], table_ref[kind]))
        applied = jnp.concatenate([totals[:, :side], totals[:, side:]], axis=0)
        basis_tile = basis_parts(i + 1, j + 1)
        with_basis = with_basis + pair_sum(
            stacked(applied), basis_tile[:prior], basis_tile[prior:]
        )
        right = jnp.concatenate([applied, own, jnp.zeros_like(own)], axis=0)
        with_own = with_own + pair_sum(stacked(own), *split(right))
    halves = [
        jnp.concatenate(
            [
                with_basis[part * block : (part + 1) * block],
                folded(with_own[:, part * block : (part + 1) * block]),
                folded(with_own[:, 2 * block : 3 * block]),
            ],
            axis=0,
        )
        for part in range(2)
    ]
    sent_ref[...], kept_ref[...] = pick(odd_y, halves[0], halves[1])


def folded(square):
    return jnp.concatenate([square[n * 8 : (n + 1) * 8] for n in range(4)], axis=1)


def unfolded(rows):
    return jnp.concatenate([rows[:, n * 32 : (n + 1) * 32] for n in range(4)], axis=0)


def factor_kernel(inverse_rows, sums_ref, work_ref):
    block = work_ref.shape[0]
    gram = unfolded(sums_ref[block + 8 :, :]) * inverse_rows
    row_ids = lax.broadcasted_iota(jnp.int32, (block, block), 0)
    column_ids = lax.broadcasted_iota(jnp.int32, (block, block), 1)
    unit = jnp.where(row_ids == column_ids, 1.0, 0.0).astype(F32)
    work = jnp.concatenate([gram, unit], axis=1)
    rows = lax.broadcasted_iota(jnp.int32, work.shape, 0)
    group = 4
    for j in range(0, block, group):
        columns = [
            jnp.broadcast_to(work[:, j + a : j + a + 1], work.shape) for a in range(group)
        ]
        pivots = [work[j + a : j + a + 1, :] for a in range(group)]
        for a in range(group):
            at = j + a
            ratio = columns[a] * (1.0 / columns[a][at : at + 1, :])
            for b in range(a + 1, group):
                columns[b] = columns[b] - ratio * columns[b][at : at + 1, :]
                pivots[b] = pivots[b] - ratio[j + b : j + b + 1, :] * pivots[a]
            work = work - jnp.where(rows > at, ratio, 0.0) * pivots[a]
    work = work * lax.rsqrt(jnp.sum(work[:, :block] * unit, axis=1, keepdims=True))
    work_ref[...] = work


def finish_kernel(
    inverse_rows,
    flags_ref,
    work_ref,
    sums_ref,
    other_ref,
    weighted_low_ref,
    weighted_high_ref,
    new_ref,
    factor_ref,
    reduced_ref,
):
    count_y, block, _ = weighted_low_ref.shape
    prior = sums_ref.shape[1]
    tiles = 2 * count_y
    row_ids = lax.broadcasted_iota(jnp.int32, (block, block), 0)
    column_ids = lax.broadcasted_iota(jnp.int32, (block, block), 1)
    factor_ref[...] = jnp.where(column_ids >= row_ids, work_ref[:, :block], 0.0)
    inverse = work_ref[:, block:]
    for tile in range(tiles):
        own = (weighted_low_ref, weighted_high_ref)[tile // count_y][tile % count_y]
        new_ref[pl.ds(tile, block, stride=tiles), :] = mul3(inverse, own)
    odd_y = flag_at(flags_ref, 0)
    halves = pick(odd_y, other_ref[...], sums_ref[: block + 8, :])
    for part, half in enumerate(halves):
        reduced_ref[part, :, :prior] = mul3(inverse, half[:block] * inverse_rows)
        own = unfolded(half[block:]) * inverse_rows
        reduced_ref[part, :, prior:] = mul3_t(mul3_t(inverse, own), inverse)


def swap(value, mask):
    axes = ("px", "py")
    pairs = [(i, i ^ mask) for i in range(lax.axis_size(axes))]
    return lax.ppermute(value, axes, pairs)


def exchange(message_a, message_b, axis):
    count = lax.axis_size(axis)
    pairs = [(i, ((i + 1) ^ 1) - 1) for i in range(count)]
    pairs = [(i, j if 0 <= j < count else i) for i, j in pairs]
    near = [(i, i ^ 1) for i in range(count)]
    return lax.ppermute(message_a, axis, near), lax.ppermute(message_b, axis, pairs)


def total_over(value, first, last):
    while first < last:
        value = value + swap(value, first)
        first *= 2
    return value


def half_total(sent, kept):
    kept = kept + swap(sent, 1)
    others = [swap(kept, mask) for mask in (2, 4, 6, 8, 10, 12, 14)]
    pairs = [kept + others[0]] + [others[n] + others[n + 1] for n in (1, 3, 5)]
    kept = (pairs[0] + pairs[1]) + (pairs[2] + pairs[3])
    return total_over(kept, 16, lax.axis_size(("px", "py")))


def shape(*dims, dtype=F32):
    return jax.ShapeDtypeStruct(dims, dtype)


def shards(prior_basis, previous, neighbours, tile_kinds, stiff_tiles, mass_tiles):
    block = previous.shape[0]
    prior, count_x, count_y, side = prior_basis.shape
    tiles = count_x * count_y
    wide = count_y + 2
    rest = prior - block
    kinds = stiff_tiles.shape[0]
    inverse_rows = 1.0 / (tiles * side * lax.axis_size("px") * lax.axis_size("py"))
    basis = prior_basis.reshape(-1, side)
    vectors = jnp.concatenate([basis, previous.reshape(-1, side)], axis=0)
    codes = [array.transpose(1, 2, 0).reshape(tiles, -1) for array in (neighbours, tile_kinds)]
    code_scratch = [pltpu.SMEM(array.shape, jnp.int32) for array in codes]
    code_scratch += [pltpu.SemaphoreType.DMA((2,))]
    at_y, at_x = lax.axis_index("py"), lax.axis_index("px")
    bits = (at_y & 1) + 2 * (at_x & 1)
    bits += 4 * (at_y > 0) + 8 * (at_y < lax.axis_size("py") - 1)
    bits += 16 * (at_x > 0) + 32 * (at_x < lax.axis_size("px") - 1)
    flags = ((bits >> lax.broadcasted_iota(jnp.int32, (8, side), 0)) & 1).astype(F32)

    def call(kernel, inputs, outputs, scratch=(), plain=0, limit=8, cost=None):
        specs = [ANY] * plain + [VMEM] * (len(inputs) - plain)
        return pl.pallas_call(
            kernel,
            out_shape=outputs,
            in_specs=specs,
            out_specs=[VMEM] * len(outputs),
            scratch_shapes=scratch,
            compiler_params=pltpu.CompilerParams(vmem_limit_bytes=limit * MIB),
            cost_estimate=cost,
        )(*inputs)

    side_a, side_b, row_a, row_b = call(
        pack_kernel,
        (flags, vectors),
        [shape(count_x, 2 * block, side)] * 2 + [shape(count_y, 2 * block, side)] * 2,
    )
    rest_a, rest_b = call(rest_kernel, (flags, vectors), [shape(count_y, rest, side)] * 2)
    from_side_a, from_side_b = exchange(side_a, side_b, "py")
    from_row_a, from_row_b = exchange(row_a, row_b, "px")
    from_side_a, rest_a, rest_b = lax.optimization_barrier((from_side_a, rest_a, rest_b))
    from_rest_a, from_rest_b = exchange(rest_a, rest_b, "px")
    corner_a, corner_b = call(
        corners_kernel,
        (flags, from_side_a, from_side_b),
        [shape(2, 2 * block, side)] * 2,
    )
    from_corner_a, from_corner_b = exchange(corner_a, corner_b, "px")
    rest_side_a, rest_side_b = call(
        columns_kernel,
        (flags, rest_a, rest_b, from_rest_a, from_rest_b),
        [shape(4, rest, side)] * 2,
    )
    rest_side_a, rest_side_b = exchange(rest_side_a, rest_side_b, "py")
    residual_a, residual_b, partial, current = call(
        residual_kernel,
        (
            *codes,
            flags,
            row_a,
            row_b,
            from_row_a,
            from_row_b,
            from_side_a,
            from_side_b,
            from_corner_a,
            from_corner_b,
            rest_a,
            rest_b,
            stiff_tiles,
            mass_tiles,
        ),
        [shape(count_y + 1, block, side), shape(count_y, block, side)]
        + [shape(block, prior), shape(4 * wide, block, side)],
        [pltpu.VMEM((4 * wide, 2 * block, 2 * side), BF16)]
        + [pltpu.VMEM((kinds, 2 * side, 2 * side), BF16)]
        + code_scratch,
        plain=2,
        cost=pl.CostEstimate(flops=10**9, bytes_accessed=0, transcendentals=0),
    )
    count_py = lax.axis_size("py")
    from_row_a, from_row_b = exchange(residual_a, residual_b, "px")
    if lax.axis_size("px") == 4:
        far, cross = swap(partial, 2 * count_py), swap(partial, 3 * count_py)
        partial = (partial + far) + (from_row_a[-1] + cross)
    else:
        partial = total_over(
            partial + from_row_a[-1], 2 * count_py, count_py * lax.axis_size("px")
        )
    partial, rest_side_a, rest_side_b = lax.optimization_barrier(
        (partial, rest_side_a, rest_side_b)
    )
    side_a, side_b = call(
        columns_kernel,
        (flags, residual_a, residual_b, from_row_a, from_row_b, partial),
        [shape(5, block, side), shape(4, block, side)],
    )
    from_side_a, from_side_b = exchange(side_a, side_b, "py")
    partial = total_over(partial + from_side_a[-1], 2, count_py)
    basis_parts, table = call(
        prepare_kernel,
        (flags, rest_a, rest_b, from_rest_a, from_rest_b, current, stiff_tiles, mass_tiles),
        [shape(4 * count_y, 2 * prior, side, dtype=BF16)]
        + [shape(kinds, 2 * side, 2 * side, dtype=BF16)],
        cost=pl.CostEstimate(flops=10**9, bytes_accessed=0, transcendentals=0),
    )
    weighted_low, weighted_high, coupling, sent, kept = call(
        functools.partial(operators_kernel, inverse_rows),
        (
            *codes,
            flags,
            partial,
            residual_a,
            residual_b,
            from_row_a,
            from_row_b,
            from_side_a,
            from_side_b,
            rest_side_a,
            rest_side_b,
            current,
            basis_parts,
            table,
        ),
        [shape(count_y, block, side)] * 2
        + [shape(block, prior)]
        + [shape(block + 16, prior)] * 2,
        [pltpu.VMEM((4 * wide, 2 * block, 2 * side), BF16)] + code_scratch,
        plain=2,
    )
    kept = half_total(sent, kept)
    other = swap(kept[: block + 8], 1)
    (work,) = call(
        functools.partial(factor_kernel, inverse_rows),
        (kept,),
        [shape(block, 2 * block)],
        cost=pl.CostEstimate(flops=10**9, bytes_accessed=0, transcendentals=0),
    )
    new_block, factor, reduced = call(
        functools.partial(finish_kernel, inverse_rows),
        (flags, work, kept, other, weighted_low, weighted_high),
        [
            shape(block * tiles, side),
            shape(block, block),
            shape(2, block, prior + block),
        ],
    )
    return (
        new_block.reshape(previous.shape),
        coupling.T,
        factor,
        reduced.swapaxes(1, 2),
    )


def solution(mesh):
    placed = (
        P("case", "px", "py", None),
        P("case", "px", "py", None),
        P(None, "px", "py"),
        P(None, "px", "py"),
        P(),
        P(),
    )
    return jax.shard_map(
        shards,
        mesh=mesh,
        in_specs=placed,
        out_specs=(
            P("case", "px", "py", None),
            P("case", None),
            P("case", None),
            P("case", None, None),
        ),
        check_vma=False,
    )
```

```python
import functools

import jax
import jax.numpy as jnp
from jax import lax
from jax.experimental import pallas as pl
from jax.experimental.pallas import tpu as pltpu
from jax.sharding import PartitionSpec as P

F32 = jnp.float32
BF16 = jnp.bfloat16
VMEM = pl.BlockSpec(memory_space=pltpu.VMEM)
ANY = pl.BlockSpec(memory_space=pl.ANY)
MIB = 1024 * 1024


def split(value):
    high = value.astype(BF16)
    return high, (value - high.astype(F32)).astype(BF16)


def mul(left, right):
    return jnp.dot(left, right, preferred_element_type=F32)


def mul_t(left, right):
    return lax.dot_general(left, right, (((1,), (1,)), ((), ())), preferred_element_type=F32)


def mul3(left, right):
    left_high, left_low = split(left)
    right_high, right_low = split(right)
    return mul(left_high, right_high) + (mul(left_high, right_low) + mul(left_low, right_high))


def mul3_t(left, right):
    left_high, left_low = split(left)
    right_high, right_low = split(right)
    return mul_t(left_high, right_high) + (
        mul_t(left_high, right_low) + mul_t(left_low, right_high)
    )


def split_tables(stiff_ref, mass_ref, table_ref, parts_axis):
    side = stiff_ref.shape[1]
    spans = (slice(0, side), slice(side, 2 * side))
    for kind in range(stiff_ref.shape[0]):
        for matrix, ref in zip(spans, (stiff_ref, mass_ref)):
            for part, value in zip(spans, split(ref[kind])):
                if parts_axis == 1:
                    table_ref[kind, matrix, part] = value
                else:
                    table_ref[kind, part, matrix] = value


def stacked(value):
    return jnp.concatenate(split(value), axis=0)


def deep(value):
    high, low = split(value)
    upper = jnp.concatenate([high, high], axis=1)
    return jnp.concatenate([upper, jnp.concatenate([low, jnp.zeros_like(low)], axis=1)], axis=0)


def halves_sum(value):
    half = value.shape[0] // 2
    return value[:half] + value[half:]


def pair_sum(left, right_high, right_low):
    rows = left.shape[0] // 2
    return halves_sum(mul_t(left, right_high)) + mul_t(left[:rows], right_low)


def pick(flag, first, second):
    flag = flag > 0.0
    return jnp.where(flag, first, second), jnp.where(flag, second, first)


def flag_at(flags_ref, place):
    return flags_ref[place : place + 1, :]


def code_copies(code_refs, local_refs, semaphores):
    return [
        pltpu.make_async_copy(ref, local, semaphores.at[n])
        for n, (ref, local) in enumerate(zip(code_refs, local_refs))
    ]


def source_and_kind(neighbours_ref, kinds_ref, tile, k, count_y):
    neighbour = neighbours_ref[tile, k]
    down = (neighbour * 11) >> 5
    first = (tile // count_y) * (count_y + 2) + tile % count_y
    return first + neighbour + down * (count_y - 1), kinds_ref[tile, k]


def pack_kernel(flags_ref, vectors_ref, side_a_ref, side_b_ref, row_a_ref, row_b_ref):
    count_y, both, _ = row_a_ref.shape
    tiles = 2 * count_y
    odd_y, odd_x = flag_at(flags_ref, 0), flag_at(flags_ref, 1)

    first = vectors_ref.shape[0] - both * tiles

    def tile_of(i, j):
        return vectors_ref[pl.ds(first + i * count_y + j, both, stride=tiles), :]

    for i in range(2):
        side_a_ref[i], side_b_ref[i] = pick(odd_y, tile_of(i, 0), tile_of(i, count_y - 1))
    for j in range(count_y):
        row_a_ref[j], row_b_ref[j] = pick(odd_x, tile_of(0, j), tile_of(1, j))


def rest_kernel(flags_ref, vectors_ref, rest_a_ref, rest_b_ref):
    count_y, rest, _ = rest_a_ref.shape
    odd_x = flag_at(flags_ref, 1)
    for j in range(count_y):
        rest_a_ref[j], rest_b_ref[j] = pick(
            odd_x,
            vectors_ref[pl.ds(j, rest, stride=2 * count_y), :],
            vectors_ref[pl.ds(count_y + j, rest, stride=2 * count_y), :],
        )


def corners_kernel(flags_ref, side_a_ref, side_b_ref, corner_a_ref, corner_b_ref):
    odd_y, odd_x = flag_at(flags_ref, 0), flag_at(flags_ref, 1)
    ends = [pick(odd_y, side_a_ref[i], side_b_ref[i]) for i in range(2)]
    for place in range(2):
        corner_a_ref[place], corner_b_ref[place] = pick(odd_x, ends[0][place], ends[1][place])


def columns_kernel(
    flags_ref, row_a_ref, row_b_ref, from_row_a_ref, from_row_b_ref, *refs
):
    odd_y, odd_x = flag_at(flags_ref, 0), flag_at(flags_ref, 1)
    side_a_ref, side_b_ref = refs[-2:]
    columns = []
    for j in (0, row_b_ref.shape[0] - 1):
        column = list(pick(odd_x, from_row_a_ref[j], from_row_b_ref[j]))
        column[1:1] = pick(odd_x, row_a_ref[j], row_b_ref[j])
        columns.append(column)
    for i in range(4):
        side_a_ref[i], side_b_ref[i] = pick(odd_y, columns[0][i], columns[1][i])
    if len(refs) == 3:
        side_a_ref[4] = refs[0][...]


def residual_kernel(
    neighbours_hbm_ref,
    kinds_hbm_ref,
    flags_ref,
    row_a_ref,
    row_b_ref,
    from_row_a_ref,
    from_row_b_ref,
    from_side_a_ref,
    from_side_b_ref,
    from_corner_a_ref,
    from_corner_b_ref,
    rest_a_ref,
    rest_b_ref,
    stiff_ref,
    mass_ref,
    residual_a_ref,
    residual_b_ref,
    partial_ref,
    current_ref,
    ext_ref,
    table_ref,
    neighbours_ref,
    kinds_ref,
    semaphores,
):
    copies = code_copies(
        (neighbours_hbm_ref, kinds_hbm_ref), (neighbours_ref, kinds_ref), semaphores
    )
    for copy in copies:
        copy.start()
    split_tables(stiff_ref, mass_ref, table_ref, 1)
    count_y, both, side = row_a_ref.shape
    wide = count_y + 2
    block = both // 2
    rest = rest_a_ref.shape[1]
    odd_y, odd_x, in_low_y, in_high_y, in_low_x, in_high_x = (
        flag_at(flags_ref, place) for place in range(6)
    )

    def store(i, j, value):
        current_ref[i * wide + j] = value[:block]
        for part in range(2):
            high, low = split(value[part * block : (part + 1) * block])
            ext_ref[i * wide + j, :block, part * side : (part + 1) * side] = high
            ext_ref[i * wide + j, block:, part * side : (part + 1) * side] = low

    own = {}
    for j in range(count_y):
        own[0, j], own[1, j] = pick(odd_x, row_a_ref[j], row_b_ref[j])
        store(1, j + 1, own[0, j])
        store(2, j + 1, own[1, j])
        low, high = pick(odd_x, from_row_a_ref[j], from_row_b_ref[j])
        store(0, j + 1, low * in_low_x)
        store(3, j + 1, high * in_high_x)
    for i in range(2):
        low, high = pick(odd_y, from_side_a_ref[i], from_side_b_ref[i])
        store(i + 1, 0, low * in_low_y)
        store(i + 1, wide - 1, high * in_high_y)
    for place, j, inside in ((0, 0, in_low_y), (1, wide - 1, in_high_y)):
        low, high = pick(odd_x, from_corner_a_ref[place], from_corner_b_ref[place])
        store(0, j, low * (in_low_x * inside))
        store(3, j, high * (in_high_x * inside))
    for copy in copies:
        copy.wait()
    partial = jnp.zeros((block, rest + block), F32)
    totals = {}
    for tile in range(2 * count_y):
        i, j = tile // count_y, tile % count_y
        total = 4.0 * own[i, j][:block] + own[i, j][block:]
        for k in range(neighbours_ref.shape[1]):
            source, kind = source_and_kind(neighbours_ref, kinds_ref, tile, k, count_y)
            pair = mul(ext_ref[source], table_ref[kind])
            total = total + (pair[:block, :side] + (pair[block:, :side] + pair[:block, side:]))
        totals[i, j] = total
        rest_tile = pick(odd_x, rest_a_ref[j], rest_b_ref[j])[i]
        basis_tile = jnp.concatenate([rest_tile, own[i, j][:block]], axis=0)
        partial = partial + pair_sum(stacked(total), *split(basis_tile))
    for j in range(count_y):
        residual_a_ref[j], residual_b_ref[j] = pick(odd_x, totals[0, j], totals[1, j])
    residual_a_ref[count_y] = partial
    partial_ref[...] = partial


def prepare_kernel(
    flags_ref,
    rest_a_ref,
    rest_b_ref,
    from_rest_a_ref,
    from_rest_b_ref,
    current_ref,
    stiff_ref,
    mass_ref,
    basis_ref,
    table_ref,
):
    count_y, rest, _ = rest_a_ref.shape
    prior = rest + current_ref.shape[1]
    odd_x = flag_at(flags_ref, 1)
    split_tables(stiff_ref, mass_ref, table_ref, 0)
    for j in range(count_y):
        rests = list(pick(odd_x, from_rest_a_ref[j], from_rest_b_ref[j]))
        rests[1:1] = pick(odd_x, rest_a_ref[j], rest_b_ref[j])
        for i in range(4):
            tile = jnp.concatenate([rests[i], current_ref[i * (count_y + 2) + j + 1]], axis=0)
            basis_ref[i * count_y + j, :prior, :], basis_ref[i * count_y + j, prior:, :] = split(
                tile
            )


def operators_kernel(
    inverse_rows,
    neighbours_hbm_ref,
    kinds_hbm_ref,
    flags_ref,
    partial_ref,
    row_a_ref,
    row_b_ref,
    from_row_a_ref,
    from_row_b_ref,
    from_side_a_ref,
    from_side_b_ref,
    rest_side_a_ref,
    rest_side_b_ref,
    current_ref,
    basis_ref,
    table_ref,
    weighted_low_ref,
    weighted_high_ref,
    coupling_ref,
    sent_ref,
    kept_ref,
    ext_ref,
    neighbours_ref,
    kinds_ref,
    semaphores,
):
    copies = code_copies(
        (neighbours_hbm_ref, kinds_hbm_ref), (neighbours_ref, kinds_ref), semaphores
    )
    for copy in copies:
        copy.start()
    count_y, block, side = weighted_low_ref.shape
    wide = count_y + 2
    rest = rest_side_a_ref.shape[1]
    prior = rest + block
    odd_y, odd_x, in_low_y, in_high_y, in_low_x, in_high_x = (
        flag_at(flags_ref, place) for place in range(6)
    )
    coupling = partial_ref[...] * inverse_rows
    coupling_ref[...] = coupling
    coupling_deep = deep(coupling)

    def basis_parts(i, j):
        if 0 < j < wide - 1:
            return basis_ref[i * count_y + j - 1]
        rest_tile = pick(odd_y, rest_side_a_ref[i], rest_side_b_ref[i])[j // (wide - 1)]
        return stacked(jnp.concatenate([rest_tile, current_ref[i * wide + j]], axis=0))

    for j in range(wide):
        if 0 < j < wide - 1:
            rows = list(pick(odd_x, from_row_a_ref[j - 1], from_row_b_ref[j - 1]))
            rows[1:1] = pick(odd_x, row_a_ref[j - 1], row_b_ref[j - 1])
        else:
            rows = [
                pick(odd_y, from_side_a_ref[i], from_side_b_ref[i])[j // (wide - 1)]
                for i in range(4)
            ]
        for i in range(4):
            value = rows[i] - halves_sum(mul(coupling_deep, basis_parts(i, j)))
            if i == 0:
                value = value * in_low_x
            if i == 3:
                value = value * in_high_x
            if j == 0:
                value = value * in_low_y
            if j == wide - 1:
                value = value * in_high_y
            if 0 < i < 3 and 0 < j < wide - 1:
                (weighted_low_ref, weighted_high_ref)[i - 1][j - 1] = value
            ext_ref[i * wide + j] = deep(value)
    for copy in copies:
        copy.wait()
    with_basis = jnp.zeros((2 * block, prior), F32)
    with_own = jnp.zeros((block, 4 * block), F32)
    for tile in range(2 * count_y):
        i, j = tile // count_y, tile % count_y
        own = (weighted_low_ref, weighted_high_ref)[i][j]
        totals = jnp.concatenate([4.0 * own, own], axis=1)
        for k in range(neighbours_ref.shape[1]):
            source, kind = source_and_kind(neighbours_ref, kinds_ref, tile, k, count_y)
            totals = totals + halves_sum(mul(ext_ref[source], table_ref[kind]))
        applied = jnp.concatenate([totals[:, :side], totals[:, side:]], axis=0)
        basis_tile = basis_parts(i + 1, j + 1)
        with_basis = with_basis + pair_sum(
            stacked(applied), basis_tile[:prior], basis_tile[prior:]
        )
        right = jnp.concatenate([applied, own, jnp.zeros_like(own)], axis=0)
        with_own = with_own + pair_sum(stacked(own), *split(right))
    halves = [
        jnp.concatenate(
            [
                with_basis[part * block : (part + 1) * block],
                folded(with_own[:, part * block : (part + 1) * block]),
                folded(with_own[:, 2 * block : 3 * block]),
            ],
            axis=0,
        )
        for part in range(2)
    ]
    sent_ref[...], kept_ref[...] = pick(odd_y, halves[0], halves[1])


def folded(square):
    return jnp.concatenate([square[n * 8 : (n + 1) * 8] for n in range(4)], axis=1)


def unfolded(rows):
    return jnp.concatenate([rows[:, n * 32 : (n + 1) * 32] for n in range(4)], axis=0)


def factor_kernel(inverse_rows, sums_ref, work_ref):
    block = work_ref.shape[0]
    gram = unfolded(sums_ref[block + 8 :, :]) * inverse_rows
    row_ids = lax.broadcasted_iota(jnp.int32, (block, block), 0)
    column_ids = lax.broadcasted_iota(jnp.int32, (block, block), 1)
    unit = jnp.where(row_ids == column_ids, 1.0, 0.0).astype(F32)
    work = jnp.concatenate([gram, unit], axis=1)
    rows = lax.broadcasted_iota(jnp.int32, work.shape, 0)
    group = 4
    for j in range(0, block, group):
        columns = [
            jnp.broadcast_to(work[:, j + a : j + a + 1], work.shape) for a in range(group)
        ]
        pivots = [work[j + a : j + a + 1, :] for a in range(group)]
        for a in range(group):
            at = j + a
            ratio = columns[a] * (1.0 / columns[a][at : at + 1, :])
            for b in range(a + 1, group):
                columns[b] = columns[b] - ratio * columns[b][at : at + 1, :]
                pivots[b] = pivots[b] - ratio[j + b : j + b + 1, :] * pivots[a]
            work = work - jnp.where(rows > at, ratio, 0.0) * pivots[a]
    work = work * lax.rsqrt(jnp.sum(work[:, :block] * unit, axis=1, keepdims=True))
    work_ref[...] = work


def finish_kernel(
    inverse_rows,
    flags_ref,
    work_ref,
    sums_ref,
    other_ref,
    weighted_low_ref,
    weighted_high_ref,
    new_ref,
    factor_ref,
    reduced_ref,
):
    count_y, block, _ = weighted_low_ref.shape
    prior = sums_ref.shape[1]
    tiles = 2 * count_y
    row_ids = lax.broadcasted_iota(jnp.int32, (block, block), 0)
    column_ids = lax.broadcasted_iota(jnp.int32, (block, block), 1)
    factor_ref[...] = jnp.where(column_ids >= row_ids, work_ref[:, :block], 0.0)
    inverse = work_ref[:, block:]
    for tile in range(tiles):
        own = (weighted_low_ref, weighted_high_ref)[tile // count_y][tile % count_y]
        new_ref[pl.ds(tile, block, stride=tiles), :] = mul3(inverse, own)
    odd_y = flag_at(flags_ref, 0)
    halves = pick(odd_y, other_ref[...], sums_ref[: block + 8, :])
    for part, half in enumerate(halves):
        reduced_ref[part, :, :prior] = mul3(inverse, half[:block] * inverse_rows)
        own = unfolded(half[block:]) * inverse_rows
        reduced_ref[part, :, prior:] = mul3_t(mul3_t(inverse, own), inverse)


def swap(value, mask):
    axes = ("px", "py")
    pairs = [(i, i ^ mask) for i in range(lax.axis_size(axes))]
    return lax.ppermute(value, axes, pairs)


def exchange(message_a, message_b, axis):
    cases, count = lax.axis_size("case"), lax.axis_size(axis)
    near = [(i, i ^ 1) for i in range(count)]
    pairs = []
    for case in range(cases):
        for i in range(count):
            j = ((i + 1) ^ 1) - 1
            target = (case, j) if 0 <= j < count else ((case ^ 1) % cases, i)
            pairs.append((case * count + i, target[0] * count + target[1]))
    return lax.ppermute(message_a, axis, near), lax.ppermute(message_b, ("case", axis), pairs)


def total_over(value, first, last):
    while first < last:
        value = value + swap(value, first)
        first *= 2
    return value


def half_total(sent, kept):
    kept = kept + swap(sent, 1)
    kept = (kept + swap(kept, 6)) + (swap(kept, 2) + swap(kept, 4))
    return total_over(kept, 8, lax.axis_size(("px", "py")))


def shape(*dims, dtype=F32):
    return jax.ShapeDtypeStruct(dims, dtype)


def shards(prior_basis, previous, neighbours, tile_kinds, stiff_tiles, mass_tiles):
    block = previous.shape[0]
    prior, count_x, count_y, side = prior_basis.shape
    tiles = count_x * count_y
    wide = count_y + 2
    rest = prior - block
    kinds = stiff_tiles.shape[0]
    inverse_rows = 1.0 / (tiles * side * lax.axis_size("px") * lax.axis_size("py"))
    basis = prior_basis.reshape(-1, side)
    vectors = jnp.concatenate([basis, previous.reshape(-1, side)], axis=0)
    codes = [array.transpose(1, 2, 0).reshape(tiles, -1) for array in (neighbours, tile_kinds)]
    code_scratch = [pltpu.SMEM(array.shape, jnp.int32) for array in codes]
    code_scratch += [pltpu.SemaphoreType.DMA((2,))]
    at_y, at_x = lax.axis_index("py"), lax.axis_index("px")
    bits = (at_y & 1) + 2 * (at_x & 1)
    bits += 4 * (at_y > 0) + 8 * (at_y < lax.axis_size("py") - 1)
    bits += 16 * (at_x > 0) + 32 * (at_x < lax.axis_size("px") - 1)
    flags = ((bits >> lax.broadcasted_iota(jnp.int32, (8, side), 0)) & 1).astype(F32)

    def call(kernel, inputs, outputs, scratch=(), plain=0, limit=8, cost=None):
        specs = [ANY] * plain + [VMEM] * (len(inputs) - plain)
        return pl.pallas_call(
            kernel,
            out_shape=outputs,
            in_specs=specs,
            out_specs=[VMEM] * len(outputs),
            scratch_shapes=scratch,
            compiler_params=pltpu.CompilerParams(vmem_limit_bytes=limit * MIB),
            cost_estimate=cost,
        )(*inputs)

    side_a, side_b, row_a, row_b = call(
        pack_kernel,
        (flags, vectors),
        [shape(count_x, 2 * block, side)] * 2 + [shape(count_y, 2 * block, side)] * 2,
    )
    rest_a, rest_b = call(rest_kernel, (flags, vectors), [shape(count_y, rest, side)] * 2)
    from_side_a, from_side_b = exchange(side_a, side_b, "py")
    from_row_a, from_row_b = exchange(row_a, row_b, "px")
    from_side_a, rest_a, rest_b = lax.optimization_barrier((from_side_a, rest_a, rest_b))
    from_rest_a, from_rest_b = exchange(rest_a, rest_b, "px")
    corner_a, corner_b = call(
        corners_kernel,
        (flags, from_side_a, from_side_b),
        [shape(2, 2 * block, side)] * 2,
    )
    from_corner_a, from_corner_b = exchange(corner_a, corner_b, "px")
    rest_side_a, rest_side_b = call(
        columns_kernel,
        (flags, rest_a, rest_b, from_rest_a, from_rest_b),
        [shape(4, rest, side)] * 2,
    )
    rest_side_a, rest_side_b = exchange(rest_side_a, rest_side_b, "py")
    residual_a, residual_b, partial, current = call(
        residual_kernel,
        (
            *codes,
            flags,
            row_a,
            row_b,
            from_row_a,
            from_row_b,
            from_side_a,
            from_side_b,
            from_corner_a,
            from_corner_b,
            rest_a,
            rest_b,
            stiff_tiles,
            mass_tiles,
        ),
        [shape(count_y + 1, block, side), shape(count_y, block, side)]
        + [shape(block, prior), shape(4 * wide, block, side)],
        [pltpu.VMEM((4 * wide, 2 * block, 2 * side), BF16)]
        + [pltpu.VMEM((kinds, 2 * side, 2 * side), BF16)]
        + code_scratch,
        plain=2,
        cost=pl.CostEstimate(flops=10**9, bytes_accessed=0, transcendentals=0),
    )
    count_py = lax.axis_size("py")
    from_row_a, from_row_b = exchange(residual_a, residual_b, "px")
    partial = total_over(
        partial + from_row_a[-1], 2 * count_py, count_py * lax.axis_size("px")
    )
    partial, rest_side_a, rest_side_b = lax.optimization_barrier(
        (partial, rest_side_a, rest_side_b)
    )
    side_a, side_b = call(
        columns_kernel,
        (flags, residual_a, residual_b, from_row_a, from_row_b, partial),
        [shape(5, block, side), shape(4, block, side)],
    )
    from_side_a, from_side_b = exchange(side_a, side_b, "py")
    partial = total_over(partial + from_side_a[-1], 2, count_py)
    basis_parts, table = call(
        prepare_kernel,
        (flags, rest_a, rest_b, from_rest_a, from_rest_b, current, stiff_tiles, mass_tiles),
        [shape(4 * count_y, 2 * prior, side, dtype=BF16)]
        + [shape(kinds, 2 * side, 2 * side, dtype=BF16)],
        cost=pl.CostEstimate(flops=10**9, bytes_accessed=0, transcendentals=0),
    )
    weighted_low, weighted_high, coupling, sent, kept = call(
        functools.partial(operators_kernel, inverse_rows),
        (
            *codes,
            flags,
            partial,
            residual_a,
            residual_b,
            from_row_a,
            from_row_b,
            from_side_a,
            from_side_b,
            rest_side_a,
            rest_side_b,
            current,
            basis_parts,
            table,
        ),
        [shape(count_y, block, side)] * 2
        + [shape(block, prior)]
        + [shape(block + 16, prior)] * 2,
        [pltpu.VMEM((4 * wide, 2 * block, 2 * side), BF16)] + code_scratch,
        plain=2,
    )
    kept = half_total(sent, kept)
    other = swap(kept[: block + 8], 1)
    (work,) = call(
        functools.partial(factor_kernel, inverse_rows),
        (kept,),
        [shape(block, 2 * block)],
        cost=pl.CostEstimate(flops=10**9, bytes_accessed=0, transcendentals=0),
    )
    new_block, factor, reduced = call(
        functools.partial(finish_kernel, inverse_rows),
        (flags, work, kept, other, weighted_low, weighted_high),
        [
            shape(block * tiles, side),
            shape(block, block),
            shape(2, block, prior + block),
        ],
    )
    return (
        new_block.reshape(previous.shape),
        coupling.T,
        factor,
        reduced.swapaxes(1, 2),
    )


def solution(mesh):
    placed = (
        P("case", "px", "py", None),
        P("case", "px", "py", None),
        P(None, "px", "py"),
        P(None, "px", "py"),
        P(),
        P(),
    )
    return jax.shard_map(
        shards,
        mesh=mesh,
        in_specs=placed,
        out_specs=(
            P("case", "px", "py", None),
            P("case", None),
            P("case", None),
            P("case", None, None),
        ),
        check_vma=False,
    )
```

```python
import functools

import jax
import jax.numpy as jnp
from jax import lax
from jax.experimental import pallas as pl
from jax.experimental.pallas import tpu as pltpu
from jax.sharding import PartitionSpec as P

F32 = jnp.float32
BF16 = jnp.bfloat16
VMEM = pl.BlockSpec(memory_space=pltpu.VMEM)
ANY = pl.BlockSpec(memory_space=pl.ANY)
MIB = 1024 * 1024


def split(value):
    high = value.astype(BF16)
    return high, (value - high.astype(F32)).astype(BF16)


def mul(left, right):
    return jnp.dot(left, right, preferred_element_type=F32)


def mul_t(left, right):
    return lax.dot_general(left, right, (((1,), (1,)), ((), ())), preferred_element_type=F32)


def mul3(left, right):
    left_high, left_low = split(left)
    right_high, right_low = split(right)
    return mul(left_high, right_high) + (mul(left_high, right_low) + mul(left_low, right_high))


def mul3_t(left, right):
    left_high, left_low = split(left)
    right_high, right_low = split(right)
    return mul_t(left_high, right_high) + (
        mul_t(left_high, right_low) + mul_t(left_low, right_high)
    )


def split_tables(stiff_ref, mass_ref, table_ref, parts_axis):
    side = stiff_ref.shape[1]
    spans = (slice(0, side), slice(side, 2 * side))
    for kind in range(stiff_ref.shape[0]):
        for matrix, ref in zip(spans, (stiff_ref, mass_ref)):
            for part, value in zip(spans, split(ref[kind])):
                if parts_axis == 1:
                    table_ref[kind, matrix, part] = value
                else:
                    table_ref[kind, part, matrix] = value


def stacked(value):
    return jnp.concatenate(split(value), axis=0)


def deep(value):
    high, low = split(value)
    upper = jnp.concatenate([high, high], axis=1)
    return jnp.concatenate([upper, jnp.concatenate([low, jnp.zeros_like(low)], axis=1)], axis=0)


def halves_sum(value):
    half = value.shape[0] // 2
    return value[:half] + value[half:]


def pair_sum(left, right_high, right_low):
    rows = left.shape[0] // 2
    return halves_sum(mul_t(left, right_high)) + mul_t(left[:rows], right_low)


def pick(flag, first, second):
    flag = flag > 0.0
    return jnp.where(flag, first, second), jnp.where(flag, second, first)


def flag_at(flags_ref, place):
    return flags_ref[place : place + 1, :]


def code_copies(code_refs, local_refs, semaphores):
    return [
        pltpu.make_async_copy(ref, local, semaphores.at[n])
        for n, (ref, local) in enumerate(zip(code_refs, local_refs))
    ]


def source_and_kind(neighbours_ref, kinds_ref, tile, k, count_y):
    neighbour = neighbours_ref[tile, k]
    down = (neighbour * 11) >> 5
    first = (tile // count_y) * (count_y + 2) + tile % count_y
    return first + neighbour + down * (count_y - 1), kinds_ref[tile, k]


def pack_kernel(flags_ref, vectors_ref, side_a_ref, side_b_ref, row_a_ref, row_b_ref):
    count_y, both, _ = row_a_ref.shape
    tiles = 2 * count_y
    odd_y, odd_x = flag_at(flags_ref, 0), flag_at(flags_ref, 1)

    first = vectors_ref.shape[0] - both * tiles

    def tile_of(i, j):
        return vectors_ref[pl.ds(first + i * count_y + j, both, stride=tiles), :]

    for i in range(2):
        side_a_ref[i], side_b_ref[i] = pick(odd_y, tile_of(i, 0), tile_of(i, count_y - 1))
    for j in range(count_y):
        row_a_ref[j], row_b_ref[j] = pick(odd_x, tile_of(0, j), tile_of(1, j))


def rest_kernel(flags_ref, vectors_ref, rest_a_ref, rest_b_ref):
    count_y, rest, _ = rest_a_ref.shape
    odd_x = flag_at(flags_ref, 1)
    for j in range(count_y):
        rest_a_ref[j], rest_b_ref[j] = pick(
            odd_x,
            vectors_ref[pl.ds(j, rest, stride=2 * count_y), :],
            vectors_ref[pl.ds(count_y + j, rest, stride=2 * count_y), :],
        )


def corners_kernel(flags_ref, side_a_ref, side_b_ref, corner_a_ref, corner_b_ref):
    odd_y, odd_x = flag_at(flags_ref, 0), flag_at(flags_ref, 1)
    ends = [pick(odd_y, side_a_ref[i], side_b_ref[i]) for i in range(2)]
    for place in range(2):
        corner_a_ref[place], corner_b_ref[place] = pick(odd_x, ends[0][place], ends[1][place])


def columns_kernel(
    flags_ref, row_a_ref, row_b_ref, from_row_a_ref, from_row_b_ref, *refs
):
    odd_y, odd_x = flag_at(flags_ref, 0), flag_at(flags_ref, 1)
    side_a_ref, side_b_ref = refs[-2:]
    columns = []
    for j in (0, row_b_ref.shape[0] - 1):
        column = list(pick(odd_x, from_row_a_ref[j], from_row_b_ref[j]))
        column[1:1] = pick(odd_x, row_a_ref[j], row_b_ref[j])
        columns.append(column)
    for i in range(4):
        side_a_ref[i], side_b_ref[i] = pick(odd_y, columns[0][i], columns[1][i])
    if len(refs) == 3:
        side_a_ref[4] = refs[0][...]


def residual_kernel(
    neighbours_hbm_ref,
    kinds_hbm_ref,
    flags_ref,
    row_a_ref,
    row_b_ref,
    from_row_a_ref,
    from_row_b_ref,
    from_side_a_ref,
    from_side_b_ref,
    from_corner_a_ref,
    from_corner_b_ref,
    rest_a_ref,
    rest_b_ref,
    stiff_ref,
    mass_ref,
    residual_a_ref,
    residual_b_ref,
    partial_ref,
    current_ref,
    ext_ref,
    table_ref,
    neighbours_ref,
    kinds_ref,
    semaphores,
):
    copies = code_copies(
        (neighbours_hbm_ref, kinds_hbm_ref), (neighbours_ref, kinds_ref), semaphores
    )
    for copy in copies:
        copy.start()
    split_tables(stiff_ref, mass_ref, table_ref, 1)
    count_y, both, side = row_a_ref.shape
    wide = count_y + 2
    block = both // 2
    rest = rest_a_ref.shape[1]
    odd_y, odd_x, in_low_y, in_high_y, in_low_x, in_high_x = (
        flag_at(flags_ref, place) for place in range(6)
    )

    def store(i, j, value):
        current_ref[i * wide + j] = value[:block]
        for part in range(2):
            high, low = split(value[part * block : (part + 1) * block])
            ext_ref[i * wide + j, :block, part * side : (part + 1) * side] = high
            ext_ref[i * wide + j, block:, part * side : (part + 1) * side] = low

    own = {}
    for j in range(count_y):
        own[0, j], own[1, j] = pick(odd_x, row_a_ref[j], row_b_ref[j])
        store(1, j + 1, own[0, j])
        store(2, j + 1, own[1, j])
        low, high = pick(odd_x, from_row_a_ref[j], from_row_b_ref[j])
        store(0, j + 1, low * in_low_x)
        store(3, j + 1, high * in_high_x)
    for i in range(2):
        low, high = pick(odd_y, from_side_a_ref[i], from_side_b_ref[i])
        store(i + 1, 0, low * in_low_y)
        store(i + 1, wide - 1, high * in_high_y)
    for place, j, inside in ((0, 0, in_low_y), (1, wide - 1, in_high_y)):
        low, high = pick(odd_x, from_corner_a_ref[place], from_corner_b_ref[place])
        store(0, j, low * (in_low_x * inside))
        store(3, j, high * (in_high_x * inside))
    for copy in copies:
        copy.wait()
    partial = jnp.zeros((block, rest + block), F32)
    totals = {}
    for tile in range(2 * count_y):
        i, j = tile // count_y, tile % count_y
        total = 4.0 * own[i, j][:block] + own[i, j][block:]
        for k in range(neighbours_ref.shape[1]):
            source, kind = source_and_kind(neighbours_ref, kinds_ref, tile, k, count_y)
            pair = mul(ext_ref[source], table_ref[kind])
            total = total + (pair[:block, :side] + (pair[block:, :side] + pair[:block, side:]))
        totals[i, j] = total
        rest_tile = pick(odd_x, rest_a_ref[j], rest_b_ref[j])[i]
        basis_tile = jnp.concatenate([rest_tile, own[i, j][:block]], axis=0)
        partial = partial + pair_sum(stacked(total), *split(basis_tile))
    for j in range(count_y):
        residual_a_ref[j], residual_b_ref[j] = pick(odd_x, totals[0, j], totals[1, j])
    residual_a_ref[count_y] = partial
    partial_ref[...] = partial


def prepare_kernel(
    flags_ref,
    rest_a_ref,
    rest_b_ref,
    from_rest_a_ref,
    from_rest_b_ref,
    current_ref,
    stiff_ref,
    mass_ref,
    basis_ref,
    table_ref,
):
    count_y, rest, _ = rest_a_ref.shape
    prior = rest + current_ref.shape[1]
    odd_x = flag_at(flags_ref, 1)
    split_tables(stiff_ref, mass_ref, table_ref, 0)
    for j in range(count_y):
        rests = list(pick(odd_x, from_rest_a_ref[j], from_rest_b_ref[j]))
        rests[1:1] = pick(odd_x, rest_a_ref[j], rest_b_ref[j])
        for i in range(4):
            tile = jnp.concatenate([rests[i], current_ref[i * (count_y + 2) + j + 1]], axis=0)
            basis_ref[i * count_y + j, :prior, :], basis_ref[i * count_y + j, prior:, :] = split(
                tile
            )


def operators_kernel(
    inverse_rows,
    neighbours_hbm_ref,
    kinds_hbm_ref,
    flags_ref,
    partial_ref,
    row_a_ref,
    row_b_ref,
    from_row_a_ref,
    from_row_b_ref,
    from_side_a_ref,
    from_side_b_ref,
    rest_side_a_ref,
    rest_side_b_ref,
    current_ref,
    basis_ref,
    table_ref,
    weighted_low_ref,
    weighted_high_ref,
    coupling_ref,
    sent_ref,
    kept_ref,
    ext_ref,
    neighbours_ref,
    kinds_ref,
    semaphores,
):
    copies = code_copies(
        (neighbours_hbm_ref, kinds_hbm_ref), (neighbours_ref, kinds_ref), semaphores
    )
    for copy in copies:
        copy.start()
    count_y, block, side = weighted_low_ref.shape
    wide = count_y + 2
    rest = rest_side_a_ref.shape[1]
    prior = rest + block
    odd_y, odd_x, in_low_y, in_high_y, in_low_x, in_high_x = (
        flag_at(flags_ref, place) for place in range(6)
    )
    coupling = partial_ref[...] * inverse_rows
    coupling_ref[...] = coupling
    coupling_deep = deep(coupling)

    def basis_parts(i, j):
        if 0 < j < wide - 1:
            return basis_ref[i * count_y + j - 1]
        rest_tile = pick(odd_y, rest_side_a_ref[i], rest_side_b_ref[i])[j // (wide - 1)]
        return stacked(jnp.concatenate([rest_tile, current_ref[i * wide + j]], axis=0))

    for j in range(wide):
        if 0 < j < wide - 1:
            rows = list(pick(odd_x, from_row_a_ref[j - 1], from_row_b_ref[j - 1]))
            rows[1:1] = pick(odd_x, row_a_ref[j - 1], row_b_ref[j - 1])
        else:
            rows = [
                pick(odd_y, from_side_a_ref[i], from_side_b_ref[i])[j // (wide - 1)]
                for i in range(4)
            ]
        for i in range(4):
            value = rows[i] - halves_sum(mul(coupling_deep, basis_parts(i, j)))
            if i == 0:
                value = value * in_low_x
            if i == 3:
                value = value * in_high_x
            if j == 0:
                value = value * in_low_y
            if j == wide - 1:
                value = value * in_high_y
            if 0 < i < 3 and 0 < j < wide - 1:
                (weighted_low_ref, weighted_high_ref)[i - 1][j - 1] = value
            ext_ref[i * wide + j] = deep(value)
    for copy in copies:
        copy.wait()
    with_basis = jnp.zeros((2 * block, prior), F32)
    with_own = jnp.zeros((block, 4 * block), F32)
    for tile in range(2 * count_y):
        i, j = tile // count_y, tile % count_y
        own = (weighted_low_ref, weighted_high_ref)[i][j]
        totals = jnp.concatenate([4.0 * own, own], axis=1)
        for k in range(neighbours_ref.shape[1]):
            source, kind = source_and_kind(neighbours_ref, kinds_ref, tile, k, count_y)
            totals = totals + halves_sum(mul(ext_ref[source], table_ref[kind]))
        applied = jnp.concatenate([totals[:, :side], totals[:, side:]], axis=0)
        basis_tile = basis_parts(i + 1, j + 1)
        with_basis = with_basis + pair_sum(
            stacked(applied), basis_tile[:prior], basis_tile[prior:]
        )
        right = jnp.concatenate([applied, own, jnp.zeros_like(own)], axis=0)
        with_own = with_own + pair_sum(stacked(own), *split(right))
    halves = [
        jnp.concatenate(
            [
                with_basis[part * block : (part + 1) * block],
                folded(with_own[:, part * block : (part + 1) * block]),
                folded(with_own[:, 2 * block : 3 * block]),
            ],
            axis=0,
        )
        for part in range(2)
    ]
    sent_ref[...], kept_ref[...] = pick(odd_y, halves[0], halves[1])


def folded(square):
    return jnp.concatenate([square[n * 8 : (n + 1) * 8] for n in range(4)], axis=1)


def unfolded(rows):
    return jnp.concatenate([rows[:, n * 32 : (n + 1) * 32] for n in range(4)], axis=0)


def factor_kernel(inverse_rows, sums_ref, work_ref):
    block = work_ref.shape[0]
    gram = unfolded(sums_ref[block + 8 :, :]) * inverse_rows
    row_ids = lax.broadcasted_iota(jnp.int32, (block, block), 0)
    column_ids = lax.broadcasted_iota(jnp.int32, (block, block), 1)
    unit = jnp.where(row_ids == column_ids, 1.0, 0.0).astype(F32)
    work = jnp.concatenate([gram, unit], axis=1)
    rows = lax.broadcasted_iota(jnp.int32, work.shape, 0)
    group = 4
    for j in range(0, block, group):
        columns = [
            jnp.broadcast_to(work[:, j + a : j + a + 1], work.shape) for a in range(group)
        ]
        pivots = [work[j + a : j + a + 1, :] for a in range(group)]
        for a in range(group):
            at = j + a
            ratio = columns[a] * (1.0 / columns[a][at : at + 1, :])
            for b in range(a + 1, group):
                columns[b] = columns[b] - ratio * columns[b][at : at + 1, :]
                pivots[b] = pivots[b] - ratio[j + b : j + b + 1, :] * pivots[a]
            work = work - jnp.where(rows > at, ratio, 0.0) * pivots[a]
    work = work * lax.rsqrt(jnp.sum(work[:, :block] * unit, axis=1, keepdims=True))
    work_ref[...] = work


def finish_kernel(
    inverse_rows,
    flags_ref,
    work_ref,
    sums_ref,
    other_ref,
    weighted_low_ref,
    weighted_high_ref,
    new_ref,
    factor_ref,
    reduced_ref,
):
    count_y, block, _ = weighted_low_ref.shape
    prior = sums_ref.shape[1]
    tiles = 2 * count_y
    row_ids = lax.broadcasted_iota(jnp.int32, (block, block), 0)
    column_ids = lax.broadcasted_iota(jnp.int32, (block, block), 1)
    factor_ref[...] = jnp.where(column_ids >= row_ids, work_ref[:, :block], 0.0)
    inverse = work_ref[:, block:]
    for tile in range(tiles):
        own = (weighted_low_ref, weighted_high_ref)[tile // count_y][tile % count_y]
        new_ref[pl.ds(tile, block, stride=tiles), :] = mul3(inverse, own)
    odd_y = flag_at(flags_ref, 0)
    halves = pick(odd_y, other_ref[...], sums_ref[: block + 8, :])
    for part, half in enumerate(halves):
        reduced_ref[part, :, :prior] = mul3(inverse, half[:block] * inverse_rows)
        own = unfolded(half[block:]) * inverse_rows
        reduced_ref[part, :, prior:] = mul3_t(mul3_t(inverse, own), inverse)


def swap(value, mask):
    axes = ("px", "py")
    pairs = [(i, i ^ mask) for i in range(lax.axis_size(axes))]
    return lax.ppermute(value, axes, pairs)


def exchange(message_a, message_b, axis):
    cases, count = lax.axis_size("case"), lax.axis_size(axis)
    near = [(i, i ^ 1) for i in range(count)]
    pairs = []
    for case in range(cases):
        for i in range(count):
            j = ((i + 1) ^ 1) - 1
            target = (case, j) if 0 <= j < count else ((case ^ 1) % cases, i)
            pairs.append((case * count + i, target[0] * count + target[1]))
    return lax.ppermute(message_a, axis, near), lax.ppermute(message_b, ("case", axis), pairs)


def total_over(value, first, last):
    while first < last:
        value = value + swap(value, first)
        first *= 2
    return value


def half_total(sent, kept):
    kept = kept + swap(sent, 1)
    kept = (kept + swap(kept, 6)) + (swap(kept, 2) + swap(kept, 4))
    return total_over(kept, 8, lax.axis_size(("px", "py")))


def shape(*dims, dtype=F32):
    return jax.ShapeDtypeStruct(dims, dtype)


def shards(prior_basis, previous, neighbours, tile_kinds, stiff_tiles, mass_tiles):
    block = previous.shape[0]
    prior, count_x, count_y, side = prior_basis.shape
    tiles = count_x * count_y
    wide = count_y + 2
    rest = prior - block
    kinds = stiff_tiles.shape[0]
    inverse_rows = 1.0 / (tiles * side * lax.axis_size("px") * lax.axis_size("py"))
    basis = prior_basis.reshape(-1, side)
    vectors = jnp.concatenate([basis, previous.reshape(-1, side)], axis=0)
    codes = [array.transpose(1, 2, 0).reshape(tiles, -1) for array in (neighbours, tile_kinds)]
    code_scratch = [pltpu.SMEM(array.shape, jnp.int32) for array in codes]
    code_scratch += [pltpu.SemaphoreType.DMA((2,))]
    at_y, at_x = lax.axis_index("py"), lax.axis_index("px")
    bits = (at_y & 1) + 2 * (at_x & 1)
    bits += 4 * (at_y > 0) + 8 * (at_y < lax.axis_size("py") - 1)
    bits += 16 * (at_x > 0) + 32 * (at_x < lax.axis_size("px") - 1)
    flags = ((bits >> lax.broadcasted_iota(jnp.int32, (8, side), 0)) & 1).astype(F32)

    def call(kernel, inputs, outputs, scratch=(), plain=0, limit=8, cost=None):
        specs = [ANY] * plain + [VMEM] * (len(inputs) - plain)
        return pl.pallas_call(
            kernel,
            out_shape=outputs,
            in_specs=specs,
            out_specs=[VMEM] * len(outputs),
            scratch_shapes=scratch,
            compiler_params=pltpu.CompilerParams(vmem_limit_bytes=limit * MIB),
            cost_estimate=cost,
        )(*inputs)

    side_a, side_b, row_a, row_b = call(
        pack_kernel,
        (flags, vectors),
        [shape(count_x, 2 * block, side)] * 2 + [shape(count_y, 2 * block, side)] * 2,
    )
    rest_a, rest_b = call(rest_kernel, (flags, vectors), [shape(count_y, rest, side)] * 2)
    from_side_a, from_side_b = exchange(side_a, side_b, "py")
    from_row_a, from_row_b = exchange(row_a, row_b, "px")
    from_side_a, rest_a, rest_b = lax.optimization_barrier((from_side_a, rest_a, rest_b))
    from_rest_a, from_rest_b = exchange(rest_a, rest_b, "px")
    corner_a, corner_b = call(
        corners_kernel,
        (flags, from_side_a, from_side_b),
        [shape(2, 2 * block, side)] * 2,
    )
    from_corner_a, from_corner_b = exchange(corner_a, corner_b, "px")
    rest_side_a, rest_side_b = call(
        columns_kernel,
        (flags, rest_a, rest_b, from_rest_a, from_rest_b),
        [shape(4, rest, side)] * 2,
    )
    rest_side_a, rest_side_b = exchange(rest_side_a, rest_side_b, "py")
    residual_a, residual_b, partial, current = call(
        residual_kernel,
        (
            *codes,
            flags,
            row_a,
            row_b,
            from_row_a,
            from_row_b,
            from_side_a,
            from_side_b,
            from_corner_a,
            from_corner_b,
            rest_a,
            rest_b,
            stiff_tiles,
            mass_tiles,
        ),
        [shape(count_y + 1, block, side), shape(count_y, block, side)]
        + [shape(block, prior), shape(4 * wide, block, side)],
        [pltpu.VMEM((4 * wide, 2 * block, 2 * side), BF16)]
        + [pltpu.VMEM((kinds, 2 * side, 2 * side), BF16)]
        + code_scratch,
        plain=2,
        cost=pl.CostEstimate(flops=10**9, bytes_accessed=0, transcendentals=0),
    )
    count_py = lax.axis_size("py")
    from_row_a, from_row_b = exchange(residual_a, residual_b, "px")
    partial = total_over(
        partial + from_row_a[-1], 2 * count_py, count_py * lax.axis_size("px")
    )
    side_a, side_b = call(
        columns_kernel,
        (flags, residual_a, residual_b, from_row_a, from_row_b, partial),
        [shape(5, block, side), shape(4, block, side)],
    )
    from_side_a, from_side_b = exchange(side_a, side_b, "py")
    from_side_a, rest_side_a, rest_side_b = lax.optimization_barrier(
        (from_side_a, rest_side_a, rest_side_b)
    )
    partial = total_over(partial + from_side_a[-1], 2, count_py)
    basis_parts, table = call(
        prepare_kernel,
        (flags, rest_a, rest_b, from_rest_a, from_rest_b, current, stiff_tiles, mass_tiles),
        [shape(4 * count_y, 2 * prior, side, dtype=BF16)]
        + [shape(kinds, 2 * side, 2 * side, dtype=BF16)],
        cost=pl.CostEstimate(flops=10**9, bytes_accessed=0, transcendentals=0),
    )
    weighted_low, weighted_high, coupling, sent, kept = call(
        functools.partial(operators_kernel, inverse_rows),
        (
            *codes,
            flags,
            partial,
            residual_a,
            residual_b,
            from_row_a,
            from_row_b,
            from_side_a,
            from_side_b,
            rest_side_a,
            rest_side_b,
            current,
            basis_parts,
            table,
        ),
        [shape(count_y, block, side)] * 2
        + [shape(block, prior)]
        + [shape(block + 16, prior)] * 2,
        [pltpu.VMEM((4 * wide, 2 * block, 2 * side), BF16)] + code_scratch,
        plain=2,
    )
    kept = half_total(sent, kept)
    other = swap(kept[: block + 8], 1)
    (work,) = call(
        functools.partial(factor_kernel, inverse_rows),
        (kept,),
        [shape(block, 2 * block)],
        cost=pl.CostEstimate(flops=10**9, bytes_accessed=0, transcendentals=0),
    )
    new_block, factor, reduced = call(
        functools.partial(finish_kernel, inverse_rows),
        (flags, work, kept, other, weighted_low, weighted_high),
        [
            shape(block * tiles, side),
            shape(block, block),
            shape(2, block, prior + block),
        ],
    )
    return (
        new_block.reshape(previous.shape),
        coupling.T,
        factor,
        reduced.swapaxes(1, 2),
    )


def solution(mesh):
    placed = (
        P("case", "px", "py", None),
        P("case", "px", "py", None),
        P(None, "px", "py"),
        P(None, "px", "py"),
        P(),
        P(),
    )
    return jax.shard_map(
        shards,
        mesh=mesh,
        in_specs=placed,
        out_specs=(
            P("case", "px", "py", None),
            P("case", None),
            P("case", None),
            P("case", None, None),
        ),
        check_vma=False,
    )
```

```python
import functools

import jax
import jax.numpy as jnp
from jax import lax
from jax.experimental import pallas as pl
from jax.experimental.pallas import tpu as pltpu
from jax.sharding import PartitionSpec as P

F32 = jnp.float32
BF16 = jnp.bfloat16
VMEM = pl.BlockSpec(memory_space=pltpu.VMEM)
ANY = pl.BlockSpec(memory_space=pl.ANY)
MIB = 1024 * 1024


def split(value):
    high = value.astype(BF16)
    return high, (value - high.astype(F32)).astype(BF16)


def mul(left, right):
    return jnp.dot(left, right, preferred_element_type=F32)


def mul_t(left, right):
    return lax.dot_general(left, right, (((1,), (1,)), ((), ())), preferred_element_type=F32)


def mul3(left, right):
    left_high, left_low = split(left)
    right_high, right_low = split(right)
    return mul(left_high, right_high) + (mul(left_high, right_low) + mul(left_low, right_high))


def mul3_t(left, right):
    left_high, left_low = split(left)
    right_high, right_low = split(right)
    return mul_t(left_high, right_high) + (
        mul_t(left_high, right_low) + mul_t(left_low, right_high)
    )


def split_tables(stiff_ref, mass_ref, table_ref, parts_axis):
    side = stiff_ref.shape[1]
    spans = (slice(0, side), slice(side, 2 * side))
    for kind in range(stiff_ref.shape[0]):
        for matrix, ref in zip(spans, (stiff_ref, mass_ref)):
            for part, value in zip(spans, split(ref[kind])):
                if parts_axis == 1:
                    table_ref[kind, matrix, part] = value
                else:
                    table_ref[kind, part, matrix] = value


def stacked(value):
    return jnp.concatenate(split(value), axis=0)


def deep(value):
    high, low = split(value)
    upper = jnp.concatenate([high, high], axis=1)
    return jnp.concatenate([upper, jnp.concatenate([low, jnp.zeros_like(low)], axis=1)], axis=0)


def halves_sum(value):
    half = value.shape[0] // 2
    return value[:half] + value[half:]


def pair_sum(left, right_high, right_low):
    rows = left.shape[0] // 2
    return halves_sum(mul_t(left, right_high)) + mul_t(left[:rows], right_low)


def pick(flag, first, second):
    flag = flag > 0.0
    return jnp.where(flag, first, second), jnp.where(flag, second, first)


def flag_at(flags_ref, place):
    return flags_ref[place : place + 1, :]


def code_copies(code_refs, local_refs, semaphores):
    return [
        pltpu.make_async_copy(ref, local, semaphores.at[n])
        for n, (ref, local) in enumerate(zip(code_refs, local_refs))
    ]


def source_and_kind(neighbours_ref, kinds_ref, tile, k, count_y):
    neighbour = neighbours_ref[tile, k]
    down = (neighbour * 11) >> 5
    first = (tile // count_y) * (count_y + 2) + tile % count_y
    return first + neighbour + down * (count_y - 1), kinds_ref[tile, k]


def pack_kernel(flags_ref, vectors_ref, side_a_ref, side_b_ref, row_a_ref, row_b_ref):
    count_y, both, _ = row_a_ref.shape
    tiles = 2 * count_y
    odd_y, odd_x = flag_at(flags_ref, 0), flag_at(flags_ref, 1)

    first = vectors_ref.shape[0] - both * tiles

    def tile_of(i, j):
        return vectors_ref[pl.ds(first + i * count_y + j, both, stride=tiles), :]

    for i in range(2):
        side_a_ref[i], side_b_ref[i] = pick(odd_y, tile_of(i, 0), tile_of(i, count_y - 1))
    for j in range(count_y):
        row_a_ref[j], row_b_ref[j] = pick(odd_x, tile_of(0, j), tile_of(1, j))


def rest_kernel(flags_ref, vectors_ref, rest_a_ref, rest_b_ref):
    count_y, rest, _ = rest_a_ref.shape
    odd_x = flag_at(flags_ref, 1)
    for j in range(count_y):
        rest_a_ref[j], rest_b_ref[j] = pick(
            odd_x,
            vectors_ref[pl.ds(j, rest, stride=2 * count_y), :],
            vectors_ref[pl.ds(count_y + j, rest, stride=2 * count_y), :],
        )


def corners_kernel(flags_ref, side_a_ref, side_b_ref, corner_a_ref, corner_b_ref):
    odd_y, odd_x = flag_at(flags_ref, 0), flag_at(flags_ref, 1)
    ends = [pick(odd_y, side_a_ref[i], side_b_ref[i]) for i in range(2)]
    for place in range(2):
        corner_a_ref[place], corner_b_ref[place] = pick(odd_x, ends[0][place], ends[1][place])


def columns_kernel(
    flags_ref, row_a_ref, row_b_ref, from_row_a_ref, from_row_b_ref, *refs
):
    odd_y, odd_x = flag_at(flags_ref, 0), flag_at(flags_ref, 1)
    side_a_ref, side_b_ref = refs[-2:]
    columns = []
    for j in (0, row_b_ref.shape[0] - 1):
        column = list(pick(odd_x, from_row_a_ref[j], from_row_b_ref[j]))
        column[1:1] = pick(odd_x, row_a_ref[j], row_b_ref[j])
        columns.append(column)
    for i in range(4):
        side_a_ref[i], side_b_ref[i] = pick(odd_y, columns[0][i], columns[1][i])
    if len(refs) == 3:
        side_a_ref[4] = refs[0][...]


def residual_kernel(
    neighbours_hbm_ref,
    kinds_hbm_ref,
    flags_ref,
    row_a_ref,
    row_b_ref,
    from_row_a_ref,
    from_row_b_ref,
    from_side_a_ref,
    from_side_b_ref,
    from_corner_a_ref,
    from_corner_b_ref,
    rest_a_ref,
    rest_b_ref,
    stiff_ref,
    mass_ref,
    residual_a_ref,
    residual_b_ref,
    partial_ref,
    current_ref,
    ext_ref,
    table_ref,
    neighbours_ref,
    kinds_ref,
    semaphores,
):
    copies = code_copies(
        (neighbours_hbm_ref, kinds_hbm_ref), (neighbours_ref, kinds_ref), semaphores
    )
    for copy in copies:
        copy.start()
    split_tables(stiff_ref, mass_ref, table_ref, 1)
    count_y, both, side = row_a_ref.shape
    wide = count_y + 2
    block = both // 2
    rest = rest_a_ref.shape[1]
    odd_y, odd_x, in_low_y, in_high_y, in_low_x, in_high_x = (
        flag_at(flags_ref, place) for place in range(6)
    )

    def store(i, j, value):
        current_ref[i * wide + j] = value[:block]
        for part in range(2):
            high, low = split(value[part * block : (part + 1) * block])
            ext_ref[i * wide + j, :block, part * side : (part + 1) * side] = high
            ext_ref[i * wide + j, block:, part * side : (part + 1) * side] = low

    own = {}
    for j in range(count_y):
        own[0, j], own[1, j] = pick(odd_x, row_a_ref[j], row_b_ref[j])
        store(1, j + 1, own[0, j])
        store(2, j + 1, own[1, j])
        low, high = pick(odd_x, from_row_a_ref[j], from_row_b_ref[j])
        store(0, j + 1, low * in_low_x)
        store(3, j + 1, high * in_high_x)
    for i in range(2):
        low, high = pick(odd_y, from_side_a_ref[i], from_side_b_ref[i])
        store(i + 1, 0, low * in_low_y)
        store(i + 1, wide - 1, high * in_high_y)
    for place, j, inside in ((0, 0, in_low_y), (1, wide - 1, in_high_y)):
        low, high = pick(odd_x, from_corner_a_ref[place], from_corner_b_ref[place])
        store(0, j, low * (in_low_x * inside))
        store(3, j, high * (in_high_x * inside))
    for copy in copies:
        copy.wait()
    partial = jnp.zeros((block, rest + block), F32)
    totals = {}
    for tile in range(2 * count_y):
        i, j = tile // count_y, tile % count_y
        total = 4.0 * own[i, j][:block] + own[i, j][block:]
        for k in range(neighbours_ref.shape[1]):
            source, kind = source_and_kind(neighbours_ref, kinds_ref, tile, k, count_y)
            pair = mul(ext_ref[source], table_ref[kind])
            total = total + (pair[:block, :side] + (pair[block:, :side] + pair[:block, side:]))
        totals[i, j] = total
        rest_tile = pick(odd_x, rest_a_ref[j], rest_b_ref[j])[i]
        basis_tile = jnp.concatenate([rest_tile, own[i, j][:block]], axis=0)
        partial = partial + pair_sum(stacked(total), *split(basis_tile))
    for j in range(count_y):
        residual_a_ref[j], residual_b_ref[j] = pick(odd_x, totals[0, j], totals[1, j])
    residual_a_ref[count_y] = partial
    partial_ref[...] = partial


def prepare_kernel(
    flags_ref,
    rest_a_ref,
    rest_b_ref,
    from_rest_a_ref,
    from_rest_b_ref,
    current_ref,
    stiff_ref,
    mass_ref,
    basis_ref,
    table_ref,
):
    count_y, rest, _ = rest_a_ref.shape
    prior = rest + current_ref.shape[1]
    odd_x = flag_at(flags_ref, 1)
    split_tables(stiff_ref, mass_ref, table_ref, 0)
    for j in range(count_y):
        rests = list(pick(odd_x, from_rest_a_ref[j], from_rest_b_ref[j]))
        rests[1:1] = pick(odd_x, rest_a_ref[j], rest_b_ref[j])
        for i in range(4):
            tile = jnp.concatenate([rests[i], current_ref[i * (count_y + 2) + j + 1]], axis=0)
            basis_ref[i * count_y + j, :prior, :], basis_ref[i * count_y + j, prior:, :] = split(
                tile
            )


def operators_kernel(
    inverse_rows,
    neighbours_hbm_ref,
    kinds_hbm_ref,
    flags_ref,
    partial_ref,
    row_a_ref,
    row_b_ref,
    from_row_a_ref,
    from_row_b_ref,
    from_side_a_ref,
    from_side_b_ref,
    rest_side_a_ref,
    rest_side_b_ref,
    current_ref,
    basis_ref,
    table_ref,
    weighted_low_ref,
    weighted_high_ref,
    coupling_ref,
    sent_ref,
    kept_ref,
    ext_ref,
    neighbours_ref,
    kinds_ref,
    semaphores,
):
    copies = code_copies(
        (neighbours_hbm_ref, kinds_hbm_ref), (neighbours_ref, kinds_ref), semaphores
    )
    for copy in copies:
        copy.start()
    count_y, block, side = weighted_low_ref.shape
    wide = count_y + 2
    rest = rest_side_a_ref.shape[1]
    prior = rest + block
    odd_y, odd_x, in_low_y, in_high_y, in_low_x, in_high_x = (
        flag_at(flags_ref, place) for place in range(6)
    )
    coupling = partial_ref[...] * inverse_rows
    coupling_ref[...] = coupling
    coupling_deep = deep(coupling)

    def basis_parts(i, j):
        if 0 < j < wide - 1:
            return basis_ref[i * count_y + j - 1]
        rest_tile = pick(odd_y, rest_side_a_ref[i], rest_side_b_ref[i])[j // (wide - 1)]
        return stacked(jnp.concatenate([rest_tile, current_ref[i * wide + j]], axis=0))

    for j in range(wide):
        if 0 < j < wide - 1:
            rows = list(pick(odd_x, from_row_a_ref[j - 1], from_row_b_ref[j - 1]))
            rows[1:1] = pick(odd_x, row_a_ref[j - 1], row_b_ref[j - 1])
        else:
            rows = [
                pick(odd_y, from_side_a_ref[i], from_side_b_ref[i])[j // (wide - 1)]
                for i in range(4)
            ]
        for i in range(4):
            value = rows[i] - halves_sum(mul(coupling_deep, basis_parts(i, j)))
            if i == 0:
                value = value * in_low_x
            if i == 3:
                value = value * in_high_x
            if j == 0:
                value = value * in_low_y
            if j == wide - 1:
                value = value * in_high_y
            if 0 < i < 3 and 0 < j < wide - 1:
                (weighted_low_ref, weighted_high_ref)[i - 1][j - 1] = value
            ext_ref[i * wide + j] = deep(value)
    for copy in copies:
        copy.wait()
    with_basis = jnp.zeros((2 * block, prior), F32)
    with_own = jnp.zeros((block, 4 * block), F32)
    for tile in range(2 * count_y):
        i, j = tile // count_y, tile % count_y
        own = (weighted_low_ref, weighted_high_ref)[i][j]
        totals = jnp.concatenate([4.0 * own, own], axis=1)
        for k in range(neighbours_ref.shape[1]):
            source, kind = source_and_kind(neighbours_ref, kinds_ref, tile, k, count_y)
            totals = totals + halves_sum(mul(ext_ref[source], table_ref[kind]))
        applied = jnp.concatenate([totals[:, :side], totals[:, side:]], axis=0)
        basis_tile = basis_parts(i + 1, j + 1)
        with_basis = with_basis + pair_sum(
            stacked(applied), basis_tile[:prior], basis_tile[prior:]
        )
        right = jnp.concatenate([applied, own, jnp.zeros_like(own)], axis=0)
        with_own = with_own + pair_sum(stacked(own), *split(right))
    halves = [
        jnp.concatenate(
            [
                with_basis[part * block : (part + 1) * block],
                folded(with_own[:, part * block : (part + 1) * block]),
                folded(with_own[:, 2 * block : 3 * block]),
            ],
            axis=0,
        )
        for part in range(2)
    ]
    sent_ref[...], kept_ref[...] = pick(odd_y, halves[0], halves[1])


def folded(square):
    return jnp.concatenate([square[n * 8 : (n + 1) * 8] for n in range(4)], axis=1)


def unfolded(rows):
    return jnp.concatenate([rows[:, n * 32 : (n + 1) * 32] for n in range(4)], axis=0)


def factor_kernel(inverse_rows, sums_ref, work_ref):
    block = work_ref.shape[0]
    gram = unfolded(sums_ref[block + 8 :, :]) * inverse_rows
    row_ids = lax.broadcasted_iota(jnp.int32, (block, block), 0)
    column_ids = lax.broadcasted_iota(jnp.int32, (block, block), 1)
    unit = jnp.where(row_ids == column_ids, 1.0, 0.0).astype(F32)
    work = jnp.concatenate([gram, unit], axis=1)
    rows = lax.broadcasted_iota(jnp.int32, work.shape, 0)
    group = 8
    for j in range(0, block, group):
        columns = [
            jnp.broadcast_to(work[:, j + a : j + a + 1], work.shape) for a in range(group)
        ]
        pivots = [work[j + a : j + a + 1, :] for a in range(group)]
        for a in range(group):
            at = j + a
            ratio = columns[a] * (1.0 / columns[a][at : at + 1, :])
            for b in range(a + 1, group):
                columns[b] = columns[b] - ratio * columns[b][at : at + 1, :]
                pivots[b] = pivots[b] - ratio[j + b : j + b + 1, :] * pivots[a]
            work = work - jnp.where(rows > at, ratio, 0.0) * pivots[a]
    work = work * lax.rsqrt(jnp.sum(work[:, :block] * unit, axis=1, keepdims=True))
    work_ref[...] = work


def finish_kernel(
    inverse_rows,
    flags_ref,
    work_ref,
    sums_ref,
    other_ref,
    weighted_low_ref,
    weighted_high_ref,
    new_ref,
    factor_ref,
    reduced_ref,
):
    count_y, block, _ = weighted_low_ref.shape
    prior = sums_ref.shape[1]
    tiles = 2 * count_y
    row_ids = lax.broadcasted_iota(jnp.int32, (block, block), 0)
    column_ids = lax.broadcasted_iota(jnp.int32, (block, block), 1)
    factor_ref[...] = jnp.where(column_ids >= row_ids, work_ref[:, :block], 0.0)
    inverse = work_ref[:, block:]
    for tile in range(tiles):
        own = (weighted_low_ref, weighted_high_ref)[tile // count_y][tile % count_y]
        new_ref[pl.ds(tile, block, stride=tiles), :] = mul3(inverse, own)
    odd_y = flag_at(flags_ref, 0)
    halves = pick(odd_y, other_ref[...], sums_ref[: block + 8, :])
    for part, half in enumerate(halves):
        reduced_ref[part, :, :prior] = mul3(inverse, half[:block] * inverse_rows)
        own = unfolded(half[block:]) * inverse_rows
        reduced_ref[part, :, prior:] = mul3_t(mul3_t(inverse, own), inverse)


def swap(value, mask):
    axes = ("px", "py")
    pairs = [(i, i ^ mask) for i in range(lax.axis_size(axes))]
    return lax.ppermute(value, axes, pairs)


def exchange(message_a, message_b, axis):
    cases, count = lax.axis_size("case"), lax.axis_size(axis)
    near = [(i, i ^ 1) for i in range(count)]
    pairs = []
    for case in range(cases):
        for i in range(count):
            j = ((i + 1) ^ 1) - 1
            target = (case, j) if 0 <= j < count else ((case ^ 1) % cases, i)
            pairs.append((case * count + i, target[0] * count + target[1]))
    return lax.ppermute(message_a, axis, near), lax.ppermute(message_b, ("case", axis), pairs)


def total_over(value, first, last):
    while first < last:
        value = value + swap(value, first)
        first *= 2
    return value


def half_total(sent, kept):
    kept = kept + swap(sent, 1)
    count_py = lax.axis_size("py")
    kept = total_over(kept, 2, count_py)
    if lax.axis_size("px") != 4:
        return total_over(kept, count_py, count_py * lax.axis_size("px"))
    near, far, cross = (swap(kept, step * count_py) for step in (1, 2, 3))
    return (kept + far) + (near + cross)


def shape(*dims, dtype=F32):
    return jax.ShapeDtypeStruct(dims, dtype)


def shards(prior_basis, previous, neighbours, tile_kinds, stiff_tiles, mass_tiles):
    block = previous.shape[0]
    prior, count_x, count_y, side = prior_basis.shape
    tiles = count_x * count_y
    wide = count_y + 2
    rest = prior - block
    kinds = stiff_tiles.shape[0]
    inverse_rows = 1.0 / (tiles * side * lax.axis_size("px") * lax.axis_size("py"))
    basis = prior_basis.reshape(-1, side)
    vectors = jnp.concatenate([basis, previous.reshape(-1, side)], axis=0)
    codes = [array.transpose(1, 2, 0).reshape(tiles, -1) for array in (neighbours, tile_kinds)]
    code_scratch = [pltpu.SMEM(array.shape, jnp.int32) for array in codes]
    code_scratch += [pltpu.SemaphoreType.DMA((2,))]
    at_y, at_x = lax.axis_index("py"), lax.axis_index("px")
    bits = (at_y & 1) + 2 * (at_x & 1)
    bits += 4 * (at_y > 0) + 8 * (at_y < lax.axis_size("py") - 1)
    bits += 16 * (at_x > 0) + 32 * (at_x < lax.axis_size("px") - 1)
    flags = ((bits >> lax.broadcasted_iota(jnp.int32, (8, side), 0)) & 1).astype(F32)

    def call(kernel, inputs, outputs, scratch=(), plain=0, limit=8, cost=None):
        specs = [ANY] * plain + [VMEM] * (len(inputs) - plain)
        return pl.pallas_call(
            kernel,
            out_shape=outputs,
            in_specs=specs,
            out_specs=[VMEM] * len(outputs),
            scratch_shapes=scratch,
            compiler_params=pltpu.CompilerParams(vmem_limit_bytes=limit * MIB),
            cost_estimate=cost,
        )(*inputs)

    side_a, side_b, row_a, row_b = call(
        pack_kernel,
        (flags, vectors),
        [shape(count_x, 2 * block, side)] * 2 + [shape(count_y, 2 * block, side)] * 2,
    )
    rest_a, rest_b = call(rest_kernel, (flags, vectors), [shape(count_y, rest, side)] * 2)
    from_side_a, from_side_b = exchange(side_a, side_b, "py")
    from_row_a, from_row_b = exchange(row_a, row_b, "px")
    from_side_a, rest_a, rest_b = lax.optimization_barrier((from_side_a, rest_a, rest_b))
    from_rest_a, from_rest_b = exchange(rest_a, rest_b, "px")
    corner_a, corner_b = call(
        corners_kernel,
        (flags, from_side_a, from_side_b),
        [shape(2, 2 * block, side)] * 2,
    )
    from_corner_a, from_corner_b = exchange(corner_a, corner_b, "px")
    rest_side_a, rest_side_b = call(
        columns_kernel,
        (flags, rest_a, rest_b, from_rest_a, from_rest_b),
        [shape(4, rest, side)] * 2,
    )
    rest_side_a, rest_side_b = exchange(rest_side_a, rest_side_b, "py")
    residual_a, residual_b, partial, current = call(
        residual_kernel,
        (
            *codes,
            flags,
            row_a,
            row_b,
            from_row_a,
            from_row_b,
            from_side_a,
            from_side_b,
            from_corner_a,
            from_corner_b,
            rest_a,
            rest_b,
            stiff_tiles,
            mass_tiles,
        ),
        [shape(count_y + 1, block, side), shape(count_y, block, side)]
        + [shape(block, prior), shape(4 * wide, block, side)],
        [pltpu.VMEM((4 * wide, 2 * block, 2 * side), BF16)]
        + [pltpu.VMEM((kinds, 2 * side, 2 * side), BF16)]
        + code_scratch,
        plain=2,
        cost=pl.CostEstimate(flops=10**9, bytes_accessed=0, transcendentals=0),
    )
    count_py = lax.axis_size("py")
    from_row_a, from_row_b = exchange(residual_a, residual_b, "px")
    partial = total_over(
        partial + from_row_a[-1], 2 * count_py, count_py * lax.axis_size("px")
    )
    partial, rest_side_a, rest_side_b = lax.optimization_barrier(
        (partial, rest_side_a, rest_side_b)
    )
    side_a, side_b = call(
        columns_kernel,
        (flags, residual_a, residual_b, from_row_a, from_row_b, partial),
        [shape(5, block, side), shape(4, block, side)],
    )
    from_side_a, from_side_b = exchange(side_a, side_b, "py")
    partial = total_over(partial + from_side_a[-1], 2, count_py)
    basis_parts, table = call(
        prepare_kernel,
        (flags, rest_a, rest_b, from_rest_a, from_rest_b, current, stiff_tiles, mass_tiles),
        [shape(4 * count_y, 2 * prior, side, dtype=BF16)]
        + [shape(kinds, 2 * side, 2 * side, dtype=BF16)],
        cost=pl.CostEstimate(flops=10**9, bytes_accessed=0, transcendentals=0),
    )
    weighted_low, weighted_high, coupling, sent, kept = call(
        functools.partial(operators_kernel, inverse_rows),
        (
            *codes,
            flags,
            partial,
            residual_a,
            residual_b,
            from_row_a,
            from_row_b,
            from_side_a,
            from_side_b,
            rest_side_a,
            rest_side_b,
            current,
            basis_parts,
            table,
        ),
        [shape(count_y, block, side)] * 2
        + [shape(block, prior)]
        + [shape(block + 16, prior)] * 2,
        [pltpu.VMEM((4 * wide, 2 * block, 2 * side), BF16)] + code_scratch,
        plain=2,
    )
    kept = half_total(sent, kept)
    other = swap(kept[: block + 8], 1)
    (work,) = call(
        functools.partial(factor_kernel, inverse_rows),
        (kept,),
        [shape(block, 2 * block)],
        cost=pl.CostEstimate(flops=10**9, bytes_accessed=0, transcendentals=0),
    )
    new_block, factor, reduced = call(
        functools.partial(finish_kernel, inverse_rows),
        (flags, work, kept, other, weighted_low, weighted_high),
        [
            shape(block * tiles, side),
            shape(block, block),
            shape(2, block, prior + block),
        ],
    )
    return (
        new_block.reshape(previous.shape),
        coupling.T,
        factor,
        reduced.swapaxes(1, 2),
    )


def solution(mesh):
    placed = (
        P("case", "px", "py", None),
        P("case", "px", "py", None),
        P(None, "px", "py"),
        P(None, "px", "py"),
        P(),
        P(),
    )
    return jax.shard_map(
        shards,
        mesh=mesh,
        in_specs=placed,
        out_specs=(
            P("case", "px", "py", None),
            P("case", None),
            P("case", None),
            P("case", None, None),
        ),
        check_vma=False,
    )
```

```python
import functools

import jax
import jax.numpy as jnp
from jax import lax
from jax.experimental import pallas as pl
from jax.experimental.pallas import tpu as pltpu
from jax.sharding import PartitionSpec as P

F32 = jnp.float32
BF16 = jnp.bfloat16
VMEM = pl.BlockSpec(memory_space=pltpu.VMEM)
ANY = pl.BlockSpec(memory_space=pl.ANY)
MIB = 1024 * 1024


def split(value):
    high = value.astype(BF16)
    return high, (value - high.astype(F32)).astype(BF16)


def mul(left, right):
    return jnp.dot(left, right, preferred_element_type=F32)


def mul_t(left, right):
    return lax.dot_general(left, right, (((1,), (1,)), ((), ())), preferred_element_type=F32)


def mul3(left, right):
    left_high, left_low = split(left)
    right_high, right_low = split(right)
    return mul(left_high, right_high) + (mul(left_high, right_low) + mul(left_low, right_high))


def mul3_t(left, right):
    left_high, left_low = split(left)
    right_high, right_low = split(right)
    return mul_t(left_high, right_high) + (
        mul_t(left_high, right_low) + mul_t(left_low, right_high)
    )


def split_tables(stiff_ref, mass_ref, table_ref, parts_axis):
    side = stiff_ref.shape[1]
    spans = (slice(0, side), slice(side, 2 * side))
    for kind in range(stiff_ref.shape[0]):
        for matrix, ref in zip(spans, (stiff_ref, mass_ref)):
            for part, value in zip(spans, split(ref[kind])):
                if parts_axis == 1:
                    table_ref[kind, matrix, part] = value
                else:
                    table_ref[kind, part, matrix] = value


def stacked(value):
    return jnp.concatenate(split(value), axis=0)


def deep(value):
    high, low = split(value)
    upper = jnp.concatenate([high, high], axis=1)
    return jnp.concatenate([upper, jnp.concatenate([low, jnp.zeros_like(low)], axis=1)], axis=0)


def halves_sum(value):
    half = value.shape[0] // 2
    return value[:half] + value[half:]


def pair_sum(left, right_high, right_low):
    rows = left.shape[0] // 2
    return halves_sum(mul_t(left, right_high)) + mul_t(left[:rows], right_low)


def pick(flag, first, second):
    flag = flag > 0.0
    return jnp.where(flag, first, second), jnp.where(flag, second, first)


def flag_at(flags_ref, place):
    return flags_ref[place : place + 1, :]


def code_copies(code_refs, local_refs, semaphores):
    return [
        pltpu.make_async_copy(ref, local, semaphores.at[n])
        for n, (ref, local) in enumerate(zip(code_refs, local_refs))
    ]


def source_and_kind(neighbours_ref, kinds_ref, tile, k, count_y):
    neighbour = neighbours_ref[tile, k]
    down = (neighbour * 11) >> 5
    first = (tile // count_y) * (count_y + 2) + tile % count_y
    return first + neighbour + down * (count_y - 1), kinds_ref[tile, k]


def pack_kernel(flags_ref, vectors_ref, side_a_ref, side_b_ref, row_a_ref, row_b_ref):
    count_y, both, _ = row_a_ref.shape
    tiles = 2 * count_y
    odd_y, odd_x = flag_at(flags_ref, 0), flag_at(flags_ref, 1)

    first = vectors_ref.shape[0] - both * tiles

    def tile_of(i, j):
        return vectors_ref[pl.ds(first + i * count_y + j, both, stride=tiles), :]

    for i in range(2):
        side_a_ref[i], side_b_ref[i] = pick(odd_y, tile_of(i, 0), tile_of(i, count_y - 1))
    for j in range(count_y):
        row_a_ref[j], row_b_ref[j] = pick(odd_x, tile_of(0, j), tile_of(1, j))


def rest_kernel(flags_ref, vectors_ref, rest_a_ref, rest_b_ref):
    count_y, rest, _ = rest_a_ref.shape
    odd_x = flag_at(flags_ref, 1)
    for j in range(count_y):
        rest_a_ref[j], rest_b_ref[j] = pick(
            odd_x,
            vectors_ref[pl.ds(j, rest, stride=2 * count_y), :],
            vectors_ref[pl.ds(count_y + j, rest, stride=2 * count_y), :],
        )


def corners_kernel(flags_ref, side_a_ref, side_b_ref, corner_a_ref, corner_b_ref):
    odd_y, odd_x = flag_at(flags_ref, 0), flag_at(flags_ref, 1)
    ends = [pick(odd_y, side_a_ref[i], side_b_ref[i]) for i in range(2)]
    for place in range(2):
        corner_a_ref[place], corner_b_ref[place] = pick(odd_x, ends[0][place], ends[1][place])


def columns_kernel(
    flags_ref, row_a_ref, row_b_ref, from_row_a_ref, from_row_b_ref, *refs
):
    odd_y, odd_x = flag_at(flags_ref, 0), flag_at(flags_ref, 1)
    side_a_ref, side_b_ref = refs[-2:]
    columns = []
    for j in (0, row_b_ref.shape[0] - 1):
        column = list(pick(odd_x, from_row_a_ref[j], from_row_b_ref[j]))
        column[1:1] = pick(odd_x, row_a_ref[j], row_b_ref[j])
        columns.append(column)
    for i in range(4):
        side_a_ref[i], side_b_ref[i] = pick(odd_y, columns[0][i], columns[1][i])
    if len(refs) == 3:
        side_a_ref[4] = refs[0][...]


def residual_kernel(
    neighbours_hbm_ref,
    kinds_hbm_ref,
    flags_ref,
    row_a_ref,
    row_b_ref,
    from_row_a_ref,
    from_row_b_ref,
    from_side_a_ref,
    from_side_b_ref,
    from_corner_a_ref,
    from_corner_b_ref,
    rest_a_ref,
    rest_b_ref,
    stiff_ref,
    mass_ref,
    residual_a_ref,
    residual_b_ref,
    partial_ref,
    current_ref,
    ext_ref,
    table_ref,
    neighbours_ref,
    kinds_ref,
    semaphores,
):
    copies = code_copies(
        (neighbours_hbm_ref, kinds_hbm_ref), (neighbours_ref, kinds_ref), semaphores
    )
    for copy in copies:
        copy.start()
    split_tables(stiff_ref, mass_ref, table_ref, 1)
    count_y, both, side = row_a_ref.shape
    wide = count_y + 2
    block = both // 2
    rest = rest_a_ref.shape[1]
    odd_y, odd_x, in_low_y, in_high_y, in_low_x, in_high_x = (
        flag_at(flags_ref, place) for place in range(6)
    )

    def store(i, j, value):
        current_ref[i * wide + j] = value[:block]
        for part in range(2):
            high, low = split(value[part * block : (part + 1) * block])
            ext_ref[i * wide + j, :block, part * side : (part + 1) * side] = high
            ext_ref[i * wide + j, block:, part * side : (part + 1) * side] = low

    own = {}
    for j in range(count_y):
        own[0, j], own[1, j] = pick(odd_x, row_a_ref[j], row_b_ref[j])
        store(1, j + 1, own[0, j])
        store(2, j + 1, own[1, j])
        low, high = pick(odd_x, from_row_a_ref[j], from_row_b_ref[j])
        store(0, j + 1, low * in_low_x)
        store(3, j + 1, high * in_high_x)
    for i in range(2):
        low, high = pick(odd_y, from_side_a_ref[i], from_side_b_ref[i])
        store(i + 1, 0, low * in_low_y)
        store(i + 1, wide - 1, high * in_high_y)
    for place, j, inside in ((0, 0, in_low_y), (1, wide - 1, in_high_y)):
        low, high = pick(odd_x, from_corner_a_ref[place], from_corner_b_ref[place])
        store(0, j, low * (in_low_x * inside))
        store(3, j, high * (in_high_x * inside))
    for copy in copies:
        copy.wait()
    partial = jnp.zeros((block, rest + block), F32)
    totals = {}
    for tile in range(2 * count_y):
        i, j = tile // count_y, tile % count_y
        total = 4.0 * own[i, j][:block] + own[i, j][block:]
        for k in range(neighbours_ref.shape[1]):
            source, kind = source_and_kind(neighbours_ref, kinds_ref, tile, k, count_y)
            pair = mul(ext_ref[source], table_ref[kind])
            total = total + (pair[:block, :side] + (pair[block:, :side] + pair[:block, side:]))
        totals[i, j] = total
        rest_tile = pick(odd_x, rest_a_ref[j], rest_b_ref[j])[i]
        basis_tile = jnp.concatenate([rest_tile, own[i, j][:block]], axis=0)
        partial = partial + pair_sum(stacked(total), *split(basis_tile))
    for j in range(count_y):
        residual_a_ref[j], residual_b_ref[j] = pick(odd_x, totals[0, j], totals[1, j])
    residual_a_ref[count_y] = partial
    partial_ref[...] = partial


def prepare_kernel(
    flags_ref,
    rest_a_ref,
    rest_b_ref,
    from_rest_a_ref,
    from_rest_b_ref,
    current_ref,
    stiff_ref,
    mass_ref,
    basis_ref,
    turned_ref,
    table_ref,
):
    count_y, rest, _ = rest_a_ref.shape
    prior = rest + current_ref.shape[1]
    odd_x = flag_at(flags_ref, 1)
    split_tables(stiff_ref, mass_ref, table_ref, 0)
    for j in range(count_y):
        rests = list(pick(odd_x, from_rest_a_ref[j], from_rest_b_ref[j]))
        rests[1:1] = pick(odd_x, rest_a_ref[j], rest_b_ref[j])
        for i in range(4):
            tile = jnp.concatenate([rests[i], current_ref[i * (count_y + 2) + j + 1]], axis=0)
            basis_ref[i * count_y + j, :prior, :], basis_ref[i * count_y + j, prior:, :] = split(
                tile
            )
            if 0 < i < 3:
                place = (i - 1) * count_y + j
                turned_ref[place, :, :prior], turned_ref[place, :, prior:] = split(tile.T)


def operators_kernel(
    inverse_rows,
    neighbours_hbm_ref,
    kinds_hbm_ref,
    flags_ref,
    partial_ref,
    row_a_ref,
    row_b_ref,
    from_row_a_ref,
    from_row_b_ref,
    from_side_a_ref,
    from_side_b_ref,
    rest_side_a_ref,
    rest_side_b_ref,
    current_ref,
    basis_ref,
    turned_ref,
    table_ref,
    weighted_low_ref,
    weighted_high_ref,
    coupling_ref,
    sent_ref,
    kept_ref,
    ext_ref,
    neighbours_ref,
    kinds_ref,
    semaphores,
):
    copies = code_copies(
        (neighbours_hbm_ref, kinds_hbm_ref), (neighbours_ref, kinds_ref), semaphores
    )
    for copy in copies:
        copy.start()
    count_y, block, side = weighted_low_ref.shape
    wide = count_y + 2
    rest = rest_side_a_ref.shape[1]
    prior = rest + block
    odd_y, odd_x, in_low_y, in_high_y, in_low_x, in_high_x = (
        flag_at(flags_ref, place) for place in range(6)
    )
    coupling = partial_ref[...] * inverse_rows
    coupling_ref[...] = coupling
    coupling_deep = deep(coupling)

    def basis_parts(i, j):
        if 0 < j < wide - 1:
            return basis_ref[i * count_y + j - 1]
        rest_tile = pick(odd_y, rest_side_a_ref[i], rest_side_b_ref[i])[j // (wide - 1)]
        return stacked(jnp.concatenate([rest_tile, current_ref[i * wide + j]], axis=0))

    for j in range(wide):
        if 0 < j < wide - 1:
            rows = list(pick(odd_x, from_row_a_ref[j - 1], from_row_b_ref[j - 1]))
            rows[1:1] = pick(odd_x, row_a_ref[j - 1], row_b_ref[j - 1])
        else:
            rows = [
                pick(odd_y, from_side_a_ref[i], from_side_b_ref[i])[j // (wide - 1)]
                for i in range(4)
            ]
        for i in range(4):
            value = rows[i] - halves_sum(mul(coupling_deep, basis_parts(i, j)))
            if i == 0:
                value = value * in_low_x
            if i == 3:
                value = value * in_high_x
            if j == 0:
                value = value * in_low_y
            if j == wide - 1:
                value = value * in_high_y
            if 0 < i < 3 and 0 < j < wide - 1:
                (weighted_low_ref, weighted_high_ref)[i - 1][j - 1] = value
            ext_ref[i * wide + j] = deep(value)
    for copy in copies:
        copy.wait()
    with_basis = jnp.zeros((2 * block, prior), F32)
    with_own = jnp.zeros((block, 4 * block), F32)
    for tile in range(2 * count_y):
        i, j = tile // count_y, tile % count_y
        own = (weighted_low_ref, weighted_high_ref)[i][j]
        totals = jnp.concatenate([4.0 * own, own], axis=1)
        for k in range(neighbours_ref.shape[1]):
            source, kind = source_and_kind(neighbours_ref, kinds_ref, tile, k, count_y)
            totals = totals + halves_sum(mul(ext_ref[source], table_ref[kind]))
        applied = jnp.concatenate([totals[:, :side], totals[:, side:]], axis=0)
        pairs = mul(stacked(applied), turned_ref[tile])
        with_basis = with_basis + (
            halves_sum(pairs[:, :prior]) + pairs[: 2 * block, prior:]
        )
        right = jnp.concatenate([applied, own, jnp.zeros_like(own)], axis=0)
        with_own = with_own + pair_sum(stacked(own), *split(right))
    halves = [
        jnp.concatenate(
            [
                with_basis[part * block : (part + 1) * block],
                folded(with_own[:, part * block : (part + 1) * block]),
                folded(with_own[:, 2 * block : 3 * block]),
            ],
            axis=0,
        )
        for part in range(2)
    ]
    sent_ref[...], kept_ref[...] = pick(odd_y, halves[0], halves[1])


def folded(square):
    return jnp.concatenate([square[n * 8 : (n + 1) * 8] for n in range(4)], axis=1)


def unfolded(rows):
    return jnp.concatenate([rows[:, n * 32 : (n + 1) * 32] for n in range(4)], axis=0)


def factor_kernel(inverse_rows, sums_ref, work_ref):
    block = work_ref.shape[0]
    gram = unfolded(sums_ref[block + 8 :, :]) * inverse_rows
    row_ids = lax.broadcasted_iota(jnp.int32, (block, block), 0)
    column_ids = lax.broadcasted_iota(jnp.int32, (block, block), 1)
    unit = jnp.where(row_ids == column_ids, 1.0, 0.0).astype(F32)
    rest = jnp.concatenate([gram, unit], axis=1)
    group = 8
    done = []
    for j in range(0, block, group):
        rows = lax.broadcasted_iota(jnp.int32, rest.shape, 0)
        columns = [
            jnp.broadcast_to(rest[:, j + a : j + a + 1], rest.shape) for a in range(group)
        ]
        pivots = [rest[a : a + 1, :] for a in range(group)]
        for a in range(group):
            ratio = columns[a] * (1.0 / columns[a][a : a + 1, :])
            for b in range(a + 1, group):
                columns[b] = columns[b] - ratio * columns[b][a : a + 1, :]
                pivots[b] = pivots[b] - ratio[b : b + 1, :] * pivots[a]
            rest = rest - jnp.where(rows > a, ratio, 0.0) * pivots[a]
        done.append(rest[:group])
        rest = rest[group:]
    work = jnp.concatenate(done, axis=0)
    work = work * lax.rsqrt(jnp.sum(work[:, :block] * unit, axis=1, keepdims=True))
    work_ref[...] = work


def finish_kernel(
    inverse_rows,
    flags_ref,
    work_ref,
    sums_ref,
    other_ref,
    weighted_low_ref,
    weighted_high_ref,
    new_ref,
    factor_ref,
    reduced_ref,
):
    count_y, block, _ = weighted_low_ref.shape
    prior = sums_ref.shape[1]
    tiles = 2 * count_y
    row_ids = lax.broadcasted_iota(jnp.int32, (block, block), 0)
    column_ids = lax.broadcasted_iota(jnp.int32, (block, block), 1)
    factor_ref[...] = jnp.where(column_ids >= row_ids, work_ref[:, :block], 0.0)
    inverse = work_ref[:, block:]
    for tile in range(tiles):
        own = (weighted_low_ref, weighted_high_ref)[tile // count_y][tile % count_y]
        new_ref[pl.ds(tile, block, stride=tiles), :] = mul3(inverse, own)
    odd_y = flag_at(flags_ref, 0)
    halves = pick(odd_y, other_ref[...], sums_ref[: block + 8, :])
    for part, half in enumerate(halves):
        reduced_ref[part, :, :prior] = mul3(inverse, half[:block] * inverse_rows)
        own = unfolded(half[block:]) * inverse_rows
        reduced_ref[part, :, prior:] = mul3_t(mul3_t(inverse, own), inverse)


def swap(value, mask):
    axes = ("px", "py")
    pairs = [(i, i ^ mask) for i in range(lax.axis_size(axes))]
    return lax.ppermute(value, axes, pairs)


def exchange(message_a, message_b, axis):
    cases, count = lax.axis_size("case"), lax.axis_size(axis)
    near = [(i, i ^ 1) for i in range(count)]
    pairs = []
    for case in range(cases):
        for i in range(count):
            j = ((i + 1) ^ 1) - 1
            target = (case, j) if 0 <= j < count else ((case ^ 1) % cases, i)
            pairs.append((case * count + i, target[0] * count + target[1]))
    return lax.ppermute(message_a, axis, near), lax.ppermute(message_b, ("case", axis), pairs)


def total_over(value, first, last):
    while first < last:
        value = value + swap(value, first)
        first *= 2
    return value


def half_total(sent, kept):
    kept = kept + swap(sent, 1)
    kept = (kept + swap(kept, 6)) + (swap(kept, 2) + swap(kept, 4))
    return total_over(kept, 8, lax.axis_size(("px", "py")))


def shape(*dims, dtype=F32):
    return jax.ShapeDtypeStruct(dims, dtype)


def shards(prior_basis, previous, neighbours, tile_kinds, stiff_tiles, mass_tiles):
    block = previous.shape[0]
    prior, count_x, count_y, side = prior_basis.shape
    tiles = count_x * count_y
    wide = count_y + 2
    rest = prior - block
    kinds = stiff_tiles.shape[0]
    inverse_rows = 1.0 / (tiles * side * lax.axis_size("px") * lax.axis_size("py"))
    basis = prior_basis.reshape(-1, side)
    vectors = jnp.concatenate([basis, previous.reshape(-1, side)], axis=0)
    codes = [array.transpose(1, 2, 0).reshape(tiles, -1) for array in (neighbours, tile_kinds)]
    code_scratch = [pltpu.SMEM(array.shape, jnp.int32) for array in codes]
    code_scratch += [pltpu.SemaphoreType.DMA((2,))]
    at_y, at_x = lax.axis_index("py"), lax.axis_index("px")
    bits = (at_y & 1) + 2 * (at_x & 1)
    bits += 4 * (at_y > 0) + 8 * (at_y < lax.axis_size("py") - 1)
    bits += 16 * (at_x > 0) + 32 * (at_x < lax.axis_size("px") - 1)
    flags = ((bits >> lax.broadcasted_iota(jnp.int32, (8, side), 0)) & 1).astype(F32)

    def call(kernel, inputs, outputs, scratch=(), plain=0, limit=8, cost=None):
        specs = [ANY] * plain + [VMEM] * (len(inputs) - plain)
        return pl.pallas_call(
            kernel,
            out_shape=outputs,
            in_specs=specs,
            out_specs=[VMEM] * len(outputs),
            scratch_shapes=scratch,
            compiler_params=pltpu.CompilerParams(vmem_limit_bytes=limit * MIB),
            cost_estimate=cost,
        )(*inputs)

    side_a, side_b, row_a, row_b = call(
        pack_kernel,
        (flags, vectors),
        [shape(count_x, 2 * block, side)] * 2 + [shape(count_y, 2 * block, side)] * 2,
    )
    rest_a, rest_b = call(rest_kernel, (flags, vectors), [shape(count_y, rest, side)] * 2)
    from_side_a, from_side_b = exchange(side_a, side_b, "py")
    from_row_a, from_row_b = exchange(row_a, row_b, "px")
    from_side_a, rest_a, rest_b = lax.optimization_barrier((from_side_a, rest_a, rest_b))
    from_rest_a, from_rest_b = exchange(rest_a, rest_b, "px")
    corner_a, corner_b = call(
        corners_kernel,
        (flags, from_side_a, from_side_b),
        [shape(2, 2 * block, side)] * 2,
    )
    from_corner_a, from_corner_b = exchange(corner_a, corner_b, "px")
    rest_side_a, rest_side_b = call(
        columns_kernel,
        (flags, rest_a, rest_b, from_rest_a, from_rest_b),
        [shape(4, rest, side)] * 2,
    )
    rest_side_a, rest_side_b = exchange(rest_side_a, rest_side_b, "py")
    residual_a, residual_b, partial, current = call(
        residual_kernel,
        (
            *codes,
            flags,
            row_a,
            row_b,
            from_row_a,
            from_row_b,
            from_side_a,
            from_side_b,
            from_corner_a,
            from_corner_b,
            rest_a,
            rest_b,
            stiff_tiles,
            mass_tiles,
        ),
        [shape(count_y + 1, block, side), shape(count_y, block, side)]
        + [shape(block, prior), shape(4 * wide, block, side)],
        [pltpu.VMEM((4 * wide, 2 * block, 2 * side), BF16)]
        + [pltpu.VMEM((kinds, 2 * side, 2 * side), BF16)]
        + code_scratch,
        plain=2,
        cost=pl.CostEstimate(flops=10**9, bytes_accessed=0, transcendentals=0),
    )
    count_py = lax.axis_size("py")
    from_row_a, from_row_b = exchange(residual_a, residual_b, "px")
    partial = total_over(
        partial + from_row_a[-1], 2 * count_py, count_py * lax.axis_size("px")
    )
    partial, rest_side_a, rest_side_b = lax.optimization_barrier(
        (partial, rest_side_a, rest_side_b)
    )
    side_a, side_b = call(
        columns_kernel,
        (flags, residual_a, residual_b, from_row_a, from_row_b, partial),
        [shape(5, block, side), shape(4, block, side)],
    )
    from_side_a, from_side_b = exchange(side_a, side_b, "py")
    partial = total_over(partial + from_side_a[-1], 2, count_py)
    basis_parts, turned, table = call(
        prepare_kernel,
        (flags, rest_a, rest_b, from_rest_a, from_rest_b, current, stiff_tiles, mass_tiles),
        [shape(4 * count_y, 2 * prior, side, dtype=BF16)]
        + [shape(tiles, side, 2 * prior, dtype=BF16)]
        + [shape(kinds, 2 * side, 2 * side, dtype=BF16)],
        cost=pl.CostEstimate(flops=10**9, bytes_accessed=0, transcendentals=0),
    )
    weighted_low, weighted_high, coupling, sent, kept = call(
        functools.partial(operators_kernel, inverse_rows),
        (
            *codes,
            flags,
            partial,
            residual_a,
            residual_b,
            from_row_a,
            from_row_b,
            from_side_a,
            from_side_b,
            rest_side_a,
            rest_side_b,
            current,
            basis_parts,
            turned,
            table,
        ),
        [shape(count_y, block, side)] * 2
        + [shape(block, prior)]
        + [shape(block + 16, prior)] * 2,
        [pltpu.VMEM((4 * wide, 2 * block, 2 * side), BF16)] + code_scratch,
        plain=2,
    )
    kept = half_total(sent, kept)
    other = swap(kept[: block + 8], 1)
    (work,) = call(
        functools.partial(factor_kernel, inverse_rows),
        (kept,),
        [shape(block, 2 * block)],
        cost=pl.CostEstimate(flops=10**9, bytes_accessed=0, transcendentals=0),
    )
    new_block, factor, reduced = call(
        functools.partial(finish_kernel, inverse_rows),
        (flags, work, kept, other, weighted_low, weighted_high),
        [
            shape(block * tiles, side),
            shape(block, block),
            shape(2, block, prior + block),
        ],
    )
    return (
        new_block.reshape(previous.shape),
        coupling.T,
        factor,
        reduced.swapaxes(1, 2),
    )


def solution(mesh):
    placed = (
        P("case", "px", "py", None),
        P("case", "px", "py", None),
        P(None, "px", "py"),
        P(None, "px", "py"),
        P(),
        P(),
    )
    return jax.shard_map(
        shards,
        mesh=mesh,
        in_specs=placed,
        out_specs=(
            P("case", "px", "py", None),
            P("case", None),
            P("case", None),
            P("case", None, None),
        ),
        check_vma=False,
    )
```

```python
import functools

import jax
import jax.numpy as jnp
from jax import lax
from jax.experimental import pallas as pl
from jax.experimental.pallas import tpu as pltpu
from jax.sharding import PartitionSpec as P

F32 = jnp.float32
BF16 = jnp.bfloat16
VMEM = pl.BlockSpec(memory_space=pltpu.VMEM)
ANY = pl.BlockSpec(memory_space=pl.ANY)
MIB = 1024 * 1024


def split(value):
    high = value.astype(BF16)
    return high, (value - high.astype(F32)).astype(BF16)


def mul(left, right):
    return jnp.dot(left, right, preferred_element_type=F32)


def mul_t(left, right):
    return lax.dot_general(left, right, (((1,), (1,)), ((), ())), preferred_element_type=F32)


def mul3(left, right):
    left_high, left_low = split(left)
    right_high, right_low = split(right)
    return mul(left_high, right_high) + (mul(left_high, right_low) + mul(left_low, right_high))


def mul3_t(left, right):
    left_high, left_low = split(left)
    right_high, right_low = split(right)
    return mul_t(left_high, right_high) + (
        mul_t(left_high, right_low) + mul_t(left_low, right_high)
    )


def split_tables(stiff_ref, mass_ref, table_ref, parts_axis):
    side = stiff_ref.shape[1]
    spans = (slice(0, side), slice(side, 2 * side))
    for kind in range(stiff_ref.shape[0]):
        for matrix, ref in zip(spans, (stiff_ref, mass_ref)):
            for part, value in zip(spans, split(ref[kind])):
                if parts_axis == 1:
                    table_ref[kind, matrix, part] = value
                else:
                    table_ref[kind, part, matrix] = value


def stacked(value):
    return jnp.concatenate(split(value), axis=0)


def deep(value):
    high, low = split(value)
    upper = jnp.concatenate([high, high], axis=1)
    return jnp.concatenate([upper, jnp.concatenate([low, jnp.zeros_like(low)], axis=1)], axis=0)


def halves_sum(value):
    half = value.shape[0] // 2
    return value[:half] + value[half:]


def mul_deep(left_deep, right):
    return halves_sum(mul(left_deep, stacked(right)))


def pair_sum(left, right_high, right_low):
    rows = left.shape[0] // 2
    return halves_sum(mul_t(left, right_high)) + mul_t(left[:rows], right_low)


def pick(flag, first, second):
    flag = flag > 0.0
    return jnp.where(flag, first, second), jnp.where(flag, second, first)


def flag_at(flags_ref, place):
    return flags_ref[place : place + 1, :]


def code_copies(code_refs, local_refs, semaphores):
    return [
        pltpu.make_async_copy(ref, local, semaphores.at[n])
        for n, (ref, local) in enumerate(zip(code_refs, local_refs))
    ]


def source_and_kind(neighbours_ref, kinds_ref, tile, k, count_y):
    neighbour = neighbours_ref[tile, k]
    down = (neighbour * 11) >> 5
    first = (tile // count_y) * (count_y + 2) + tile % count_y
    return first + neighbour + down * (count_y - 1), kinds_ref[tile, k]


def pack_kernel(flags_ref, vectors_ref, side_a_ref, side_b_ref, row_a_ref, row_b_ref):
    count_y, both, _ = row_a_ref.shape
    tiles = 2 * count_y
    odd_y, odd_x = flag_at(flags_ref, 0), flag_at(flags_ref, 1)

    first = vectors_ref.shape[0] - both * tiles

    def tile_of(i, j):
        return vectors_ref[pl.ds(first + i * count_y + j, both, stride=tiles), :]

    for i in range(2):
        side_a_ref[i], side_b_ref[i] = pick(odd_y, tile_of(i, 0), tile_of(i, count_y - 1))
    for j in range(count_y):
        row_a_ref[j], row_b_ref[j] = pick(odd_x, tile_of(0, j), tile_of(1, j))


def rest_kernel(flags_ref, vectors_ref, rest_a_ref, rest_b_ref):
    count_y, rest, _ = rest_a_ref.shape
    odd_x = flag_at(flags_ref, 1)
    for j in range(count_y):
        rest_a_ref[j], rest_b_ref[j] = pick(
            odd_x,
            vectors_ref[pl.ds(j, rest, stride=2 * count_y), :],
            vectors_ref[pl.ds(count_y + j, rest, stride=2 * count_y), :],
        )


def corners_kernel(flags_ref, side_a_ref, side_b_ref, corner_a_ref, corner_b_ref):
    odd_y, odd_x = flag_at(flags_ref, 0), flag_at(flags_ref, 1)
    ends = [pick(odd_y, side_a_ref[i], side_b_ref[i]) for i in range(2)]
    for place in range(2):
        corner_a_ref[place], corner_b_ref[place] = pick(odd_x, ends[0][place], ends[1][place])


def columns_kernel(
    flags_ref, row_a_ref, row_b_ref, from_row_a_ref, from_row_b_ref, *refs
):
    odd_y, odd_x = flag_at(flags_ref, 0), flag_at(flags_ref, 1)
    side_a_ref, side_b_ref = refs[-2:]
    columns = []
    for j in (0, row_b_ref.shape[0] - 1):
        column = list(pick(odd_x, from_row_a_ref[j], from_row_b_ref[j]))
        column[1:1] = pick(odd_x, row_a_ref[j], row_b_ref[j])
        columns.append(column)
    for i in range(4):
        side_a_ref[i], side_b_ref[i] = pick(odd_y, columns[0][i], columns[1][i])
    if len(refs) == 3:
        side_a_ref[4] = refs[0][...]


def residual_kernel(
    neighbours_hbm_ref,
    kinds_hbm_ref,
    flags_ref,
    row_a_ref,
    row_b_ref,
    from_row_a_ref,
    from_row_b_ref,
    from_side_a_ref,
    from_side_b_ref,
    from_corner_a_ref,
    from_corner_b_ref,
    rest_a_ref,
    rest_b_ref,
    stiff_ref,
    mass_ref,
    residual_a_ref,
    residual_b_ref,
    partial_ref,
    current_ref,
    ext_ref,
    table_ref,
    neighbours_ref,
    kinds_ref,
    semaphores,
):
    copies = code_copies(
        (neighbours_hbm_ref, kinds_hbm_ref), (neighbours_ref, kinds_ref), semaphores
    )
    for copy in copies:
        copy.start()
    split_tables(stiff_ref, mass_ref, table_ref, 1)
    count_y, both, side = row_a_ref.shape
    wide = count_y + 2
    block = both // 2
    rest = rest_a_ref.shape[1]
    odd_y, odd_x, in_low_y, in_high_y, in_low_x, in_high_x = (
        flag_at(flags_ref, place) for place in range(6)
    )

    def store(i, j, value):
        current_ref[i * wide + j] = value[:block]
        for part in range(2):
            high, low = split(value[part * block : (part + 1) * block])
            ext_ref[i * wide + j, :block, part * side : (part + 1) * side] = high
            ext_ref[i * wide + j, block:, part * side : (part + 1) * side] = low

    own = {}
    for j in range(count_y):
        own[0, j], own[1, j] = pick(odd_x, row_a_ref[j], row_b_ref[j])
        store(1, j + 1, own[0, j])
        store(2, j + 1, own[1, j])
        low, high = pick(odd_x, from_row_a_ref[j], from_row_b_ref[j])
        store(0, j + 1, low * in_low_x)
        store(3, j + 1, high * in_high_x)
    for i in range(2):
        low, high = pick(odd_y, from_side_a_ref[i], from_side_b_ref[i])
        store(i + 1, 0, low * in_low_y)
        store(i + 1, wide - 1, high * in_high_y)
    for place, j, inside in ((0, 0, in_low_y), (1, wide - 1, in_high_y)):
        low, high = pick(odd_x, from_corner_a_ref[place], from_corner_b_ref[place])
        store(0, j, low * (in_low_x * inside))
        store(3, j, high * (in_high_x * inside))
    for copy in copies:
        copy.wait()
    partial = jnp.zeros((block, rest + block), F32)
    totals = {}
    for tile in range(2 * count_y):
        i, j = tile // count_y, tile % count_y
        total = 4.0 * own[i, j][:block] + own[i, j][block:]
        for k in range(neighbours_ref.shape[1]):
            source, kind = source_and_kind(neighbours_ref, kinds_ref, tile, k, count_y)
            pair = mul(ext_ref[source], table_ref[kind])
            total = total + (pair[:block, :side] + (pair[block:, :side] + pair[:block, side:]))
        totals[i, j] = total
        rest_tile = pick(odd_x, rest_a_ref[j], rest_b_ref[j])[i]
        basis_tile = jnp.concatenate([rest_tile, own[i, j][:block]], axis=0)
        partial = partial + pair_sum(stacked(total), *split(basis_tile))
    for j in range(count_y):
        residual_a_ref[j], residual_b_ref[j] = pick(odd_x, totals[0, j], totals[1, j])
    residual_a_ref[count_y] = partial
    partial_ref[...] = partial


def prepare_kernel(
    flags_ref,
    rest_a_ref,
    rest_b_ref,
    from_rest_a_ref,
    from_rest_b_ref,
    current_ref,
    stiff_ref,
    mass_ref,
    basis_ref,
    table_ref,
):
    count_y, rest, _ = rest_a_ref.shape
    prior = rest + current_ref.shape[1]
    odd_x = flag_at(flags_ref, 1)
    split_tables(stiff_ref, mass_ref, table_ref, 0)
    for j in range(count_y):
        rests = list(pick(odd_x, from_rest_a_ref[j], from_rest_b_ref[j]))
        rests[1:1] = pick(odd_x, rest_a_ref[j], rest_b_ref[j])
        for i in range(4):
            tile = jnp.concatenate([rests[i], current_ref[i * (count_y + 2) + j + 1]], axis=0)
            basis_ref[i * count_y + j, :prior, :], basis_ref[i * count_y + j, prior:, :] = split(
                tile
            )


def operators_kernel(
    inverse_rows,
    neighbours_hbm_ref,
    kinds_hbm_ref,
    flags_ref,
    partial_ref,
    row_a_ref,
    row_b_ref,
    from_row_a_ref,
    from_row_b_ref,
    from_side_a_ref,
    from_side_b_ref,
    rest_side_a_ref,
    rest_side_b_ref,
    current_ref,
    basis_ref,
    table_ref,
    weighted_low_ref,
    weighted_high_ref,
    coupling_ref,
    sent_ref,
    kept_ref,
    ext_ref,
    neighbours_ref,
    kinds_ref,
    semaphores,
):
    copies = code_copies(
        (neighbours_hbm_ref, kinds_hbm_ref), (neighbours_ref, kinds_ref), semaphores
    )
    for copy in copies:
        copy.start()
    count_y, block, side = weighted_low_ref.shape
    wide = count_y + 2
    rest = rest_side_a_ref.shape[1]
    prior = rest + block
    odd_y, odd_x, in_low_y, in_high_y, in_low_x, in_high_x = (
        flag_at(flags_ref, place) for place in range(6)
    )
    coupling = partial_ref[...] * inverse_rows
    coupling_ref[...] = coupling
    coupling_deep = deep(coupling)

    def basis_parts(i, j):
        if 0 < j < wide - 1:
            return basis_ref[i * count_y + j - 1]
        rest_tile = pick(odd_y, rest_side_a_ref[i], rest_side_b_ref[i])[j // (wide - 1)]
        return stacked(jnp.concatenate([rest_tile, current_ref[i * wide + j]], axis=0))

    for j in range(wide):
        if 0 < j < wide - 1:
            rows = list(pick(odd_x, from_row_a_ref[j - 1], from_row_b_ref[j - 1]))
            rows[1:1] = pick(odd_x, row_a_ref[j - 1], row_b_ref[j - 1])
        else:
            rows = [
                pick(odd_y, from_side_a_ref[i], from_side_b_ref[i])[j // (wide - 1)]
                for i in range(4)
            ]
        for i in range(4):
            value = rows[i] - halves_sum(mul(coupling_deep, basis_parts(i, j)))
            if i == 0:
                value = value * in_low_x
            if i == 3:
                value = value * in_high_x
            if j == 0:
                value = value * in_low_y
            if j == wide - 1:
                value = value * in_high_y
            if 0 < i < 3 and 0 < j < wide - 1:
                (weighted_low_ref, weighted_high_ref)[i - 1][j - 1] = value
            ext_ref[i * wide + j] = deep(value)
    for copy in copies:
        copy.wait()
    with_basis = jnp.zeros((2 * block, prior), F32)
    with_own = jnp.zeros((block, 4 * block), F32)
    for tile in range(2 * count_y):
        i, j = tile // count_y, tile % count_y
        own = (weighted_low_ref, weighted_high_ref)[i][j]
        totals = jnp.concatenate([4.0 * own, own], axis=1)
        for k in range(neighbours_ref.shape[1]):
            source, kind = source_and_kind(neighbours_ref, kinds_ref, tile, k, count_y)
            totals = totals + halves_sum(mul(ext_ref[source], table_ref[kind]))
        applied = jnp.concatenate([totals[:, :side], totals[:, side:]], axis=0)
        basis_tile = basis_parts(i + 1, j + 1)
        with_basis = with_basis + pair_sum(
            stacked(applied), basis_tile[:prior], basis_tile[prior:]
        )
        right = jnp.concatenate([applied, own, jnp.zeros_like(own)], axis=0)
        with_own = with_own + pair_sum(stacked(own), *split(right))
    halves = [
        jnp.concatenate(
            [
                with_basis[part * block : (part + 1) * block],
                folded(with_own[:, part * block : (part + 1) * block]),
                folded(with_own[:, 2 * block : 3 * block]),
            ],
            axis=0,
        )
        for part in range(2)
    ]
    sent_ref[...], kept_ref[...] = pick(odd_y, halves[0], halves[1])


def folded(square):
    return jnp.concatenate([square[n * 8 : (n + 1) * 8] for n in range(4)], axis=1)


def unfolded(rows):
    return jnp.concatenate([rows[:, n * 32 : (n + 1) * 32] for n in range(4)], axis=0)


def factor_kernel(inverse_rows, sums_ref, work_ref):
    block = work_ref.shape[0]
    gram = unfolded(sums_ref[block + 8 :, :]) * inverse_rows
    row_ids = lax.broadcasted_iota(jnp.int32, (block, block), 0)
    column_ids = lax.broadcasted_iota(jnp.int32, (block, block), 1)
    unit = jnp.where(row_ids == column_ids, 1.0, 0.0).astype(F32)
    rest = jnp.concatenate([gram, unit], axis=1)
    group = 8
    done = []
    for j in range(0, block, group):
        rows = lax.broadcasted_iota(jnp.int32, rest.shape, 0)
        columns = [
            jnp.broadcast_to(rest[:, j + a : j + a + 1], rest.shape) for a in range(group)
        ]
        pivots = [rest[a : a + 1, :] for a in range(group)]
        for a in range(group):
            ratio = columns[a] * (1.0 / columns[a][a : a + 1, :])
            for b in range(a + 1, group):
                columns[b] = columns[b] - ratio * columns[b][a : a + 1, :]
                pivots[b] = pivots[b] - ratio[b : b + 1, :] * pivots[a]
            rest = rest - jnp.where(rows > a, ratio, 0.0) * pivots[a]
        done.append(rest[:group])
        rest = rest[group:]
    work = jnp.concatenate(done, axis=0)
    work = work * lax.rsqrt(jnp.sum(work[:, :block] * unit, axis=1, keepdims=True))
    work_ref[...] = work


def finish_kernel(
    inverse_rows,
    flags_ref,
    work_ref,
    sums_ref,
    other_ref,
    weighted_low_ref,
    weighted_high_ref,
    new_ref,
    factor_ref,
    reduced_ref,
):
    count_y, block, _ = weighted_low_ref.shape
    prior = sums_ref.shape[1]
    tiles = 2 * count_y
    row_ids = lax.broadcasted_iota(jnp.int32, (block, block), 0)
    column_ids = lax.broadcasted_iota(jnp.int32, (block, block), 1)
    factor_ref[...] = jnp.where(column_ids >= row_ids, work_ref[:, :block], 0.0)
    inverse = work_ref[:, block:]
    inverse_deep = deep(inverse)
    for tile in range(tiles):
        own = (weighted_low_ref, weighted_high_ref)[tile // count_y][tile % count_y]
        new_ref[pl.ds(tile, block, stride=tiles), :] = mul_deep(inverse_deep, own)
    odd_y = flag_at(flags_ref, 0)
    halves = pick(odd_y, other_ref[...], sums_ref[: block + 8, :])
    for part, half in enumerate(halves):
        reduced_ref[part, :, :prior] = mul_deep(inverse_deep, half[:block] * inverse_rows)
        own = unfolded(half[block:]) * inverse_rows
        reduced_ref[part, :, prior:] = mul3_t(mul3_t(inverse, own), inverse)


def swap(value, mask):
    axes = ("px", "py")
    pairs = [(i, i ^ mask) for i in range(lax.axis_size(axes))]
    return lax.ppermute(value, axes, pairs)


def exchange(message_a, message_b, axis):
    cases, count = lax.axis_size("case"), lax.axis_size(axis)
    near = [(i, i ^ 1) for i in range(count)]
    pairs = []
    for case in range(cases):
        for i in range(count):
            j = ((i + 1) ^ 1) - 1
            target = (case, j) if 0 <= j < count else ((case ^ 1) % cases, i)
            pairs.append((case * count + i, target[0] * count + target[1]))
    return lax.ppermute(message_a, axis, near), lax.ppermute(message_b, ("case", axis), pairs)


def total_over(value, first, last):
    while first < last:
        value = value + swap(value, first)
        first *= 2
    return value


def half_total(sent, kept):
    kept = kept + swap(sent, 1)
    kept = (kept + swap(kept, 6)) + (swap(kept, 2) + swap(kept, 4))
    return total_over(kept, 8, lax.axis_size(("px", "py")))


def shape(*dims, dtype=F32):
    return jax.ShapeDtypeStruct(dims, dtype)


def shards(prior_basis, previous, neighbours, tile_kinds, stiff_tiles, mass_tiles):
    block = previous.shape[0]
    prior, count_x, count_y, side = prior_basis.shape
    tiles = count_x * count_y
    wide = count_y + 2
    rest = prior - block
    kinds = stiff_tiles.shape[0]
    inverse_rows = 1.0 / (tiles * side * lax.axis_size("px") * lax.axis_size("py"))
    basis = prior_basis.reshape(-1, side)
    vectors = jnp.concatenate([basis, previous.reshape(-1, side)], axis=0)
    codes = [array.transpose(1, 2, 0).reshape(tiles, -1) for array in (neighbours, tile_kinds)]
    code_scratch = [pltpu.SMEM(array.shape, jnp.int32) for array in codes]
    code_scratch += [pltpu.SemaphoreType.DMA((2,))]
    at_y, at_x = lax.axis_index("py"), lax.axis_index("px")
    bits = (at_y & 1) + 2 * (at_x & 1)
    bits += 4 * (at_y > 0) + 8 * (at_y < lax.axis_size("py") - 1)
    bits += 16 * (at_x > 0) + 32 * (at_x < lax.axis_size("px") - 1)
    flags = ((bits >> lax.broadcasted_iota(jnp.int32, (8, side), 0)) & 1).astype(F32)

    def call(kernel, inputs, outputs, scratch=(), plain=0, limit=8, cost=None):
        specs = [ANY] * plain + [VMEM] * (len(inputs) - plain)
        return pl.pallas_call(
            kernel,
            out_shape=outputs,
            in_specs=specs,
            out_specs=[VMEM] * len(outputs),
            scratch_shapes=scratch,
            compiler_params=pltpu.CompilerParams(vmem_limit_bytes=limit * MIB),
            cost_estimate=cost,
        )(*inputs)

    side_a, side_b, row_a, row_b = call(
        pack_kernel,
        (flags, vectors),
        [shape(count_x, 2 * block, side)] * 2 + [shape(count_y, 2 * block, side)] * 2,
    )
    rest_a, rest_b = call(rest_kernel, (flags, vectors), [shape(count_y, rest, side)] * 2)
    from_side_a, from_side_b = exchange(side_a, side_b, "py")
    from_row_a, from_row_b = exchange(row_a, row_b, "px")
    from_side_a, rest_a, rest_b = lax.optimization_barrier((from_side_a, rest_a, rest_b))
    from_rest_a, from_rest_b = exchange(rest_a, rest_b, "px")
    corner_a, corner_b = call(
        corners_kernel,
        (flags, from_side_a, from_side_b),
        [shape(2, 2 * block, side)] * 2,
    )
    from_corner_a, from_corner_b = exchange(corner_a, corner_b, "px")
    rest_side_a, rest_side_b = call(
        columns_kernel,
        (flags, rest_a, rest_b, from_rest_a, from_rest_b),
        [shape(4, rest, side)] * 2,
    )
    rest_side_a, rest_side_b = exchange(rest_side_a, rest_side_b, "py")
    residual_a, residual_b, partial, current = call(
        residual_kernel,
        (
            *codes,
            flags,
            row_a,
            row_b,
            from_row_a,
            from_row_b,
            from_side_a,
            from_side_b,
            from_corner_a,
            from_corner_b,
            rest_a,
            rest_b,
            stiff_tiles,
            mass_tiles,
        ),
        [shape(count_y + 1, block, side), shape(count_y, block, side)]
        + [shape(block, prior), shape(4 * wide, block, side)],
        [pltpu.VMEM((4 * wide, 2 * block, 2 * side), BF16)]
        + [pltpu.VMEM((kinds, 2 * side, 2 * side), BF16)]
        + code_scratch,
        plain=2,
        cost=pl.CostEstimate(flops=10**9, bytes_accessed=0, transcendentals=0),
    )
    count_py = lax.axis_size("py")
    from_row_a, from_row_b = exchange(residual_a, residual_b, "px")
    partial = total_over(
        partial + from_row_a[-1], 2 * count_py, count_py * lax.axis_size("px")
    )
    partial, rest_side_a, rest_side_b = lax.optimization_barrier(
        (partial, rest_side_a, rest_side_b)
    )
    side_a, side_b = call(
        columns_kernel,
        (flags, residual_a, residual_b, from_row_a, from_row_b, partial),
        [shape(5, block, side), shape(4, block, side)],
    )
    from_side_a, from_side_b = exchange(side_a, side_b, "py")
    partial = total_over(partial + from_side_a[-1], 2, count_py)
    basis_parts, table = call(
        prepare_kernel,
        (flags, rest_a, rest_b, from_rest_a, from_rest_b, current, stiff_tiles, mass_tiles),
        [shape(4 * count_y, 2 * prior, side, dtype=BF16)]
        + [shape(kinds, 2 * side, 2 * side, dtype=BF16)],
        cost=pl.CostEstimate(flops=10**9, bytes_accessed=0, transcendentals=0),
    )
    weighted_low, weighted_high, coupling, sent, kept = call(
        functools.partial(operators_kernel, inverse_rows),
        (
            *codes,
            flags,
            partial,
            residual_a,
            residual_b,
            from_row_a,
            from_row_b,
            from_side_a,
            from_side_b,
            rest_side_a,
            rest_side_b,
            current,
            basis_parts,
            table,
        ),
        [shape(count_y, block, side)] * 2
        + [shape(block, prior)]
        + [shape(block + 16, prior)] * 2,
        [pltpu.VMEM((4 * wide, 2 * block, 2 * side), BF16)] + code_scratch,
        plain=2,
    )
    kept = half_total(sent, kept)
    other = swap(kept[: block + 8], 1)
    (work,) = call(
        functools.partial(factor_kernel, inverse_rows),
        (kept,),
        [shape(block, 2 * block)],
        cost=pl.CostEstimate(flops=10**9, bytes_accessed=0, transcendentals=0),
    )
    new_block, factor, reduced = call(
        functools.partial(finish_kernel, inverse_rows),
        (flags, work, kept, other, weighted_low, weighted_high),
        [
            shape(block * tiles, side),
            shape(block, block),
            shape(2, block, prior + block),
        ],
    )
    return (
        new_block.reshape(previous.shape),
        coupling.T,
        factor,
        reduced.swapaxes(1, 2),
    )


def solution(mesh):
    placed = (
        P("case", "px", "py", None),
        P("case", "px", "py", None),
        P(None, "px", "py"),
        P(None, "px", "py"),
        P(),
        P(),
    )
    return jax.shard_map(
        shards,
        mesh=mesh,
        in_specs=placed,
        out_specs=(
            P("case", "px", "py", None),
            P("case", None),
            P("case", None),
            P("case", None, None),
        ),
        check_vma=False,
    )
```

```python
import functools

import jax
import jax.numpy as jnp
from jax import lax
from jax.experimental import pallas as pl
from jax.experimental.pallas import tpu as pltpu
from jax.sharding import PartitionSpec as P

F32 = jnp.float32
BF16 = jnp.bfloat16
VMEM = pl.BlockSpec(memory_space=pltpu.VMEM)
ANY = pl.BlockSpec(memory_space=pl.ANY)
MIB = 1024 * 1024


def split(value):
    high = value.astype(BF16)
    return high, (value - high.astype(F32)).astype(BF16)


def mul(left, right):
    return jnp.dot(left, right, preferred_element_type=F32)


def mul_t(left, right):
    return lax.dot_general(left, right, (((1,), (1,)), ((), ())), preferred_element_type=F32)


def mul3(left, right):
    left_high, left_low = split(left)
    right_high, right_low = split(right)
    return mul(left_high, right_high) + (mul(left_high, right_low) + mul(left_low, right_high))


def mul3_t(left, right):
    left_high, left_low = split(left)
    right_high, right_low = split(right)
    return mul_t(left_high, right_high) + (
        mul_t(left_high, right_low) + mul_t(left_low, right_high)
    )


def split_tables(stiff_ref, mass_ref, table_ref, parts_axis):
    side = stiff_ref.shape[1]
    spans = (slice(0, side), slice(side, 2 * side))
    for kind in range(stiff_ref.shape[0]):
        for matrix, ref in zip(spans, (stiff_ref, mass_ref)):
            for part, value in zip(spans, split(ref[kind])):
                if parts_axis == 1:
                    table_ref[kind, matrix, part] = value
                else:
                    table_ref[kind, part, matrix] = value


def stacked(value):
    return jnp.concatenate(split(value), axis=0)


def deep(value):
    high, low = split(value)
    upper = jnp.concatenate([high, high], axis=1)
    return jnp.concatenate([upper, jnp.concatenate([low, jnp.zeros_like(low)], axis=1)], axis=0)


def halves_sum(value):
    half = value.shape[0] // 2
    return value[:half] + value[half:]


def mul_deep(left_deep, right):
    return halves_sum(mul(left_deep, stacked(right)))


def pair_sum(left, right_high, right_low):
    rows = left.shape[0] // 2
    return halves_sum(mul_t(left, right_high)) + mul_t(left[:rows], right_low)


def pick(flag, first, second):
    flag = flag > 0.0
    return jnp.where(flag, first, second), jnp.where(flag, second, first)


def flag_at(flags_ref, place):
    return flags_ref[place : place + 1, :]


def code_copies(code_refs, local_refs, semaphores):
    return [
        pltpu.make_async_copy(ref, local, semaphores.at[n])
        for n, (ref, local) in enumerate(zip(code_refs, local_refs))
    ]


def source_and_kind(neighbours_ref, kinds_ref, tile, k, count_y):
    neighbour = neighbours_ref[tile, k]
    down = (neighbour * 11) >> 5
    first = (tile // count_y) * (count_y + 2) + tile % count_y
    return first + neighbour + down * (count_y - 1), kinds_ref[tile, k]


def pack_kernel(flags_ref, vectors_ref, side_a_ref, side_b_ref, row_a_ref, row_b_ref):
    count_y, both, _ = row_a_ref.shape
    tiles = 2 * count_y
    odd_y, odd_x = flag_at(flags_ref, 0), flag_at(flags_ref, 1)

    first = vectors_ref.shape[0] - both * tiles

    def tile_of(i, j):
        return vectors_ref[pl.ds(first + i * count_y + j, both, stride=tiles), :]

    for i in range(2):
        side_a_ref[i], side_b_ref[i] = pick(odd_y, tile_of(i, 0), tile_of(i, count_y - 1))
    for j in range(count_y):
        row_a_ref[j], row_b_ref[j] = pick(odd_x, tile_of(0, j), tile_of(1, j))


def rest_kernel(flags_ref, vectors_ref, rest_a_ref, rest_b_ref):
    count_y, rest, _ = rest_a_ref.shape
    odd_x = flag_at(flags_ref, 1)
    for j in range(count_y):
        rest_a_ref[j], rest_b_ref[j] = pick(
            odd_x,
            vectors_ref[pl.ds(j, rest, stride=2 * count_y), :],
            vectors_ref[pl.ds(count_y + j, rest, stride=2 * count_y), :],
        )


def corners_kernel(flags_ref, side_a_ref, side_b_ref, corner_a_ref, corner_b_ref):
    odd_y, odd_x = flag_at(flags_ref, 0), flag_at(flags_ref, 1)
    ends = [pick(odd_y, side_a_ref[i], side_b_ref[i]) for i in range(2)]
    for place in range(2):
        corner_a_ref[place], corner_b_ref[place] = pick(odd_x, ends[0][place], ends[1][place])


def columns_kernel(
    flags_ref, row_a_ref, row_b_ref, from_row_a_ref, from_row_b_ref, *refs
):
    odd_y, odd_x = flag_at(flags_ref, 0), flag_at(flags_ref, 1)
    side_a_ref, side_b_ref = refs[-2:]
    columns = []
    for j in (0, row_b_ref.shape[0] - 1):
        column = list(pick(odd_x, from_row_a_ref[j], from_row_b_ref[j]))
        column[1:1] = pick(odd_x, row_a_ref[j], row_b_ref[j])
        columns.append(column)
    for i in range(4):
        side_a_ref[i], side_b_ref[i] = pick(odd_y, columns[0][i], columns[1][i])
    if len(refs) == 3:
        side_a_ref[4] = refs[0][...]


def residual_kernel(
    neighbours_hbm_ref,
    kinds_hbm_ref,
    flags_ref,
    row_a_ref,
    row_b_ref,
    from_row_a_ref,
    from_row_b_ref,
    from_side_a_ref,
    from_side_b_ref,
    from_corner_a_ref,
    from_corner_b_ref,
    rest_a_ref,
    rest_b_ref,
    stiff_ref,
    mass_ref,
    residual_a_ref,
    residual_b_ref,
    partial_ref,
    current_ref,
    ext_ref,
    table_ref,
    neighbours_ref,
    kinds_ref,
    semaphores,
    total_ref,
    parts_ref,
    prior_ref,
):
    copies = code_copies(
        (neighbours_hbm_ref, kinds_hbm_ref), (neighbours_ref, kinds_ref), semaphores
    )
    for copy in copies:
        copy.start()
    split_tables(stiff_ref, mass_ref, table_ref, 1)
    count_y, both, side = row_a_ref.shape
    wide = count_y + 2
    block = both // 2
    rest = rest_a_ref.shape[1]
    odd_y, odd_x, in_low_y, in_high_y, in_low_x, in_high_x = (
        flag_at(flags_ref, place) for place in range(6)
    )

    def store(i, j, value):
        current_ref[i * wide + j] = value[:block]
        for part in range(2):
            high, low = split(value[part * block : (part + 1) * block])
            ext_ref[i * wide + j, :block, part * side : (part + 1) * side] = high
            ext_ref[i * wide + j, block:, part * side : (part + 1) * side] = low

    def own_tile(i, j):
        return pick(odd_x, row_a_ref[j], row_b_ref[j])[i]

    for j in range(count_y):
        store(1, j + 1, own_tile(0, j))
        store(2, j + 1, own_tile(1, j))
        low, high = pick(odd_x, from_row_a_ref[j], from_row_b_ref[j])
        store(0, j + 1, low * in_low_x)
        store(3, j + 1, high * in_high_x)
    for i in range(2):
        low, high = pick(odd_y, from_side_a_ref[i], from_side_b_ref[i])
        store(i + 1, 0, low * in_low_y)
        store(i + 1, wide - 1, high * in_high_y)
    for place, j, inside in ((0, 0, in_low_y), (1, wide - 1, in_high_y)):
        low, high = pick(odd_x, from_corner_a_ref[place], from_corner_b_ref[place])
        store(0, j, low * (in_low_x * inside))
        store(3, j, high * (in_high_x * inside))
    for copy in copies:
        copy.wait()
    for tile in range(2 * count_y):
        i, j = tile // count_y, tile % count_y
        own = own_tile(i, j)
        total = 4.0 * own[:block] + own[block:]
        for k in range(neighbours_ref.shape[1]):
            source, kind = source_and_kind(neighbours_ref, kinds_ref, tile, k, count_y)
            pair = mul(ext_ref[source], table_ref[kind])
            total = total + (pair[:block, :side] + (pair[block:, :side] + pair[:block, side:]))
        total_ref[tile] = total
        span = slice(tile * side, (tile + 1) * side)
        parts_ref[:, span] = stacked(total)
        rest_tile = pick(odd_x, rest_a_ref[j], rest_b_ref[j])[i]
        basis_tile = jnp.concatenate([rest_tile, own[:block]], axis=0)
        prior_ref[0, :, span], prior_ref[1, :, span] = split(basis_tile)
    partial = pair_sum(parts_ref[...], prior_ref[0], prior_ref[1])
    for j in range(count_y):
        residual_a_ref[j], residual_b_ref[j] = pick(
            odd_x, total_ref[j], total_ref[count_y + j]
        )
    residual_a_ref[count_y] = partial
    partial_ref[...] = partial


def prepare_kernel(
    flags_ref,
    rest_a_ref,
    rest_b_ref,
    from_rest_a_ref,
    from_rest_b_ref,
    current_ref,
    stiff_ref,
    mass_ref,
    basis_ref,
    prior_ref,
    table_ref,
):
    count_y, rest, side = rest_a_ref.shape
    prior = rest + current_ref.shape[1]
    odd_x = flag_at(flags_ref, 1)
    split_tables(stiff_ref, mass_ref, table_ref, 0)
    for j in range(count_y):
        rests = list(pick(odd_x, from_rest_a_ref[j], from_rest_b_ref[j]))
        rests[1:1] = pick(odd_x, rest_a_ref[j], rest_b_ref[j])
        for i in range(4):
            tile = jnp.concatenate([rests[i], current_ref[i * (count_y + 2) + j + 1]], axis=0)
            high, low = split(tile)
            basis_ref[i * count_y + j, :prior, :] = high
            basis_ref[i * count_y + j, prior:, :] = low
            if 0 < i < 3:
                place = (i - 1) * count_y + j
                span = slice(place * side, (place + 1) * side)
                prior_ref[0, :, span] = high
                prior_ref[1, :, span] = low


def operators_kernel(
    inverse_rows,
    neighbours_hbm_ref,
    kinds_hbm_ref,
    flags_ref,
    partial_ref,
    row_a_ref,
    row_b_ref,
    from_row_a_ref,
    from_row_b_ref,
    from_side_a_ref,
    from_side_b_ref,
    rest_side_a_ref,
    rest_side_b_ref,
    current_ref,
    basis_ref,
    prior_ref,
    table_ref,
    weighted_low_ref,
    weighted_high_ref,
    coupling_ref,
    sent_ref,
    kept_ref,
    ext_ref,
    neighbours_ref,
    kinds_ref,
    semaphores,
    parts_ref,
):
    copies = code_copies(
        (neighbours_hbm_ref, kinds_hbm_ref), (neighbours_ref, kinds_ref), semaphores
    )
    for copy in copies:
        copy.start()
    count_y, block, side = weighted_low_ref.shape
    wide = count_y + 2
    rest = rest_side_a_ref.shape[1]
    prior = rest + block
    odd_y, odd_x, in_low_y, in_high_y, in_low_x, in_high_x = (
        flag_at(flags_ref, place) for place in range(6)
    )
    coupling = partial_ref[...] * inverse_rows
    coupling_ref[...] = coupling
    coupling_deep = deep(coupling)

    def basis_parts(i, j):
        if 0 < j < wide - 1:
            return basis_ref[i * count_y + j - 1]
        rest_tile = pick(odd_y, rest_side_a_ref[i], rest_side_b_ref[i])[j // (wide - 1)]
        return stacked(jnp.concatenate([rest_tile, current_ref[i * wide + j]], axis=0))

    for j in range(wide):
        if 0 < j < wide - 1:
            rows = list(pick(odd_x, from_row_a_ref[j - 1], from_row_b_ref[j - 1]))
            rows[1:1] = pick(odd_x, row_a_ref[j - 1], row_b_ref[j - 1])
        else:
            rows = [
                pick(odd_y, from_side_a_ref[i], from_side_b_ref[i])[j // (wide - 1)]
                for i in range(4)
            ]
        for i in range(4):
            value = rows[i] - halves_sum(mul(coupling_deep, basis_parts(i, j)))
            if i == 0:
                value = value * in_low_x
            if i == 3:
                value = value * in_high_x
            if j == 0:
                value = value * in_low_y
            if j == wide - 1:
                value = value * in_high_y
            if 0 < i < 3 and 0 < j < wide - 1:
                (weighted_low_ref, weighted_high_ref)[i - 1][j - 1] = value
            ext_ref[i * wide + j] = deep(value)
    for copy in copies:
        copy.wait()
    for tile in range(2 * count_y):
        i, j = tile // count_y, tile % count_y
        own = (weighted_low_ref, weighted_high_ref)[i][j]
        totals = jnp.concatenate([4.0 * own, own], axis=1)
        for k in range(neighbours_ref.shape[1]):
            source, kind = source_and_kind(neighbours_ref, kinds_ref, tile, k, count_y)
            totals = totals + halves_sum(mul(ext_ref[source], table_ref[kind]))
        rows = jnp.concatenate([totals[:, :side], totals[:, side:], own, own], axis=0)
        span = slice(tile * side, (tile + 1) * side)
        parts_ref[0, :, span], parts_ref[1, :, span] = split(rows)
    applied = [parts_ref[part, : 2 * block, :] for part in range(2)]
    own_parts = [parts_ref[part, 2 * block : 3 * block, :] for part in range(2)]
    with_basis = mul_t(applied[0], prior_ref[0]) + (
        mul_t(applied[0], prior_ref[1]) + mul_t(applied[1], prior_ref[0])
    )
    with_own = mul_t(own_parts[0], parts_ref[0]) + (
        mul_t(own_parts[0], parts_ref[1]) + mul_t(own_parts[1], parts_ref[0])
    )
    halves = [
        jnp.concatenate(
            [
                with_basis[part * block : (part + 1) * block],
                folded(with_own[:, part * block : (part + 1) * block]),
                folded(with_own[:, 2 * block : 3 * block]),
            ],
            axis=0,
        )
        for part in range(2)
    ]
    sent_ref[...], kept_ref[...] = pick(odd_y, halves[0], halves[1])


def folded(square):
    return jnp.concatenate([square[n * 8 : (n + 1) * 8] for n in range(4)], axis=1)


def unfolded(rows):
    return jnp.concatenate([rows[:, n * 32 : (n + 1) * 32] for n in range(4)], axis=0)


def factor_kernel(inverse_rows, sums_ref, work_ref):
    block = work_ref.shape[0]
    gram = unfolded(sums_ref[block + 8 :, :]) * inverse_rows
    row_ids = lax.broadcasted_iota(jnp.int32, (block, block), 0)
    column_ids = lax.broadcasted_iota(jnp.int32, (block, block), 1)
    unit = jnp.where(row_ids == column_ids, 1.0, 0.0).astype(F32)
    rest = jnp.concatenate([gram, unit], axis=1)
    group = 8
    done = []
    for j in range(0, block, group):
        rows = lax.broadcasted_iota(jnp.int32, rest.shape, 0)
        columns = [
            jnp.broadcast_to(rest[:, j + a : j + a + 1], rest.shape) for a in range(group)
        ]
        pivots = [rest[a : a + 1, :] for a in range(group)]
        for a in range(group):
            ratio = columns[a] * (1.0 / columns[a][a : a + 1, :])
            for b in range(a + 1, group):
                columns[b] = columns[b] - ratio * columns[b][a : a + 1, :]
                pivots[b] = pivots[b] - ratio[b : b + 1, :] * pivots[a]
            rest = rest - jnp.where(rows > a, ratio, 0.0) * pivots[a]
        done.append(rest[:group])
        rest = rest[group:]
    work = jnp.concatenate(done, axis=0)
    work = work * lax.rsqrt(jnp.sum(work[:, :block] * unit, axis=1, keepdims=True))
    work_ref[...] = work


def finish_kernel(
    inverse_rows,
    flags_ref,
    work_ref,
    sums_ref,
    other_ref,
    weighted_low_ref,
    weighted_high_ref,
    new_ref,
    factor_ref,
    reduced_ref,
):
    count_y, block, _ = weighted_low_ref.shape
    prior = sums_ref.shape[1]
    tiles = 2 * count_y
    row_ids = lax.broadcasted_iota(jnp.int32, (block, block), 0)
    column_ids = lax.broadcasted_iota(jnp.int32, (block, block), 1)
    factor_ref[...] = jnp.where(column_ids >= row_ids, work_ref[:, :block], 0.0)
    inverse = work_ref[:, block:]
    inverse_deep = deep(inverse)
    for tile in range(tiles):
        own = (weighted_low_ref, weighted_high_ref)[tile // count_y][tile % count_y]
        new_ref[pl.ds(tile, block, stride=tiles), :] = mul_deep(inverse_deep, own)
    odd_y = flag_at(flags_ref, 0)
    halves = pick(odd_y, other_ref[...], sums_ref[: block + 8, :])
    for part, half in enumerate(halves):
        reduced_ref[part, :, :prior] = mul_deep(inverse_deep, half[:block] * inverse_rows)
        own = unfolded(half[block:]) * inverse_rows
        reduced_ref[part, :, prior:] = mul3_t(mul3_t(inverse, own), inverse)


def swap(value, mask):
    axes = ("px", "py")
    pairs = [(i, i ^ mask) for i in range(lax.axis_size(axes))]
    return lax.ppermute(value, axes, pairs)


def exchange(message_a, message_b, axis):
    cases, count = lax.axis_size("case"), lax.axis_size(axis)
    near = [(i, i ^ 1) for i in range(count)]
    pairs = []
    for case in range(cases):
        for i in range(count):
            j = ((i + 1) ^ 1) - 1
            target = (case, j) if 0 <= j < count else ((case ^ 1) % cases, i)
            pairs.append((case * count + i, target[0] * count + target[1]))
    return lax.ppermute(message_a, axis, near), lax.ppermute(message_b, ("case", axis), pairs)


def total_over(value, first, last):
    while first < last:
        value = value + swap(value, first)
        first *= 2
    return value


def half_total(sent, kept):
    kept = kept + swap(sent, 1)
    kept = (kept + swap(kept, 6)) + (swap(kept, 2) + swap(kept, 4))
    return total_over(kept, 8, lax.axis_size(("px", "py")))


def shape(*dims, dtype=F32):
    return jax.ShapeDtypeStruct(dims, dtype)


def shards(prior_basis, previous, neighbours, tile_kinds, stiff_tiles, mass_tiles):
    block = previous.shape[0]
    prior, count_x, count_y, side = prior_basis.shape
    tiles = count_x * count_y
    wide = count_y + 2
    rest = prior - block
    kinds = stiff_tiles.shape[0]
    inverse_rows = 1.0 / (tiles * side * lax.axis_size("px") * lax.axis_size("py"))
    basis = prior_basis.reshape(-1, side)
    vectors = jnp.concatenate([basis, previous.reshape(-1, side)], axis=0)
    codes = [array.transpose(1, 2, 0).reshape(tiles, -1) for array in (neighbours, tile_kinds)]
    code_scratch = [pltpu.SMEM(array.shape, jnp.int32) for array in codes]
    code_scratch += [pltpu.SemaphoreType.DMA((2,))]
    at_y, at_x = lax.axis_index("py"), lax.axis_index("px")
    bits = (at_y & 1) + 2 * (at_x & 1)
    bits += 4 * (at_y > 0) + 8 * (at_y < lax.axis_size("py") - 1)
    bits += 16 * (at_x > 0) + 32 * (at_x < lax.axis_size("px") - 1)
    flags = ((bits >> lax.broadcasted_iota(jnp.int32, (8, side), 0)) & 1).astype(F32)

    def call(kernel, inputs, outputs, scratch=(), plain=0, limit=8, cost=None):
        specs = [ANY] * plain + [VMEM] * (len(inputs) - plain)
        return pl.pallas_call(
            kernel,
            out_shape=outputs,
            in_specs=specs,
            out_specs=[VMEM] * len(outputs),
            scratch_shapes=scratch,
            compiler_params=pltpu.CompilerParams(vmem_limit_bytes=limit * MIB),
            cost_estimate=cost,
        )(*inputs)

    side_a, side_b, row_a, row_b = call(
        pack_kernel,
        (flags, vectors),
        [shape(count_x, 2 * block, side)] * 2 + [shape(count_y, 2 * block, side)] * 2,
    )
    rest_a, rest_b = call(rest_kernel, (flags, vectors), [shape(count_y, rest, side)] * 2)
    from_side_a, from_side_b = exchange(side_a, side_b, "py")
    from_row_a, from_row_b = exchange(row_a, row_b, "px")
    from_side_a, rest_a, rest_b = lax.optimization_barrier((from_side_a, rest_a, rest_b))
    from_rest_a, from_rest_b = exchange(rest_a, rest_b, "px")
    corner_a, corner_b = call(
        corners_kernel,
        (flags, from_side_a, from_side_b),
        [shape(2, 2 * block, side)] * 2,
    )
    from_corner_a, from_corner_b = exchange(corner_a, corner_b, "px")
    rest_side_a, rest_side_b = call(
        columns_kernel,
        (flags, rest_a, rest_b, from_rest_a, from_rest_b),
        [shape(4, rest, side)] * 2,
    )
    rest_side_a, rest_side_b = exchange(rest_side_a, rest_side_b, "py")
    residual_a, residual_b, partial, current = call(
        residual_kernel,
        (
            *codes,
            flags,
            row_a,
            row_b,
            from_row_a,
            from_row_b,
            from_side_a,
            from_side_b,
            from_corner_a,
            from_corner_b,
            rest_a,
            rest_b,
            stiff_tiles,
            mass_tiles,
        ),
        [shape(count_y + 1, block, side), shape(count_y, block, side)]
        + [shape(block, prior), shape(4 * wide, block, side)],
        [pltpu.VMEM((4 * wide, 2 * block, 2 * side), BF16)]
        + [pltpu.VMEM((kinds, 2 * side, 2 * side), BF16)]
        + code_scratch
        + [
            pltpu.VMEM((tiles, block, side), F32),
            pltpu.VMEM((2 * block, tiles * side), BF16),
            pltpu.VMEM((2, prior, tiles * side), BF16),
        ],
        plain=2,
        cost=pl.CostEstimate(flops=10**9, bytes_accessed=0, transcendentals=0),
    )
    count_py = lax.axis_size("py")
    from_row_a, from_row_b = exchange(residual_a, residual_b, "px")
    partial = total_over(
        partial + from_row_a[-1], 2 * count_py, count_py * lax.axis_size("px")
    )
    partial, rest_side_a, rest_side_b = lax.optimization_barrier(
        (partial, rest_side_a, rest_side_b)
    )
    side_a, side_b = call(
        columns_kernel,
        (flags, residual_a, residual_b, from_row_a, from_row_b, partial),
        [shape(5, block, side), shape(4, block, side)],
    )
    from_side_a, from_side_b = exchange(side_a, side_b, "py")
    partial = total_over(partial + from_side_a[-1], 2, count_py)
    basis_parts, prior_parts, table = call(
        prepare_kernel,
        (flags, rest_a, rest_b, from_rest_a, from_rest_b, current, stiff_tiles, mass_tiles),
        [shape(4 * count_y, 2 * prior, side, dtype=BF16)]
        + [shape(2, prior, tiles * side, dtype=BF16)]
        + [shape(kinds, 2 * side, 2 * side, dtype=BF16)],
        cost=pl.CostEstimate(flops=10**9, bytes_accessed=0, transcendentals=0),
    )
    weighted_low, weighted_high, coupling, sent, kept = call(
        functools.partial(operators_kernel, inverse_rows),
        (
            *codes,
            flags,
            partial,
            residual_a,
            residual_b,
            from_row_a,
            from_row_b,
            from_side_a,
            from_side_b,
            rest_side_a,
            rest_side_b,
            current,
            basis_parts,
            prior_parts,
            table,
        ),
        [shape(count_y, block, side)] * 2
        + [shape(block, prior)]
        + [shape(block + 16, prior)] * 2,
        [pltpu.VMEM((4 * wide, 2 * block, 2 * side), BF16)]
        + code_scratch
        + [pltpu.VMEM((2, 4 * block, tiles * side), BF16)],
        plain=2,
    )
    kept = half_total(sent, kept)
    other = swap(kept[: block + 8], 1)
    (work,) = call(
        functools.partial(factor_kernel, inverse_rows),
        (kept,),
        [shape(block, 2 * block)],
        cost=pl.CostEstimate(flops=10**9, bytes_accessed=0, transcendentals=0),
    )
    new_block, factor, reduced = call(
        functools.partial(finish_kernel, inverse_rows),
        (flags, work, kept, other, weighted_low, weighted_high),
        [
            shape(block * tiles, side),
            shape(block, block),
            shape(2, block, prior + block),
        ],
    )
    return (
        new_block.reshape(previous.shape),
        coupling.T,
        factor,
        reduced.swapaxes(1, 2),
    )


def solution(mesh):
    placed = (
        P("case", "px", "py", None),
        P("case", "px", "py", None),
        P(None, "px", "py"),
        P(None, "px", "py"),
        P(),
        P(),
    )
    return jax.shard_map(
        shards,
        mesh=mesh,
        in_specs=placed,
        out_specs=(
            P("case", "px", "py", None),
            P("case", None),
            P("case", None),
            P("case", None, None),
        ),
        check_vma=False,
    )
```

```python
import functools

import jax
import jax.numpy as jnp
from jax import lax
from jax.experimental import pallas as pl
from jax.experimental.pallas import tpu as pltpu
from jax.sharding import PartitionSpec as P

F32 = jnp.float32
BF16 = jnp.bfloat16
VMEM = pl.BlockSpec(memory_space=pltpu.VMEM)
ANY = pl.BlockSpec(memory_space=pl.ANY)
MIB = 1024 * 1024


def split(value):
    high = value.astype(BF16)
    return high, (value - high.astype(F32)).astype(BF16)


def mul(left, right):
    return jnp.dot(left, right, preferred_element_type=F32)


def mul_t(left, right):
    return lax.dot_general(left, right, (((1,), (1,)), ((), ())), preferred_element_type=F32)


def mul3(left, right):
    left_high, left_low = split(left)
    right_high, right_low = split(right)
    return mul(left_high, right_high) + (mul(left_high, right_low) + mul(left_low, right_high))


def mul3_t(left, right):
    left_high, left_low = split(left)
    right_high, right_low = split(right)
    return mul_t(left_high, right_high) + (
        mul_t(left_high, right_low) + mul_t(left_low, right_high)
    )


def split_tables(stiff_ref, mass_ref, table_ref, parts_axis):
    side = stiff_ref.shape[1]
    spans = (slice(0, side), slice(side, 2 * side))
    for kind in range(stiff_ref.shape[0]):
        for matrix, ref in zip(spans, (stiff_ref, mass_ref)):
            for part, value in zip(spans, split(ref[kind])):
                if parts_axis == 1:
                    table_ref[kind, matrix, part] = value
                else:
                    table_ref[kind, part, matrix] = value


def stacked(value):
    return jnp.concatenate(split(value), axis=0)


def deep(value):
    high, low = split(value)
    upper = jnp.concatenate([high, high], axis=1)
    return jnp.concatenate([upper, jnp.concatenate([low, jnp.zeros_like(low)], axis=1)], axis=0)


def halves_sum(value):
    half = value.shape[0] // 2
    return value[:half] + value[half:]


def mul_deep(left_deep, right):
    return halves_sum(mul(left_deep, stacked(right)))


def pair_sum(left, right_high, right_low):
    rows = left.shape[0] // 2
    return halves_sum(mul_t(left, right_high)) + mul_t(left[:rows], right_low)


def pick(flag, first, second):
    flag = flag > 0.0
    return jnp.where(flag, first, second), jnp.where(flag, second, first)


def flag_at(flags_ref, place):
    return flags_ref[place : place + 1, :]


def code_copies(code_refs, local_refs, semaphores):
    return [
        pltpu.make_async_copy(ref, local, semaphores.at[n])
        for n, (ref, local) in enumerate(zip(code_refs, local_refs))
    ]


def source_and_kind(neighbours_ref, kinds_ref, tile, k, count_y):
    neighbour = neighbours_ref[tile, k]
    down = (neighbour * 11) >> 5
    first = (tile // count_y) * (count_y + 2) + tile % count_y
    return first + neighbour + down * (count_y - 1), kinds_ref[tile, k]


def pack_kernel(flags_ref, vectors_ref, side_a_ref, side_b_ref, row_a_ref, row_b_ref):
    count_y, both, _ = row_a_ref.shape
    tiles = 2 * count_y
    odd_y, odd_x = flag_at(flags_ref, 0), flag_at(flags_ref, 1)

    first = vectors_ref.shape[0] - both * tiles

    def tile_of(i, j):
        return vectors_ref[pl.ds(first + i * count_y + j, both, stride=tiles), :]

    for i in range(2):
        side_a_ref[i], side_b_ref[i] = pick(odd_y, tile_of(i, 0), tile_of(i, count_y - 1))
    for j in range(count_y):
        row_a_ref[j], row_b_ref[j] = pick(odd_x, tile_of(0, j), tile_of(1, j))


def rest_kernel(flags_ref, vectors_ref, rest_a_ref, rest_b_ref):
    count_y, rest, _ = rest_a_ref.shape
    odd_x = flag_at(flags_ref, 1)
    for j in range(count_y):
        rest_a_ref[j], rest_b_ref[j] = pick(
            odd_x,
            vectors_ref[pl.ds(j, rest, stride=2 * count_y), :],
            vectors_ref[pl.ds(count_y + j, rest, stride=2 * count_y), :],
        )


def corners_kernel(flags_ref, side_a_ref, side_b_ref, corner_a_ref, corner_b_ref):
    odd_y, odd_x = flag_at(flags_ref, 0), flag_at(flags_ref, 1)
    ends = [pick(odd_y, side_a_ref[i], side_b_ref[i]) for i in range(2)]
    for place in range(2):
        corner_a_ref[place], corner_b_ref[place] = pick(odd_x, ends[0][place], ends[1][place])


def columns_kernel(
    flags_ref, row_a_ref, row_b_ref, from_row_a_ref, from_row_b_ref, *refs
):
    odd_y, odd_x = flag_at(flags_ref, 0), flag_at(flags_ref, 1)
    side_a_ref, side_b_ref = refs[-2:]
    columns = []
    for j in (0, row_b_ref.shape[0] - 1):
        column = list(pick(odd_x, from_row_a_ref[j], from_row_b_ref[j]))
        column[1:1] = pick(odd_x, row_a_ref[j], row_b_ref[j])
        columns.append(column)
    for i in range(4):
        side_a_ref[i], side_b_ref[i] = pick(odd_y, columns[0][i], columns[1][i])
    if len(refs) == 3:
        side_a_ref[4] = refs[0][...]


def residual_kernel(
    neighbours_hbm_ref,
    kinds_hbm_ref,
    flags_ref,
    row_a_ref,
    row_b_ref,
    from_row_a_ref,
    from_row_b_ref,
    from_side_a_ref,
    from_side_b_ref,
    from_corner_a_ref,
    from_corner_b_ref,
    rest_a_ref,
    rest_b_ref,
    stiff_ref,
    mass_ref,
    residual_a_ref,
    residual_b_ref,
    partial_ref,
    current_ref,
    ext_ref,
    table_ref,
    neighbours_ref,
    kinds_ref,
    semaphores,
    total_ref,
    parts_ref,
    prior_ref,
):
    copies = code_copies(
        (neighbours_hbm_ref, kinds_hbm_ref), (neighbours_ref, kinds_ref), semaphores
    )
    for copy in copies:
        copy.start()
    split_tables(stiff_ref, mass_ref, table_ref, 1)
    count_y, both, side = row_a_ref.shape
    wide = count_y + 2
    block = both // 2
    rest = rest_a_ref.shape[1]
    odd_y, odd_x, in_low_y, in_high_y, in_low_x, in_high_x = (
        flag_at(flags_ref, place) for place in range(6)
    )

    def store(i, j, value):
        current_ref[i * wide + j] = value[:block]
        for part in range(2):
            high, low = split(value[part * block : (part + 1) * block])
            ext_ref[i * wide + j, :block, part * side : (part + 1) * side] = high
            ext_ref[i * wide + j, block:, part * side : (part + 1) * side] = low

    def own_tile(i, j):
        return pick(odd_x, row_a_ref[j], row_b_ref[j])[i]

    for j in range(count_y):
        store(1, j + 1, own_tile(0, j))
        store(2, j + 1, own_tile(1, j))
        low, high = pick(odd_x, from_row_a_ref[j], from_row_b_ref[j])
        store(0, j + 1, low * in_low_x)
        store(3, j + 1, high * in_high_x)
    for i in range(2):
        low, high = pick(odd_y, from_side_a_ref[i], from_side_b_ref[i])
        store(i + 1, 0, low * in_low_y)
        store(i + 1, wide - 1, high * in_high_y)
    for place, j, inside in ((0, 0, in_low_y), (1, wide - 1, in_high_y)):
        low, high = pick(odd_x, from_corner_a_ref[place], from_corner_b_ref[place])
        store(0, j, low * (in_low_x * inside))
        store(3, j, high * (in_high_x * inside))
    for copy in copies:
        copy.wait()
    for tile in range(2 * count_y):
        i, j = tile // count_y, tile % count_y
        own = own_tile(i, j)
        total = 4.0 * own[:block] + own[block:]
        for k in range(neighbours_ref.shape[1]):
            source, kind = source_and_kind(neighbours_ref, kinds_ref, tile, k, count_y)
            pair = mul(ext_ref[source], table_ref[kind])
            total = total + (pair[:block, :side] + (pair[block:, :side] + pair[:block, side:]))
        total_ref[tile] = total
        span = slice(tile * side, (tile + 1) * side)
        parts_ref[:, span] = stacked(total)
        rest_tile = pick(odd_x, rest_a_ref[j], rest_b_ref[j])[i]
        basis_tile = jnp.concatenate([rest_tile, own[:block]], axis=0)
        prior_ref[0, :, span], prior_ref[1, :, span] = split(basis_tile)
    partial = pair_sum(parts_ref[...], prior_ref[0], prior_ref[1])
    for j in range(count_y):
        residual_a_ref[j], residual_b_ref[j] = pick(
            odd_x, total_ref[j], total_ref[count_y + j]
        )
    residual_a_ref[count_y] = partial
    partial_ref[...] = partial


def prepare_kernel(
    flags_ref,
    rest_a_ref,
    rest_b_ref,
    from_rest_a_ref,
    from_rest_b_ref,
    rest_side_a_ref,
    rest_side_b_ref,
    current_ref,
    stiff_ref,
    mass_ref,
    basis_ref,
    prior_ref,
    table_ref,
):
    count_y, rest, side = rest_a_ref.shape
    wide = count_y + 2
    prior = rest + current_ref.shape[1]
    odd_y, odd_x = flag_at(flags_ref, 0), flag_at(flags_ref, 1)
    split_tables(stiff_ref, mass_ref, table_ref, 0)
    for j in range(wide):
        if 0 < j < wide - 1:
            rests = list(pick(odd_x, from_rest_a_ref[j - 1], from_rest_b_ref[j - 1]))
            rests[1:1] = pick(odd_x, rest_a_ref[j - 1], rest_b_ref[j - 1])
        else:
            rests = [
                pick(odd_y, rest_side_a_ref[i], rest_side_b_ref[i])[j // (wide - 1)]
                for i in range(4)
            ]
        for i in range(4):
            place = i * wide + j
            high, low = split(jnp.concatenate([rests[i], current_ref[place]], axis=0))
            basis_ref[place, :prior, :] = high
            basis_ref[place, prior:, :] = low
            if 0 < i < 3 and 0 < j < wide - 1:
                tile = (i - 1) * count_y + j - 1
                span = slice(tile * side, (tile + 1) * side)
                prior_ref[0, :, span] = high
                prior_ref[1, :, span] = low


def operators_kernel(
    inverse_rows,
    neighbours_hbm_ref,
    kinds_hbm_ref,
    flags_ref,
    partial_ref,
    row_a_ref,
    row_b_ref,
    from_row_a_ref,
    from_row_b_ref,
    from_side_a_ref,
    from_side_b_ref,
    basis_ref,
    prior_ref,
    table_ref,
    weighted_low_ref,
    weighted_high_ref,
    sent_ref,
    kept_ref,
    ext_ref,
    neighbours_ref,
    kinds_ref,
    semaphores,
    parts_ref,
):
    copies = code_copies(
        (neighbours_hbm_ref, kinds_hbm_ref), (neighbours_ref, kinds_ref), semaphores
    )
    for copy in copies:
        copy.start()
    count_y, block, side = weighted_low_ref.shape
    wide = count_y + 2
    odd_y, odd_x, in_low_y, in_high_y, in_low_x, in_high_x = (
        flag_at(flags_ref, place) for place in range(6)
    )
    coupling_deep = deep(partial_ref[...] * inverse_rows)

    for j in range(wide):
        if 0 < j < wide - 1:
            rows = list(pick(odd_x, from_row_a_ref[j - 1], from_row_b_ref[j - 1]))
            rows[1:1] = pick(odd_x, row_a_ref[j - 1], row_b_ref[j - 1])
        else:
            rows = [
                pick(odd_y, from_side_a_ref[i], from_side_b_ref[i])[j // (wide - 1)]
                for i in range(4)
            ]
        for i in range(4):
            value = rows[i] - halves_sum(mul(coupling_deep, basis_ref[i * wide + j]))
            if i == 0:
                value = value * in_low_x
            if i == 3:
                value = value * in_high_x
            if j == 0:
                value = value * in_low_y
            if j == wide - 1:
                value = value * in_high_y
            if 0 < i < 3 and 0 < j < wide - 1:
                (weighted_low_ref, weighted_high_ref)[i - 1][j - 1] = value
            ext_ref[i * wide + j] = deep(value)
    for copy in copies:
        copy.wait()
    for tile in range(2 * count_y):
        i, j = tile // count_y, tile % count_y
        own = (weighted_low_ref, weighted_high_ref)[i][j]
        totals = jnp.concatenate([4.0 * own, own], axis=1)
        for k in range(neighbours_ref.shape[1]):
            source, kind = source_and_kind(neighbours_ref, kinds_ref, tile, k, count_y)
            totals = totals + halves_sum(mul(ext_ref[source], table_ref[kind]))
        rows = jnp.concatenate([totals[:, :side], totals[:, side:], own, own], axis=0)
        span = slice(tile * side, (tile + 1) * side)
        parts_ref[0, :, span], parts_ref[1, :, span] = split(rows)
    applied = [parts_ref[part, : 2 * block, :] for part in range(2)]
    own_parts = [parts_ref[part, 2 * block : 3 * block, :] for part in range(2)]
    with_basis = mul_t(applied[0], prior_ref[0]) + (
        mul_t(applied[0], prior_ref[1]) + mul_t(applied[1], prior_ref[0])
    )
    with_own = mul_t(own_parts[0], parts_ref[0]) + (
        mul_t(own_parts[0], parts_ref[1]) + mul_t(own_parts[1], parts_ref[0])
    )
    halves = [
        jnp.concatenate(
            [
                with_basis[part * block : (part + 1) * block],
                folded(with_own[:, part * block : (part + 1) * block]),
                folded(with_own[:, 2 * block : 3 * block]),
            ],
            axis=0,
        )
        for part in range(2)
    ]
    sent_ref[...], kept_ref[...] = pick(odd_y, halves[0], halves[1])


def folded(square):
    return jnp.concatenate([square[n * 8 : (n + 1) * 8] for n in range(4)], axis=1)


def unfolded(rows):
    return jnp.concatenate([rows[:, n * 32 : (n + 1) * 32] for n in range(4)], axis=0)


def factor_kernel(inverse_rows, sums_ref, work_ref):
    block = work_ref.shape[0]
    gram = unfolded(sums_ref[block + 8 :, :]) * inverse_rows
    row_ids = lax.broadcasted_iota(jnp.int32, (block, block), 0)
    column_ids = lax.broadcasted_iota(jnp.int32, (block, block), 1)
    unit = jnp.where(row_ids == column_ids, 1.0, 0.0).astype(F32)
    rest = jnp.concatenate([gram, unit], axis=1)
    group = 8
    done = []
    for j in range(0, block, group):
        rows = lax.broadcasted_iota(jnp.int32, rest.shape, 0)
        columns = [
            jnp.broadcast_to(rest[:, j + a : j + a + 1], rest.shape) for a in range(group)
        ]
        pivots = [rest[a : a + 1, :] for a in range(group)]
        for a in range(group):
            ratio = columns[a] * (1.0 / columns[a][a : a + 1, :])
            for b in range(a + 1, group):
                columns[b] = columns[b] - ratio * columns[b][a : a + 1, :]
                pivots[b] = pivots[b] - ratio[b : b + 1, :] * pivots[a]
            rest = rest - jnp.where(rows > a, ratio, 0.0) * pivots[a]
        done.append(rest[:group])
        rest = rest[group:]
    work = jnp.concatenate(done, axis=0)
    work = work * lax.rsqrt(jnp.sum(work[:, :block] * unit, axis=1, keepdims=True))
    work_ref[...] = work


def finish_kernel(
    inverse_rows,
    flags_ref,
    work_ref,
    sums_ref,
    other_ref,
    partial_ref,
    weighted_low_ref,
    weighted_high_ref,
    new_ref,
    coupling_ref,
    factor_ref,
    reduced_ref,
):
    coupling_ref[...] = partial_ref[...] * inverse_rows
    count_y, block, _ = weighted_low_ref.shape
    prior = sums_ref.shape[1]
    tiles = 2 * count_y
    row_ids = lax.broadcasted_iota(jnp.int32, (block, block), 0)
    column_ids = lax.broadcasted_iota(jnp.int32, (block, block), 1)
    factor_ref[...] = jnp.where(column_ids >= row_ids, work_ref[:, :block], 0.0)
    inverse = work_ref[:, block:]
    inverse_deep = deep(inverse)
    for tile in range(tiles):
        own = (weighted_low_ref, weighted_high_ref)[tile // count_y][tile % count_y]
        new_ref[pl.ds(tile, block, stride=tiles), :] = mul_deep(inverse_deep, own)
    odd_y = flag_at(flags_ref, 0)
    halves = pick(odd_y, other_ref[...], sums_ref[: block + 8, :])
    for part, half in enumerate(halves):
        reduced_ref[part, :, :prior] = mul_deep(inverse_deep, half[:block] * inverse_rows)
        own = unfolded(half[block:]) * inverse_rows
        reduced_ref[part, :, prior:] = mul3_t(mul3_t(inverse, own), inverse)


def swap(value, mask):
    axes = ("px", "py")
    pairs = [(i, i ^ mask) for i in range(lax.axis_size(axes))]
    return lax.ppermute(value, axes, pairs)


def exchange(message_a, message_b, axis):
    cases, count = lax.axis_size("case"), lax.axis_size(axis)
    near = [(i, i ^ 1) for i in range(count)]
    pairs = []
    for case in range(cases):
        for i in range(count):
            j = ((i + 1) ^ 1) - 1
            target = (case, j) if 0 <= j < count else ((case ^ 1) % cases, i)
            pairs.append((case * count + i, target[0] * count + target[1]))
    return lax.ppermute(message_a, axis, near), lax.ppermute(message_b, ("case", axis), pairs)


def total_over(value, first, last):
    while first < last:
        value = value + swap(value, first)
        first *= 2
    return value


def half_total(sent, kept):
    kept = kept + swap(sent, 1)
    kept = (kept + swap(kept, 6)) + (swap(kept, 2) + swap(kept, 4))
    return total_over(kept, 8, lax.axis_size(("px", "py")))


def shape(*dims, dtype=F32):
    return jax.ShapeDtypeStruct(dims, dtype)


def shards(prior_basis, previous, neighbours, tile_kinds, stiff_tiles, mass_tiles):
    block = previous.shape[0]
    prior, count_x, count_y, side = prior_basis.shape
    tiles = count_x * count_y
    wide = count_y + 2
    rest = prior - block
    kinds = stiff_tiles.shape[0]
    inverse_rows = 1.0 / (tiles * side * lax.axis_size("px") * lax.axis_size("py"))
    basis = prior_basis.reshape(-1, side)
    vectors = jnp.concatenate([basis, previous.reshape(-1, side)], axis=0)
    codes = [array.transpose(1, 2, 0).reshape(tiles, -1) for array in (neighbours, tile_kinds)]
    code_scratch = [pltpu.SMEM(array.shape, jnp.int32) for array in codes]
    code_scratch += [pltpu.SemaphoreType.DMA((2,))]
    at_y, at_x = lax.axis_index("py"), lax.axis_index("px")
    bits = (at_y & 1) + 2 * (at_x & 1)
    bits += 4 * (at_y > 0) + 8 * (at_y < lax.axis_size("py") - 1)
    bits += 16 * (at_x > 0) + 32 * (at_x < lax.axis_size("px") - 1)
    flags = ((bits >> lax.broadcasted_iota(jnp.int32, (8, side), 0)) & 1).astype(F32)

    def call(kernel, inputs, outputs, scratch=(), plain=0, limit=8, cost=None):
        specs = [ANY] * plain + [VMEM] * (len(inputs) - plain)
        return pl.pallas_call(
            kernel,
            out_shape=outputs,
            in_specs=specs,
            out_specs=[VMEM] * len(outputs),
            scratch_shapes=scratch,
            compiler_params=pltpu.CompilerParams(vmem_limit_bytes=limit * MIB),
            cost_estimate=cost,
        )(*inputs)

    side_a, side_b, row_a, row_b = call(
        pack_kernel,
        (flags, vectors),
        [shape(count_x, 2 * block, side)] * 2 + [shape(count_y, 2 * block, side)] * 2,
    )
    rest_a, rest_b = call(rest_kernel, (flags, vectors), [shape(count_y, rest, side)] * 2)
    from_side_a, from_side_b = exchange(side_a, side_b, "py")
    from_row_a, from_row_b = exchange(row_a, row_b, "px")
    from_side_a, rest_a, rest_b = lax.optimization_barrier((from_side_a, rest_a, rest_b))
    from_rest_a, from_rest_b = exchange(rest_a, rest_b, "px")
    corner_a, corner_b = call(
        corners_kernel,
        (flags, from_side_a, from_side_b),
        [shape(2, 2 * block, side)] * 2,
    )
    from_corner_a, from_corner_b = exchange(corner_a, corner_b, "px")
    rest_side_a, rest_side_b = call(
        columns_kernel,
        (flags, rest_a, rest_b, from_rest_a, from_rest_b),
        [shape(4, rest, side)] * 2,
    )
    rest_side_a, rest_side_b = exchange(rest_side_a, rest_side_b, "py")
    residual_a, residual_b, partial, current = call(
        residual_kernel,
        (
            *codes,
            flags,
            row_a,
            row_b,
            from_row_a,
            from_row_b,
            from_side_a,
            from_side_b,
            from_corner_a,
            from_corner_b,
            rest_a,
            rest_b,
            stiff_tiles,
            mass_tiles,
        ),
        [shape(count_y + 1, block, side), shape(count_y, block, side)]
        + [shape(block, prior), shape(4 * wide, block, side)],
        [pltpu.VMEM((4 * wide, 2 * block, 2 * side), BF16)]
        + [pltpu.VMEM((kinds, 2 * side, 2 * side), BF16)]
        + code_scratch
        + [
            pltpu.VMEM((tiles, block, side), F32),
            pltpu.VMEM((2 * block, tiles * side), BF16),
            pltpu.VMEM((2, prior, tiles * side), BF16),
        ],
        plain=2,
        cost=pl.CostEstimate(flops=10**9, bytes_accessed=0, transcendentals=0),
    )
    count_py = lax.axis_size("py")
    from_row_a, from_row_b = exchange(residual_a, residual_b, "px")
    partial = total_over(
        partial + from_row_a[-1], 2 * count_py, count_py * lax.axis_size("px")
    )
    partial, rest_side_a, rest_side_b = lax.optimization_barrier(
        (partial, rest_side_a, rest_side_b)
    )
    side_a, side_b = call(
        columns_kernel,
        (flags, residual_a, residual_b, from_row_a, from_row_b, partial),
        [shape(5, block, side), shape(4, block, side)],
    )
    from_side_a, from_side_b = exchange(side_a, side_b, "py")
    partial = total_over(partial + from_side_a[-1], 2, count_py)
    basis_parts, prior_parts, table = call(
        prepare_kernel,
        (
            flags,
            rest_a,
            rest_b,
            from_rest_a,
            from_rest_b,
            rest_side_a,
            rest_side_b,
            current,
            stiff_tiles,
            mass_tiles,
        ),
        [shape(4 * wide, 2 * prior, side, dtype=BF16)]
        + [shape(2, prior, tiles * side, dtype=BF16)]
        + [shape(kinds, 2 * side, 2 * side, dtype=BF16)],
        cost=pl.CostEstimate(flops=10**9, bytes_accessed=0, transcendentals=0),
    )
    weighted_low, weighted_high, sent, kept = call(
        functools.partial(operators_kernel, inverse_rows),
        (
            *codes,
            flags,
            partial,
            residual_a,
            residual_b,
            from_row_a,
            from_row_b,
            from_side_a,
            from_side_b,
            basis_parts,
            prior_parts,
            table,
        ),
        [shape(count_y, block, side)] * 2 + [shape(block + 16, prior)] * 2,
        [pltpu.VMEM((4 * wide, 2 * block, 2 * side), BF16)]
        + code_scratch
        + [pltpu.VMEM((2, 4 * block, tiles * side), BF16)],
        plain=2,
    )
    kept = half_total(sent, kept)
    other = swap(kept[: block + 8], 1)
    (work,) = call(
        functools.partial(factor_kernel, inverse_rows),
        (kept,),
        [shape(block, 2 * block)],
        cost=pl.CostEstimate(flops=10**9, bytes_accessed=0, transcendentals=0),
    )
    new_block, coupling, factor, reduced = call(
        functools.partial(finish_kernel, inverse_rows),
        (flags, work, kept, other, partial, weighted_low, weighted_high),
        [
            shape(block * tiles, side),
            shape(block, prior),
            shape(block, block),
            shape(2, block, prior + block),
        ],
    )
    return (
        new_block.reshape(previous.shape),
        coupling.T,
        factor,
        reduced.swapaxes(1, 2),
    )


def solution(mesh):
    placed = (
        P("case", "px", "py", None),
        P("case", "px", "py", None),
        P(None, "px", "py"),
        P(None, "px", "py"),
        P(),
        P(),
    )
    return jax.shard_map(
        shards,
        mesh=mesh,
        in_specs=placed,
        out_specs=(
            P("case", "px", "py", None),
            P("case", None),
            P("case", None),
            P("case", None, None),
        ),
        check_vma=False,
    )
```

```python
import functools

import jax
import jax.numpy as jnp
from jax import lax
from jax.experimental import pallas as pl
from jax.experimental.pallas import tpu as pltpu
from jax.sharding import PartitionSpec as P

F32 = jnp.float32
BF16 = jnp.bfloat16
VMEM = pl.BlockSpec(memory_space=pltpu.VMEM)
ANY = pl.BlockSpec(memory_space=pl.ANY)
MIB = 1024 * 1024


def split(value):
    high = value.astype(BF16)
    return high, (value - high.astype(F32)).astype(BF16)


def mul(left, right):
    return jnp.dot(left, right, preferred_element_type=F32)


def mul_t(left, right):
    return lax.dot_general(left, right, (((1,), (1,)), ((), ())), preferred_element_type=F32)


def mul3(left, right):
    left_high, left_low = split(left)
    right_high, right_low = split(right)
    return mul(left_high, right_high) + (mul(left_high, right_low) + mul(left_low, right_high))


def mul3_t(left, right):
    left_high, left_low = split(left)
    right_high, right_low = split(right)
    return mul_t(left_high, right_high) + (
        mul_t(left_high, right_low) + mul_t(left_low, right_high)
    )


def split_tables(stiff_ref, mass_ref, table_ref, parts_axis):
    side = stiff_ref.shape[1]
    spans = (slice(0, side), slice(side, 2 * side))
    for kind in range(stiff_ref.shape[0]):
        for matrix, ref in zip(spans, (stiff_ref, mass_ref)):
            for part, value in zip(spans, split(ref[kind])):
                if parts_axis == 1:
                    table_ref[kind, matrix, part] = value
                else:
                    table_ref[kind, part, matrix] = value


def stacked(value):
    return jnp.concatenate(split(value), axis=0)


def deep(value):
    high, low = split(value)
    upper = jnp.concatenate([high, high], axis=1)
    return jnp.concatenate([upper, jnp.concatenate([low, jnp.zeros_like(low)], axis=1)], axis=0)


def halves_sum(value):
    half = value.shape[0] // 2
    return value[:half] + value[half:]


def mul_deep(left_deep, right):
    return halves_sum(mul(left_deep, stacked(right)))


def pair_sum(left, right_high, right_low):
    rows = left.shape[0] // 2
    return halves_sum(mul_t(left, right_high)) + mul_t(left[:rows], right_low)


def pick(flag, first, second):
    flag = flag > 0.0
    return jnp.where(flag, first, second), jnp.where(flag, second, first)


def flag_at(flags_ref, place):
    return flags_ref[place : place + 1, :]


def code_copies(code_refs, local_refs, semaphores):
    return [
        pltpu.make_async_copy(ref, local, semaphores.at[n])
        for n, (ref, local) in enumerate(zip(code_refs, local_refs))
    ]


def source_and_kind(neighbours_ref, kinds_ref, tile, k, count_y):
    neighbour = neighbours_ref[tile, k]
    down = (neighbour * 11) >> 5
    first = (tile // count_y) * (count_y + 2) + tile % count_y
    return first + neighbour + down * (count_y - 1), kinds_ref[tile, k]


def pack_kernel(flags_ref, vectors_ref, side_a_ref, side_b_ref, row_a_ref, row_b_ref):
    count_y, both, _ = row_a_ref.shape
    tiles = 2 * count_y
    odd_y, odd_x = flag_at(flags_ref, 0), flag_at(flags_ref, 1)

    first = vectors_ref.shape[0] - both * tiles

    def tile_of(i, j):
        return vectors_ref[pl.ds(first + i * count_y + j, both, stride=tiles), :]

    for i in range(2):
        side_a_ref[i], side_b_ref[i] = pick(odd_y, tile_of(i, 0), tile_of(i, count_y - 1))
    for j in range(count_y):
        row_a_ref[j], row_b_ref[j] = pick(odd_x, tile_of(0, j), tile_of(1, j))


def rest_kernel(flags_ref, vectors_ref, rest_a_ref, rest_b_ref):
    count_y, rest, _ = rest_a_ref.shape
    odd_x = flag_at(flags_ref, 1)
    for j in range(count_y):
        rest_a_ref[j], rest_b_ref[j] = pick(
            odd_x,
            vectors_ref[pl.ds(j, rest, stride=2 * count_y), :],
            vectors_ref[pl.ds(count_y + j, rest, stride=2 * count_y), :],
        )


def corners_kernel(flags_ref, side_a_ref, side_b_ref, corner_a_ref, corner_b_ref):
    odd_y, odd_x = flag_at(flags_ref, 0), flag_at(flags_ref, 1)
    ends = [pick(odd_y, side_a_ref[i], side_b_ref[i]) for i in range(2)]
    for place in range(2):
        corner_a_ref[place], corner_b_ref[place] = pick(odd_x, ends[0][place], ends[1][place])


def columns_kernel(
    flags_ref, row_a_ref, row_b_ref, from_row_a_ref, from_row_b_ref, *refs
):
    odd_y, odd_x = flag_at(flags_ref, 0), flag_at(flags_ref, 1)
    side_a_ref, side_b_ref = refs[-2:]
    columns = []
    for j in (0, row_b_ref.shape[0] - 1):
        column = list(pick(odd_x, from_row_a_ref[j], from_row_b_ref[j]))
        column[1:1] = pick(odd_x, row_a_ref[j], row_b_ref[j])
        columns.append(column)
    for i in range(4):
        side_a_ref[i], side_b_ref[i] = pick(odd_y, columns[0][i], columns[1][i])
    if len(refs) == 3:
        side_a_ref[4] = refs[0][...]


def residual_kernel(
    neighbours_hbm_ref,
    kinds_hbm_ref,
    flags_ref,
    row_a_ref,
    row_b_ref,
    from_row_a_ref,
    from_row_b_ref,
    from_side_a_ref,
    from_side_b_ref,
    from_corner_a_ref,
    from_corner_b_ref,
    rest_a_ref,
    rest_b_ref,
    stiff_ref,
    mass_ref,
    residual_a_ref,
    residual_b_ref,
    partial_ref,
    current_ref,
    ext_ref,
    table_ref,
    neighbours_ref,
    kinds_ref,
    semaphores,
    total_ref,
    parts_ref,
    prior_ref,
):
    copies = code_copies(
        (neighbours_hbm_ref, kinds_hbm_ref), (neighbours_ref, kinds_ref), semaphores
    )
    for copy in copies:
        copy.start()
    split_tables(stiff_ref, mass_ref, table_ref, 1)
    count_y, both, side = row_a_ref.shape
    wide = count_y + 2
    block = both // 2
    rest = rest_a_ref.shape[1]
    odd_y, odd_x, in_low_y, in_high_y, in_low_x, in_high_x = (
        flag_at(flags_ref, place) for place in range(6)
    )

    def store(i, j, value):
        current_ref[i * wide + j] = value[:block]
        for part in range(2):
            high, low = split(value[part * block : (part + 1) * block])
            ext_ref[i * wide + j, :block, part * side : (part + 1) * side] = high
            ext_ref[i * wide + j, block:, part * side : (part + 1) * side] = low

    def own_tile(i, j):
        return pick(odd_x, row_a_ref[j], row_b_ref[j])[i]

    for j in range(count_y):
        store(1, j + 1, own_tile(0, j))
        store(2, j + 1, own_tile(1, j))
        low, high = pick(odd_x, from_row_a_ref[j], from_row_b_ref[j])
        store(0, j + 1, low * in_low_x)
        store(3, j + 1, high * in_high_x)
    for i in range(2):
        low, high = pick(odd_y, from_side_a_ref[i], from_side_b_ref[i])
        store(i + 1, 0, low * in_low_y)
        store(i + 1, wide - 1, high * in_high_y)
    for place, j, inside in ((0, 0, in_low_y), (1, wide - 1, in_high_y)):
        low, high = pick(odd_x, from_corner_a_ref[place], from_corner_b_ref[place])
        store(0, j, low * (in_low_x * inside))
        store(3, j, high * (in_high_x * inside))
    for copy in copies:
        copy.wait()
    for tile in range(2 * count_y):
        i, j = tile // count_y, tile % count_y
        own = own_tile(i, j)
        total = 4.0 * own[:block] + own[block:]
        for k in range(neighbours_ref.shape[1]):
            source, kind = source_and_kind(neighbours_ref, kinds_ref, tile, k, count_y)
            pair = mul(ext_ref[source], table_ref[kind])
            total = total + (pair[:block, :side] + (pair[block:, :side] + pair[:block, side:]))
        total_ref[tile] = total
        span = slice(tile * side, (tile + 1) * side)
        parts_ref[:, span] = stacked(total)
        rest_tile = pick(odd_x, rest_a_ref[j], rest_b_ref[j])[i]
        basis_tile = jnp.concatenate([rest_tile, own[:block]], axis=0)
        prior_ref[0, :, span], prior_ref[1, :, span] = split(basis_tile)
    partial = pair_sum(parts_ref[...], prior_ref[0], prior_ref[1])
    for j in range(count_y):
        residual_a_ref[j], residual_b_ref[j] = pick(
            odd_x, total_ref[j], total_ref[count_y + j]
        )
    residual_a_ref[count_y] = partial
    partial_ref[...] = partial


def prepare_kernel(
    flags_ref,
    rest_a_ref,
    rest_b_ref,
    from_rest_a_ref,
    from_rest_b_ref,
    rest_side_a_ref,
    rest_side_b_ref,
    current_ref,
    stiff_ref,
    mass_ref,
    basis_ref,
    prior_ref,
    table_ref,
):
    count_y, rest, side = rest_a_ref.shape
    wide = count_y + 2
    prior = rest + current_ref.shape[1]
    odd_y, odd_x = flag_at(flags_ref, 0), flag_at(flags_ref, 1)
    split_tables(stiff_ref, mass_ref, table_ref, 0)
    for j in range(wide):
        if 0 < j < wide - 1:
            rests = list(pick(odd_x, from_rest_a_ref[j - 1], from_rest_b_ref[j - 1]))
            rests[1:1] = pick(odd_x, rest_a_ref[j - 1], rest_b_ref[j - 1])
        else:
            rests = [
                pick(odd_y, rest_side_a_ref[i], rest_side_b_ref[i])[j // (wide - 1)]
                for i in range(4)
            ]
        for i in range(4):
            place = i * wide + j
            high, low = split(jnp.concatenate([rests[i], current_ref[place]], axis=0))
            columns = slice(j * side, (j + 1) * side)
            basis_ref[i, :prior, columns] = high
            basis_ref[i, prior:, columns] = low
            if 0 < i < 3 and 0 < j < wide - 1:
                tile = (i - 1) * count_y + j - 1
                span = slice(tile * side, (tile + 1) * side)
                prior_ref[0, :, span] = high
                prior_ref[1, :, span] = low


def operators_kernel(
    inverse_rows,
    neighbours_hbm_ref,
    kinds_hbm_ref,
    flags_ref,
    partial_ref,
    row_a_ref,
    row_b_ref,
    from_row_a_ref,
    from_row_b_ref,
    from_side_a_ref,
    from_side_b_ref,
    basis_ref,
    prior_ref,
    table_ref,
    weighted_low_ref,
    weighted_high_ref,
    sent_ref,
    kept_ref,
    ext_ref,
    neighbours_ref,
    kinds_ref,
    semaphores,
    parts_ref,
):
    copies = code_copies(
        (neighbours_hbm_ref, kinds_hbm_ref), (neighbours_ref, kinds_ref), semaphores
    )
    for copy in copies:
        copy.start()
    count_y, block, side = weighted_low_ref.shape
    wide = count_y + 2
    odd_y, odd_x, in_low_y, in_high_y, in_low_x, in_high_x = (
        flag_at(flags_ref, place) for place in range(6)
    )
    coupling_deep = deep(partial_ref[...] * inverse_rows)

    for i in range(4):
        moved = halves_sum(mul(coupling_deep, basis_ref[i]))
        for j in range(wide):
            if 0 < j < wide - 1:
                rows = list(pick(odd_x, from_row_a_ref[j - 1], from_row_b_ref[j - 1]))
                rows[1:1] = pick(odd_x, row_a_ref[j - 1], row_b_ref[j - 1])
                value = rows[i]
            else:
                value = pick(odd_y, from_side_a_ref[i], from_side_b_ref[i])[j // (wide - 1)]
            value = value - moved[:, j * side : (j + 1) * side]
            if i == 0:
                value = value * in_low_x
            if i == 3:
                value = value * in_high_x
            if j == 0:
                value = value * in_low_y
            if j == wide - 1:
                value = value * in_high_y
            if 0 < i < 3 and 0 < j < wide - 1:
                (weighted_low_ref, weighted_high_ref)[i - 1][j - 1] = value
            ext_ref[i * wide + j] = deep(value)
    for copy in copies:
        copy.wait()
    for tile in range(2 * count_y):
        i, j = tile // count_y, tile % count_y
        own = (weighted_low_ref, weighted_high_ref)[i][j]
        totals = jnp.concatenate([4.0 * own, own], axis=1)
        for k in range(neighbours_ref.shape[1]):
            source, kind = source_and_kind(neighbours_ref, kinds_ref, tile, k, count_y)
            totals = totals + halves_sum(mul(ext_ref[source], table_ref[kind]))
        rows = jnp.concatenate([totals[:, :side], totals[:, side:], own, own], axis=0)
        span = slice(tile * side, (tile + 1) * side)
        parts_ref[0, :, span], parts_ref[1, :, span] = split(rows)
    applied = [parts_ref[part, : 2 * block, :] for part in range(2)]
    own_parts = [parts_ref[part, 2 * block : 3 * block, :] for part in range(2)]
    with_basis = mul_t(applied[0], prior_ref[0]) + (
        mul_t(applied[0], prior_ref[1]) + mul_t(applied[1], prior_ref[0])
    )
    with_own = mul_t(own_parts[0], parts_ref[0]) + (
        mul_t(own_parts[0], parts_ref[1]) + mul_t(own_parts[1], parts_ref[0])
    )
    halves = [
        jnp.concatenate(
            [
                with_basis[part * block : (part + 1) * block],
                folded(with_own[:, part * block : (part + 1) * block]),
                folded(with_own[:, 2 * block : 3 * block]),
            ],
            axis=0,
        )
        for part in range(2)
    ]
    sent_ref[...], kept_ref[...] = pick(odd_y, halves[0], halves[1])


def folded(square):
    return jnp.concatenate([square[n * 8 : (n + 1) * 8] for n in range(4)], axis=1)


def unfolded(rows):
    return jnp.concatenate([rows[:, n * 32 : (n + 1) * 32] for n in range(4)], axis=0)


def factor_kernel(inverse_rows, sums_ref, work_ref):
    block = work_ref.shape[0]
    gram = unfolded(sums_ref[block + 8 :, :]) * inverse_rows
    row_ids = lax.broadcasted_iota(jnp.int32, (block, block), 0)
    column_ids = lax.broadcasted_iota(jnp.int32, (block, block), 1)
    unit = jnp.where(row_ids == column_ids, 1.0, 0.0).astype(F32)
    rest = jnp.concatenate([gram, unit], axis=1)
    group = 8
    done = []
    for j in range(0, block, group):
        rows = lax.broadcasted_iota(jnp.int32, rest.shape, 0)
        columns = [
            jnp.broadcast_to(rest[:, j + a : j + a + 1], rest.shape) for a in range(group)
        ]
        pivots = [rest[a : a + 1, :] for a in range(group)]
        for a in range(group):
            ratio = columns[a] * (1.0 / columns[a][a : a + 1, :])
            for b in range(a + 1, group):
                columns[b] = columns[b] - ratio * columns[b][a : a + 1, :]
                pivots[b] = pivots[b] - ratio[b : b + 1, :] * pivots[a]
            rest = rest - jnp.where(rows > a, ratio, 0.0) * pivots[a]
        done.append(rest[:group])
        rest = rest[group:]
    work = jnp.concatenate(done, axis=0)
    work = work * lax.rsqrt(jnp.sum(work[:, :block] * unit, axis=1, keepdims=True))
    work_ref[...] = work


def finish_kernel(
    inverse_rows,
    flags_ref,
    work_ref,
    sums_ref,
    other_ref,
    partial_ref,
    weighted_low_ref,
    weighted_high_ref,
    new_ref,
    coupling_ref,
    factor_ref,
    reduced_ref,
):
    coupling_ref[...] = partial_ref[...] * inverse_rows
    count_y, block, _ = weighted_low_ref.shape
    prior = sums_ref.shape[1]
    tiles = 2 * count_y
    row_ids = lax.broadcasted_iota(jnp.int32, (block, block), 0)
    column_ids = lax.broadcasted_iota(jnp.int32, (block, block), 1)
    factor_ref[...] = jnp.where(column_ids >= row_ids, work_ref[:, :block], 0.0)
    inverse = work_ref[:, block:]
    inverse_deep = deep(inverse)
    for tile in range(tiles):
        own = (weighted_low_ref, weighted_high_ref)[tile // count_y][tile % count_y]
        new_ref[pl.ds(tile, block, stride=tiles), :] = mul_deep(inverse_deep, own)
    odd_y = flag_at(flags_ref, 0)
    halves = pick(odd_y, other_ref[...], sums_ref[: block + 8, :])
    for part, half in enumerate(halves):
        reduced_ref[part, :, :prior] = mul_deep(inverse_deep, half[:block] * inverse_rows)
        own = unfolded(half[block:]) * inverse_rows
        reduced_ref[part, :, prior:] = mul3_t(mul3_t(inverse, own), inverse)


def swap(value, mask):
    axes = ("px", "py")
    pairs = [(i, i ^ mask) for i in range(lax.axis_size(axes))]
    return lax.ppermute(value, axes, pairs)


def exchange(message_a, message_b, axis):
    cases, count = lax.axis_size("case"), lax.axis_size(axis)
    near = [(i, i ^ 1) for i in range(count)]
    pairs = []
    for case in range(cases):
        for i in range(count):
            j = ((i + 1) ^ 1) - 1
            target = (case, j) if 0 <= j < count else ((case ^ 1) % cases, i)
            pairs.append((case * count + i, target[0] * count + target[1]))
    return lax.ppermute(message_a, axis, near), lax.ppermute(message_b, ("case", axis), pairs)


def total_over(value, first, last):
    while first < last:
        value = value + swap(value, first)
        first *= 2
    return value


def half_total(sent, kept):
    kept = kept + swap(sent, 1)
    kept = (kept + swap(kept, 6)) + (swap(kept, 2) + swap(kept, 4))
    return total_over(kept, 8, lax.axis_size(("px", "py")))


def shape(*dims, dtype=F32):
    return jax.ShapeDtypeStruct(dims, dtype)


def shards(prior_basis, previous, neighbours, tile_kinds, stiff_tiles, mass_tiles):
    block = previous.shape[0]
    prior, count_x, count_y, side = prior_basis.shape
    tiles = count_x * count_y
    wide = count_y + 2
    rest = prior - block
    kinds = stiff_tiles.shape[0]
    inverse_rows = 1.0 / (tiles * side * lax.axis_size("px") * lax.axis_size("py"))
    basis = prior_basis.reshape(-1, side)
    first = lax.optimization_barrier(jnp.int32(rest * tiles))
    current_rows = lax.dynamic_slice_in_dim(basis, first, block * tiles, axis=0)
    vectors = jnp.concatenate([current_rows, previous.reshape(-1, side)], axis=0)
    codes = [array.transpose(1, 2, 0).reshape(tiles, -1) for array in (neighbours, tile_kinds)]
    code_scratch = [pltpu.SMEM(array.shape, jnp.int32) for array in codes]
    code_scratch += [pltpu.SemaphoreType.DMA((2,))]
    at_y, at_x = lax.axis_index("py"), lax.axis_index("px")
    bits = (at_y & 1) + 2 * (at_x & 1)
    bits += 4 * (at_y > 0) + 8 * (at_y < lax.axis_size("py") - 1)
    bits += 16 * (at_x > 0) + 32 * (at_x < lax.axis_size("px") - 1)
    flags = ((bits >> lax.broadcasted_iota(jnp.int32, (8, side), 0)) & 1).astype(F32)

    def call(kernel, inputs, outputs, scratch=(), plain=0, limit=8, cost=None):
        specs = [ANY] * plain + [VMEM] * (len(inputs) - plain)
        return pl.pallas_call(
            kernel,
            out_shape=outputs,
            in_specs=specs,
            out_specs=[VMEM] * len(outputs),
            scratch_shapes=scratch,
            compiler_params=pltpu.CompilerParams(vmem_limit_bytes=limit * MIB),
            cost_estimate=cost,
        )(*inputs)

    side_a, side_b, row_a, row_b = call(
        pack_kernel,
        (flags, vectors),
        [shape(count_x, 2 * block, side)] * 2 + [shape(count_y, 2 * block, side)] * 2,
    )
    rest_a, rest_b = call(rest_kernel, (flags, basis), [shape(count_y, rest, side)] * 2)
    from_side_a, from_side_b = exchange(side_a, side_b, "py")
    from_row_a, from_row_b = exchange(row_a, row_b, "px")
    from_side_a, rest_a, rest_b = lax.optimization_barrier((from_side_a, rest_a, rest_b))
    from_rest_a, from_rest_b = exchange(rest_a, rest_b, "px")
    corner_a, corner_b = call(
        corners_kernel,
        (flags, from_side_a, from_side_b),
        [shape(2, 2 * block, side)] * 2,
    )
    from_corner_a, from_corner_b = exchange(corner_a, corner_b, "px")
    rest_side_a, rest_side_b = call(
        columns_kernel,
        (flags, rest_a, rest_b, from_rest_a, from_rest_b),
        [shape(4, rest, side)] * 2,
    )
    rest_side_a, rest_side_b = exchange(rest_side_a, rest_side_b, "py")
    residual_a, residual_b, partial, current = call(
        residual_kernel,
        (
            *codes,
            flags,
            row_a,
            row_b,
            from_row_a,
            from_row_b,
            from_side_a,
            from_side_b,
            from_corner_a,
            from_corner_b,
            rest_a,
            rest_b,
            stiff_tiles,
            mass_tiles,
        ),
        [shape(count_y + 1, block, side), shape(count_y, block, side)]
        + [shape(block, prior), shape(4 * wide, block, side)],
        [pltpu.VMEM((4 * wide, 2 * block, 2 * side), BF16)]
        + [pltpu.VMEM((kinds, 2 * side, 2 * side), BF16)]
        + code_scratch
        + [
            pltpu.VMEM((tiles, block, side), F32),
            pltpu.VMEM((2 * block, tiles * side), BF16),
            pltpu.VMEM((2, prior, tiles * side), BF16),
        ],
        plain=2,
        cost=pl.CostEstimate(flops=10**9, bytes_accessed=0, transcendentals=0),
    )
    count_py = lax.axis_size("py")
    from_row_a, from_row_b = exchange(residual_a, residual_b, "px")
    partial = total_over(
        partial + from_row_a[-1], 2 * count_py, count_py * lax.axis_size("px")
    )
    partial, rest_side_a, rest_side_b = lax.optimization_barrier(
        (partial, rest_side_a, rest_side_b)
    )
    side_a, side_b = call(
        columns_kernel,
        (flags, residual_a, residual_b, from_row_a, from_row_b, partial),
        [shape(5, block, side), shape(4, block, side)],
    )
    from_side_a, from_side_b = exchange(side_a, side_b, "py")
    partial = total_over(partial + from_side_a[-1], 2, count_py)
    basis_parts, prior_parts, table = call(
        prepare_kernel,
        (
            flags,
            rest_a,
            rest_b,
            from_rest_a,
            from_rest_b,
            rest_side_a,
            rest_side_b,
            current,
            stiff_tiles,
            mass_tiles,
        ),
        [shape(4, 2 * prior, wide * side, dtype=BF16)]
        + [shape(2, prior, tiles * side, dtype=BF16)]
        + [shape(kinds, 2 * side, 2 * side, dtype=BF16)],
        cost=pl.CostEstimate(flops=10**9, bytes_accessed=0, transcendentals=0),
    )
    weighted_low, weighted_high, sent, kept = call(
        functools.partial(operators_kernel, inverse_rows),
        (
            *codes,
            flags,
            partial,
            residual_a,
            residual_b,
            from_row_a,
            from_row_b,
            from_side_a,
            from_side_b,
            basis_parts,
            prior_parts,
            table,
        ),
        [shape(count_y, block, side)] * 2 + [shape(block + 16, prior)] * 2,
        [pltpu.VMEM((4 * wide, 2 * block, 2 * side), BF16)]
        + code_scratch
        + [pltpu.VMEM((2, 4 * block, tiles * side), BF16)],
        plain=2,
    )
    kept = half_total(sent, kept)
    other = swap(kept[: block + 8], 1)
    (work,) = call(
        functools.partial(factor_kernel, inverse_rows),
        (kept,),
        [shape(block, 2 * block)],
        cost=pl.CostEstimate(flops=10**9, bytes_accessed=0, transcendentals=0),
    )
    new_block, coupling, factor, reduced = call(
        functools.partial(finish_kernel, inverse_rows),
        (flags, work, kept, other, partial, weighted_low, weighted_high),
        [
            shape(block * tiles, side),
            shape(block, prior),
            shape(block, block),
            shape(2, block, prior + block),
        ],
    )
    return (
        new_block.reshape(previous.shape),
        coupling.T,
        factor,
        reduced.swapaxes(1, 2),
    )


def solution(mesh):
    placed = (
        P("case", "px", "py", None),
        P("case", "px", "py", None),
        P(None, "px", "py"),
        P(None, "px", "py"),
        P(),
        P(),
    )
    return jax.shard_map(
        shards,
        mesh=mesh,
        in_specs=placed,
        out_specs=(
            P("case", "px", "py", None),
            P("case", None),
            P("case", None),
            P("case", None, None),
        ),
        check_vma=False,
    )
```

```python
import functools

import jax
import jax.numpy as jnp
from jax import lax
from jax.experimental import pallas as pl
from jax.experimental.pallas import tpu as pltpu
from jax.sharding import PartitionSpec as P

F32 = jnp.float32
BF16 = jnp.bfloat16
VMEM = pl.BlockSpec(memory_space=pltpu.VMEM)
ANY = pl.BlockSpec(memory_space=pl.ANY)
MIB = 1024 * 1024


def split(value):
    high = value.astype(BF16)
    return high, (value - high.astype(F32)).astype(BF16)


def mul(left, right):
    return jnp.dot(left, right, preferred_element_type=F32)


def mul_t(left, right):
    return lax.dot_general(left, right, (((1,), (1,)), ((), ())), preferred_element_type=F32)


def mul3(left, right):
    left_high, left_low = split(left)
    right_high, right_low = split(right)
    return mul(left_high, right_high) + (mul(left_high, right_low) + mul(left_low, right_high))


def mul3_t(left, right):
    left_high, left_low = split(left)
    right_high, right_low = split(right)
    return mul_t(left_high, right_high) + (
        mul_t(left_high, right_low) + mul_t(left_low, right_high)
    )


def split_tables(stiff_ref, mass_ref, table_ref, parts_axis):
    side = stiff_ref.shape[1]
    spans = (slice(0, side), slice(side, 2 * side))
    for kind in range(stiff_ref.shape[0]):
        for matrix, ref in zip(spans, (stiff_ref, mass_ref)):
            for part, value in zip(spans, split(ref[kind])):
                if parts_axis == 1:
                    table_ref[kind, matrix, part] = value
                else:
                    table_ref[kind, part, matrix] = value


def stacked(value):
    return jnp.concatenate(split(value), axis=0)


def deep(value):
    high, low = split(value)
    upper = jnp.concatenate([high, high], axis=1)
    return jnp.concatenate([upper, jnp.concatenate([low, jnp.zeros_like(low)], axis=1)], axis=0)


def halves_sum(value):
    half = value.shape[0] // 2
    return value[:half] + value[half:]


def mul_deep(left_deep, right):
    return halves_sum(mul(left_deep, stacked(right)))


def pair_sum(left, right_high, right_low):
    rows = left.shape[0] // 2
    return halves_sum(mul_t(left, right_high)) + mul_t(left[:rows], right_low)


def pick(flag, first, second):
    flag = flag > 0.0
    return jnp.where(flag, first, second), jnp.where(flag, second, first)


def flag_at(flags_ref, place):
    return flags_ref[place : place + 1, :]


def code_copies(code_refs, local_refs, semaphores):
    return [
        pltpu.make_async_copy(ref, local, semaphores.at[n])
        for n, (ref, local) in enumerate(zip(code_refs, local_refs))
    ]


def source_and_kind(neighbours_ref, kinds_ref, tile, k, count_y):
    neighbour = neighbours_ref[tile, k]
    down = (neighbour * 11) >> 5
    first = (tile // count_y) * (count_y + 2) + tile % count_y
    return first + neighbour + down * (count_y - 1), kinds_ref[tile, k]


def pack_kernel(flags_ref, vectors_ref, side_a_ref, side_b_ref, row_a_ref, row_b_ref):
    count_y, both, _ = row_a_ref.shape
    tiles = 2 * count_y
    odd_y, odd_x = flag_at(flags_ref, 0), flag_at(flags_ref, 1)

    first = vectors_ref.shape[0] - both * tiles

    def tile_of(i, j):
        return vectors_ref[pl.ds(first + i * count_y + j, both, stride=tiles), :]

    for i in range(2):
        side_a_ref[i], side_b_ref[i] = pick(odd_y, tile_of(i, 0), tile_of(i, count_y - 1))
    for j in range(count_y):
        row_a_ref[j], row_b_ref[j] = pick(odd_x, tile_of(0, j), tile_of(1, j))


def rest_kernel(flags_ref, vectors_ref, rest_a_ref, rest_b_ref):
    count_y, rest, _ = rest_a_ref.shape
    odd_x = flag_at(flags_ref, 1)
    for j in range(count_y):
        rest_a_ref[j], rest_b_ref[j] = pick(
            odd_x,
            vectors_ref[pl.ds(j, rest, stride=2 * count_y), :],
            vectors_ref[pl.ds(count_y + j, rest, stride=2 * count_y), :],
        )


def corners_kernel(flags_ref, side_a_ref, side_b_ref, corner_a_ref, corner_b_ref):
    odd_y, odd_x = flag_at(flags_ref, 0), flag_at(flags_ref, 1)
    ends = [pick(odd_y, side_a_ref[i], side_b_ref[i]) for i in range(2)]
    for place in range(2):
        corner_a_ref[place], corner_b_ref[place] = pick(odd_x, ends[0][place], ends[1][place])


def columns_kernel(
    flags_ref, row_a_ref, row_b_ref, from_row_a_ref, from_row_b_ref, *refs
):
    odd_y, odd_x = flag_at(flags_ref, 0), flag_at(flags_ref, 1)
    side_a_ref, side_b_ref = refs[-2:]
    columns = []
    for j in (0, row_b_ref.shape[0] - 1):
        column = list(pick(odd_x, from_row_a_ref[j], from_row_b_ref[j]))
        column[1:1] = pick(odd_x, row_a_ref[j], row_b_ref[j])
        columns.append(column)
    for i in range(4):
        side_a_ref[i], side_b_ref[i] = pick(odd_y, columns[0][i], columns[1][i])
    if len(refs) == 3:
        side_a_ref[4] = refs[0][...]


def residual_kernel(
    neighbours_hbm_ref,
    kinds_hbm_ref,
    flags_ref,
    row_a_ref,
    row_b_ref,
    from_row_a_ref,
    from_row_b_ref,
    from_side_a_ref,
    from_side_b_ref,
    from_corner_a_ref,
    from_corner_b_ref,
    rest_a_ref,
    rest_b_ref,
    stiff_ref,
    mass_ref,
    residual_a_ref,
    residual_b_ref,
    partial_ref,
    current_ref,
    ext_ref,
    table_ref,
    neighbours_ref,
    kinds_ref,
    semaphores,
    total_ref,
    parts_ref,
    prior_ref,
):
    copies = code_copies(
        (neighbours_hbm_ref, kinds_hbm_ref), (neighbours_ref, kinds_ref), semaphores
    )
    for copy in copies:
        copy.start()
    split_tables(stiff_ref, mass_ref, table_ref, 1)
    count_y, both, side = row_a_ref.shape
    wide = count_y + 2
    block = both // 2
    rest = rest_a_ref.shape[1]
    odd_y, odd_x, in_low_y, in_high_y, in_low_x, in_high_x = (
        flag_at(flags_ref, place) for place in range(6)
    )

    def store(i, j, value):
        current_ref[i * wide + j] = value[:block]
        for part in range(2):
            high, low = split(value[part * block : (part + 1) * block])
            ext_ref[i * wide + j, :block, part * side : (part + 1) * side] = high
            ext_ref[i * wide + j, block:, part * side : (part + 1) * side] = low

    def own_tile(i, j):
        return pick(odd_x, row_a_ref[j], row_b_ref[j])[i]

    for j in range(count_y):
        store(1, j + 1, own_tile(0, j))
        store(2, j + 1, own_tile(1, j))
        low, high = pick(odd_x, from_row_a_ref[j], from_row_b_ref[j])
        store(0, j + 1, low * in_low_x)
        store(3, j + 1, high * in_high_x)
    for i in range(2):
        low, high = pick(odd_y, from_side_a_ref[i], from_side_b_ref[i])
        store(i + 1, 0, low * in_low_y)
        store(i + 1, wide - 1, high * in_high_y)
    for place, j, inside in ((0, 0, in_low_y), (1, wide - 1, in_high_y)):
        low, high = pick(odd_x, from_corner_a_ref[place], from_corner_b_ref[place])
        store(0, j, low * (in_low_x * inside))
        store(3, j, high * (in_high_x * inside))
    for copy in copies:
        copy.wait()
    for tile in range(2 * count_y):
        i, j = tile // count_y, tile % count_y
        own = own_tile(i, j)
        total = 4.0 * own[:block] + own[block:]
        for k in range(neighbours_ref.shape[1]):
            source, kind = source_and_kind(neighbours_ref, kinds_ref, tile, k, count_y)
            pair = mul(ext_ref[source], table_ref[kind])
            total = total + (pair[:block, :side] + (pair[block:, :side] + pair[:block, side:]))
        total_ref[tile] = total
        span = slice(tile * side, (tile + 1) * side)
        parts_ref[:, span] = stacked(total)
        rest_tile = pick(odd_x, rest_a_ref[j], rest_b_ref[j])[i]
        basis_tile = jnp.concatenate([rest_tile, own[:block]], axis=0)
        prior_ref[0, :, span], prior_ref[1, :, span] = split(basis_tile)
    partial = pair_sum(parts_ref[...], prior_ref[0], prior_ref[1])
    for j in range(count_y):
        residual_a_ref[j], residual_b_ref[j] = pick(
            odd_x, total_ref[j], total_ref[count_y + j]
        )
    residual_a_ref[count_y] = partial
    partial_ref[...] = partial


def prepare_kernel(
    flags_ref,
    rest_a_ref,
    rest_b_ref,
    from_rest_a_ref,
    from_rest_b_ref,
    rest_side_a_ref,
    rest_side_b_ref,
    current_ref,
    stiff_ref,
    mass_ref,
    basis_ref,
    prior_ref,
    table_ref,
):
    count_y, rest, side = rest_a_ref.shape
    wide = count_y + 2
    prior = rest + current_ref.shape[1]
    odd_y, odd_x = flag_at(flags_ref, 0), flag_at(flags_ref, 1)
    split_tables(stiff_ref, mass_ref, table_ref, 0)
    for j in range(wide):
        if 0 < j < wide - 1:
            rests = list(pick(odd_x, from_rest_a_ref[j - 1], from_rest_b_ref[j - 1]))
            rests[1:1] = pick(odd_x, rest_a_ref[j - 1], rest_b_ref[j - 1])
        else:
            rests = [
                pick(odd_y, rest_side_a_ref[i], rest_side_b_ref[i])[j // (wide - 1)]
                for i in range(4)
            ]
        for i in range(4):
            place = i * wide + j
            high, low = split(jnp.concatenate([rests[i], current_ref[place]], axis=0))
            columns = slice(j * side, (j + 1) * side)
            basis_ref[i, :prior, columns] = high
            basis_ref[i, prior:, columns] = low
            if 0 < i < 3 and 0 < j < wide - 1:
                tile = (i - 1) * count_y + j - 1
                span = slice(tile * side, (tile + 1) * side)
                prior_ref[0, :, span] = high
                prior_ref[1, :, span] = low


def operators_kernel(
    inverse_rows,
    neighbours_hbm_ref,
    kinds_hbm_ref,
    flags_ref,
    partial_ref,
    row_a_ref,
    row_b_ref,
    from_row_a_ref,
    from_row_b_ref,
    from_side_a_ref,
    from_side_b_ref,
    basis_ref,
    prior_ref,
    table_ref,
    weighted_low_ref,
    weighted_high_ref,
    sent_ref,
    kept_ref,
    ext_ref,
    neighbours_ref,
    kinds_ref,
    semaphores,
    parts_ref,
):
    copies = code_copies(
        (neighbours_hbm_ref, kinds_hbm_ref), (neighbours_ref, kinds_ref), semaphores
    )
    for copy in copies:
        copy.start()
    count_y, block, side = weighted_low_ref.shape
    wide = count_y + 2
    odd_y, odd_x, in_low_y, in_high_y, in_low_x, in_high_x = (
        flag_at(flags_ref, place) for place in range(6)
    )
    coupling_deep = deep(partial_ref[...] * inverse_rows)

    for i in range(4):
        moved = halves_sum(mul(coupling_deep, basis_ref[i]))
        for j in range(wide):
            if 0 < j < wide - 1:
                rows = list(pick(odd_x, from_row_a_ref[j - 1], from_row_b_ref[j - 1]))
                rows[1:1] = pick(odd_x, row_a_ref[j - 1], row_b_ref[j - 1])
                value = rows[i]
            else:
                value = pick(odd_y, from_side_a_ref[i], from_side_b_ref[i])[j // (wide - 1)]
            value = value - moved[:, j * side : (j + 1) * side]
            if i == 0:
                value = value * in_low_x
            if i == 3:
                value = value * in_high_x
            if j == 0:
                value = value * in_low_y
            if j == wide - 1:
                value = value * in_high_y
            if 0 < i < 3 and 0 < j < wide - 1:
                (weighted_low_ref, weighted_high_ref)[i - 1][j - 1] = value
            ext_ref[i * wide + j] = deep(value)
    for copy in copies:
        copy.wait()
    for tile in range(2 * count_y):
        i, j = tile // count_y, tile % count_y
        own = (weighted_low_ref, weighted_high_ref)[i][j]
        totals = jnp.concatenate([4.0 * own, own], axis=1)
        for k in range(neighbours_ref.shape[1]):
            source, kind = source_and_kind(neighbours_ref, kinds_ref, tile, k, count_y)
            totals = totals + halves_sum(mul(ext_ref[source], table_ref[kind]))
        rows = jnp.concatenate([totals[:, :side], totals[:, side:], own, own], axis=0)
        span = slice(tile * side, (tile + 1) * side)
        parts_ref[0, :, span], parts_ref[1, :, span] = split(rows)
    applied = [parts_ref[part, : 2 * block, :] for part in range(2)]
    own_parts = [parts_ref[part, 2 * block : 3 * block, :] for part in range(2)]
    with_basis = mul_t(applied[0], prior_ref[0]) + (
        mul_t(applied[0], prior_ref[1]) + mul_t(applied[1], prior_ref[0])
    )
    with_own = mul_t(own_parts[0], parts_ref[0]) + (
        mul_t(own_parts[0], parts_ref[1]) + mul_t(own_parts[1], parts_ref[0])
    )
    halves = [
        jnp.concatenate(
            [
                with_basis[part * block : (part + 1) * block],
                folded(with_own[:, part * block : (part + 1) * block]),
                folded(with_own[:, 2 * block : 3 * block]),
            ],
            axis=0,
        )
        for part in range(2)
    ]
    sent_ref[...], kept_ref[...] = pick(odd_y, halves[0], halves[1])


def folded(square):
    return jnp.concatenate([square[n * 8 : (n + 1) * 8] for n in range(4)], axis=1)


def unfolded(rows):
    return jnp.concatenate([rows[:, n * 32 : (n + 1) * 32] for n in range(4)], axis=0)


def factor_kernel(inverse_rows, sums_ref, work_ref):
    block = work_ref.shape[0]
    gram = unfolded(sums_ref[block + 8 :, :]) * inverse_rows
    row_ids = lax.broadcasted_iota(jnp.int32, (block, block), 0)
    column_ids = lax.broadcasted_iota(jnp.int32, (block, block), 1)
    unit = jnp.where(row_ids == column_ids, 1.0, 0.0).astype(F32)
    rest = jnp.concatenate([gram, unit], axis=1)
    group = 8
    done = []
    for j in range(0, block, group):
        rows = lax.broadcasted_iota(jnp.int32, rest.shape, 0)
        columns = [
            jnp.broadcast_to(rest[:, j + a : j + a + 1], rest.shape) for a in range(group)
        ]
        pivots = [rest[a : a + 1, :] for a in range(group)]
        for a in range(group):
            ratio = columns[a] * (1.0 / columns[a][a : a + 1, :])
            for b in range(a + 1, group):
                columns[b] = columns[b] - ratio * columns[b][a : a + 1, :]
                pivots[b] = pivots[b] - ratio[b : b + 1, :] * pivots[a]
            rest = rest - jnp.where(rows > a, ratio, 0.0) * pivots[a]
        done.append(rest[:group])
        rest = rest[group:]
    work = jnp.concatenate(done, axis=0)
    work = work * lax.rsqrt(jnp.sum(work[:, :block] * unit, axis=1, keepdims=True))
    work_ref[...] = work


def finish_kernel(
    inverse_rows,
    flags_ref,
    work_ref,
    sums_ref,
    other_ref,
    partial_ref,
    weighted_low_ref,
    weighted_high_ref,
    new_ref,
    coupling_ref,
    factor_ref,
    reduced_ref,
):
    coupling_ref[...] = partial_ref[...] * inverse_rows
    count_y, block, _ = weighted_low_ref.shape
    prior = sums_ref.shape[1]
    tiles = 2 * count_y
    row_ids = lax.broadcasted_iota(jnp.int32, (block, block), 0)
    column_ids = lax.broadcasted_iota(jnp.int32, (block, block), 1)
    factor_ref[...] = jnp.where(column_ids >= row_ids, work_ref[:, :block], 0.0)
    inverse = work_ref[:, block:]
    inverse_deep = deep(inverse)
    for tile in range(tiles):
        own = (weighted_low_ref, weighted_high_ref)[tile // count_y][tile % count_y]
        new_ref[pl.ds(tile, block, stride=tiles), :] = mul_deep(inverse_deep, own)
    odd_y = flag_at(flags_ref, 0)
    halves = pick(odd_y, other_ref[...], sums_ref[: block + 8, :])
    for part, half in enumerate(halves):
        reduced_ref[part, :, :prior] = mul_deep(inverse_deep, half[:block] * inverse_rows)
        own = unfolded(half[block:]) * inverse_rows
        reduced_ref[part, :, prior:] = mul3_t(mul3_t(inverse, own), inverse)


def swap(value, mask):
    axes = ("px", "py")
    pairs = [(i, i ^ mask) for i in range(lax.axis_size(axes))]
    return lax.ppermute(value, axes, pairs)


def exchange(message_a, message_b, axis):
    cases, count = lax.axis_size("case"), lax.axis_size(axis)
    near = [(i, i ^ 1) for i in range(count)]
    pairs = []
    for case in range(cases):
        for i in range(count):
            j = ((i + 1) ^ 1) - 1
            target = (case, j) if 0 <= j < count else ((case ^ 1) % cases, i)
            pairs.append((case * count + i, target[0] * count + target[1]))
    return lax.ppermute(message_a, axis, near), lax.ppermute(message_b, ("case", axis), pairs)


def total_over(value, first, last):
    while first < last:
        value = value + swap(value, first)
        first *= 2
    return value


def half_total(sent, kept):
    kept = kept + swap(sent, 1)
    kept = (kept + swap(kept, 6)) + (swap(kept, 2) + swap(kept, 4))
    return total_over(kept, 8, lax.axis_size(("px", "py")))


def shape(*dims, dtype=F32):
    return jax.ShapeDtypeStruct(dims, dtype)


def shards(prior_basis, previous, neighbours, tile_kinds, stiff_tiles, mass_tiles):
    block = previous.shape[0]
    prior, count_x, count_y, side = prior_basis.shape
    tiles = count_x * count_y
    wide = count_y + 2
    rest = prior - block
    kinds = stiff_tiles.shape[0]
    inverse_rows = 1.0 / (tiles * side * lax.axis_size("px") * lax.axis_size("py"))
    basis = prior_basis.reshape(-1, side)
    vectors = jnp.concatenate([basis, previous.reshape(-1, side)], axis=0)
    codes = [array.transpose(1, 2, 0).reshape(tiles, -1) for array in (neighbours, tile_kinds)]
    code_scratch = [pltpu.SMEM(array.shape, jnp.int32) for array in codes]
    code_scratch += [pltpu.SemaphoreType.DMA((2,))]
    at_y, at_x = lax.axis_index("py"), lax.axis_index("px")
    bits = (at_y & 1) + 2 * (at_x & 1)
    bits += 4 * (at_y > 0) + 8 * (at_y < lax.axis_size("py") - 1)
    bits += 16 * (at_x > 0) + 32 * (at_x < lax.axis_size("px") - 1)
    flags = ((bits >> lax.broadcasted_iota(jnp.int32, (8, side), 0)) & 1).astype(F32)

    def call(kernel, inputs, outputs, scratch=(), plain=0, limit=8, cost=None):
        specs = [ANY] * plain + [VMEM] * (len(inputs) - plain)
        return pl.pallas_call(
            kernel,
            out_shape=outputs,
            in_specs=specs,
            out_specs=[VMEM] * len(outputs),
            scratch_shapes=scratch,
            compiler_params=pltpu.CompilerParams(vmem_limit_bytes=limit * MIB),
            cost_estimate=cost,
        )(*inputs)

    side_a, side_b, row_a, row_b = call(
        pack_kernel,
        (flags, vectors),
        [shape(count_x, 2 * block, side)] * 2 + [shape(count_y, 2 * block, side)] * 2,
    )
    rest_a, rest_b = call(rest_kernel, (flags, vectors), [shape(count_y, rest, side)] * 2)
    from_side_a, from_side_b = exchange(side_a, side_b, "py")
    from_row_a, from_row_b = exchange(row_a, row_b, "px")
    from_side_a, rest_a, rest_b = lax.optimization_barrier((from_side_a, rest_a, rest_b))
    from_rest_a, from_rest_b = exchange(rest_a, rest_b, "px")
    corner_a, corner_b = call(
        corners_kernel,
        (flags, from_side_a, from_side_b),
        [shape(2, 2 * block, side)] * 2,
    )
    from_corner_a, from_corner_b = exchange(corner_a, corner_b, "px")
    rest_side_a, rest_side_b = call(
        columns_kernel,
        (flags, rest_a, rest_b, from_rest_a, from_rest_b),
        [shape(4, rest, side)] * 2,
    )
    rest_side_a, rest_side_b = exchange(rest_side_a, rest_side_b, "py")
    residual_a, residual_b, partial, current = call(
        residual_kernel,
        (
            *codes,
            flags,
            row_a,
            row_b,
            from_row_a,
            from_row_b,
            from_side_a,
            from_side_b,
            from_corner_a,
            from_corner_b,
            rest_a,
            rest_b,
            stiff_tiles,
            mass_tiles,
        ),
        [shape(count_y + 1, block, side), shape(count_y, block, side)]
        + [shape(block, prior), shape(4 * wide, block, side)],
        [pltpu.VMEM((4 * wide, 2 * block, 2 * side), BF16)]
        + [pltpu.VMEM((kinds, 2 * side, 2 * side), BF16)]
        + code_scratch
        + [
            pltpu.VMEM((tiles, block, side), F32),
            pltpu.VMEM((2 * block, tiles * side), BF16),
            pltpu.VMEM((2, prior, tiles * side), BF16),
        ],
        plain=2,
        cost=pl.CostEstimate(flops=10**9, bytes_accessed=0, transcendentals=0),
    )
    count_py = lax.axis_size("py")
    from_row_a, from_row_b = exchange(residual_a, residual_b, "px")
    partial = total_over(
        partial + from_row_a[-1], 2 * count_py, count_py * lax.axis_size("px")
    )
    partial, rest_side_a, rest_side_b = lax.optimization_barrier(
        (partial, rest_side_a, rest_side_b)
    )
    side_a, side_b = call(
        columns_kernel,
        (flags, residual_a, residual_b, from_row_a, from_row_b, partial),
        [shape(5, block, side), shape(4, block, side)],
    )
    from_side_a, from_side_b = exchange(side_a, side_b, "py")
    partial = total_over(partial + from_side_a[-1], 2, count_py)
    basis_parts, prior_parts, table = call(
        prepare_kernel,
        (
            flags,
            rest_a,
            rest_b,
            from_rest_a,
            from_rest_b,
            rest_side_a,
            rest_side_b,
            current,
            stiff_tiles,
            mass_tiles,
        ),
        [shape(4, 2 * prior, wide * side, dtype=BF16)]
        + [shape(2, prior, tiles * side, dtype=BF16)]
        + [shape(kinds, 2 * side, 2 * side, dtype=BF16)],
        cost=pl.CostEstimate(flops=10**9, bytes_accessed=0, transcendentals=0),
    )
    weighted_low, weighted_high, sent, kept = call(
        functools.partial(operators_kernel, inverse_rows),
        (
            *codes,
            flags,
            partial,
            residual_a,
            residual_b,
            from_row_a,
            from_row_b,
            from_side_a,
            from_side_b,
            basis_parts,
            prior_parts,
            table,
        ),
        [shape(count_y, block, side)] * 2 + [shape(block + 16, prior)] * 2,
        [pltpu.VMEM((4 * wide, 2 * block, 2 * side), BF16)]
        + code_scratch
        + [pltpu.VMEM((2, 4 * block, tiles * side), BF16)],
        plain=2,
    )
    kept = half_total(sent, kept)
    other = swap(kept[: block + 8], 1)
    (work,) = call(
        functools.partial(factor_kernel, inverse_rows),
        (kept,),
        [shape(block, 2 * block)],
        cost=pl.CostEstimate(flops=10**9, bytes_accessed=0, transcendentals=0),
    )
    new_block, coupling, factor, reduced = call(
        functools.partial(finish_kernel, inverse_rows),
        (flags, work, kept, other, partial, weighted_low, weighted_high),
        [
            shape(block * tiles, side),
            shape(block, prior),
            shape(block, block),
            shape(2, block, prior + block),
        ],
    )
    return (
        new_block.reshape(previous.shape),
        coupling.T,
        factor,
        reduced.swapaxes(1, 2),
    )


def solution(mesh):
    placed = (
        P("case", "px", "py", None),
        P("case", "px", "py", None),
        P(None, "px", "py"),
        P(None, "px", "py"),
        P(),
        P(),
    )
    return jax.shard_map(
        shards,
        mesh=mesh,
        in_specs=placed,
        out_specs=(
            P("case", "px", "py", None),
            P("case", None),
            P("case", None),
            P("case", None, None),
        ),
        check_vma=False,
    )
```

```python
import functools

import jax
import jax.numpy as jnp
from jax import lax
from jax.experimental import pallas as pl
from jax.experimental.pallas import tpu as pltpu
from jax.sharding import PartitionSpec as P

F32 = jnp.float32
BF16 = jnp.bfloat16
VMEM = pl.BlockSpec(memory_space=pltpu.VMEM)
ANY = pl.BlockSpec(memory_space=pl.ANY)
MIB = 1024 * 1024


def split(value):
    high = value.astype(BF16)
    return high, (value - high.astype(F32)).astype(BF16)


def mul(left, right):
    return jnp.dot(left, right, preferred_element_type=F32)


def mul_t(left, right):
    return lax.dot_general(left, right, (((1,), (1,)), ((), ())), preferred_element_type=F32)


def mul3(left, right):
    left_high, left_low = split(left)
    right_high, right_low = split(right)
    return mul(left_high, right_high) + (mul(left_high, right_low) + mul(left_low, right_high))


def mul3_t(left, right):
    left_high, left_low = split(left)
    right_high, right_low = split(right)
    return mul_t(left_high, right_high) + (
        mul_t(left_high, right_low) + mul_t(left_low, right_high)
    )


def split_tables(stiff_ref, mass_ref, table_ref, parts_axis):
    side = stiff_ref.shape[1]
    spans = (slice(0, side), slice(side, 2 * side))
    for kind in range(stiff_ref.shape[0]):
        for matrix, ref in zip(spans, (stiff_ref, mass_ref)):
            for part, value in zip(spans, split(ref[kind])):
                if parts_axis == 1:
                    table_ref[kind, matrix, part] = value
                else:
                    table_ref[kind, part, matrix] = value


def stacked(value):
    return jnp.concatenate(split(value), axis=0)


def deep(value):
    high, low = split(value)
    upper = jnp.concatenate([high, high], axis=1)
    return jnp.concatenate([upper, jnp.concatenate([low, jnp.zeros_like(low)], axis=1)], axis=0)


def halves_sum(value):
    half = value.shape[0] // 2
    return value[:half] + value[half:]


def mul_deep(left_deep, right):
    return halves_sum(mul(left_deep, stacked(right)))


def pair_sum(left, right_high, right_low):
    rows = left.shape[0] // 2
    return halves_sum(mul_t(left, right_high)) + mul_t(left[:rows], right_low)


def pick(flag, first, second):
    flag = flag > 0.0
    return jnp.where(flag, first, second), jnp.where(flag, second, first)


def flag_at(flags_ref, place):
    return flags_ref[place : place + 1, :]


def code_copies(code_refs, local_refs, semaphores):
    return [
        pltpu.make_async_copy(ref, local, semaphores.at[n])
        for n, (ref, local) in enumerate(zip(code_refs, local_refs))
    ]


def source_and_kind(neighbours_ref, kinds_ref, tile, k, count_y):
    neighbour = neighbours_ref[tile, k]
    down = (neighbour * 11) >> 5
    first = (tile // count_y) * (count_y + 2) + tile % count_y
    return first + neighbour + down * (count_y - 1), kinds_ref[tile, k]


def pack_kernel(flags_ref, vectors_ref, side_a_ref, side_b_ref, row_a_ref, row_b_ref):
    count_y, both, _ = row_a_ref.shape
    tiles = 2 * count_y
    odd_y, odd_x = flag_at(flags_ref, 0), flag_at(flags_ref, 1)

    first = vectors_ref.shape[0] - both * tiles

    def tile_of(i, j):
        return vectors_ref[pl.ds(first + i * count_y + j, both, stride=tiles), :]

    for i in range(2):
        side_a_ref[i], side_b_ref[i] = pick(odd_y, tile_of(i, 0), tile_of(i, count_y - 1))
    for j in range(count_y):
        row_a_ref[j], row_b_ref[j] = pick(odd_x, tile_of(0, j), tile_of(1, j))


def rest_kernel(flags_ref, vectors_ref, rest_a_ref, rest_b_ref):
    count_y, rest, _ = rest_a_ref.shape
    odd_x = flag_at(flags_ref, 1)
    for j in range(count_y):
        rest_a_ref[j], rest_b_ref[j] = pick(
            odd_x,
            vectors_ref[pl.ds(j, rest, stride=2 * count_y), :],
            vectors_ref[pl.ds(count_y + j, rest, stride=2 * count_y), :],
        )


def corners_kernel(flags_ref, side_a_ref, side_b_ref, corner_a_ref, corner_b_ref):
    odd_y, odd_x = flag_at(flags_ref, 0), flag_at(flags_ref, 1)
    ends = [pick(odd_y, side_a_ref[i], side_b_ref[i]) for i in range(2)]
    for place in range(2):
        corner_a_ref[place], corner_b_ref[place] = pick(odd_x, ends[0][place], ends[1][place])


def columns_kernel(
    flags_ref, row_a_ref, row_b_ref, from_row_a_ref, from_row_b_ref, *refs
):
    odd_y, odd_x = flag_at(flags_ref, 0), flag_at(flags_ref, 1)
    side_a_ref, side_b_ref = refs[-2:]
    columns = []
    for j in (0, row_b_ref.shape[0] - 1):
        column = list(pick(odd_x, from_row_a_ref[j], from_row_b_ref[j]))
        column[1:1] = pick(odd_x, row_a_ref[j], row_b_ref[j])
        columns.append(column)
    for i in range(4):
        side_a_ref[i], side_b_ref[i] = pick(odd_y, columns[0][i], columns[1][i])
    if len(refs) == 3:
        side_a_ref[4] = refs[0][...]


def residual_kernel(
    neighbours_hbm_ref,
    kinds_hbm_ref,
    flags_ref,
    row_a_ref,
    row_b_ref,
    from_row_a_ref,
    from_row_b_ref,
    from_side_a_ref,
    from_side_b_ref,
    from_corner_a_ref,
    from_corner_b_ref,
    rest_a_ref,
    rest_b_ref,
    stiff_ref,
    mass_ref,
    residual_a_ref,
    residual_b_ref,
    partial_ref,
    current_ref,
    ext_ref,
    table_ref,
    neighbours_ref,
    kinds_ref,
    semaphores,
    total_ref,
    parts_ref,
    prior_ref,
):
    copies = code_copies(
        (neighbours_hbm_ref, kinds_hbm_ref), (neighbours_ref, kinds_ref), semaphores
    )
    for copy in copies:
        copy.start()
    split_tables(stiff_ref, mass_ref, table_ref, 1)
    count_y, both, side = row_a_ref.shape
    wide = count_y + 2
    block = both // 2
    rest = rest_a_ref.shape[1]
    odd_y, odd_x, in_low_y, in_high_y, in_low_x, in_high_x = (
        flag_at(flags_ref, place) for place in range(6)
    )

    def store(i, j, value):
        current_ref[i * wide + j] = value[:block]
        for part in range(2):
            high, low = split(value[part * block : (part + 1) * block])
            ext_ref[i * wide + j, :block, part * side : (part + 1) * side] = high
            ext_ref[i * wide + j, block:, part * side : (part + 1) * side] = low

    def own_tile(i, j):
        return pick(odd_x, row_a_ref[j], row_b_ref[j])[i]

    for j in range(count_y):
        store(1, j + 1, own_tile(0, j))
        store(2, j + 1, own_tile(1, j))
        low, high = pick(odd_x, from_row_a_ref[j], from_row_b_ref[j])
        store(0, j + 1, low * in_low_x)
        store(3, j + 1, high * in_high_x)
    for i in range(2):
        low, high = pick(odd_y, from_side_a_ref[i], from_side_b_ref[i])
        store(i + 1, 0, low * in_low_y)
        store(i + 1, wide - 1, high * in_high_y)
    for place, j, inside in ((0, 0, in_low_y), (1, wide - 1, in_high_y)):
        low, high = pick(odd_x, from_corner_a_ref[place], from_corner_b_ref[place])
        store(0, j, low * (in_low_x * inside))
        store(3, j, high * (in_high_x * inside))
    for copy in copies:
        copy.wait()
    for tile in range(2 * count_y):
        i, j = tile // count_y, tile % count_y
        own = own_tile(i, j)
        total = 4.0 * own[:block] + own[block:]
        for k in range(neighbours_ref.shape[1]):
            source, kind = source_and_kind(neighbours_ref, kinds_ref, tile, k, count_y)
            pair = mul(ext_ref[source], table_ref[kind])
            total = total + (pair[:block, :side] + (pair[block:, :side] + pair[:block, side:]))
        total_ref[tile] = total
        span = slice(tile * side, (tile + 1) * side)
        parts_ref[:, span] = stacked(total)
        rest_tile = pick(odd_x, rest_a_ref[j], rest_b_ref[j])[i]
        basis_tile = jnp.concatenate([rest_tile, own[:block]], axis=0)
        prior_ref[0, :, span], prior_ref[1, :, span] = split(basis_tile)
    partial = pair_sum(parts_ref[...], prior_ref[0], prior_ref[1])
    for j in range(count_y):
        residual_a_ref[j], residual_b_ref[j] = pick(
            odd_x, total_ref[j], total_ref[count_y + j]
        )
    residual_a_ref[count_y] = partial
    partial_ref[...] = partial


def prepare_kernel(
    flags_ref,
    rest_a_ref,
    rest_b_ref,
    from_rest_a_ref,
    from_rest_b_ref,
    rest_side_a_ref,
    rest_side_b_ref,
    current_ref,
    stiff_ref,
    mass_ref,
    basis_ref,
    prior_ref,
    table_ref,
):
    count_y, rest, side = rest_a_ref.shape
    wide = count_y + 2
    prior = rest + current_ref.shape[1]
    odd_y, odd_x = flag_at(flags_ref, 0), flag_at(flags_ref, 1)
    split_tables(stiff_ref, mass_ref, table_ref, 0)
    for j in range(wide):
        if 0 < j < wide - 1:
            rests = list(pick(odd_x, from_rest_a_ref[j - 1], from_rest_b_ref[j - 1]))
            rests[1:1] = pick(odd_x, rest_a_ref[j - 1], rest_b_ref[j - 1])
        else:
            rests = [
                pick(odd_y, rest_side_a_ref[i], rest_side_b_ref[i])[j // (wide - 1)]
                for i in range(4)
            ]
        for i in range(4):
            place = i * wide + j
            high, low = split(jnp.concatenate([rests[i], current_ref[place]], axis=0))
            columns = slice(j * side, (j + 1) * side)
            basis_ref[i, :prior, columns] = high
            basis_ref[i, prior:, columns] = low
            if 0 < i < 3 and 0 < j < wide - 1:
                tile = (i - 1) * count_y + j - 1
                span = slice(tile * side, (tile + 1) * side)
                prior_ref[0, :, span] = high
                prior_ref[1, :, span] = low


def operators_kernel(
    inverse_rows,
    neighbours_hbm_ref,
    kinds_hbm_ref,
    flags_ref,
    partial_ref,
    row_a_ref,
    row_b_ref,
    from_row_a_ref,
    from_row_b_ref,
    from_side_a_ref,
    from_side_b_ref,
    basis_ref,
    prior_ref,
    table_ref,
    weighted_low_ref,
    weighted_high_ref,
    sent_ref,
    kept_ref,
    ext_ref,
    neighbours_ref,
    kinds_ref,
    semaphores,
    parts_ref,
):
    copies = code_copies(
        (neighbours_hbm_ref, kinds_hbm_ref), (neighbours_ref, kinds_ref), semaphores
    )
    for copy in copies:
        copy.start()
    count_y, block, side = weighted_low_ref.shape
    wide = count_y + 2
    odd_y, odd_x, in_low_y, in_high_y, in_low_x, in_high_x = (
        flag_at(flags_ref, place) for place in range(6)
    )
    coupling_deep = deep(partial_ref[...] * inverse_rows)

    for i in range(4):
        moved = halves_sum(mul(coupling_deep, basis_ref[i]))
        for j in range(wide):
            if 0 < j < wide - 1:
                rows = list(pick(odd_x, from_row_a_ref[j - 1], from_row_b_ref[j - 1]))
                rows[1:1] = pick(odd_x, row_a_ref[j - 1], row_b_ref[j - 1])
                value = rows[i]
            else:
                value = pick(odd_y, from_side_a_ref[i], from_side_b_ref[i])[j // (wide - 1)]
            value = value - moved[:, j * side : (j + 1) * side]
            if i == 0:
                value = value * in_low_x
            if i == 3:
                value = value * in_high_x
            if j == 0:
                value = value * in_low_y
            if j == wide - 1:
                value = value * in_high_y
            if 0 < i < 3 and 0 < j < wide - 1:
                (weighted_low_ref, weighted_high_ref)[i - 1][j - 1] = value
            ext_ref[i * wide + j] = deep(value)
    for copy in copies:
        copy.wait()
    for tile in range(2 * count_y):
        i, j = tile // count_y, tile % count_y
        own = (weighted_low_ref, weighted_high_ref)[i][j]
        totals = jnp.concatenate([4.0 * own, own], axis=1)
        for k in range(neighbours_ref.shape[1]):
            source, kind = source_and_kind(neighbours_ref, kinds_ref, tile, k, count_y)
            totals = totals + halves_sum(mul(ext_ref[source], table_ref[kind]))
        rows = jnp.concatenate([totals[:, :side], totals[:, side:], own, own], axis=0)
        span = slice(tile * side, (tile + 1) * side)
        parts_ref[0, :, span], parts_ref[1, :, span] = split(rows)
    applied = [parts_ref[part, : 2 * block, :] for part in range(2)]
    own_parts = [parts_ref[part, 2 * block : 3 * block, :] for part in range(2)]
    with_basis = mul_t(applied[0], prior_ref[0]) + (
        mul_t(applied[0], prior_ref[1]) + mul_t(applied[1], prior_ref[0])
    )
    with_own = mul_t(own_parts[0], parts_ref[0]) + (
        mul_t(own_parts[0], parts_ref[1]) + mul_t(own_parts[1], parts_ref[0])
    )
    halves = [
        jnp.concatenate(
            [
                with_basis[part * block : (part + 1) * block],
                folded(with_own[:, part * block : (part + 1) * block]),
                folded(with_own[:, 2 * block : 3 * block]),
            ],
            axis=0,
        )
        for part in range(2)
    ]
    sent_ref[...], kept_ref[...] = pick(odd_y, halves[0], halves[1])


def folded(square):
    return jnp.concatenate([square[n * 8 : (n + 1) * 8] for n in range(4)], axis=1)


def unfolded(rows):
    return jnp.concatenate([rows[:, n * 32 : (n + 1) * 32] for n in range(4)], axis=0)


def factor_kernel(inverse_rows, sums_ref, work_ref):
    block = work_ref.shape[0]
    gram = unfolded(sums_ref[block + 8 :, :]) * inverse_rows
    row_ids = lax.broadcasted_iota(jnp.int32, (block, block), 0)
    column_ids = lax.broadcasted_iota(jnp.int32, (block, block), 1)
    unit = jnp.where(row_ids == column_ids, 1.0, 0.0).astype(F32)
    rest = jnp.concatenate([gram, unit], axis=1)
    group = 8
    done = []
    for j in range(0, block, group):
        rows = lax.broadcasted_iota(jnp.int32, rest.shape, 0)
        columns = [
            jnp.broadcast_to(rest[:, j + a : j + a + 1], rest.shape) for a in range(group)
        ]
        pivots = [rest[a : a + 1, :] for a in range(group)]
        for a in range(group):
            ratio = columns[a] * (1.0 / columns[a][a : a + 1, :])
            for b in range(a + 1, group):
                columns[b] = columns[b] - ratio * columns[b][a : a + 1, :]
                pivots[b] = pivots[b] - ratio[b : b + 1, :] * pivots[a]
            rest = rest - jnp.where(rows > a, ratio, 0.0) * pivots[a]
        done.append(rest[:group])
        rest = rest[group:]
    work = jnp.concatenate(done, axis=0)
    work = work * lax.rsqrt(jnp.sum(work[:, :block] * unit, axis=1, keepdims=True))
    work_ref[...] = work


def finish_kernel(
    inverse_rows,
    flags_ref,
    work_ref,
    sums_ref,
    other_ref,
    partial_ref,
    weighted_low_ref,
    weighted_high_ref,
    new_ref,
    coupling_ref,
    factor_ref,
    reduced_ref,
):
    coupling_ref[...] = partial_ref[...] * inverse_rows
    count_y, block, _ = weighted_low_ref.shape
    prior = sums_ref.shape[1]
    tiles = 2 * count_y
    row_ids = lax.broadcasted_iota(jnp.int32, (block, block), 0)
    column_ids = lax.broadcasted_iota(jnp.int32, (block, block), 1)
    factor_ref[...] = jnp.where(column_ids >= row_ids, work_ref[:, :block], 0.0)
    inverse = work_ref[:, block:]
    inverse_deep = deep(inverse)
    for tile in range(tiles):
        own = (weighted_low_ref, weighted_high_ref)[tile // count_y][tile % count_y]
        new_ref[pl.ds(tile, block, stride=tiles), :] = mul_deep(inverse_deep, own)
    odd_y = flag_at(flags_ref, 0)
    halves = pick(odd_y, other_ref[...], sums_ref[: block + 8, :])
    for part, half in enumerate(halves):
        reduced_ref[part, :, :prior] = mul_deep(inverse_deep, half[:block] * inverse_rows)
        own = unfolded(half[block:]) * inverse_rows
        reduced_ref[part, :, prior:] = mul3_t(mul3_t(inverse, own), inverse)


def swap(value, mask):
    axes = ("px", "py")
    pairs = [(i, i ^ mask) for i in range(lax.axis_size(axes))]
    return lax.ppermute(value, axes, pairs)


def exchange(message_a, message_b, axis):
    cases, count = lax.axis_size("case"), lax.axis_size(axis)
    near = [(i, i ^ 1) for i in range(count)]
    pairs = []
    for case in range(cases):
        for i in range(count):
            j = ((i + 1) ^ 1) - 1
            target = (case, j) if 0 <= j < count else ((case ^ 1) % cases, i)
            pairs.append((case * count + i, target[0] * count + target[1]))
    return lax.ppermute(message_a, axis, near), lax.ppermute(message_b, ("case", axis), pairs)


def total_over(value, first, last):
    while first < last:
        value = value + swap(value, first)
        first *= 2
    return value


def half_total(sent, kept):
    kept = kept + swap(sent, 1)
    kept = (kept + swap(kept, 2)) + (swap(kept, 4) + swap(kept, 6))
    return total_over(kept, 8, lax.axis_size(("px", "py")))


def shape(*dims, dtype=F32):
    return jax.ShapeDtypeStruct(dims, dtype)


def shards(prior_basis, previous, neighbours, tile_kinds, stiff_tiles, mass_tiles):
    block = previous.shape[0]
    prior, count_x, count_y, side = prior_basis.shape
    tiles = count_x * count_y
    wide = count_y + 2
    rest = prior - block
    kinds = stiff_tiles.shape[0]
    inverse_rows = 1.0 / (tiles * side * lax.axis_size("px") * lax.axis_size("py"))
    basis = prior_basis.reshape(-1, side)
    vectors = jnp.concatenate([basis, previous.reshape(-1, side)], axis=0)
    codes = [array.transpose(1, 2, 0).reshape(tiles, -1) for array in (neighbours, tile_kinds)]
    code_scratch = [pltpu.SMEM(array.shape, jnp.int32) for array in codes]
    code_scratch += [pltpu.SemaphoreType.DMA((2,))]
    at_y, at_x = lax.axis_index("py"), lax.axis_index("px")
    bits = (at_y & 1) + 2 * (at_x & 1)
    bits += 4 * (at_y > 0) + 8 * (at_y < lax.axis_size("py") - 1)
    bits += 16 * (at_x > 0) + 32 * (at_x < lax.axis_size("px") - 1)
    flags = ((bits >> lax.broadcasted_iota(jnp.int32, (8, side), 0)) & 1).astype(F32)

    def call(kernel, inputs, outputs, scratch=(), plain=0, limit=8, cost=None):
        specs = [ANY] * plain + [VMEM] * (len(inputs) - plain)
        return pl.pallas_call(
            kernel,
            out_shape=outputs,
            in_specs=specs,
            out_specs=[VMEM] * len(outputs),
            scratch_shapes=scratch,
            compiler_params=pltpu.CompilerParams(vmem_limit_bytes=limit * MIB),
            cost_estimate=cost,
        )(*inputs)

    side_a, side_b, row_a, row_b = call(
        pack_kernel,
        (flags, vectors),
        [shape(count_x, 2 * block, side)] * 2 + [shape(count_y, 2 * block, side)] * 2,
    )
    rest_a, rest_b = call(rest_kernel, (flags, vectors), [shape(count_y, rest, side)] * 2)
    from_side_a, from_side_b = exchange(side_a, side_b, "py")
    from_row_a, from_row_b = exchange(row_a, row_b, "px")
    from_side_a, rest_a, rest_b = lax.optimization_barrier((from_side_a, rest_a, rest_b))
    from_rest_a, from_rest_b = exchange(rest_a, rest_b, "px")
    corner_a, corner_b = call(
        corners_kernel,
        (flags, from_side_a, from_side_b),
        [shape(2, 2 * block, side)] * 2,
    )
    from_corner_a, from_corner_b = exchange(corner_a, corner_b, "px")
    rest_side_a, rest_side_b = call(
        columns_kernel,
        (flags, rest_a, rest_b, from_rest_a, from_rest_b),
        [shape(4, rest, side)] * 2,
    )
    rest_side_a, rest_side_b = exchange(rest_side_a, rest_side_b, "py")
    residual_a, residual_b, partial, current = call(
        residual_kernel,
        (
            *codes,
            flags,
            row_a,
            row_b,
            from_row_a,
            from_row_b,
            from_side_a,
            from_side_b,
            from_corner_a,
            from_corner_b,
            rest_a,
            rest_b,
            stiff_tiles,
            mass_tiles,
        ),
        [shape(count_y + 1, block, side), shape(count_y, block, side)]
        + [shape(block, prior), shape(4 * wide, block, side)],
        [pltpu.VMEM((4 * wide, 2 * block, 2 * side), BF16)]
        + [pltpu.VMEM((kinds, 2 * side, 2 * side), BF16)]
        + code_scratch
        + [
            pltpu.VMEM((tiles, block, side), F32),
            pltpu.VMEM((2 * block, tiles * side), BF16),
            pltpu.VMEM((2, prior, tiles * side), BF16),
        ],
        plain=2,
        cost=pl.CostEstimate(flops=10**9, bytes_accessed=0, transcendentals=0),
    )
    count_py = lax.axis_size("py")
    from_row_a, from_row_b = exchange(residual_a, residual_b, "px")
    partial = total_over(
        partial + from_row_a[-1], 2 * count_py, count_py * lax.axis_size("px")
    )
    partial, rest_side_a, rest_side_b = lax.optimization_barrier(
        (partial, rest_side_a, rest_side_b)
    )
    side_a, side_b = call(
        columns_kernel,
        (flags, residual_a, residual_b, from_row_a, from_row_b, partial),
        [shape(5, block, side), shape(4, block, side)],
    )
    from_side_a, from_side_b = exchange(side_a, side_b, "py")
    partial = total_over(partial + from_side_a[-1], 2, count_py)
    basis_parts, prior_parts, table = call(
        prepare_kernel,
        (
            flags,
            rest_a,
            rest_b,
            from_rest_a,
            from_rest_b,
            rest_side_a,
            rest_side_b,
            current,
            stiff_tiles,
            mass_tiles,
        ),
        [shape(4, 2 * prior, wide * side, dtype=BF16)]
        + [shape(2, prior, tiles * side, dtype=BF16)]
        + [shape(kinds, 2 * side, 2 * side, dtype=BF16)],
        cost=pl.CostEstimate(flops=10**9, bytes_accessed=0, transcendentals=0),
    )
    weighted_low, weighted_high, sent, kept = call(
        functools.partial(operators_kernel, inverse_rows),
        (
            *codes,
            flags,
            partial,
            residual_a,
            residual_b,
            from_row_a,
            from_row_b,
            from_side_a,
            from_side_b,
            basis_parts,
            prior_parts,
            table,
        ),
        [shape(count_y, block, side)] * 2 + [shape(block + 16, prior)] * 2,
        [pltpu.VMEM((4 * wide, 2 * block, 2 * side), BF16)]
        + code_scratch
        + [pltpu.VMEM((2, 4 * block, tiles * side), BF16)],
        plain=2,
    )
    kept = half_total(sent, kept)
    other = swap(kept[: block + 8], 1)
    (work,) = call(
        functools.partial(factor_kernel, inverse_rows),
        (kept,),
        [shape(block, 2 * block)],
        cost=pl.CostEstimate(flops=10**9, bytes_accessed=0, transcendentals=0),
    )
    new_block, coupling, factor, reduced = call(
        functools.partial(finish_kernel, inverse_rows),
        (flags, work, kept, other, partial, weighted_low, weighted_high),
        [
            shape(block * tiles, side),
            shape(block, prior),
            shape(block, block),
            shape(2, block, prior + block),
        ],
    )
    return (
        new_block.reshape(previous.shape),
        coupling.T,
        factor,
        reduced.swapaxes(1, 2),
    )


def solution(mesh):
    placed = (
        P("case", "px", "py", None),
        P("case", "px", "py", None),
        P(None, "px", "py"),
        P(None, "px", "py"),
        P(),
        P(),
    )
    return jax.shard_map(
        shards,
        mesh=mesh,
        in_specs=placed,
        out_specs=(
            P("case", "px", "py", None),
            P("case", None),
            P("case", None),
            P("case", None, None),
        ),
        check_vma=False,
    )
```

```python
import functools

import jax
import jax.numpy as jnp
from jax import lax
from jax.experimental import pallas as pl
from jax.experimental.pallas import tpu as pltpu
from jax.sharding import PartitionSpec as P

F32 = jnp.float32
BF16 = jnp.bfloat16
VMEM = pl.BlockSpec(memory_space=pltpu.VMEM)
ANY = pl.BlockSpec(memory_space=pl.ANY)
MIB = 1024 * 1024


def split(value):
    high = value.astype(BF16)
    return high, (value - high.astype(F32)).astype(BF16)


def mul(left, right):
    return jnp.dot(left, right, preferred_element_type=F32)


def mul_t(left, right):
    return lax.dot_general(left, right, (((1,), (1,)), ((), ())), preferred_element_type=F32)


def mul3(left, right):
    left_high, left_low = split(left)
    right_high, right_low = split(right)
    return mul(left_high, right_high) + (mul(left_high, right_low) + mul(left_low, right_high))


def mul3_t(left, right):
    left_high, left_low = split(left)
    right_high, right_low = split(right)
    return mul_t(left_high, right_high) + (
        mul_t(left_high, right_low) + mul_t(left_low, right_high)
    )


def split_tables(stiff_ref, mass_ref, table_ref, parts_axis):
    side = stiff_ref.shape[1]
    spans = (slice(0, side), slice(side, 2 * side))
    for kind in range(stiff_ref.shape[0]):
        for matrix, ref in zip(spans, (stiff_ref, mass_ref)):
            for part, value in zip(spans, split(ref[kind])):
                if parts_axis == 1:
                    table_ref[kind, matrix, part] = value
                else:
                    table_ref[kind, part, matrix] = value


def stacked(value):
    return jnp.concatenate(split(value), axis=0)


def deep(value):
    high, low = split(value)
    upper = jnp.concatenate([high, high], axis=1)
    return jnp.concatenate([upper, jnp.concatenate([low, jnp.zeros_like(low)], axis=1)], axis=0)


def halves_sum(value):
    half = value.shape[0] // 2
    return value[:half] + value[half:]


def mul_deep(left_deep, right):
    return halves_sum(mul(left_deep, stacked(right)))


def pair_sum(left, right_high, right_low):
    rows = left.shape[0] // 2
    return halves_sum(mul_t(left, right_high)) + mul_t(left[:rows], right_low)


def pick(flag, first, second):
    flag = flag > 0.0
    return jnp.where(flag, first, second), jnp.where(flag, second, first)


def flag_at(flags_ref, place):
    return flags_ref[place : place + 1, :]


def code_copies(code_refs, local_refs, semaphores):
    return [
        pltpu.make_async_copy(ref, local, semaphores.at[n])
        for n, (ref, local) in enumerate(zip(code_refs, local_refs))
    ]


def source_and_kind(neighbours_ref, kinds_ref, tile, k, count_y):
    neighbour = neighbours_ref[tile, k]
    down = (neighbour * 11) >> 5
    first = (tile // count_y) * (count_y + 2) + tile % count_y
    return first + neighbour + down * (count_y - 1), kinds_ref[tile, k]


def pack_kernel(flags_ref, vectors_ref, side_a_ref, side_b_ref, row_a_ref, row_b_ref):
    count_y, both, _ = row_a_ref.shape
    tiles = 2 * count_y
    odd_y, odd_x = flag_at(flags_ref, 0), flag_at(flags_ref, 1)

    first = vectors_ref.shape[0] - both * tiles

    def tile_of(i, j):
        return vectors_ref[pl.ds(first + i * count_y + j, both, stride=tiles), :]

    for i in range(2):
        side_a_ref[i], side_b_ref[i] = pick(odd_y, tile_of(i, 0), tile_of(i, count_y - 1))
    for j in range(count_y):
        row_a_ref[j], row_b_ref[j] = pick(odd_x, tile_of(0, j), tile_of(1, j))


def rest_kernel(flags_ref, vectors_ref, rest_a_ref, rest_b_ref):
    count_y, rest, _ = rest_a_ref.shape
    odd_x = flag_at(flags_ref, 1)
    for j in range(count_y):
        rest_a_ref[j], rest_b_ref[j] = pick(
            odd_x,
            vectors_ref[pl.ds(j, rest, stride=2 * count_y), :],
            vectors_ref[pl.ds(count_y + j, rest, stride=2 * count_y), :],
        )


def corners_kernel(flags_ref, side_a_ref, side_b_ref, corner_a_ref, corner_b_ref):
    odd_y, odd_x = flag_at(flags_ref, 0), flag_at(flags_ref, 1)
    ends = [pick(odd_y, side_a_ref[i], side_b_ref[i]) for i in range(2)]
    for place in range(2):
        corner_a_ref[place], corner_b_ref[place] = pick(odd_x, ends[0][place], ends[1][place])


def columns_kernel(
    flags_ref, row_a_ref, row_b_ref, from_row_a_ref, from_row_b_ref, *refs
):
    odd_y, odd_x = flag_at(flags_ref, 0), flag_at(flags_ref, 1)
    side_a_ref, side_b_ref = refs[-2:]
    columns = []
    for j in (0, row_b_ref.shape[0] - 1):
        column = list(pick(odd_x, from_row_a_ref[j], from_row_b_ref[j]))
        column[1:1] = pick(odd_x, row_a_ref[j], row_b_ref[j])
        columns.append(column)
    for i in range(4):
        side_a_ref[i], side_b_ref[i] = pick(odd_y, columns[0][i], columns[1][i])
    if len(refs) == 3:
        side_a_ref[4] = refs[0][...]


def residual_kernel(
    neighbours_hbm_ref,
    kinds_hbm_ref,
    flags_ref,
    row_a_ref,
    row_b_ref,
    from_row_a_ref,
    from_row_b_ref,
    from_side_a_ref,
    from_side_b_ref,
    from_corner_a_ref,
    from_corner_b_ref,
    rest_a_ref,
    rest_b_ref,
    stiff_ref,
    mass_ref,
    residual_a_ref,
    residual_b_ref,
    partial_ref,
    current_ref,
    ext_ref,
    table_ref,
    neighbours_ref,
    kinds_ref,
    semaphores,
    total_ref,
    parts_ref,
    prior_ref,
):
    copies = code_copies(
        (neighbours_hbm_ref, kinds_hbm_ref), (neighbours_ref, kinds_ref), semaphores
    )
    for copy in copies:
        copy.start()
    split_tables(stiff_ref, mass_ref, table_ref, 1)
    count_y, both, side = row_a_ref.shape
    wide = count_y + 2
    block = both // 2
    rest = rest_a_ref.shape[1]
    odd_y, odd_x, in_low_y, in_high_y, in_low_x, in_high_x = (
        flag_at(flags_ref, place) for place in range(6)
    )

    def store(i, j, value):
        current_ref[i * wide + j] = value[:block]
        for part in range(2):
            high, low = split(value[part * block : (part + 1) * block])
            ext_ref[i * wide + j, :block, part * side : (part + 1) * side] = high
            ext_ref[i * wide + j, block:, part * side : (part + 1) * side] = low

    def own_tile(i, j):
        return pick(odd_x, row_a_ref[j], row_b_ref[j])[i]

    for j in range(count_y):
        store(1, j + 1, own_tile(0, j))
        store(2, j + 1, own_tile(1, j))
        low, high = pick(odd_x, from_row_a_ref[j], from_row_b_ref[j])
        store(0, j + 1, low * in_low_x)
        store(3, j + 1, high * in_high_x)
    for i in range(2):
        low, high = pick(odd_y, from_side_a_ref[i], from_side_b_ref[i])
        store(i + 1, 0, low * in_low_y)
        store(i + 1, wide - 1, high * in_high_y)
    for place, j, inside in ((0, 0, in_low_y), (1, wide - 1, in_high_y)):
        low, high = pick(odd_x, from_corner_a_ref[place], from_corner_b_ref[place])
        store(0, j, low * (in_low_x * inside))
        store(3, j, high * (in_high_x * inside))
    for copy in copies:
        copy.wait()
    for tile in range(2 * count_y):
        i, j = tile // count_y, tile % count_y
        own = own_tile(i, j)
        total = 4.0 * own[:block] + own[block:]
        for k in range(neighbours_ref.shape[1]):
            source, kind = source_and_kind(neighbours_ref, kinds_ref, tile, k, count_y)
            pair = mul(ext_ref[source], table_ref[kind])
            total = total + (pair[:block, :side] + (pair[block:, :side] + pair[:block, side:]))
        total_ref[tile] = total
        span = slice(tile * side, (tile + 1) * side)
        parts_ref[:, span] = stacked(total)
        rest_tile = pick(odd_x, rest_a_ref[j], rest_b_ref[j])[i]
        basis_tile = jnp.concatenate([rest_tile, own[:block]], axis=0)
        prior_ref[0, :, span], prior_ref[1, :, span] = split(basis_tile)
    partial = pair_sum(parts_ref[...], prior_ref[0], prior_ref[1])
    for j in range(count_y):
        residual_a_ref[j], residual_b_ref[j] = pick(
            odd_x, total_ref[j], total_ref[count_y + j]
        )
    residual_a_ref[count_y] = partial
    partial_ref[...] = partial


def prepare_kernel(
    flags_ref,
    rest_a_ref,
    rest_b_ref,
    from_rest_a_ref,
    from_rest_b_ref,
    rest_side_a_ref,
    rest_side_b_ref,
    current_ref,
    stiff_ref,
    mass_ref,
    basis_ref,
    prior_ref,
    table_ref,
):
    count_y, rest, side = rest_a_ref.shape
    wide = count_y + 2
    prior = rest + current_ref.shape[1]
    odd_y, odd_x = flag_at(flags_ref, 0), flag_at(flags_ref, 1)
    split_tables(stiff_ref, mass_ref, table_ref, 0)
    for j in range(wide):
        if 0 < j < wide - 1:
            rests = list(pick(odd_x, from_rest_a_ref[j - 1], from_rest_b_ref[j - 1]))
            rests[1:1] = pick(odd_x, rest_a_ref[j - 1], rest_b_ref[j - 1])
        else:
            rests = [
                pick(odd_y, rest_side_a_ref[i], rest_side_b_ref[i])[j // (wide - 1)]
                for i in range(4)
            ]
        for i in range(4):
            place = i * wide + j
            high, low = split(jnp.concatenate([rests[i], current_ref[place]], axis=0))
            columns = slice(j * side, (j + 1) * side)
            basis_ref[i, :prior, columns] = high
            basis_ref[i, prior:, columns] = low
            if 0 < i < 3 and 0 < j < wide - 1:
                tile = (i - 1) * count_y + j - 1
                span = slice(tile * side, (tile + 1) * side)
                prior_ref[0, :, span] = high
                prior_ref[1, :, span] = low


def operators_kernel(
    inverse_rows,
    neighbours_hbm_ref,
    kinds_hbm_ref,
    flags_ref,
    partial_ref,
    row_a_ref,
    row_b_ref,
    from_row_a_ref,
    from_row_b_ref,
    from_side_a_ref,
    from_side_b_ref,
    basis_ref,
    prior_ref,
    table_ref,
    weighted_low_ref,
    weighted_high_ref,
    sent_ref,
    kept_ref,
    ext_ref,
    neighbours_ref,
    kinds_ref,
    semaphores,
    parts_ref,
):
    copies = code_copies(
        (neighbours_hbm_ref, kinds_hbm_ref), (neighbours_ref, kinds_ref), semaphores
    )
    for copy in copies:
        copy.start()
    count_y, block, side = weighted_low_ref.shape
    wide = count_y + 2
    odd_y, odd_x, in_low_y, in_high_y, in_low_x, in_high_x = (
        flag_at(flags_ref, place) for place in range(6)
    )
    coupling_deep = deep(partial_ref[...] * inverse_rows)

    for i in range(4):
        moved = halves_sum(mul(coupling_deep, basis_ref[i]))
        for j in range(wide):
            if 0 < j < wide - 1:
                rows = list(pick(odd_x, from_row_a_ref[j - 1], from_row_b_ref[j - 1]))
                rows[1:1] = pick(odd_x, row_a_ref[j - 1], row_b_ref[j - 1])
                value = rows[i]
            else:
                value = pick(odd_y, from_side_a_ref[i], from_side_b_ref[i])[j // (wide - 1)]
            value = value - moved[:, j * side : (j + 1) * side]
            if i == 0:
                value = value * in_low_x
            if i == 3:
                value = value * in_high_x
            if j == 0:
                value = value * in_low_y
            if j == wide - 1:
                value = value * in_high_y
            if 0 < i < 3 and 0 < j < wide - 1:
                (weighted_low_ref, weighted_high_ref)[i - 1][j - 1] = value
            ext_ref[i * wide + j] = deep(value)
    for copy in copies:
        copy.wait()
    for tile in range(2 * count_y):
        i, j = tile // count_y, tile % count_y
        own = (weighted_low_ref, weighted_high_ref)[i][j]
        totals = jnp.concatenate([4.0 * own, own], axis=1)
        for k in range(neighbours_ref.shape[1]):
            source, kind = source_and_kind(neighbours_ref, kinds_ref, tile, k, count_y)
            totals = totals + halves_sum(mul(ext_ref[source], table_ref[kind]))
        rows = jnp.concatenate([totals[:, :side], totals[:, side:], own, own], axis=0)
        span = slice(tile * side, (tile + 1) * side)
        parts_ref[0, :, span], parts_ref[1, :, span] = split(rows)
    applied = [parts_ref[part, : 2 * block, :] for part in range(2)]
    own_parts = [parts_ref[part, 2 * block : 3 * block, :] for part in range(2)]
    with_basis = mul_t(applied[0], prior_ref[0]) + (
        mul_t(applied[0], prior_ref[1]) + mul_t(applied[1], prior_ref[0])
    )
    with_own = mul_t(own_parts[0], parts_ref[0]) + (
        mul_t(own_parts[0], parts_ref[1]) + mul_t(own_parts[1], parts_ref[0])
    )
    halves = [
        jnp.concatenate(
            [
                with_basis[part * block : (part + 1) * block],
                folded(with_own[:, part * block : (part + 1) * block]),
                folded(with_own[:, 2 * block : 3 * block]),
            ],
            axis=0,
        )
        for part in range(2)
    ]
    sent_ref[...], kept_ref[...] = pick(odd_y, halves[0], halves[1])


def folded(square):
    return jnp.concatenate([square[n * 8 : (n + 1) * 8] for n in range(4)], axis=1)


def unfolded(rows):
    return jnp.concatenate([rows[:, n * 32 : (n + 1) * 32] for n in range(4)], axis=0)


def factor_kernel(inverse_rows, sums_ref, work_ref):
    block = work_ref.shape[0]
    gram = unfolded(sums_ref[block + 8 :, :]) * inverse_rows
    row_ids = lax.broadcasted_iota(jnp.int32, (block, block), 0)
    column_ids = lax.broadcasted_iota(jnp.int32, (block, block), 1)
    unit = jnp.where(row_ids == column_ids, 1.0, 0.0).astype(F32)
    rest = jnp.concatenate([gram, unit], axis=1)
    group = 8
    done = []
    for j in range(0, block, group):
        rows = lax.broadcasted_iota(jnp.int32, rest.shape, 0)
        columns = [
            jnp.broadcast_to(rest[:, j + a : j + a + 1], rest.shape) for a in range(group)
        ]
        pivots = [rest[a : a + 1, :] for a in range(group)]
        for a in range(group):
            ratio = columns[a] * (1.0 / columns[a][a : a + 1, :])
            for b in range(a + 1, group):
                columns[b] = columns[b] - ratio * columns[b][a : a + 1, :]
                pivots[b] = pivots[b] - ratio[b : b + 1, :] * pivots[a]
            rest = rest - jnp.where(rows > a, ratio, 0.0) * pivots[a]
        done.append(rest[:group])
        rest = rest[group:]
    work = jnp.concatenate(done, axis=0)
    work = work * lax.rsqrt(jnp.sum(work[:, :block] * unit, axis=1, keepdims=True))
    work_ref[...] = work


def finish_kernel(
    inverse_rows,
    flags_ref,
    work_ref,
    sums_ref,
    other_ref,
    partial_ref,
    weighted_low_ref,
    weighted_high_ref,
    new_ref,
    coupling_ref,
    factor_ref,
    reduced_ref,
):
    coupling_ref[...] = partial_ref[...] * inverse_rows
    count_y, block, _ = weighted_low_ref.shape
    prior = sums_ref.shape[1]
    tiles = 2 * count_y
    row_ids = lax.broadcasted_iota(jnp.int32, (block, block), 0)
    column_ids = lax.broadcasted_iota(jnp.int32, (block, block), 1)
    factor_ref[...] = jnp.where(column_ids >= row_ids, work_ref[:, :block], 0.0)
    inverse = work_ref[:, block:]
    inverse_deep = deep(inverse)
    for tile in range(tiles):
        own = (weighted_low_ref, weighted_high_ref)[tile // count_y][tile % count_y]
        new_ref[pl.ds(tile, block, stride=tiles), :] = mul_deep(inverse_deep, own)
    odd_y = flag_at(flags_ref, 0)
    halves = pick(odd_y, other_ref[...], sums_ref[: block + 8, :])
    for part, half in enumerate(halves):
        reduced_ref[part, :, :prior] = mul_deep(inverse_deep, half[:block] * inverse_rows)
        own = unfolded(half[block:]) * inverse_rows
        reduced_ref[part, :, prior:] = mul3_t(mul3_t(inverse, own), inverse)


def swap(value, mask):
    axes = ("px", "py")
    pairs = [(i, i ^ mask) for i in range(lax.axis_size(axes))]
    return lax.ppermute(value, axes, pairs)


def exchange(message_a, message_b, axis):
    cases, count = lax.axis_size("case"), lax.axis_size(axis)
    near = [(i, i ^ 1) for i in range(count)]
    pairs = []
    for case in range(cases):
        for i in range(count):
            j = ((i + 1) ^ 1) - 1
            target = (case, j) if 0 <= j < count else ((case ^ 1) % cases, i)
            pairs.append((case * count + i, target[0] * count + target[1]))
    return lax.ppermute(message_a, axis, near), lax.ppermute(message_b, ("case", axis), pairs)


def total_over(value, first, last):
    while first < last:
        value = value + swap(value, first)
        first *= 2
    return value


def half_total(sent, kept):
    kept = kept + swap(sent, 1)
    kept = (kept + swap(kept, 6)) + (swap(kept, 2) + swap(kept, 4))
    return total_over(kept, 8, lax.axis_size(("px", "py")))


def shape(*dims, dtype=F32):
    return jax.ShapeDtypeStruct(dims, dtype)


def shards(prior_basis, previous, neighbours, tile_kinds, stiff_tiles, mass_tiles):
    block = previous.shape[0]
    prior, count_x, count_y, side = prior_basis.shape
    tiles = count_x * count_y
    wide = count_y + 2
    rest = prior - block
    kinds = stiff_tiles.shape[0]
    inverse_rows = 1.0 / (tiles * side * lax.axis_size("px") * lax.axis_size("py"))
    basis = prior_basis.reshape(-1, side)
    vectors = jnp.concatenate([basis, previous.reshape(-1, side)], axis=0)
    codes = [array.transpose(1, 2, 0).reshape(tiles, -1) for array in (neighbours, tile_kinds)]
    code_scratch = [pltpu.SMEM(array.shape, jnp.int32) for array in codes]
    code_scratch += [pltpu.SemaphoreType.DMA((2,))]
    at_y, at_x = lax.axis_index("py"), lax.axis_index("px")
    bits = (at_y & 1) + 2 * (at_x & 1)
    bits += 4 * (at_y > 0) + 8 * (at_y < lax.axis_size("py") - 1)
    bits += 16 * (at_x > 0) + 32 * (at_x < lax.axis_size("px") - 1)
    flags = ((bits >> lax.broadcasted_iota(jnp.int32, (8, side), 0)) & 1).astype(F32)

    def call(kernel, inputs, outputs, scratch=(), plain=0, limit=8, cost=None):
        specs = [ANY] * plain + [VMEM] * (len(inputs) - plain)
        return pl.pallas_call(
            kernel,
            out_shape=outputs,
            in_specs=specs,
            out_specs=[VMEM] * len(outputs),
            scratch_shapes=scratch,
            compiler_params=pltpu.CompilerParams(vmem_limit_bytes=limit * MIB),
            cost_estimate=cost,
        )(*inputs)

    side_a, side_b, row_a, row_b = call(
        pack_kernel,
        (flags, vectors),
        [shape(count_x, 2 * block, side)] * 2 + [shape(count_y, 2 * block, side)] * 2,
    )
    rest_a, rest_b = call(rest_kernel, (flags, vectors), [shape(count_y, rest, side)] * 2)
    from_side_a, from_side_b = exchange(side_a, side_b, "py")
    from_row_a, from_row_b = exchange(row_a, row_b, "px")
    from_side_a, rest_a, rest_b = lax.optimization_barrier((from_side_a, rest_a, rest_b))
    from_rest_a, from_rest_b = exchange(rest_a, rest_b, "px")
    corner_a, corner_b = call(
        corners_kernel,
        (flags, from_side_a, from_side_b),
        [shape(2, 2 * block, side)] * 2,
    )
    from_corner_a, from_corner_b = exchange(corner_a, corner_b, "px")
    rest_side_a, rest_side_b = call(
        columns_kernel,
        (flags, rest_a, rest_b, from_rest_a, from_rest_b),
        [shape(4, rest, side)] * 2,
    )
    rest_side_a, rest_side_b = exchange(rest_side_a, rest_side_b, "py")
    residual_a, residual_b, partial, current = call(
        residual_kernel,
        (
            *codes,
            flags,
            row_a,
            row_b,
            from_row_a,
            from_row_b,
            from_side_a,
            from_side_b,
            from_corner_a,
            from_corner_b,
            rest_a,
            rest_b,
            stiff_tiles,
            mass_tiles,
        ),
        [shape(count_y + 1, block, side), shape(count_y, block, side)]
        + [shape(block, prior), shape(4 * wide, block, side)],
        [pltpu.VMEM((4 * wide, 2 * block, 2 * side), BF16)]
        + [pltpu.VMEM((kinds, 2 * side, 2 * side), BF16)]
        + code_scratch
        + [
            pltpu.VMEM((tiles, block, side), F32),
            pltpu.VMEM((2 * block, tiles * side), BF16),
            pltpu.VMEM((2, prior, tiles * side), BF16),
        ],
        plain=2,
        cost=pl.CostEstimate(flops=10**9, bytes_accessed=0, transcendentals=0),
    )
    count_py = lax.axis_size("py")
    from_row_a, from_row_b = exchange(residual_a, residual_b, "px")
    partial = total_over(
        partial + from_row_a[-1], 2 * count_py, count_py * lax.axis_size("px")
    )
    side_a, side_b = call(
        columns_kernel,
        (flags, residual_a, residual_b, from_row_a, from_row_b, partial),
        [shape(5, block, side), shape(4, block, side)],
    )
    from_side_a, from_side_b = exchange(side_a, side_b, "py")
    from_side_a, rest_side_a, rest_side_b = lax.optimization_barrier(
        (from_side_a, rest_side_a, rest_side_b)
    )
    partial = total_over(partial + from_side_a[-1], 2, count_py)
    basis_parts, prior_parts, table = call(
        prepare_kernel,
        (
            flags,
            rest_a,
            rest_b,
            from_rest_a,
            from_rest_b,
            rest_side_a,
            rest_side_b,
            current,
            stiff_tiles,
            mass_tiles,
        ),
        [shape(4, 2 * prior, wide * side, dtype=BF16)]
        + [shape(2, prior, tiles * side, dtype=BF16)]
        + [shape(kinds, 2 * side, 2 * side, dtype=BF16)],
        cost=pl.CostEstimate(flops=10**9, bytes_accessed=0, transcendentals=0),
    )
    weighted_low, weighted_high, sent, kept = call(
        functools.partial(operators_kernel, inverse_rows),
        (
            *codes,
            flags,
            partial,
            residual_a,
            residual_b,
            from_row_a,
            from_row_b,
            from_side_a,
            from_side_b,
            basis_parts,
            prior_parts,
            table,
        ),
        [shape(count_y, block, side)] * 2 + [shape(block + 16, prior)] * 2,
        [pltpu.VMEM((4 * wide, 2 * block, 2 * side), BF16)]
        + code_scratch
        + [pltpu.VMEM((2, 4 * block, tiles * side), BF16)],
        plain=2,
    )
    kept = half_total(sent, kept)
    other = swap(kept[: block + 8], 1)
    (work,) = call(
        functools.partial(factor_kernel, inverse_rows),
        (kept,),
        [shape(block, 2 * block)],
        cost=pl.CostEstimate(flops=10**9, bytes_accessed=0, transcendentals=0),
    )
    new_block, coupling, factor, reduced = call(
        functools.partial(finish_kernel, inverse_rows),
        (flags, work, kept, other, partial, weighted_low, weighted_high),
        [
            shape(block * tiles, side),
            shape(block, prior),
            shape(block, block),
            shape(2, block, prior + block),
        ],
    )
    return (
        new_block.reshape(previous.shape),
        coupling.T,
        factor,
        reduced.swapaxes(1, 2),
    )


def solution(mesh):
    placed = (
        P("case", "px", "py", None),
        P("case", "px", "py", None),
        P(None, "px", "py"),
        P(None, "px", "py"),
        P(),
        P(),
    )
    return jax.shard_map(
        shards,
        mesh=mesh,
        in_specs=placed,
        out_specs=(
            P("case", "px", "py", None),
            P("case", None),
            P("case", None),
            P("case", None, None),
        ),
        check_vma=False,
    )
```
